32 devices in a mesh: lat: 4 (over z), lon: 8 (over y, x, core).
Axes of the slice: x: 2, y: 2, z: 4, core: 2. Of those that a mesh axis runs over, the one named last changes fastest.
Arguments:
- tokens: bfloat16 [72, 192, 1024], P('lat', 'lon'), may hold values from -6 to 6
- qkv_weight: bfloat16 [1024, 3072], replicated, may hold values from -1 to 1
- out_weight: bfloat16 [1024, 1024], replicated, may hold values from -0.1875 to 0.1875
- merge_weight: bfloat16 [4096, 2048], P(None, 'lon'), may hold values from -0.09375 to 0.09375
- up_weight: bfloat16 [2048, 8192], P(None, 'lon'), may hold values from -0.125 to 0.125
- down_weight: bfloat16 [8192, 2048], P('lon'), may hold values from -0.0625 to 0.0625
Outputs:
- middle_out: bfloat16 [72, 192, 1024], P('lat', 'lon')
- coarse_out: bfloat16 [36, 96, 2048], P('lat', 'lon')
The draws below stay inside these ranges and needn't reach their ends.
All inputs are finite; a program needn't handle non-finite values.
Results may differ from the reference program's by a relative error of at most 0.013.
Values may be sent and summed in bfloat16 or wider, within the bound.
No kernel may reach another device: no remote copies, remote signals or barrier semaphores. Data moves between devices by JAX's collectives and lax.ppermute only.
A program may use at most 128 MiB of HBM per device.

```python
import math
import jax
import jax.numpy as jnp
from jax import lax

D = 1024
DC = 2048
FF = 8192
HEADS = 16
WLAT = 6
WLON = 12
NLAT = 72
NLON = 192


def draw_qkv_weight(key, part):
    first = jax.random.fold_in(jax.random.fold_in(key, 17), 0)
    base = jax.random.normal(first, (D, 3 * D), jnp.float32) / math.sqrt(D)
    return jnp.clip(base, -1.0, 1.0).astype(jnp.bfloat16)


def steps_of(rng, extent, pieces, least, high):
    def one(axis_at, parts):
        draws = jax.random.uniform(jax.random.fold_in(jax.random.fold_in(rng, 6), axis_at), (parts,), jnp.float32, least / len(pieces), high / len(pieces))
        return jnp.repeat(jnp.exp(draws), extent[axis_at] // parts).reshape((-1,) + (1,) * (len(extent) - axis_at - 1))

    factor_of = one(*pieces[0])
    for cut in pieces[1:]:
        factor_of = factor_of * one(*cut)
    return factor_of


def gaussian(rng, dims, scale, most, cuts=(), kind=jnp.bfloat16):
    loudness = steps_of(rng, dims, cuts, -0.22, 0.18) if cuts else 1.0
    array = jax.random.normal(rng, dims, jnp.float32) * scale * loudness
    return jnp.minimum(jnp.maximum(array, -most), most).astype(kind)


def setup_inputs(seed: int = 0) -> dict:
    seeds = jax.random.split(jax.random.key(seed), 7)
    tokens = gaussian(seeds[0], (NLAT, NLON, D), 1.0, 6.0, ((0, 4), (1, 8)))
    qkv_weight = draw_qkv_weight(jax.random.fold_in(seeds[6], 71), 0)
    out_weight = gaussian(seeds[2], (D, D), D ** -0.5, 0.1875)
    merge_weight = gaussian(seeds[3], (4 * D, DC), (4 * D) ** -0.5, 0.09375, ((1, 8),))
    up_weight = gaussian(seeds[4], (DC, FF), DC ** -0.5, 0.125, ((1, 8),))
    down_weight = gaussian(seeds[5], (FF, DC), FF ** -0.5, 0.0625, ((0, 8),))
    return dict(tokens=tokens, qkv_weight=qkv_weight, out_weight=out_weight, merge_weight=merge_weight, up_weight=up_weight, down_weight=down_weight)


def normalize(values):
    center = values - lax.optimization_barrier(jnp.mean(values, axis=-1, keepdims=True))
    spread = lax.optimization_barrier(jnp.mean(center * center, axis=-1, keepdims=True))
    return center * lax.rsqrt(spread + 1e-05)

def to_windows(grid):
    height, breadth, depth = grid.shape
    shaped = grid.reshape(height // WLAT, WLAT, breadth // WLON, WLON, depth)
    return shaped.transpose(0, 2, 1, 3, 4).reshape(-1, WLAT * WLON, depth)

def from_windows(windows, height, breadth):
    depth = windows.shape[-1]
    shaped = windows.reshape(height // WLAT, breadth // WLON, WLAT, WLON, depth)
    return shaped.transpose(0, 2, 1, 3, 4).reshape(height, breadth, depth)

def attend(query, keys, values, key_valid):
    scale = 1.0 / query.shape[-1] ** 0.5
    scores = jnp.einsum('wqhd,wkhd->whqk', query.astype(jnp.float32), keys.astype(jnp.float32)) * scale
    scores = jnp.where(key_valid[:, None, None, :], scores, jnp.float32(-1e+30))
    top = lax.optimization_barrier(jnp.max(scores, axis=-1, keepdims=True))
    raised = jnp.exp(scores - top)
    weights = (raised / lax.optimization_barrier(jnp.sum(raised, axis=-1, keepdims=True))).astype(jnp.bfloat16)
    summed = jnp.einsum('whqk,wkhd->wqhd', weights.astype(jnp.float32), values.astype(jnp.float32))
    return summed.astype(jnp.bfloat16)

def reference(tokens, qkv_weight, out_weight, merge_weight, up_weight, down_weight):
    nlat, nlon, width = tokens.shape
    rim_lat = WLAT // 2
    rim_lon = WLON // 2
    head_size = width // HEADS
    normed = normalize(tokens.astype(jnp.float32)).astype(jnp.bfloat16)
    projected = jnp.dot(normed.reshape(-1, width), qkv_weight, preferred_element_type=jnp.float32)
    projected = projected.astype(jnp.bfloat16).reshape(nlat, nlon, 3 * width)
    projected = jnp.roll(projected, rim_lon, axis=1)
    projected = jnp.pad(projected, ((rim_lat, rim_lat), (0, 0), (0, 0)))
    position = jnp.arange(nlat + 2 * rim_lat, dtype=jnp.int32) - rim_lat
    row_valid = (position >= 0) & (position < nlat)
    band_count = (nlat + 2 * rim_lat) // WLAT
    bands = projected.reshape(band_count, WLAT, nlon, 3 * width)
    band_valid = row_valid.reshape(band_count, WLAT)

    def one_band(item):
        band, valid = item
        windows = to_windows(band)
        count = windows.shape[0]
        flags = to_windows(jnp.broadcast_to(valid[:, None, None], (WLAT, nlon, 1)))[..., 0]
        split = windows.reshape(count, WLAT * WLON, 3, HEADS, head_size)
        result = attend(split[:, :, 0], split[:, :, 1], split[:, :, 2], flags)
        return from_windows(result.reshape(count, WLAT * WLON, width), WLAT, nlon)
    attended = lax.map(one_band, (bands, band_valid)).reshape(nlat + 2 * rim_lat, nlon, width)
    attended = jnp.roll(attended[rim_lat:rim_lat + nlat], -rim_lon, axis=1)
    mixed = jnp.dot(attended.reshape(-1, width), out_weight, preferred_element_type=jnp.float32)
    middle_out = (tokens.reshape(-1, width).astype(jnp.float32) + mixed).astype(jnp.bfloat16)
    middle_out = middle_out.reshape(nlat, nlon, width)
    patches = middle_out.reshape(nlat // 2, 2, nlon // 2, 2, width).transpose(0, 2, 1, 3, 4)
    merged = normalize(patches.reshape(-1, 4 * width).astype(jnp.float32)).astype(jnp.bfloat16)
    coarse = jnp.dot(merged, merge_weight, preferred_element_type=jnp.float32).astype(jnp.bfloat16)
    coarse_normed = normalize(coarse.astype(jnp.float32)).astype(jnp.bfloat16)
    hidden = jax.nn.gelu(jnp.dot(coarse_normed, up_weight, preferred_element_type=jnp.float32), approximate=False)
    hidden = hidden.astype(jnp.bfloat16)
    summed = jnp.dot(hidden, down_weight, preferred_element_type=jnp.float32)
    coarse_out = (coarse.astype(jnp.float32) + summed).astype(jnp.bfloat16)
    return (middle_out, coarse_out.reshape(nlat // 2, nlon // 2, -1))
```

```python
import functools

import jax
import jax.numpy as jnp
import numpy as np
from jax import lax
from jax.experimental import pallas as pl
from jax.experimental.pallas import tpu as pltpu
from jax.sharding import PartitionSpec as P

HEADS = 16
WLAT = 6
WLON = 12
RIM_LAT = WLAT // 2
RIM_LON = WLON // 2
SIDE = 8
GROUP = 4
F32 = jnp.float32
BF16 = jnp.bfloat16


def up16(n):
    return -(-n // 16) * 16


def params(mib=48, **kw):
    return pltpu.CompilerParams(vmem_limit_bytes=mib * 2**20, **kw)


class Bands:
    def __init__(self, rows, columns):
        assert (rows - WLAT) % WLAT == 0 and (columns - WLON) % WLON == 0
        self.rows, self.columns = rows, columns
        inner = (rows - WLAT) // WLAT
        self.height = [RIM_LAT] + [WLAT] * inner + [RIM_LAT]
        self.count = len(self.height)
        self.first = [sum(self.height[:b]) for b in range(self.count)]
        self.widths = [RIM_LON] + [WLON] * ((columns - WLON) // WLON) + [RIM_LON]
        self.own = [h * columns for h in self.height]
        self.own_padded = [up16(n) for n in self.own]
        self.own_at = [sum(self.own_padded[:b]) for b in range(self.count)]
        self.own_total = sum(self.own_padded)
        edge = RIM_LAT * (columns + 2 * SIDE)
        self.halo = [
            2 * h * SIDE + (edge if b in (0, self.count - 1) else 0)
            for b, h in enumerate(self.height)
        ]
        self.halo_padded = [up16(n) for n in self.halo]
        self.halo_at = [sum(self.halo_padded[:b]) for b in range(self.count)]
        self.halo_total = sum(self.halo_padded)
        self.keys = len(self.widths) * WLAT * WLON

    def source(self, b, i, j):
        columns, h, first = self.columns, self.height[b], self.first[b]
        if 0 <= i < self.rows:
            if 0 <= j < columns:
                return (i - first) * columns + j
            at = self.own_padded[b] + (i - first) * SIDE
            return at + (j + SIDE if j < 0 else h * SIDE + j - columns)
        at = self.own_padded[b] + 2 * h * SIDE
        i = i + RIM_LAT if i < 0 else i - self.rows
        if 0 <= j < columns:
            return at + i * columns + j
        at += RIM_LAT * columns + i * SIDE
        return at + (j + SIDE if j < 0 else RIM_LAT * SIDE + j - columns)

    def key_matrix(self, b):
        g = np.zeros((self.keys, self.own_padded[b] + self.halo_padded[b]), np.float32)
        top = self.first[b] - (RIM_LAT if b == 0 else 0)
        at = 0
        for c in range(len(self.widths)):
            for i in range(WLAT):
                for j in range(WLON):
                    g[at, self.source(b, top + i, c * WLON - RIM_LON + j)] = 1
                    at += 1
        return g.astype(BF16)

    def query_matrix(self, b):
        g = np.zeros((GROUP * self.own[b], self.own_padded[b]), np.float32)
        head = np.zeros((GROUP * self.own[b],), np.int32)
        at = left = 0
        for width in self.widths:
            for k in range(GROUP):
                for i in range(self.height[b]):
                    for j in range(width):
                        g[at, i * self.columns + left + j] = 1
                        head[at] = k
                        at += 1
            left += width
        return g.astype(BF16), head

    def patch_matrix(self):
        cells = self.rows * self.columns // 4
        padded = up16(cells)
        g = np.zeros((4 * padded, self.rows * self.columns), np.float32)
        for r in range(self.rows // 2):
            for c in range(self.columns // 2):
                for k in range(4):
                    to = k * padded + r * (self.columns // 2) + c
                    g[to, (2 * r + k // 2) * self.columns + 2 * c + k % 2] = 1
        return g.astype(BF16)


def normalize(values):
    center = values - jnp.mean(values, axis=-1, keepdims=True)
    spread = jnp.mean(center * center, axis=-1, keepdims=True)
    return center * lax.rsqrt(spread + 1e-05)


def own_kernel(bands, tokens_ref, weight_ref, out_ref, normed_ref):
    @pl.when(pl.program_id(0) == 0)
    def _():
        values = tokens_ref[...].astype(F32)
        normed = normalize(values.reshape(-1, values.shape[-1]))
        pieces = []
        for b in range(bands.count):
            at = bands.first[b] * bands.columns
            pieces.append(normed[at : at + bands.own[b]])
            if bands.own_padded[b] > bands.own[b]:
                pieces.append(jnp.zeros((bands.own_padded[b] - bands.own[b], normed.shape[1]), F32))
        normed_ref[...] = jnp.concatenate(pieces, axis=0).astype(BF16)

    out_ref[...] = jnp.dot(normed_ref[...], weight_ref[...], preferred_element_type=F32).astype(BF16)


def own_projection(bands, tokens, weight):
    rows, columns, width = tokens.shape
    out = weight.shape[1]
    block = 512
    return pl.pallas_call(
        functools.partial(own_kernel, bands),
        grid=(out // block,),
        in_specs=[
            pl.BlockSpec((rows, columns, width), lambda n: (0, 0, 0)),
            pl.BlockSpec((width, block), lambda n: (0, n)),
        ],
        out_specs=pl.BlockSpec((bands.own_total, block), lambda n: (0, n)),
        out_shape=jax.ShapeDtypeStruct((bands.own_total, out), BF16),
        scratch_shapes=[pltpu.VMEM((bands.own_total, width), BF16)],
        compiler_params=params(),
        cost_estimate=pl.CostEstimate(
            flops=2 * bands.own_total * width * out, bytes_accessed=2 * width * out, transcendentals=0
        ),
        name="own_projection",
    )(tokens, weight)


def halo_kernel(bands, *refs):
    *parts, weight_ref, out_ref, normed_ref = refs

    @pl.when(pl.program_id(0) == 0)
    def _():
        west, east, north, south, nw, ne, sw, se = [
            normalize(p[...].astype(F32).reshape(-1, p.shape[-1])) for p in parts
        ]
        pieces = []
        for b in range(bands.count):
            at, size = bands.first[b] * SIDE, bands.height[b] * SIDE
            pieces += [west[at : at + size], east[at : at + size]]
            if b == 0:
                pieces += [north, nw, ne]
            if b == bands.count - 1:
                pieces += [south, sw, se]
            if bands.halo_padded[b] > bands.halo[b]:
                pieces.append(jnp.zeros((bands.halo_padded[b] - bands.halo[b], west.shape[1]), F32))
        normed_ref[...] = jnp.concatenate(pieces, axis=0).astype(BF16)

    out_ref[...] = jnp.dot(normed_ref[...], weight_ref[...], preferred_element_type=F32).astype(BF16)


def halo_projection(bands, parts, weight):
    width, out = weight.shape
    block = 512
    skip = width // block
    return pl.pallas_call(
        functools.partial(halo_kernel, bands),
        grid=((out - width) // block,),
        in_specs=[pl.BlockSpec(p.shape, lambda n: (0, 0, 0)) for p in parts]
        + [pl.BlockSpec((width, block), lambda n: (0, n + skip))],
        out_specs=pl.BlockSpec((bands.halo_total, block), lambda n: (0, n)),
        out_shape=jax.ShapeDtypeStruct((bands.halo_total, out - width), BF16),
        scratch_shapes=[pltpu.VMEM((bands.halo_total, width), BF16)],
        compiler_params=params(),
        cost_estimate=pl.CostEstimate(
            flops=2 * bands.halo_total * width * (out - width),
            bytes_accessed=2 * width * (out - width),
            transcendentals=0,
        ),
        name="halo_projection",
    )(*parts, weight)


def dot(a, b, dims=((1,), (0,))):
    return lax.dot_general(a, b, (dims, ((), ())), preferred_element_type=F32)


def attention_kernel(bands, kinds, tokens_ref, bias_ref, q_ref, k_ref, v_ref, hk_ref, hv_ref, out_w_ref, patch_ref, *rest):
    consts, (middle_ref, merged_ref, attended_ref) = rest[:-3], rest[-3:]
    group = pl.program_id(0)
    width = q_ref.shape[1]
    size = width // GROUP
    window = WLAT * WLON
    for b in range(bands.count):
        key_ref, query_ref, mask_ref, back_ref = consts[4 * kinds[b] : 4 * kinds[b] + 4]
        own = pl.ds(bands.own_at[b], bands.own_padded[b])
        halo = pl.ds(bands.halo_at[b], bands.halo_padded[b])
        keys = dot(key_ref[...], jnp.concatenate([k_ref[own, :], hk_ref[halo, :]], axis=0))
        values = dot(key_ref[...], jnp.concatenate([v_ref[own, :], hv_ref[halo, :]], axis=0))
        mask = mask_ref[...]
        query = dot(query_ref[...], q_ref[own, :]) * mask
        at = 0
        mixed = []
        for c, w in enumerate(bands.widths):
            count = GROUP * bands.height[b] * w
            part = slice(c * window, (c + 1) * window)
            scores = dot(
                (query[at : at + count] * (1.0 / size**0.5)).astype(BF16),
                keys[part].astype(BF16),
                ((1,), (1,)),
            )
            if b == 0:
                scores = scores + bias_ref[0:1, :window]
            if b == bands.count - 1:
                scores = scores + bias_ref[1:2, :window]
            top = jnp.max(scores, axis=-1, keepdims=True)
            raised = jnp.exp(scores - top)
            weights = (raised * (1.0 / jnp.sum(raised, axis=-1, keepdims=True))).astype(BF16)
            mixed.append(dot(weights, values[part].astype(BF16)) * mask[at : at + count])
            at += count
        mixed = jnp.concatenate(mixed, axis=0).astype(BF16)
        attended_ref[group, own, :] = dot(back_ref[...], mixed).astype(BF16)

    @pl.when(group == pl.num_programs(0) - 1)
    def _():
        rows, columns, depth = tokens_ref.shape
        groups = attended_ref.shape[0]
        mixed = sum(
            dot(attended_ref[g], out_w_ref[g * width : (g + 1) * width, :]) for g in range(groups)
        )
        mixed = jnp.concatenate(
            [mixed[at : at + n] for at, n in zip(bands.own_at, bands.own)], axis=0
        )
        middle = tokens_ref[...].astype(F32) + mixed.reshape(rows, columns, depth)
        middle_ref[...] = middle.astype(BF16)
        middle = middle.reshape(rows * columns, depth).astype(BF16)
        cells = rows * columns // 4
        padded = patch_ref.shape[0] // 4
        parts = [dot(patch_ref[k * padded : (k + 1) * padded, :], middle) for k in range(4)]
        total = sum(jnp.sum(p, axis=-1, keepdims=True) for p in parts)
        mean = total * (1.0 / (4 * depth))
        parts = [p - mean for p in parts]
        spread = sum(jnp.sum(p * p, axis=-1, keepdims=True) for p in parts)
        factor = lax.rsqrt(spread * (1.0 / (4 * depth)) + 1e-05)
        for k in range(4):
            merged_ref[:, k * depth : (k + 1) * depth] = (parts[k] * factor).astype(BF16)


def attention(bands, tokens, bias, own, halo, out_weight):
    rows, columns, width = tokens.shape
    groups = HEADS // GROUP
    block = width // groups
    distinct, kinds, consts = [], [], []
    for b in range(bands.count):
        kind = (bands.height[b], b == 0, b == bands.count - 1)
        if kind not in distinct:
            distinct.append(kind)
            query, head = bands.query_matrix(b)
            mask = head[:, None] == (np.arange(block) // (block // GROUP))[None, :]
            consts += [bands.key_matrix(b), query, mask.astype(np.float32), np.ascontiguousarray(query.T)]
        kinds.append(distinct.index(kind))
    patch = bands.patch_matrix()
    padded = patch.shape[0] // 4

    def whole(a):
        return pl.BlockSpec(a.shape, lambda g: (0,) * len(a.shape))

    own_total, halo_total = own.shape[0], halo.shape[0]
    return pl.pallas_call(
        functools.partial(attention_kernel, bands, kinds),
        grid=(groups,),
        in_specs=[
            whole(tokens),
            whole(bias),
            pl.BlockSpec((own_total, block), lambda g: (0, g)),
            pl.BlockSpec((own_total, block), lambda g: (0, groups + g)),
            pl.BlockSpec((own_total, block), lambda g: (0, 2 * groups + g)),
            pl.BlockSpec((halo_total, block), lambda g: (0, g)),
            pl.BlockSpec((halo_total, block), lambda g: (0, groups + g)),
            whole(out_weight),
            whole(patch),
        ]
        + [whole(c) for c in consts],
        out_specs=[whole(tokens), pl.BlockSpec((padded, 4 * width), lambda g: (0, 0))],
        out_shape=[
            jax.ShapeDtypeStruct(tokens.shape, BF16),
            jax.ShapeDtypeStruct((padded, 4 * width), BF16),
        ],
        scratch_shapes=[pltpu.VMEM((groups, own_total, block), BF16)],
        compiler_params=params(),
        cost_estimate=pl.CostEstimate(flops=8 * 10**9, bytes_accessed=10**7, transcendentals=10**6),
        name="attention",
    )(tokens, bias, own, own, own, halo, halo, out_weight, patch, *consts)


def halos(tokens):
    lat, lon = lax.axis_size("lat"), lax.axis_size("lon")
    rows, columns, _ = tokens.shape

    def send(part, south, east):
        pairs = []
        for i in range(lat):
            for j in range(lon):
                if 0 <= i + south < lat:
                    pairs.append((i * lon + j, (i + south) * lon + (j + east) % lon))
        return lax.ppermute(part, ("lat", "lon"), pairs)

    lasts, firsts = slice(rows - RIM_LAT, rows), slice(0, RIM_LAT)
    right, left = slice(columns - SIDE, columns), slice(0, SIDE)
    return [
        send(tokens[:, right], 0, 1),
        send(tokens[:, left], 0, -1),
        send(tokens[lasts], 1, 0),
        send(tokens[firsts], -1, 0),
        send(tokens[lasts, right], 1, 1),
        send(tokens[lasts, left], 1, -1),
        send(tokens[firsts, right], -1, 1),
        send(tokens[firsts, left], -1, -1),
    ]


def key_bias():
    row = jnp.arange(8, dtype=jnp.int32)[:, None]
    key = jnp.arange(128, dtype=jnp.int32)[None, :] // WLON
    north = (row == 0) & (key < RIM_LAT) & (lax.axis_index("lat") == 0)
    south = (row == 1) & (key >= RIM_LAT) & (lax.axis_index("lat") == lax.axis_size("lat") - 1)
    return jnp.where(north | south, F32(-1e30), F32(0.0))


def ffn_kernel(mine_ref, theirs_ref, up_ref, down_ref, out_mine_ref, out_theirs_ref, normed_ref, hidden_ref):
    count = mine_ref.shape[0]
    for k, ref in enumerate((mine_ref, theirs_ref)):
        normed_ref[k * count : (k + 1) * count, :] = normalize(ref[...].astype(F32)).astype(BF16)
    hidden = hidden_ref.shape[1]
    step = 256
    for at in range(0, hidden, step):
        raw = dot(normed_ref[...], up_ref[:, at : at + step])
        active = 0.5 * raw * (1.0 + lax.erf(raw * np.float32(np.sqrt(0.5))))
        hidden_ref[:, at : at + step] = active.astype(BF16)
    for at in range(0, down_ref.shape[1], step):
        out = dot(hidden_ref[...], down_ref[:, at : at + step]).astype(BF16)
        out_mine_ref[:, at : at + step] = out[:count]
        out_theirs_ref[:, at : at + step] = out[count:]


def feed_forward(mine, theirs, up, down):
    count, width = mine.shape
    hidden = up.shape[1]
    vmem = pl.BlockSpec(memory_space=pltpu.VMEM)
    return pl.pallas_call(
        ffn_kernel,
        in_specs=[vmem] * 4,
        out_specs=[vmem] * 2,
        out_shape=[jax.ShapeDtypeStruct((count, width), BF16)] * 2,
        scratch_shapes=[pltpu.VMEM((2 * count, width), BF16), pltpu.VMEM((2 * count, hidden), BF16)],
        compiler_params=params(24),
        cost_estimate=pl.CostEstimate(
            flops=8 * count * width * hidden, bytes_accessed=4 * width * hidden, transcendentals=2 * count * hidden
        ),
        name="feed_forward",
    )(mine, theirs, up, down)


def core_swap(value):
    size = lax.axis_size("lon")
    return lax.ppermute(value, "lon", [(i, i ^ 1) for i in range(size)])


def chip_swap(value, offset):
    size = lax.axis_size("lon")
    return lax.ppermute(value, "lon", [(i, i ^ (2 * offset)) for i in range(size)])


def per_device(tokens, qkv_weight, out_weight, merge_weight, up_weight, down_weight):
    rows, columns, width = tokens.shape
    bands = Bands(rows, columns)
    cells = rows * columns // 4
    parts = halos(tokens)
    own = own_projection(bands, tokens, qkv_weight)
    halo = halo_projection(bands, parts, qkv_weight)
    middle_out, merged = attention(bands, tokens, key_bias(), own, halo, out_weight)
    coarse = jnp.dot(
        merged,
        lax.all_gather(merge_weight, "lon", axis=1, tiled=True),
        preferred_element_type=jnp.float32,
    ).astype(jnp.bfloat16)
    chips = lax.axis_size("lon") // 2
    arrived = [coarse] + [chip_swap(coarse, m) for m in range(1, chips)]
    total = coarse.astype(F32)
    for m in range(chips):
        mine, theirs = feed_forward(arrived[m], core_swap(arrived[m]), up_weight, down_weight)
        summed = mine.astype(F32) + core_swap(theirs).astype(F32)
        if m:
            summed = chip_swap(summed.astype(BF16), m).astype(F32)
        total = total + summed
    coarse_out = total[:cells].astype(jnp.bfloat16)
    return (middle_out, coarse_out.reshape(rows // 2, columns // 2, -1))


def solution(mesh):
    return jax.shard_map(
        per_device,
        mesh=mesh,
        in_specs=(P("lat", "lon", None), P(), P(), P(None, "lon"), P(None, "lon"), P("lon", None)),
        out_specs=(P("lat", "lon", None), P("lat", "lon", None)),
        check_vma=False,
    )
```

```python
import functools

import jax
import jax.numpy as jnp
import numpy as np
from jax import lax
from jax.experimental import pallas as pl
from jax.experimental.pallas import tpu as pltpu
from jax.sharding import PartitionSpec as P

HEADS = 16
WLAT = 6
WLON = 12
RIM_LAT = WLAT // 2
RIM_LON = WLON // 2
SIDE = 8
GROUP = 4
F32 = jnp.float32
BF16 = jnp.bfloat16


def up16(n):
    return -(-n // 16) * 16


def params(mib=48, **kw):
    return pltpu.CompilerParams(vmem_limit_bytes=mib * 2**20, **kw)


class Bands:
    def __init__(self, rows, columns):
        assert (rows - WLAT) % WLAT == 0 and (columns - WLON) % WLON == 0
        self.rows, self.columns = rows, columns
        inner = (rows - WLAT) // WLAT
        self.height = [RIM_LAT] + [WLAT] * inner + [RIM_LAT]
        self.count = len(self.height)
        self.first = [sum(self.height[:b]) for b in range(self.count)]
        self.widths = [RIM_LON] + [WLON] * ((columns - WLON) // WLON) + [RIM_LON]
        self.own = [h * columns for h in self.height]
        self.own_padded = [up16(n) for n in self.own]
        self.own_at = [sum(self.own_padded[:b]) for b in range(self.count)]
        self.own_total = sum(self.own_padded)
        self.side = [2 * h * SIDE for h in self.height]
        assert all(n % 16 == 0 for n in self.side)
        self.side_at = [sum(self.side[:b]) for b in range(self.count)]
        self.side_total = sum(self.side)
        self.slab = columns + 2 * SIDE
        self.slab_padded = up16(RIM_LAT * self.slab)
        self.window = up16(WLAT * WLON)
        self.counts = [[GROUP * h * w for w in self.widths] for h in self.height]
        self.counts_padded = [[up16(n) for n in row] for row in self.counts]

    def edge(self, b):
        return b in (0, self.count - 1)

    def sources(self, b):
        return self.own_padded[b] + self.side[b] + (self.slab_padded if self.edge(b) else 0)

    def source(self, b, i, j):
        columns, h, first = self.columns, self.height[b], self.first[b]
        at = self.own_padded[b]
        if not 0 <= i < self.rows:
            i = i + RIM_LAT if i < 0 else i - self.rows
            return at + self.side[b] + i * self.slab + j + SIDE
        if 0 <= j < columns:
            return (i - first) * columns + j
        at += (i - first) * SIDE
        return at + (j + SIDE if j < 0 else h * SIDE + j - columns)

    def key_matrix(self, b):
        g = np.zeros((len(self.widths) * self.window, self.sources(b)), np.float32)
        top = self.first[b] - (RIM_LAT if b == 0 else 0)
        for c in range(len(self.widths)):
            for i in range(WLAT):
                for j in range(WLON):
                    at = c * self.window + i * WLON + j
                    g[at, self.source(b, top + i, c * WLON - RIM_LON + j)] = 1
        return g.astype(BF16)

    def query_matrix(self, b):
        total = sum(self.counts_padded[b])
        g = np.zeros((total, self.own_padded[b]), np.float32)
        head = np.zeros((total,), np.int32)
        start = left = 0
        for width, padded in zip(self.widths, self.counts_padded[b]):
            at = start
            for k in range(GROUP):
                for i in range(self.height[b]):
                    for j in range(width):
                        g[at, i * self.columns + left + j] = 1
                        head[at] = k
                        at += 1
            left += width
            start += padded
        return g.astype(BF16), head

    def patch_matrix(self):
        cells = self.rows * self.columns // 4
        padded = up16(cells)
        g = np.zeros((4 * padded, self.rows * self.columns), np.float32)
        for r in range(self.rows // 2):
            for c in range(self.columns // 2):
                for k in range(4):
                    to = k * padded + r * (self.columns // 2) + c
                    g[to, (2 * r + k // 2) * self.columns + 2 * c + k % 2] = 1
        return g.astype(BF16)

    def constants(self, some, block):
        distinct, kinds, consts = [], [], []
        for b in some:
            kind = (self.height[b], b == 0, b == self.count - 1)
            if kind not in distinct:
                distinct.append(kind)
                query, head = self.query_matrix(b)
                mask = head[:, None] == (np.arange(block) // (block // GROUP))[None, :]
                scale = np.float32((block // GROUP) ** -0.5)
                scaled = (query.astype(np.float32) * scale).astype(BF16)
                consts += [self.key_matrix(b), scaled, mask.astype(BF16), np.ascontiguousarray(query.T)]
            kinds.append(4 * distinct.index(kind))
        return kinds, consts


def normalize(values):
    center = values - jnp.mean(values, axis=-1, keepdims=True)
    spread = jnp.mean(center * center, axis=-1, keepdims=True)
    return center * lax.rsqrt(spread + 1e-05)


def dot(a, b, dims=((1,), (0,))):
    return lax.dot_general(a, b, (dims, ((), ())), preferred_element_type=F32)


def flat_normed(ref):
    values = ref[...].astype(F32)
    return normalize(values.reshape(-1, values.shape[-1]))


def padded_rows(values, total):
    if values.shape[0] == total:
        return values
    return jnp.concatenate([values, jnp.zeros((total - values.shape[0], values.shape[1]), values.dtype)], axis=0)


def project(normed_ref, weight_ref, out_ref, first):
    step = 256
    for at in range(0, out_ref.shape[1], step):
        part = weight_ref[:, first + at : first + at + step]
        out_ref[:, at : at + step] = dot(normed_ref[...], part).astype(BF16)


def own_kernel(bands, tokens_ref, weight_ref, out_ref, normed_ref):
    normed = flat_normed(tokens_ref)
    for b in range(bands.count):
        at = bands.first[b] * bands.columns
        part = padded_rows(normed[at : at + bands.own[b]], bands.own_padded[b])
        normed_ref[bands.own_at[b] : bands.own_at[b] + bands.own_padded[b], :] = part.astype(BF16)
    project(normed_ref, weight_ref, out_ref, 0)


def attend(bands, some, kinds, consts, own_ref, outer, bias_ref, put, scratch):
    k_ref, v_ref, q_ref, p_ref, r_ref = scratch
    width = own_ref.shape[1] // 3
    block = width * GROUP // HEADS
    window = WLAT * WLON
    units = [(n, b, g) for n, b in enumerate(some) for g in range(HEADS // GROUP)]
    for u, (n, b, g) in enumerate(units):
        keys, query, mask, _ = consts[kinds[n] : kinds[n] + 4]
        own = slice(bands.own_at[b], bands.own_at[b] + bands.own_padded[b])
        for ref, skip in ((k_ref, 0), (v_ref, width)):
            parts = [own_ref[own, width + skip + g * block : width + skip + (g + 1) * block]]
            for out_ref, at, size in outer(b):
                parts.append(out_ref[at : at + size, skip + g * block : skip + (g + 1) * block])
            ref[u] = dot(keys[...], jnp.concatenate(parts, axis=0)).astype(BF16)
        total = query.shape[0]
        q_ref[u, :total] = dot(query[...], own_ref[own, g * block : (g + 1) * block]).astype(BF16) * mask[...]
    for u, (n, b, g) in enumerate(units):
        at = 0
        for c, count in enumerate(bands.counts_padded[b]):
            scores = dot(
                q_ref[u, at : at + count], k_ref[u, c * bands.window : c * bands.window + window], ((1,), (1,))
            )
            if b == 0:
                scores = scores + bias_ref[0:1, :window]
            if b == bands.count - 1:
                scores = scores + bias_ref[1:2, :window]
            raised = jnp.exp(scores - jnp.max(scores, axis=-1, keepdims=True))
            weights = raised * (1.0 / jnp.sum(raised, axis=-1, keepdims=True))
            p_ref[u, at : at + count, :window] = weights.astype(BF16)
            at += count
    for u, (n, b, g) in enumerate(units):
        mask = consts[kinds[n] + 2]
        at = 0
        for c, count in enumerate(bands.counts_padded[b]):
            mixed = dot(
                p_ref[u, at : at + count, :window], v_ref[u, c * bands.window : c * bands.window + window]
            )
            r_ref[u, at : at + count] = mixed.astype(BF16) * mask[at : at + count]
            at += count
    for u, (n, b, g) in enumerate(units):
        back = consts[kinds[n] + 3]
        put(b, g, dot(back[...], r_ref[u, : back.shape[1]]).astype(BF16))


def attend_scratch(bands, some, block):
    units = len(some) * HEADS // GROUP
    keys = len(bands.widths) * bands.window
    rows = max(sum(bands.counts_padded[b]) for b in some)
    return [
        pltpu.VMEM((units, keys, block), BF16),
        pltpu.VMEM((units, keys, block), BF16),
        pltpu.VMEM((units, rows, block), BF16),
        pltpu.VMEM((units, rows, 128), BF16),
        pltpu.VMEM((units, rows, block), BF16),
    ]


def middle_kernel(bands, some, kinds, west_ref, east_ref, own_ref, weight_ref, *rest):
    consts, (side_ref, out_ref, normed_ref, *scratch) = rest[:-8], rest[-8:]
    width = weight_ref.shape[0]
    west, east = flat_normed(west_ref), flat_normed(east_ref)
    for b in range(bands.count):
        at, size = bands.first[b] * SIDE, bands.height[b] * SIDE
        part = jnp.concatenate([west[at : at + size], east[at : at + size]], axis=0)
        normed_ref[bands.side_at[b] : bands.side_at[b] + bands.side[b], :] = part.astype(BF16)
    project(normed_ref, weight_ref, side_ref, width)

    def outer(b):
        return [(side_ref, bands.side_at[b], bands.side[b])]

    def put(b, g, value):
        at = bands.own_at[b] - bands.own_at[1]
        block = value.shape[1]
        out_ref[at : at + bands.own_padded[b], g * block : (g + 1) * block] = value

    attend(bands, some, kinds, consts, own_ref, outer, None, put, scratch)


def edge_kernel(bands, some, kinds, tokens_ref, north_ref, south_ref, bias_ref, own_ref, side_ref, inner_ref, weight_ref, out_w_ref, patch_ref, *rest):
    consts, rest = rest[:-11], rest[-11:]
    middle_ref, upper_ref, lower_ref, normed_ref, slab_ref, attended_ref, *scratch = rest
    rows, columns, width = tokens_ref.shape
    slab = bands.slab_padded
    for k, ref in enumerate((north_ref, south_ref)):
        normed_ref[k * slab : (k + 1) * slab, :] = padded_rows(flat_normed(ref), slab).astype(BF16)
    project(normed_ref, weight_ref, slab_ref, width)

    def outer(b):
        return [
            (side_ref, bands.side_at[b], bands.side[b]),
            (slab_ref, 0 if b == 0 else slab, slab),
        ]

    def put(b, g, value):
        block = value.shape[1]
        attended_ref[bands.own_at[b] : bands.own_at[b] + bands.own_padded[b], g * block : (g + 1) * block] = value

    attended_ref[bands.own_at[1] : bands.own_at[-1], :] = inner_ref[...]
    attend(bands, some, kinds, consts, own_ref, outer, bias_ref, put, scratch)
    mixed = dot(attended_ref[...], out_w_ref[...])
    mixed = jnp.concatenate([mixed[at : at + n] for at, n in zip(bands.own_at, bands.own)], axis=0)
    middle = tokens_ref[...].astype(F32) + mixed.reshape(rows, columns, width)
    middle_ref[...] = middle.astype(BF16)
    middle = middle.reshape(rows * columns, width).astype(BF16)
    padded = patch_ref.shape[0] // 4
    parts = [dot(patch_ref[k * padded : (k + 1) * padded, :], middle) for k in range(4)]
    total = sum(jnp.sum(p, axis=-1, keepdims=True) for p in parts)
    mean = total * (1.0 / (4 * width))
    parts = [p - mean for p in parts]
    spread = sum(jnp.sum(p * p, axis=-1, keepdims=True) for p in parts)
    factor = lax.rsqrt(spread * (1.0 / (4 * width)) + 1e-05)
    for k in range(4):
        ref = (upper_ref, lower_ref)[k // 2]
        ref[:, k % 2 * width : (k % 2 + 1) * width] = (parts[k] * factor).astype(BF16)


def vmem_call(kernel, out, args, scratch, flops, name, mib=40, exps=0):
    vmem = pl.BlockSpec(memory_space=pltpu.VMEM)
    return pl.pallas_call(
        kernel,
        in_specs=[vmem] * len(args),
        out_specs=[vmem] * len(out),
        out_shape=[jax.ShapeDtypeStruct(shape, BF16) for shape in out],
        scratch_shapes=scratch,
        compiler_params=params(mib),
        cost_estimate=pl.CostEstimate(flops=flops, bytes_accessed=2**20, transcendentals=exps),
        name=name,
    )(*args)


def attention(bands, tokens, qkv_weight, out_weight):
    rows, columns, width = tokens.shape
    block = width * GROUP // HEADS
    west = shift(tokens[:, columns - SIDE :], "lon", 1, True)
    east = shift(tokens[:, :SIDE], "lon", -1, True)
    own = vmem_call(
        functools.partial(own_kernel, bands),
        [(bands.own_total, 3 * width)],
        [tokens, qkv_weight],
        [pltpu.VMEM((bands.own_total, width), BF16)],
        6 * bands.own_total * width * width,
        "own_projection",
    )[0]

    def slab(part):
        return jnp.concatenate([west[part], tokens[part], east[part]], axis=1)

    north = shift(slab(slice(rows - RIM_LAT, rows)), "lat", 1, False)
    south = shift(slab(slice(0, RIM_LAT)), "lat", -1, False)
    inner = list(range(1, bands.count - 1))
    edges = [0, bands.count - 1]
    kinds, consts = bands.constants(inner, block)
    side, attended = vmem_call(
        functools.partial(middle_kernel, bands, inner, kinds),
        [(bands.side_total, 2 * width), (bands.own_at[-1] - bands.own_at[1], width)],
        [west, east, own, qkv_weight] + consts,
        [pltpu.VMEM((bands.side_total, width), BF16)] + attend_scratch(bands, inner, block),
        5 * 10**9,
        "middle_attention",
        exps=500000,
    )
    kinds, consts = bands.constants(edges, block)
    padded = up16(rows * columns // 4)
    return vmem_call(
        functools.partial(edge_kernel, bands, edges, kinds),
        [tokens.shape, (padded, 2 * width), (padded, 2 * width)],
        [tokens, north, south, key_bias(), own, side, attended, qkv_weight, out_weight, bands.patch_matrix()] + consts,
        [
            pltpu.VMEM((2 * bands.slab_padded, width), BF16),
            pltpu.VMEM((2 * bands.slab_padded, 2 * width), BF16),
            pltpu.VMEM((bands.own_total, width), BF16),
        ]
        + attend_scratch(bands, edges, block),
        6 * 10**9,
        "edge_attention",
        exps=300000,
    )


def shift(part, axis, step, wrap):
    size = lax.axis_size(axis)
    pairs = [(i, (i + step) % size) for i in range(size) if wrap or 0 <= i + step < size]
    return lax.ppermute(part, axis, pairs)


def key_bias():
    row = jnp.arange(8, dtype=jnp.int32)[:, None]
    key = jnp.arange(128, dtype=jnp.int32)[None, :] // WLON
    north = (row == 0) & (key < RIM_LAT) & (lax.axis_index("lat") == 0)
    south = (row == 1) & (key >= RIM_LAT) & (lax.axis_index("lat") == lax.axis_size("lat") - 1)
    return jnp.where(north | south, F32(-1e30), F32(0.0))


def place_index():
    me = lax.axis_index("lon")
    return jnp.stack([me // 2, me % 2]).astype(jnp.int32)


def merge_dots(place_ref, upper, lower, mine_ref, pair_ref, x_ref, x_pair_ref, y_ref, y_pair_ref, refs):
    half, block = x_ref.shape
    at = [pl.ds(pl.multiple_of((place_ref[1] + k) % 2 * block, block), block) for k in range(2)]
    own, x, y = refs
    for k, ref in enumerate((mine_ref, pair_ref)):
        own(at[k], dot(upper, ref[:half, :]), dot(lower, ref[half:, :]))
    for k, ref in enumerate((x_ref, x_pair_ref)):
        x(at[k], dot(upper, ref[...]))
    for k, ref in enumerate((y_ref, y_pair_ref)):
        y(at[k], dot(lower, ref[...]))


def merge_own_kernel(place_ref, upper_ref, lower_ref, *refs):
    weights, (own_ref, x_ref, y_ref) = refs[:6], refs[6:]

    def own(at, a, b):
        own_ref[:, at] = a + b

    def x(at, a):
        x_ref[:, at] = a

    def y(at, b):
        y_ref[:, at] = b

    merge_dots(place_ref, upper_ref[...], lower_ref[...], *weights, (own, x, y))


def merge_other_kernel(place_ref, upper_ref, lower_ref, *refs):
    weights, (to_y_ref, to_x_ref) = refs[:6], refs[6:]
    wide = to_x_ref.shape[1] // 2

    def own(at, a, b):
        to_y_ref[:, at] = a.astype(BF16)
        to_x_ref[:, at] = b.astype(BF16)

    def x(at, a):
        to_y_ref[:, pl.ds(pl.multiple_of(wide + at.start, at.size), at.size)] = a.astype(BF16)

    def y(at, b):
        to_x_ref[:, pl.ds(pl.multiple_of(wide + at.start, at.size), at.size)] = b.astype(BF16)

    merge_dots(place_ref, upper_ref[...], lower_ref[...], *weights, (own, x, y))


def combine_kernel(place_ref, own_ref, x_ref, y_ref, from_y_ref, from_x_ref, out_ref):
    wide = own_ref.shape[1]
    chip = place_ref[0]
    from_x, from_y = from_x_ref[...].astype(F32), from_y_ref[...].astype(F32)
    parts = [
        own_ref[...],
        x_ref[...] + from_x[:, :wide],
        y_ref[...] + from_y[:, :wide],
        from_x[:, wide:] + from_y[:, wide:],
    ]
    for m, part in enumerate(parts):
        out_ref[:, pl.ds(pl.multiple_of((chip ^ m) * wide, wide), wide)] = part.astype(BF16)


def local_call(kernel, out, place, args, flops, name, mib=24):
    vmem = pl.BlockSpec(memory_space=pltpu.VMEM)
    return pl.pallas_call(
        kernel,
        in_specs=[pl.BlockSpec(memory_space=pltpu.SMEM)] + [vmem] * len(args),
        out_specs=[vmem] * len(out),
        out_shape=out,
        compiler_params=params(mib),
        cost_estimate=pl.CostEstimate(flops=flops, bytes_accessed=2**20, transcendentals=0),
        name=name,
    )(place, *args)


def merge_by_squares(upper, lower, merge_weight):
    half = merge_weight.shape[0] // 2
    block = merge_weight.shape[1]
    count = upper.shape[0]
    x = chip_swap(merge_weight[:half], 1)
    y = chip_swap(merge_weight[half:], 2)
    weights = [merge_weight, core_swap(merge_weight), x, core_swap(x), y, core_swap(y)]
    place = place_index()
    from_y = chip_swap(upper, 2)
    from_x = chip_swap(lower, 1)
    flops = 16 * count * half * block
    wide = jax.ShapeDtypeStruct((count, 2 * block), F32)
    own = local_call(merge_own_kernel, [wide] * 3, place, [upper, lower] + weights, flops, "merge_own")
    pair = jax.ShapeDtypeStruct((count, 4 * block), BF16)
    to_y, to_x = local_call(merge_other_kernel, [pair] * 2, place, [from_y, from_x] + weights, flops, "merge_other")
    back_y, back_x = chip_swap(to_y, 2), chip_swap(to_x, 1)
    out = jax.ShapeDtypeStruct((count, 8 * block), BF16)
    return local_call(combine_kernel, [out], place, [*own, back_y, back_x], 0, "combine")[0]


def merge(upper, lower, merge_weight):
    if lax.axis_size("lon") == 8:
        return merge_by_squares(upper, lower, merge_weight)
    weight = lax.all_gather(merge_weight, "lon", axis=1, tiled=True)
    return jnp.dot(jnp.concatenate([upper, lower], axis=1), weight, preferred_element_type=F32).astype(BF16)


def ffn_kernel(mine_ref, theirs_ref, up_ref, down_ref, out_mine_ref, out_theirs_ref, normed_ref, hidden_ref):
    count = mine_ref.shape[0]
    for k, ref in enumerate((mine_ref, theirs_ref)):
        normed_ref[k * count : (k + 1) * count, :] = normalize(ref[...].astype(F32)).astype(BF16)
    hidden = hidden_ref.shape[1]
    step = 256
    for at in range(0, hidden, step):
        raw = dot(normed_ref[...], up_ref[:, at : at + step])
        active = 0.5 * raw * (1.0 + lax.erf(raw * np.float32(np.sqrt(0.5))))
        hidden_ref[:, at : at + step] = active.astype(BF16)
    for at in range(0, down_ref.shape[1], step):
        out = dot(hidden_ref[...], down_ref[:, at : at + step]).astype(BF16)
        out_mine_ref[:, at : at + step] = out[:count]
        out_theirs_ref[:, at : at + step] = out[count:]


def feed_forward(mine, theirs, up, down):
    count, width = mine.shape
    hidden = up.shape[1]
    vmem = pl.BlockSpec(memory_space=pltpu.VMEM)
    return pl.pallas_call(
        ffn_kernel,
        in_specs=[vmem] * 4,
        out_specs=[vmem] * 2,
        out_shape=[jax.ShapeDtypeStruct((count, width), BF16)] * 2,
        scratch_shapes=[pltpu.VMEM((2 * count, width), BF16), pltpu.VMEM((2 * count, hidden), BF16)],
        compiler_params=params(24),
        cost_estimate=pl.CostEstimate(
            flops=8 * count * width * hidden, bytes_accessed=4 * width * hidden, transcendentals=2 * count * hidden
        ),
        name="feed_forward",
    )(mine, theirs, up, down)


def core_swap(value):
    size = lax.axis_size("lon")
    return lax.ppermute(value, "lon", [(i, i ^ 1) for i in range(size)])


def chip_swap(value, offset):
    size = lax.axis_size("lon")
    return lax.ppermute(value, "lon", [(i, i ^ (2 * offset)) for i in range(size)])


def per_device(tokens, qkv_weight, out_weight, merge_weight, up_weight, down_weight):
    rows, columns, width = tokens.shape
    bands = Bands(rows, columns)
    cells = rows * columns // 4
    middle_out, upper, lower = attention(bands, tokens, qkv_weight, out_weight)
    coarse = merge(upper, lower, merge_weight)
    chips = lax.axis_size("lon") // 2
    arrived = [coarse] + [chip_swap(coarse, m) for m in range(1, chips)]
    total = coarse.astype(F32)
    for m in range(chips):
        mine, theirs = feed_forward(arrived[m], core_swap(arrived[m]), up_weight, down_weight)
        summed = mine.astype(F32) + core_swap(theirs).astype(F32)
        if m:
            summed = chip_swap(summed.astype(BF16), m).astype(F32)
        total = total + summed
    coarse_out = total[:cells].astype(jnp.bfloat16)
    return (middle_out, coarse_out.reshape(rows // 2, columns // 2, -1))


def solution(mesh):
    return jax.shard_map(
        per_device,
        mesh=mesh,
        in_specs=(P("lat", "lon", None), P(), P(), P(None, "lon"), P(None, "lon"), P("lon", None)),
        out_specs=(P("lat", "lon", None), P("lat", "lon", None)),
        check_vma=False,
    )
```

```python
import functools

import jax
import jax.numpy as jnp
import numpy as np
from jax import lax
from jax.experimental import pallas as pl
from jax.experimental.pallas import tpu as pltpu
from jax.sharding import PartitionSpec as P

HEADS = 16
WLAT = 6
WLON = 12
RIM_LAT = WLAT // 2
RIM_LON = WLON // 2
SIDE = 8
GROUP = 4
F32 = jnp.float32
BF16 = jnp.bfloat16


def up16(n):
    return -(-n // 16) * 16


def params(mib=48, **kw):
    return pltpu.CompilerParams(vmem_limit_bytes=mib * 2**20, **kw)


class Bands:
    def __init__(self, rows, columns):
        assert (rows - WLAT) % WLAT == 0 and (columns - WLON) % WLON == 0
        self.rows, self.columns = rows, columns
        inner = (rows - WLAT) // WLAT
        self.height = [RIM_LAT] + [WLAT] * inner + [RIM_LAT]
        self.count = len(self.height)
        self.first = [sum(self.height[:b]) for b in range(self.count)]
        self.widths = [RIM_LON] + [WLON] * ((columns - WLON) // WLON) + [RIM_LON]
        self.own = [h * columns for h in self.height]
        self.own_padded = [up16(n) for n in self.own]
        self.own_at = [sum(self.own_padded[:b]) for b in range(self.count)]
        self.own_total = sum(self.own_padded)
        self.side = [2 * h * SIDE for h in self.height]
        assert all(n % 16 == 0 for n in self.side)
        self.side_at = [sum(self.side[:b]) for b in range(self.count)]
        self.side_total = sum(self.side)
        self.slab = columns + 2 * SIDE
        self.slab_padded = up16(RIM_LAT * self.slab)
        self.window = up16(WLAT * WLON)
        self.counts = [[GROUP * h * w for w in self.widths] for h in self.height]
        self.counts_padded = [[up16(n) for n in row] for row in self.counts]

    def edge(self, b):
        return b in (0, self.count - 1)

    def sources(self, b):
        return self.own_padded[b] + self.side[b] + (self.slab_padded if self.edge(b) else 0)

    def source(self, b, i, j):
        columns, h, first = self.columns, self.height[b], self.first[b]
        at = self.own_padded[b]
        if not 0 <= i < self.rows:
            i = i + RIM_LAT if i < 0 else i - self.rows
            return at + self.side[b] + i * self.slab + j + SIDE
        if 0 <= j < columns:
            return (i - first) * columns + j
        at += (i - first) * SIDE
        return at + (j + SIDE if j < 0 else h * SIDE + j - columns)

    def key_matrix(self, b):
        g = np.zeros((len(self.widths) * self.window, self.sources(b)), np.float32)
        top = self.first[b] - (RIM_LAT if b == 0 else 0)
        for c in range(len(self.widths)):
            for i in range(WLAT):
                for j in range(WLON):
                    at = c * self.window + i * WLON + j
                    g[at, self.source(b, top + i, c * WLON - RIM_LON + j)] = 1
        return g.astype(BF16)

    def query_matrix(self, b):
        total = sum(self.counts_padded[b])
        g = np.zeros((total, self.own_padded[b]), np.float32)
        head = np.zeros((total,), np.int32)
        start = left = 0
        for width, padded in zip(self.widths, self.counts_padded[b]):
            at = start
            for k in range(GROUP):
                for i in range(self.height[b]):
                    for j in range(width):
                        g[at, i * self.columns + left + j] = 1
                        head[at] = k
                        at += 1
            left += width
            start += padded
        return g.astype(BF16), head

    def patch_matrix(self):
        cells = self.rows * self.columns // 4
        padded = up16(cells)
        g = np.zeros((4 * padded, self.rows * self.columns), np.float32)
        for r in range(self.rows // 2):
            for c in range(self.columns // 2):
                for k in range(4):
                    to = k * padded + r * (self.columns // 2) + c
                    g[to, (2 * r + k // 2) * self.columns + 2 * c + k % 2] = 1
        return g.astype(BF16)

    def constants(self, some, block):
        distinct, kinds, consts = [], [], []
        for b in some:
            kind = (self.height[b], b == 0, b == self.count - 1)
            if kind not in distinct:
                distinct.append(kind)
                query, head = self.query_matrix(b)
                mask = head[:, None] == (np.arange(block) // (block // GROUP))[None, :]
                scale = np.float32((block // GROUP) ** -0.5)
                scaled = (query.astype(np.float32) * scale).astype(BF16)
                consts += [self.key_matrix(b), scaled, mask.astype(BF16), np.ascontiguousarray(query.T)]
            kinds.append(4 * distinct.index(kind))
        return kinds, consts


def normalize(values):
    center = values - jnp.mean(values, axis=-1, keepdims=True)
    spread = jnp.mean(center * center, axis=-1, keepdims=True)
    return center * lax.rsqrt(spread + 1e-05)


def dot(a, b, dims=((1,), (0,))):
    return lax.dot_general(a, b, (dims, ((), ())), preferred_element_type=F32)


def flat_normed(ref):
    values = ref[...].astype(F32)
    return normalize(values.reshape(-1, values.shape[-1]))


def padded_rows(values, total):
    if values.shape[0] == total:
        return values
    return jnp.concatenate([values, jnp.zeros((total - values.shape[0], values.shape[1]), values.dtype)], axis=0)


def project(normed_ref, weight_ref, out_ref, first):
    step = 256
    for at in range(0, out_ref.shape[1], step):
        part = weight_ref[:, first + at : first + at + step]
        out_ref[:, at : at + step] = dot(normed_ref[...], part).astype(BF16)


def own_kernel(bands, tokens_ref, weight_ref, out_ref, normed_ref):
    normed = flat_normed(tokens_ref)
    for b in range(bands.count):
        at = bands.first[b] * bands.columns
        part = padded_rows(normed[at : at + bands.own[b]], bands.own_padded[b])
        normed_ref[bands.own_at[b] : bands.own_at[b] + bands.own_padded[b], :] = part.astype(BF16)
    project(normed_ref, weight_ref, out_ref, 0)


def attend(bands, some, kinds, consts, own_ref, outer, bias_ref, put, scratch):
    k_ref, v_ref, q_ref, p_ref, r_ref = scratch
    width = own_ref.shape[1] // 3
    block = width * GROUP // HEADS
    window = WLAT * WLON
    units = [(n, b, g) for n, b in enumerate(some) for g in range(HEADS // GROUP)]
    for u, (n, b, g) in enumerate(units):
        keys, query, mask, _ = consts[kinds[n] : kinds[n] + 4]
        own = slice(bands.own_at[b], bands.own_at[b] + bands.own_padded[b])
        for ref, skip in ((k_ref, 0), (v_ref, width)):
            parts = [own_ref[own, width + skip + g * block : width + skip + (g + 1) * block]]
            for out_ref, at, size in outer(b):
                parts.append(out_ref[at : at + size, skip + g * block : skip + (g + 1) * block])
            ref[u] = dot(keys[...], jnp.concatenate(parts, axis=0)).astype(BF16)
        total = query.shape[0]
        q_ref[u, :total] = dot(query[...], own_ref[own, g * block : (g + 1) * block]).astype(BF16) * mask[...]
    for u, (n, b, g) in enumerate(units):
        at = 0
        for c, count in enumerate(bands.counts_padded[b]):
            scores = dot(
                q_ref[u, at : at + count], k_ref[u, c * bands.window : c * bands.window + window], ((1,), (1,))
            )
            if b == 0:
                scores = scores + bias_ref[0:1, :window]
            if b == bands.count - 1:
                scores = scores + bias_ref[1:2, :window]
            raised = jnp.exp(scores - jnp.max(scores, axis=-1, keepdims=True))
            weights = raised * (1.0 / jnp.sum(raised, axis=-1, keepdims=True))
            p_ref[u, at : at + count, :window] = weights.astype(BF16)
            at += count
    for u, (n, b, g) in enumerate(units):
        mask = consts[kinds[n] + 2]
        at = 0
        for c, count in enumerate(bands.counts_padded[b]):
            mixed = dot(
                p_ref[u, at : at + count, :window], v_ref[u, c * bands.window : c * bands.window + window]
            )
            r_ref[u, at : at + count] = mixed.astype(BF16) * mask[at : at + count]
            at += count
    for u, (n, b, g) in enumerate(units):
        back = consts[kinds[n] + 3]
        put(b, g, dot(back[...], r_ref[u, : back.shape[1]]).astype(BF16))


def attend_scratch(bands, some, block):
    units = len(some) * HEADS // GROUP
    keys = len(bands.widths) * bands.window
    rows = max(sum(bands.counts_padded[b]) for b in some)
    return [
        pltpu.VMEM((units, keys, block), BF16),
        pltpu.VMEM((units, keys, block), BF16),
        pltpu.VMEM((units, rows, block), BF16),
        pltpu.VMEM((units, rows, 128), BF16),
        pltpu.VMEM((units, rows, block), BF16),
    ]


def middle_kernel(bands, some, kinds, west_ref, east_ref, own_ref, weight_ref, *rest):
    consts, (side_ref, out_ref, normed_ref, *scratch) = rest[:-8], rest[-8:]
    width = weight_ref.shape[0]
    west, east = flat_normed(west_ref), flat_normed(east_ref)
    for b in range(bands.count):
        at, size = bands.first[b] * SIDE, bands.height[b] * SIDE
        part = jnp.concatenate([west[at : at + size], east[at : at + size]], axis=0)
        normed_ref[bands.side_at[b] : bands.side_at[b] + bands.side[b], :] = part.astype(BF16)
    project(normed_ref, weight_ref, side_ref, width)

    def outer(b):
        return [(side_ref, bands.side_at[b], bands.side[b])]

    def put(b, g, value):
        at = bands.own_at[b] - bands.own_at[1]
        block = value.shape[1]
        out_ref[at : at + bands.own_padded[b], g * block : (g + 1) * block] = value

    attend(bands, some, kinds, consts, own_ref, outer, None, put, scratch)


def edge_kernel(bands, some, kinds, tokens_ref, north_ref, south_ref, bias_ref, own_ref, side_ref, inner_ref, weight_ref, out_w_ref, patch_ref, *rest):
    consts, rest = rest[:-11], rest[-11:]
    middle_ref, upper_ref, lower_ref, normed_ref, slab_ref, attended_ref, *scratch = rest
    rows, columns, width = tokens_ref.shape
    slab = bands.slab_padded
    for k, ref in enumerate((north_ref, south_ref)):
        normed_ref[k * slab : (k + 1) * slab, :] = padded_rows(flat_normed(ref), slab).astype(BF16)
    project(normed_ref, weight_ref, slab_ref, width)

    def outer(b):
        return [
            (side_ref, bands.side_at[b], bands.side[b]),
            (slab_ref, 0 if b == 0 else slab, slab),
        ]

    def put(b, g, value):
        block = value.shape[1]
        attended_ref[bands.own_at[b] : bands.own_at[b] + bands.own_padded[b], g * block : (g + 1) * block] = value

    attended_ref[bands.own_at[1] : bands.own_at[-1], :] = inner_ref[...]
    attend(bands, some, kinds, consts, own_ref, outer, bias_ref, put, scratch)
    mixed = dot(attended_ref[...], out_w_ref[...])
    mixed = jnp.concatenate([mixed[at : at + n] for at, n in zip(bands.own_at, bands.own)], axis=0)
    middle = tokens_ref[...].astype(F32) + mixed.reshape(rows, columns, width)
    middle_ref[...] = middle.astype(BF16)
    middle = middle.reshape(rows * columns, width).astype(BF16)
    padded = patch_ref.shape[0] // 4
    parts = [dot(patch_ref[k * padded : (k + 1) * padded, :], middle) for k in range(4)]
    total = sum(jnp.sum(p, axis=-1, keepdims=True) for p in parts)
    mean = total * (1.0 / (4 * width))
    parts = [p - mean for p in parts]
    spread = sum(jnp.sum(p * p, axis=-1, keepdims=True) for p in parts)
    factor = lax.rsqrt(spread * (1.0 / (4 * width)) + 1e-05)
    for k in range(4):
        ref = (upper_ref, lower_ref)[k // 2]
        ref[:, k % 2 * width : (k % 2 + 1) * width] = (parts[k] * factor).astype(BF16)


def vmem_call(kernel, out, args, scratch, flops, name, mib=24, exps=0):
    vmem = pl.BlockSpec(memory_space=pltpu.VMEM)
    return pl.pallas_call(
        kernel,
        in_specs=[vmem] * len(args),
        out_specs=[vmem] * len(out),
        out_shape=[jax.ShapeDtypeStruct(shape, BF16) for shape in out],
        scratch_shapes=scratch,
        compiler_params=params(mib),
        cost_estimate=pl.CostEstimate(flops=flops, bytes_accessed=2**20, transcendentals=exps),
        name=name,
    )(*args)


def attention(bands, tokens, qkv_weight, out_weight):
    rows, columns, width = tokens.shape
    block = width * GROUP // HEADS
    west = shift(tokens[:, columns - SIDE :], "lon", 1, True)
    east = shift(tokens[:, :SIDE], "lon", -1, True)
    own = vmem_call(
        functools.partial(own_kernel, bands),
        [(bands.own_total, 3 * width)],
        [tokens, qkv_weight],
        [pltpu.VMEM((bands.own_total, width), BF16)],
        6 * bands.own_total * width * width,
        "own_projection",
        mib=16,
    )[0]

    def slab(part):
        return jnp.concatenate([west[part], tokens[part], east[part]], axis=1)

    north = shift(slab(slice(rows - RIM_LAT, rows)), "lat", 1, False)
    south = shift(slab(slice(0, RIM_LAT)), "lat", -1, False)
    inner = list(range(1, bands.count - 1))
    edges = [0, bands.count - 1]
    kinds, consts = bands.constants(inner, block)
    side, attended = vmem_call(
        functools.partial(middle_kernel, bands, inner, kinds),
        [(bands.side_total, 2 * width), (bands.own_at[-1] - bands.own_at[1], width)],
        [west, east, own, qkv_weight] + consts,
        [pltpu.VMEM((bands.side_total, width), BF16)] + attend_scratch(bands, inner, block),
        5 * 10**9,
        "middle_attention",
        exps=500000,
    )
    kinds, consts = bands.constants(edges, block)
    padded = up16(rows * columns // 4)
    return vmem_call(
        functools.partial(edge_kernel, bands, edges, kinds),
        [tokens.shape, (padded, 2 * width), (padded, 2 * width)],
        [tokens, north, south, key_bias(), own, side, attended, qkv_weight, out_weight, bands.patch_matrix()] + consts,
        [
            pltpu.VMEM((2 * bands.slab_padded, width), BF16),
            pltpu.VMEM((2 * bands.slab_padded, 2 * width), BF16),
            pltpu.VMEM((bands.own_total, width), BF16),
        ]
        + attend_scratch(bands, edges, block),
        6 * 10**9,
        "edge_attention",
        exps=300000,
    )


def shift(part, axis, step, wrap):
    size = lax.axis_size(axis)
    pairs = [(i, (i + step) % size) for i in range(size) if wrap or 0 <= i + step < size]
    return lax.ppermute(part, axis, pairs)


def key_bias():
    row = jnp.arange(8, dtype=jnp.int32)[:, None]
    key = jnp.arange(128, dtype=jnp.int32)[None, :] // WLON
    north = (row == 0) & (key < RIM_LAT) & (lax.axis_index("lat") == 0)
    south = (row == 1) & (key >= RIM_LAT) & (lax.axis_index("lat") == lax.axis_size("lat") - 1)
    return jnp.where(north | south, F32(-1e30), F32(0.0))


def place_index():
    me = lax.axis_index("lon")
    return jnp.stack([me // 2, me % 2]).astype(jnp.int32)


def merge_dots(place_ref, upper, lower, mine_ref, pair_ref, x_ref, x_pair_ref, y_ref, y_pair_ref, refs):
    half, block = x_ref.shape
    at = [pl.ds(pl.multiple_of((place_ref[1] + k) % 2 * block, block), block) for k in range(2)]
    own, x, y = refs
    for k, ref in enumerate((mine_ref, pair_ref)):
        own(at[k], dot(upper, ref[:half, :]), dot(lower, ref[half:, :]))
    for k, ref in enumerate((x_ref, x_pair_ref)):
        x(at[k], dot(upper, ref[...]))
    for k, ref in enumerate((y_ref, y_pair_ref)):
        y(at[k], dot(lower, ref[...]))


def merge_own_kernel(place_ref, upper_ref, lower_ref, *refs):
    weights, (own_ref, x_ref, y_ref) = refs[:6], refs[6:]

    def own(at, a, b):
        own_ref[:, at] = a + b

    def x(at, a):
        x_ref[:, at] = a

    def y(at, b):
        y_ref[:, at] = b

    merge_dots(place_ref, upper_ref[...], lower_ref[...], *weights, (own, x, y))


def merge_other_kernel(place_ref, upper_ref, lower_ref, *refs):
    weights, (to_y_ref, to_x_ref) = refs[:6], refs[6:]
    wide = to_x_ref.shape[1] // 2

    def own(at, a, b):
        to_y_ref[:, at] = a.astype(BF16)
        to_x_ref[:, at] = b.astype(BF16)

    def x(at, a):
        to_y_ref[:, pl.ds(pl.multiple_of(wide + at.start, at.size), at.size)] = a.astype(BF16)

    def y(at, b):
        to_x_ref[:, pl.ds(pl.multiple_of(wide + at.start, at.size), at.size)] = b.astype(BF16)

    merge_dots(place_ref, upper_ref[...], lower_ref[...], *weights, (own, x, y))


def combine_kernel(place_ref, own_ref, x_ref, y_ref, from_y_ref, from_x_ref, out_ref):
    wide = own_ref.shape[1]
    chip = place_ref[0]
    from_x, from_y = from_x_ref[...].astype(F32), from_y_ref[...].astype(F32)
    parts = [
        own_ref[...],
        x_ref[...] + from_x[:, :wide],
        y_ref[...] + from_y[:, :wide],
        from_x[:, wide:] + from_y[:, wide:],
    ]
    for m, part in enumerate(parts):
        out_ref[:, pl.ds(pl.multiple_of((chip ^ m) * wide, wide), wide)] = part.astype(BF16)


def local_call(kernel, out, place, args, flops, name, mib=16):
    vmem = pl.BlockSpec(memory_space=pltpu.VMEM)
    return pl.pallas_call(
        kernel,
        in_specs=[pl.BlockSpec(memory_space=pltpu.SMEM)] + [vmem] * len(args),
        out_specs=[vmem] * len(out),
        out_shape=out,
        compiler_params=params(mib),
        cost_estimate=pl.CostEstimate(flops=flops, bytes_accessed=2**20, transcendentals=0),
        name=name,
    )(place, *args)


def merge_by_squares(upper, lower, merge_weight):
    half = merge_weight.shape[0] // 2
    block = merge_weight.shape[1]
    count = upper.shape[0]
    x = chip_swap(merge_weight[:half], 1)
    y = chip_swap(merge_weight[half:], 2)
    x_pair, y_pair, _ = lax.optimization_barrier((x, y, upper))
    weights = [merge_weight, core_swap(merge_weight), x, core_swap(x_pair), y, core_swap(y_pair)]
    place = place_index()
    from_y = chip_swap(upper, 2)
    from_x = chip_swap(lower, 1)
    flops = 16 * count * half * block
    wide = jax.ShapeDtypeStruct((count, 2 * block), F32)
    own = local_call(merge_own_kernel, [wide] * 3, place, [upper, lower] + weights, flops, "merge_own")
    pair = jax.ShapeDtypeStruct((count, 4 * block), BF16)
    to_y, to_x = local_call(merge_other_kernel, [pair] * 2, place, [from_y, from_x] + weights, flops, "merge_other")
    back_y, back_x = chip_swap(to_y, 2), chip_swap(to_x, 1)
    out = jax.ShapeDtypeStruct((count, 8 * block), BF16)
    return local_call(combine_kernel, [out], place, [*own, back_y, back_x], 0, "combine")[0]


def merge(upper, lower, merge_weight):
    if lax.axis_size("lon") == 8:
        return merge_by_squares(upper, lower, merge_weight)
    weight = lax.all_gather(merge_weight, "lon", axis=1, tiled=True)
    return jnp.dot(jnp.concatenate([upper, lower], axis=1), weight, preferred_element_type=F32).astype(BF16)


def ffn_kernel(mine_ref, theirs_ref, up_ref, down_ref, out_mine_ref, out_theirs_ref, normed_ref, hidden_ref):
    count = mine_ref.shape[0]
    for k, ref in enumerate((mine_ref, theirs_ref)):
        normed_ref[k * count : (k + 1) * count, :] = normalize(ref[...].astype(F32)).astype(BF16)
    hidden = hidden_ref.shape[1]
    step = 256
    for at in range(0, hidden, step):
        raw = dot(normed_ref[...], up_ref[:, at : at + step])
        active = 0.5 * raw * (1.0 + lax.erf(raw * np.float32(np.sqrt(0.5))))
        hidden_ref[:, at : at + step] = active.astype(BF16)
    for at in range(0, down_ref.shape[1], step):
        out = dot(hidden_ref[...], down_ref[:, at : at + step]).astype(BF16)
        out_mine_ref[:, at : at + step] = out[:count]
        out_theirs_ref[:, at : at + step] = out[count:]


def feed_forward(mine, theirs, up, down):
    count, width = mine.shape
    hidden = up.shape[1]
    vmem = pl.BlockSpec(memory_space=pltpu.VMEM)
    return pl.pallas_call(
        ffn_kernel,
        in_specs=[vmem] * 4,
        out_specs=[vmem] * 2,
        out_shape=[jax.ShapeDtypeStruct((count, width), BF16)] * 2,
        scratch_shapes=[pltpu.VMEM((2 * count, width), BF16), pltpu.VMEM((2 * count, hidden), BF16)],
        compiler_params=params(20),
        cost_estimate=pl.CostEstimate(
            flops=8 * count * width * hidden, bytes_accessed=4 * width * hidden, transcendentals=2 * count * hidden
        ),
        name="feed_forward",
    )(mine, theirs, up, down)


def core_swap(value):
    size = lax.axis_size("lon")
    return lax.ppermute(value, "lon", [(i, i ^ 1) for i in range(size)])


def chip_swap(value, offset):
    size = lax.axis_size("lon")
    return lax.ppermute(value, "lon", [(i, i ^ (2 * offset)) for i in range(size)])


def per_device(tokens, qkv_weight, out_weight, merge_weight, up_weight, down_weight):
    rows, columns, width = tokens.shape
    bands = Bands(rows, columns)
    cells = rows * columns // 4
    middle_out, upper, lower = attention(bands, tokens, qkv_weight, out_weight)
    coarse = merge(upper, lower, merge_weight)
    chips = lax.axis_size("lon") // 2
    arrived = [coarse] + [chip_swap(coarse, m) for m in range(1, chips)]
    total = coarse.astype(F32)
    for m in range(chips):
        mine, theirs = feed_forward(arrived[m], core_swap(arrived[m]), up_weight, down_weight)
        summed = mine.astype(F32) + core_swap(theirs).astype(F32)
        if m:
            summed = chip_swap(summed.astype(BF16), m).astype(F32)
        total = total + summed
    coarse_out = total[:cells].astype(jnp.bfloat16)
    return (middle_out, coarse_out.reshape(rows // 2, columns // 2, -1))


def solution(mesh):
    return jax.shard_map(
        per_device,
        mesh=mesh,
        in_specs=(P("lat", "lon", None), P(), P(), P(None, "lon"), P(None, "lon"), P("lon", None)),
        out_specs=(P("lat", "lon", None), P("lat", "lon", None)),
        check_vma=False,
    )
```

```python
import functools

import jax
import jax.numpy as jnp
import numpy as np
from jax import lax
from jax.experimental import pallas as pl
from jax.experimental.pallas import tpu as pltpu
from jax.sharding import PartitionSpec as P

HEADS = 16
WLAT = 6
WLON = 12
RIM_LAT = WLAT // 2
RIM_LON = WLON // 2
SIDE = 8
GROUP = 4
F32 = jnp.float32
BF16 = jnp.bfloat16


def up16(n):
    return -(-n // 16) * 16


def params(mib=48, **kw):
    return pltpu.CompilerParams(vmem_limit_bytes=mib * 2**20, **kw)


class Bands:
    def __init__(self, rows, columns):
        assert (rows - WLAT) % WLAT == 0 and (columns - WLON) % WLON == 0
        self.rows, self.columns = rows, columns
        inner = (rows - WLAT) // WLAT
        self.height = [RIM_LAT] + [WLAT] * inner + [RIM_LAT]
        self.count = len(self.height)
        self.first = [sum(self.height[:b]) for b in range(self.count)]
        self.widths = [RIM_LON] + [WLON] * ((columns - WLON) // WLON) + [RIM_LON]
        self.own = [h * columns for h in self.height]
        self.own_padded = [up16(n) for n in self.own]
        self.own_at = [sum(self.own_padded[:b]) for b in range(self.count)]
        self.own_total = sum(self.own_padded)
        self.side = [2 * h * SIDE for h in self.height]
        assert all(n % 16 == 0 for n in self.side)
        self.side_at = [sum(self.side[:b]) for b in range(self.count)]
        self.side_total = sum(self.side)
        self.slab = columns + 2 * SIDE
        self.slab_padded = up16(RIM_LAT * self.slab)
        self.window = up16(WLAT * WLON)
        self.counts = [[GROUP * h * w for w in self.widths] for h in self.height]
        self.counts_padded = [[up16(n) for n in row] for row in self.counts]

    def edge(self, b):
        return b in (0, self.count - 1)

    def sources(self, b):
        return self.own_padded[b] + self.side[b] + (self.slab_padded if self.edge(b) else 0)

    def source(self, b, i, j):
        columns, h, first = self.columns, self.height[b], self.first[b]
        at = self.own_padded[b]
        if not 0 <= i < self.rows:
            i = i + RIM_LAT if i < 0 else i - self.rows
            return at + self.side[b] + i * self.slab + j + SIDE
        if 0 <= j < columns:
            return (i - first) * columns + j
        at += (i - first) * SIDE
        return at + (j + SIDE if j < 0 else h * SIDE + j - columns)

    def key_matrix(self, b):
        g = np.zeros((len(self.widths) * self.window, self.sources(b)), np.float32)
        top = self.first[b] - (RIM_LAT if b == 0 else 0)
        for c in range(len(self.widths)):
            for i in range(WLAT):
                for j in range(WLON):
                    at = c * self.window + i * WLON + j
                    g[at, self.source(b, top + i, c * WLON - RIM_LON + j)] = 1
        return g.astype(BF16)

    def query_matrix(self, b):
        total = sum(self.counts_padded[b])
        g = np.zeros((total, self.own_padded[b]), np.float32)
        head = np.zeros((total,), np.int32)
        start = left = 0
        for width, padded in zip(self.widths, self.counts_padded[b]):
            at = start
            for k in range(GROUP):
                for i in range(self.height[b]):
                    for j in range(width):
                        g[at, i * self.columns + left + j] = 1
                        head[at] = k
                        at += 1
            left += width
            start += padded
        return g.astype(BF16), head

    def patch_matrix(self):
        cells = self.rows * self.columns // 4
        padded = up16(cells)
        g = np.zeros((4 * padded, self.rows * self.columns), np.float32)
        for r in range(self.rows // 2):
            for c in range(self.columns // 2):
                for k in range(4):
                    to = k * padded + r * (self.columns // 2) + c
                    g[to, (2 * r + k // 2) * self.columns + 2 * c + k % 2] = 1
        return g.astype(BF16)

    def constants(self, some, block):
        distinct, kinds, consts = [], [], []
        for b in some:
            kind = (self.height[b], b == 0, b == self.count - 1)
            if kind not in distinct:
                distinct.append(kind)
                query, head = self.query_matrix(b)
                mask = head[:, None] == (np.arange(block) // (block // GROUP))[None, :]
                scale = np.float32((block // GROUP) ** -0.5)
                scaled = (query.astype(np.float32) * scale).astype(BF16)
                consts += [self.key_matrix(b), scaled, mask.astype(BF16), np.ascontiguousarray(query.T)]
            kinds.append(4 * distinct.index(kind))
        return kinds, consts


def normalize(values):
    center = values - jnp.mean(values, axis=-1, keepdims=True)
    spread = jnp.mean(center * center, axis=-1, keepdims=True)
    return center * lax.rsqrt(spread + 1e-05)


def dot(a, b, dims=((1,), (0,))):
    return lax.dot_general(a, b, (dims, ((), ())), preferred_element_type=F32)


def flat_normed(ref):
    values = ref[...].astype(F32)
    return normalize(values.reshape(-1, values.shape[-1]))


def padded_rows(values, total):
    if values.shape[0] == total:
        return values
    return jnp.concatenate([values, jnp.zeros((total - values.shape[0], values.shape[1]), values.dtype)], axis=0)


def project(normed_ref, weight_ref, out_ref, first):
    step = 256
    for at in range(0, out_ref.shape[1], step):
        part = weight_ref[:, first + at : first + at + step]
        out_ref[:, at : at + step] = dot(normed_ref[...], part).astype(BF16)


def own_kernel(bands, tokens_ref, weight_ref, out_ref, normed_ref):
    normed = flat_normed(tokens_ref)
    for b in range(bands.count):
        at = bands.first[b] * bands.columns
        part = padded_rows(normed[at : at + bands.own[b]], bands.own_padded[b])
        normed_ref[bands.own_at[b] : bands.own_at[b] + bands.own_padded[b], :] = part.astype(BF16)
    project(normed_ref, weight_ref, out_ref, 0)


def attend(bands, some, kinds, consts, own_ref, outer, bias_ref, put, scratch):
    k_ref, v_ref, q_ref, p_ref, r_ref = scratch
    width = own_ref.shape[1] // 3
    block = width * GROUP // HEADS
    window = WLAT * WLON
    units = [(n, b, g) for n, b in enumerate(some) for g in range(HEADS // GROUP)]
    for u, (n, b, g) in enumerate(units):
        keys, query, mask, _ = consts[kinds[n] : kinds[n] + 4]
        own = slice(bands.own_at[b], bands.own_at[b] + bands.own_padded[b])
        for ref, skip in ((k_ref, 0), (v_ref, width)):
            parts = [own_ref[own, width + skip + g * block : width + skip + (g + 1) * block]]
            for out_ref, at, size in outer(b):
                parts.append(out_ref[at : at + size, skip + g * block : skip + (g + 1) * block])
            ref[u] = dot(keys[...], jnp.concatenate(parts, axis=0)).astype(BF16)
        total = query.shape[0]
        q_ref[u, :total] = dot(query[...], own_ref[own, g * block : (g + 1) * block]).astype(BF16) * mask[...]
    for u, (n, b, g) in enumerate(units):
        at = 0
        for c, count in enumerate(bands.counts_padded[b]):
            scores = dot(
                q_ref[u, at : at + count], k_ref[u, c * bands.window : c * bands.window + window], ((1,), (1,))
            )
            if b == 0:
                scores = scores + bias_ref[0:1, :window]
            if b == bands.count - 1:
                scores = scores + bias_ref[1:2, :window]
            raised = jnp.exp(scores - jnp.max(scores, axis=-1, keepdims=True))
            weights = raised * (1.0 / jnp.sum(raised, axis=-1, keepdims=True))
            p_ref[u, at : at + count, :window] = weights.astype(BF16)
            at += count
    for u, (n, b, g) in enumerate(units):
        mask = consts[kinds[n] + 2]
        at = 0
        for c, count in enumerate(bands.counts_padded[b]):
            mixed = dot(
                p_ref[u, at : at + count, :window], v_ref[u, c * bands.window : c * bands.window + window]
            )
            r_ref[u, at : at + count] = mixed.astype(BF16) * mask[at : at + count]
            at += count
    for u, (n, b, g) in enumerate(units):
        back = consts[kinds[n] + 3]
        put(b, g, dot(back[...], r_ref[u, : back.shape[1]]).astype(BF16))


def attend_scratch(bands, some, block):
    units = len(some) * HEADS // GROUP
    keys = len(bands.widths) * bands.window
    rows = max(sum(bands.counts_padded[b]) for b in some)
    return [
        pltpu.VMEM((units, keys, block), BF16),
        pltpu.VMEM((units, keys, block), BF16),
        pltpu.VMEM((units, rows, block), BF16),
        pltpu.VMEM((units, rows, 128), BF16),
        pltpu.VMEM((units, rows, block), BF16),
    ]


def middle_kernel(bands, some, kinds, west_ref, east_ref, own_ref, weight_ref, *rest):
    consts, (side_ref, out_ref, normed_ref, *scratch) = rest[:-8], rest[-8:]
    width = weight_ref.shape[0]
    west, east = flat_normed(west_ref), flat_normed(east_ref)
    for b in range(bands.count):
        at, size = bands.first[b] * SIDE, bands.height[b] * SIDE
        part = jnp.concatenate([west[at : at + size], east[at : at + size]], axis=0)
        normed_ref[bands.side_at[b] : bands.side_at[b] + bands.side[b], :] = part.astype(BF16)
    project(normed_ref, weight_ref, side_ref, width)

    def outer(b):
        return [(side_ref, bands.side_at[b], bands.side[b])]

    def put(b, g, value):
        at = bands.own_at[b] - bands.own_at[1]
        block = value.shape[1]
        out_ref[at : at + bands.own_padded[b], g * block : (g + 1) * block] = value

    attend(bands, some, kinds, consts, own_ref, outer, None, put, scratch)


def edge_kernel(bands, some, kinds, tokens_ref, north_ref, south_ref, bias_ref, own_ref, side_ref, inner_ref, weight_ref, out_w_ref, patch_ref, *rest):
    consts, rest = rest[:-11], rest[-11:]
    middle_ref, upper_ref, lower_ref, normed_ref, slab_ref, attended_ref, *scratch = rest
    rows, columns, width = tokens_ref.shape
    slab = bands.slab_padded
    for k, ref in enumerate((north_ref, south_ref)):
        normed_ref[k * slab : (k + 1) * slab, :] = padded_rows(flat_normed(ref), slab).astype(BF16)
    project(normed_ref, weight_ref, slab_ref, width)

    def outer(b):
        return [
            (side_ref, bands.side_at[b], bands.side[b]),
            (slab_ref, 0 if b == 0 else slab, slab),
        ]

    def put(b, g, value):
        block = value.shape[1]
        attended_ref[bands.own_at[b] : bands.own_at[b] + bands.own_padded[b], g * block : (g + 1) * block] = value

    attended_ref[bands.own_at[1] : bands.own_at[-1], :] = inner_ref[...]
    attend(bands, some, kinds, consts, own_ref, outer, bias_ref, put, scratch)
    mixed = dot(attended_ref[...], out_w_ref[...])
    mixed = jnp.concatenate([mixed[at : at + n] for at, n in zip(bands.own_at, bands.own)], axis=0)
    middle = tokens_ref[...].astype(F32) + mixed.reshape(rows, columns, width)
    middle_ref[...] = middle.astype(BF16)
    middle = middle.reshape(rows * columns, width).astype(BF16)
    padded = patch_ref.shape[0] // 4
    parts = [dot(patch_ref[k * padded : (k + 1) * padded, :], middle) for k in range(4)]
    total = sum(jnp.sum(p, axis=-1, keepdims=True) for p in parts)
    mean = total * (1.0 / (4 * width))
    parts = [p - mean for p in parts]
    spread = sum(jnp.sum(p * p, axis=-1, keepdims=True) for p in parts)
    factor = lax.rsqrt(spread * (1.0 / (4 * width)) + 1e-05)
    for k in range(4):
        ref = (upper_ref, lower_ref)[k // 2]
        ref[:, k % 2 * width : (k % 2 + 1) * width] = (parts[k] * factor).astype(BF16)


def vmem_call(kernel, out, args, scratch, flops, name, mib=24, exps=0):
    vmem = pl.BlockSpec(memory_space=pltpu.VMEM)
    return pl.pallas_call(
        kernel,
        in_specs=[vmem] * len(args),
        out_specs=[vmem] * len(out),
        out_shape=[jax.ShapeDtypeStruct(shape, BF16) for shape in out],
        scratch_shapes=scratch,
        compiler_params=params(mib),
        cost_estimate=pl.CostEstimate(flops=flops, bytes_accessed=2**20, transcendentals=exps),
        name=name,
    )(*args)


def attention(bands, tokens, qkv_weight, out_weight):
    rows, columns, width = tokens.shape
    block = width * GROUP // HEADS
    west = shift(tokens[:, columns - SIDE :], "lon", 1, True)
    east = shift(tokens[:, :SIDE], "lon", -1, True)
    own = vmem_call(
        functools.partial(own_kernel, bands),
        [(bands.own_total, 3 * width)],
        [tokens, qkv_weight],
        [pltpu.VMEM((bands.own_total, width), BF16)],
        6 * bands.own_total * width * width,
        "own_projection",
        mib=16,
    )[0]

    def slab(part):
        return jnp.concatenate([west[part], tokens[part], east[part]], axis=1)

    north = shift(slab(slice(rows - RIM_LAT, rows)), "lat", 1, False)
    south = shift(slab(slice(0, RIM_LAT)), "lat", -1, False)
    inner = list(range(1, bands.count - 1))
    edges = [0, bands.count - 1]
    kinds, consts = bands.constants(inner, block)
    side, attended = vmem_call(
        functools.partial(middle_kernel, bands, inner, kinds),
        [(bands.side_total, 2 * width), (bands.own_at[-1] - bands.own_at[1], width)],
        [west, east, own, qkv_weight] + consts,
        [pltpu.VMEM((bands.side_total, width), BF16)] + attend_scratch(bands, inner, block),
        5 * 10**9,
        "middle_attention",
        exps=500000,
    )
    kinds, consts = bands.constants(edges, block)
    padded = up16(rows * columns // 4)
    return vmem_call(
        functools.partial(edge_kernel, bands, edges, kinds),
        [tokens.shape, (padded, 2 * width), (padded, 2 * width)],
        [tokens, north, south, key_bias(), own, side, attended, qkv_weight, out_weight, bands.patch_matrix()] + consts,
        [
            pltpu.VMEM((2 * bands.slab_padded, width), BF16),
            pltpu.VMEM((2 * bands.slab_padded, 2 * width), BF16),
            pltpu.VMEM((bands.own_total, width), BF16),
        ]
        + attend_scratch(bands, edges, block),
        6 * 10**9,
        "edge_attention",
        exps=300000,
    )


def shift(part, axis, step, wrap):
    size = lax.axis_size(axis)
    pairs = [(i, (i + step) % size) for i in range(size) if wrap or 0 <= i + step < size]
    return lax.ppermute(part, axis, pairs)


def key_bias():
    row = jnp.arange(8, dtype=jnp.int32)[:, None]
    key = jnp.arange(128, dtype=jnp.int32)[None, :] // WLON
    north = (row == 0) & (key < RIM_LAT) & (lax.axis_index("lat") == 0)
    south = (row == 1) & (key >= RIM_LAT) & (lax.axis_index("lat") == lax.axis_size("lat") - 1)
    return jnp.where(north | south, F32(-1e30), F32(0.0))


def place_index():
    me = lax.axis_index("lon")
    return jnp.stack([me // 2, me % 2]).astype(jnp.int32)


def merge_dots(place_ref, upper, lower, mine_ref, pair_ref, x_ref, x_pair_ref, y_ref, y_pair_ref, refs):
    half, block = x_ref.shape
    at = [pl.ds(pl.multiple_of((place_ref[1] + k) % 2 * block, block), block) for k in range(2)]
    own, x, y = refs
    for k, ref in enumerate((mine_ref, pair_ref)):
        own(at[k], dot(upper, ref[:half, :]), dot(lower, ref[half:, :]))
    for k, ref in enumerate((x_ref, x_pair_ref)):
        x(at[k], dot(upper, ref[...]))
    for k, ref in enumerate((y_ref, y_pair_ref)):
        y(at[k], dot(lower, ref[...]))


def merge_own_kernel(place_ref, upper_ref, lower_ref, *refs):
    weights, (own_ref, x_ref, y_ref) = refs[:6], refs[6:]

    def own(at, a, b):
        own_ref[:, at] = a + b

    def x(at, a):
        x_ref[:, at] = a

    def y(at, b):
        y_ref[:, at] = b

    merge_dots(place_ref, upper_ref[...], lower_ref[...], *weights, (own, x, y))


def merge_other_kernel(place_ref, upper_ref, lower_ref, *refs):
    weights, (to_y_ref, to_x_ref) = refs[:6], refs[6:]
    wide = to_x_ref.shape[1] // 2

    def own(at, a, b):
        to_y_ref[:, at] = a.astype(BF16)
        to_x_ref[:, at] = b.astype(BF16)

    def x(at, a):
        to_y_ref[:, pl.ds(pl.multiple_of(wide + at.start, at.size), at.size)] = a.astype(BF16)

    def y(at, b):
        to_x_ref[:, pl.ds(pl.multiple_of(wide + at.start, at.size), at.size)] = b.astype(BF16)

    merge_dots(place_ref, upper_ref[...], lower_ref[...], *weights, (own, x, y))


def combine_kernel(place_ref, own_ref, x_ref, y_ref, from_y_ref, from_x_ref, out_ref, low_ref, high_ref):
    wide = own_ref.shape[1]
    chip = place_ref[0]
    from_x, from_y = from_x_ref[...].astype(F32), from_y_ref[...].astype(F32)
    parts = [
        own_ref[...],
        x_ref[...] + from_x[:, :wide],
        y_ref[...] + from_y[:, :wide],
        from_x[:, wide:] + from_y[:, wide:],
    ]
    for m, part in enumerate(parts):
        out_ref[:, pl.ds(pl.multiple_of((chip ^ m) * wide, wide), wide)] = part.astype(BF16)
    low_ref[...] = out_ref[:, : 2 * wide]
    high_ref[...] = out_ref[:, 2 * wide :]


def local_call(kernel, out, place, args, flops, name, mib=16):
    vmem = pl.BlockSpec(memory_space=pltpu.VMEM)
    return pl.pallas_call(
        kernel,
        in_specs=[pl.BlockSpec(memory_space=pltpu.SMEM)] + [vmem] * len(args),
        out_specs=[vmem] * len(out),
        out_shape=out,
        compiler_params=params(mib),
        cost_estimate=pl.CostEstimate(flops=flops, bytes_accessed=2**20, transcendentals=0),
        name=name,
    )(place, *args)


def merge_by_squares(upper, lower, merge_weight):
    half = merge_weight.shape[0] // 2
    block = merge_weight.shape[1]
    count = upper.shape[0]
    x = chip_swap(merge_weight[:half], 1)
    y = chip_swap(merge_weight[half:], 2)
    x_pair, y_pair, _ = lax.optimization_barrier((x, y, upper))
    weights = [merge_weight, core_swap(merge_weight), x, core_swap(x_pair), y, core_swap(y_pair)]
    place = place_index()
    from_y = chip_swap(upper, 2)
    from_x = chip_swap(lower, 1)
    flops = 16 * count * half * block
    wide = jax.ShapeDtypeStruct((count, 2 * block), F32)
    own = local_call(merge_own_kernel, [wide] * 3, place, [upper, lower] + weights, flops, "merge_own")
    pair = jax.ShapeDtypeStruct((count, 4 * block), BF16)
    to_y, to_x = local_call(merge_other_kernel, [pair] * 2, place, [from_y, from_x] + weights, flops, "merge_other")
    back_y, back_x = chip_swap(to_y, 2), chip_swap(to_x, 1)
    outs = [jax.ShapeDtypeStruct((count, n * block), BF16) for n in (8, 4, 4)]
    return local_call(combine_kernel, outs, place, [*own, back_y, back_x], 0, "combine")


def ffn_kernel(pieces, *refs):
    inputs, (up_ref, down_ref, out_mine_ref, out_theirs_ref, normed_ref, hidden_ref) = refs[:-6], refs[-6:]
    count = out_mine_ref.shape[0]
    for k in range(2):
        parts = [ref[...].astype(F32) for ref in inputs[k * pieces : (k + 1) * pieces]]
        values = jnp.concatenate(parts, axis=1) if pieces > 1 else parts[0]
        normed_ref[k * count : (k + 1) * count, :] = normalize(values).astype(BF16)
    hidden = hidden_ref.shape[1]
    step = 256
    for at in range(0, hidden, step):
        raw = dot(normed_ref[...], up_ref[:, at : at + step])
        active = 0.5 * raw * (1.0 + lax.erf(raw * np.float32(np.sqrt(0.5))))
        hidden_ref[:, at : at + step] = active.astype(BF16)
    for at in range(0, down_ref.shape[1], step):
        out = dot(hidden_ref[...], down_ref[:, at : at + step]).astype(BF16)
        out_mine_ref[:, at : at + step] = out[:count]
        out_theirs_ref[:, at : at + step] = out[count:]


def feed_forward(mine, theirs, up, down):
    count = mine[0].shape[0]
    width, hidden = up.shape
    vmem = pl.BlockSpec(memory_space=pltpu.VMEM)
    return pl.pallas_call(
        functools.partial(ffn_kernel, len(mine)),
        in_specs=[vmem] * (2 * len(mine) + 2),
        out_specs=[vmem] * 2,
        out_shape=[jax.ShapeDtypeStruct((count, width), BF16)] * 2,
        scratch_shapes=[pltpu.VMEM((2 * count, width), BF16), pltpu.VMEM((2 * count, hidden), BF16)],
        compiler_params=params(20),
        cost_estimate=pl.CostEstimate(flops=2**10, bytes_accessed=2**10, transcendentals=0),
        name="feed_forward",
    )(*mine, *theirs, up, down)


def core_swap(value):
    size = lax.axis_size("lon")
    return lax.ppermute(value, "lon", [(i, i ^ 1) for i in range(size)])


def chip_swap(value, offset):
    size = lax.axis_size("lon")
    return lax.ppermute(value, "lon", [(i, i ^ (2 * offset)) for i in range(size)])


def coarse_by_squares(upper, lower, merge_weight, up, down):
    whole, low, high = merge_by_squares(upper, lower, merge_weight)
    y_low, x_high = chip_swap(low, 2), chip_swap(high, 1)
    y_high, x_low = chip_swap(high, 2), chip_swap(low, 1)
    first = feed_forward([whole], [core_swap(whole)], up, down)
    y_low, x_high, mine, theirs = lax.optimization_barrier((y_low, x_high, *first))
    d_low, d_high = chip_swap(y_low, 1), chip_swap(x_high, 2)
    total = whole.astype(F32) + mine.astype(F32) + core_swap(theirs).astype(F32)
    sums = []
    for m, pieces in ((1, [x_low, x_high]), (2, [y_low, y_high]), (3, [d_low, d_high])):
        pairs = [core_swap(p) for p in pieces]
        if m == 3:
            *pairs, sums[0], sums[1] = lax.optimization_barrier((*pairs, *sums))
        mine, theirs = feed_forward(pieces, pairs, up, down)
        sums.append((mine.astype(F32) + core_swap(theirs).astype(F32)).astype(BF16))
    for m in (1, 2, 3):
        total = total + chip_swap(sums[m - 1], m).astype(F32)
    return total


def coarse_by_chips(upper, lower, merge_weight, up, down):
    weight = lax.all_gather(merge_weight, "lon", axis=1, tiled=True)
    patches = jnp.concatenate([upper, lower], axis=1)
    coarse = jnp.dot(patches, weight, preferred_element_type=F32).astype(BF16)
    chips = lax.axis_size("lon") // 2
    arrived = [coarse] + [chip_swap(coarse, m) for m in range(1, chips)]
    total = coarse.astype(F32)
    for m in range(chips):
        mine, theirs = feed_forward([arrived[m]], [core_swap(arrived[m])], up, down)
        summed = mine.astype(F32) + core_swap(theirs).astype(F32)
        if m:
            summed = chip_swap(summed.astype(BF16), m).astype(F32)
        total = total + summed
    return total


def per_device(tokens, qkv_weight, out_weight, merge_weight, up_weight, down_weight):
    rows, columns, width = tokens.shape
    bands = Bands(rows, columns)
    cells = rows * columns // 4
    middle_out, upper, lower = attention(bands, tokens, qkv_weight, out_weight)
    coarse = coarse_by_squares if lax.axis_size("lon") == 8 else coarse_by_chips
    total = coarse(upper, lower, merge_weight, up_weight, down_weight)
    coarse_out = total[:cells].astype(jnp.bfloat16)
    return (middle_out, coarse_out.reshape(rows // 2, columns // 2, -1))


def solution(mesh):
    return jax.shard_map(
        per_device,
        mesh=mesh,
        in_specs=(P("lat", "lon", None), P(), P(), P(None, "lon"), P(None, "lon"), P("lon", None)),
        out_specs=(P("lat", "lon", None), P("lat", "lon", None)),
        check_vma=False,
    )
```

```python
import functools

import jax
import jax.numpy as jnp
import numpy as np
from jax import lax
from jax.experimental import pallas as pl
from jax.experimental.pallas import tpu as pltpu
from jax.sharding import PartitionSpec as P

HEADS = 16
WLAT = 6
WLON = 12
RIM_LAT = WLAT // 2
RIM_LON = WLON // 2
SIDE = 8
GROUP = 4
F32 = jnp.float32
BF16 = jnp.bfloat16


def up16(n):
    return -(-n // 16) * 16


def params(mib=48, **kw):
    return pltpu.CompilerParams(vmem_limit_bytes=mib * 2**20, **kw)


class Bands:
    def __init__(self, rows, columns):
        assert (rows - WLAT) % WLAT == 0 and (columns - WLON) % WLON == 0
        self.rows, self.columns = rows, columns
        inner = (rows - WLAT) // WLAT
        self.height = [RIM_LAT] + [WLAT] * inner + [RIM_LAT]
        self.count = len(self.height)
        self.first = [sum(self.height[:b]) for b in range(self.count)]
        self.widths = [RIM_LON] + [WLON] * ((columns - WLON) // WLON) + [RIM_LON]
        self.own = [h * columns for h in self.height]
        self.own_padded = [up16(n) for n in self.own]
        self.own_at = [sum(self.own_padded[:b]) for b in range(self.count)]
        self.own_total = sum(self.own_padded)
        self.side = [2 * h * SIDE for h in self.height]
        assert all(n % 16 == 0 for n in self.side)
        self.side_at = [sum(self.side[:b]) for b in range(self.count)]
        self.side_total = sum(self.side)
        self.slab = columns + 2 * SIDE
        self.slab_padded = up16(RIM_LAT * self.slab)
        self.window = up16(WLAT * WLON)
        self.counts = [[GROUP * h * w for w in self.widths] for h in self.height]
        self.counts_padded = [[up16(n) for n in row] for row in self.counts]

    def edge(self, b):
        return b in (0, self.count - 1)

    def sources(self, b):
        return self.own_padded[b] + self.side[b] + (self.slab_padded if self.edge(b) else 0)

    def source(self, b, i, j):
        columns, h, first = self.columns, self.height[b], self.first[b]
        at = self.own_padded[b]
        if not 0 <= i < self.rows:
            i = i + RIM_LAT if i < 0 else i - self.rows
            return at + self.side[b] + i * self.slab + j + SIDE
        if 0 <= j < columns:
            return (i - first) * columns + j
        at += (i - first) * SIDE
        return at + (j + SIDE if j < 0 else h * SIDE + j - columns)

    def key_matrix(self, b):
        g = np.zeros((len(self.widths) * self.window, self.sources(b)), np.float32)
        top = self.first[b] - (RIM_LAT if b == 0 else 0)
        for c in range(len(self.widths)):
            for i in range(WLAT):
                for j in range(WLON):
                    at = c * self.window + i * WLON + j
                    g[at, self.source(b, top + i, c * WLON - RIM_LON + j)] = 1
        return g.astype(BF16)

    def query_matrix(self, b):
        total = sum(self.counts_padded[b])
        g = np.zeros((total, self.own_padded[b]), np.float32)
        head = np.zeros((total,), np.int32)
        start = left = 0
        for width, padded in zip(self.widths, self.counts_padded[b]):
            at = start
            for k in range(GROUP):
                for i in range(self.height[b]):
                    for j in range(width):
                        g[at, i * self.columns + left + j] = 1
                        head[at] = k
                        at += 1
            left += width
            start += padded
        return g.astype(BF16), head

    def patch_matrix(self):
        cells = self.rows * self.columns // 4
        padded = up16(cells)
        g = np.zeros((4 * padded, self.rows * self.columns), np.float32)
        for r in range(self.rows // 2):
            for c in range(self.columns // 2):
                for k in range(4):
                    to = k * padded + r * (self.columns // 2) + c
                    g[to, (2 * r + k // 2) * self.columns + 2 * c + k % 2] = 1
        return g.astype(BF16)

    def constants(self, some, block):
        distinct, kinds, consts = [], [], []
        for b in some:
            kind = (self.height[b], b == 0, b == self.count - 1)
            if kind not in distinct:
                distinct.append(kind)
                query, head = self.query_matrix(b)
                mask = head[:, None] == (np.arange(block) // (block // GROUP))[None, :]
                scale = np.float32((block // GROUP) ** -0.5)
                scaled = (query.astype(np.float32) * scale).astype(BF16)
                consts += [self.key_matrix(b), scaled, mask.astype(BF16), np.ascontiguousarray(query.T)]
            kinds.append(4 * distinct.index(kind))
        return kinds, consts


def normalize(values):
    center = values - jnp.mean(values, axis=-1, keepdims=True)
    spread = jnp.mean(center * center, axis=-1, keepdims=True)
    return center * lax.rsqrt(spread + 1e-05)


def dot(a, b, dims=((1,), (0,))):
    return lax.dot_general(a, b, (dims, ((), ())), preferred_element_type=F32)


def flat_normed(ref):
    values = ref[...].astype(F32)
    return normalize(values.reshape(-1, values.shape[-1]))


def padded_rows(values, total):
    if values.shape[0] == total:
        return values
    return jnp.concatenate([values, jnp.zeros((total - values.shape[0], values.shape[1]), values.dtype)], axis=0)


def project(normed_ref, weight_ref, out_ref, first):
    step = 256
    for at in range(0, out_ref.shape[1], step):
        part = weight_ref[:, first + at : first + at + step]
        out_ref[:, at : at + step] = dot(normed_ref[...], part).astype(BF16)


def own_kernel(bands, tokens_ref, weight_ref, out_ref, normed_ref):
    normed = flat_normed(tokens_ref)
    for b in range(bands.count):
        at = bands.first[b] * bands.columns
        part = padded_rows(normed[at : at + bands.own[b]], bands.own_padded[b])
        normed_ref[bands.own_at[b] : bands.own_at[b] + bands.own_padded[b], :] = part.astype(BF16)
    project(normed_ref, weight_ref, out_ref, 0)


def attend(bands, some, kinds, consts, own_ref, outer, bias_ref, put, scratch):
    k_ref, v_ref, q_ref, p_ref, r_ref = scratch
    width = own_ref.shape[1] // 3
    block = width * GROUP // HEADS
    window = WLAT * WLON
    units = [(n, b, g) for n, b in enumerate(some) for g in range(HEADS // GROUP)]
    for u, (n, b, g) in enumerate(units):
        keys, query, mask, _ = consts[kinds[n] : kinds[n] + 4]
        own = slice(bands.own_at[b], bands.own_at[b] + bands.own_padded[b])
        for ref, skip in ((k_ref, 0), (v_ref, width)):
            parts = [own_ref[own, width + skip + g * block : width + skip + (g + 1) * block]]
            for out_ref, at, size in outer(b):
                parts.append(out_ref[at : at + size, skip + g * block : skip + (g + 1) * block])
            ref[u] = dot(keys[...], jnp.concatenate(parts, axis=0)).astype(BF16)
        total = query.shape[0]
        q_ref[u, :total] = dot(query[...], own_ref[own, g * block : (g + 1) * block]).astype(BF16) * mask[...]
    for u, (n, b, g) in enumerate(units):
        at = 0
        for c, count in enumerate(bands.counts_padded[b]):
            scores = dot(
                q_ref[u, at : at + count], k_ref[u, c * bands.window : c * bands.window + window], ((1,), (1,))
            )
            if b == 0:
                scores = scores + bias_ref[0:1, :window]
            if b == bands.count - 1:
                scores = scores + bias_ref[1:2, :window]
            raised = jnp.exp(scores - jnp.max(scores, axis=-1, keepdims=True))
            weights = raised * (1.0 / jnp.sum(raised, axis=-1, keepdims=True))
            p_ref[u, at : at + count, :window] = weights.astype(BF16)
            at += count
    for u, (n, b, g) in enumerate(units):
        mask = consts[kinds[n] + 2]
        at = 0
        for c, count in enumerate(bands.counts_padded[b]):
            mixed = dot(
                p_ref[u, at : at + count, :window], v_ref[u, c * bands.window : c * bands.window + window]
            )
            r_ref[u, at : at + count] = mixed.astype(BF16) * mask[at : at + count]
            at += count
    for u, (n, b, g) in enumerate(units):
        back = consts[kinds[n] + 3]
        put(b, g, dot(back[...], r_ref[u, : back.shape[1]]).astype(BF16))


def attend_scratch(bands, some, block):
    units = len(some) * HEADS // GROUP
    keys = len(bands.widths) * bands.window
    rows = max(sum(bands.counts_padded[b]) for b in some)
    return [
        pltpu.VMEM((units, keys, block), BF16),
        pltpu.VMEM((units, keys, block), BF16),
        pltpu.VMEM((units, rows, block), BF16),
        pltpu.VMEM((units, rows, 128), BF16),
        pltpu.VMEM((units, rows, block), BF16),
    ]


def middle_kernel(bands, some, kinds, west_ref, east_ref, own_ref, weight_ref, *rest):
    consts, (side_ref, out_ref, normed_ref, *scratch) = rest[:-8], rest[-8:]
    width = weight_ref.shape[0]
    west, east = flat_normed(west_ref), flat_normed(east_ref)
    for b in range(bands.count):
        at, size = bands.first[b] * SIDE, bands.height[b] * SIDE
        part = jnp.concatenate([west[at : at + size], east[at : at + size]], axis=0)
        normed_ref[bands.side_at[b] : bands.side_at[b] + bands.side[b], :] = part.astype(BF16)
    project(normed_ref, weight_ref, side_ref, width)

    def outer(b):
        return [(side_ref, bands.side_at[b], bands.side[b])]

    def put(b, g, value):
        at = bands.own_at[b] - bands.own_at[1]
        block = value.shape[1]
        out_ref[at : at + bands.own_padded[b], g * block : (g + 1) * block] = value

    attend(bands, some, kinds, consts, own_ref, outer, None, put, scratch)


def edge_kernel(bands, some, kinds, tokens_ref, north_ref, south_ref, bias_ref, own_ref, side_ref, inner_ref, weight_ref, out_w_ref, patch_ref, *rest):
    consts, rest = rest[:-11], rest[-11:]
    middle_ref, upper_ref, lower_ref, normed_ref, slab_ref, attended_ref, *scratch = rest
    rows, columns, width = tokens_ref.shape
    slab = bands.slab_padded
    for k, ref in enumerate((north_ref, south_ref)):
        normed_ref[k * slab : (k + 1) * slab, :] = padded_rows(flat_normed(ref), slab).astype(BF16)
    project(normed_ref, weight_ref, slab_ref, width)

    def outer(b):
        return [
            (side_ref, bands.side_at[b], bands.side[b]),
            (slab_ref, 0 if b == 0 else slab, slab),
        ]

    def put(b, g, value):
        block = value.shape[1]
        attended_ref[bands.own_at[b] : bands.own_at[b] + bands.own_padded[b], g * block : (g + 1) * block] = value

    attended_ref[bands.own_at[1] : bands.own_at[-1], :] = inner_ref[...]
    attend(bands, some, kinds, consts, own_ref, outer, bias_ref, put, scratch)
    mixed = dot(attended_ref[...], out_w_ref[...])
    mixed = jnp.concatenate([mixed[at : at + n] for at, n in zip(bands.own_at, bands.own)], axis=0)
    middle = tokens_ref[...].astype(F32) + mixed.reshape(rows, columns, width)
    middle_ref[...] = middle.astype(BF16)
    middle = middle.reshape(rows * columns, width).astype(BF16)
    padded = patch_ref.shape[0] // 4
    parts = [dot(patch_ref[k * padded : (k + 1) * padded, :], middle) for k in range(4)]
    total = sum(jnp.sum(p, axis=-1, keepdims=True) for p in parts)
    mean = total * (1.0 / (4 * width))
    parts = [p - mean for p in parts]
    spread = sum(jnp.sum(p * p, axis=-1, keepdims=True) for p in parts)
    factor = lax.rsqrt(spread * (1.0 / (4 * width)) + 1e-05)
    for k in range(4):
        ref = (upper_ref, lower_ref)[k // 2]
        ref[:, k % 2 * width : (k % 2 + 1) * width] = (parts[k] * factor).astype(BF16)


def vmem_call(kernel, out, args, scratch, flops, name, mib=24, exps=0):
    vmem = pl.BlockSpec(memory_space=pltpu.VMEM)
    return pl.pallas_call(
        kernel,
        in_specs=[vmem] * len(args),
        out_specs=[vmem] * len(out),
        out_shape=[jax.ShapeDtypeStruct(shape, BF16) for shape in out],
        scratch_shapes=scratch,
        compiler_params=params(mib),
        cost_estimate=pl.CostEstimate(flops=flops, bytes_accessed=2**20, transcendentals=exps),
        name=name,
    )(*args)


def attention(bands, tokens, qkv_weight, out_weight):
    rows, columns, width = tokens.shape
    block = width * GROUP // HEADS
    west = shift(tokens[:, columns - SIDE :], "lon", 1, True)
    east = shift(tokens[:, :SIDE], "lon", -1, True)
    own = vmem_call(
        functools.partial(own_kernel, bands),
        [(bands.own_total, 3 * width)],
        [tokens, qkv_weight],
        [pltpu.VMEM((bands.own_total, width), BF16)],
        6 * bands.own_total * width * width,
        "own_projection",
        mib=16,
    )[0]

    def slab(part):
        return jnp.concatenate([west[part], tokens[part], east[part]], axis=1)

    north = shift(slab(slice(rows - RIM_LAT, rows)), "lat", 1, False)
    south = shift(slab(slice(0, RIM_LAT)), "lat", -1, False)
    inner = list(range(1, bands.count - 1))
    edges = [0, bands.count - 1]
    kinds, consts = bands.constants(inner, block)
    side, attended = vmem_call(
        functools.partial(middle_kernel, bands, inner, kinds),
        [(bands.side_total, 2 * width), (bands.own_at[-1] - bands.own_at[1], width)],
        [west, east, own, qkv_weight] + consts,
        [pltpu.VMEM((bands.side_total, width), BF16)] + attend_scratch(bands, inner, block),
        5 * 10**9,
        "middle_attention",
        exps=500000,
    )
    kinds, consts = bands.constants(edges, block)
    padded = up16(rows * columns // 4)
    return vmem_call(
        functools.partial(edge_kernel, bands, edges, kinds),
        [tokens.shape, (padded, 2 * width), (padded, 2 * width)],
        [tokens, north, south, key_bias(), own, side, attended, qkv_weight, out_weight, bands.patch_matrix()] + consts,
        [
            pltpu.VMEM((2 * bands.slab_padded, width), BF16),
            pltpu.VMEM((2 * bands.slab_padded, 2 * width), BF16),
            pltpu.VMEM((bands.own_total, width), BF16),
        ]
        + attend_scratch(bands, edges, block),
        6 * 10**9,
        "edge_attention",
        exps=300000,
    )


def shift(part, axis, step, wrap):
    size = lax.axis_size(axis)
    pairs = [(i, (i + step) % size) for i in range(size) if wrap or 0 <= i + step < size]
    return lax.ppermute(part, axis, pairs)


def key_bias():
    row = jnp.arange(8, dtype=jnp.int32)[:, None]
    key = jnp.arange(128, dtype=jnp.int32)[None, :] // WLON
    north = (row == 0) & (key < RIM_LAT) & (lax.axis_index("lat") == 0)
    south = (row == 1) & (key >= RIM_LAT) & (lax.axis_index("lat") == lax.axis_size("lat") - 1)
    return jnp.where(north | south, F32(-1e30), F32(0.0))


def place_index():
    me = lax.axis_index("lon")
    return jnp.stack([me // 2, me % 2]).astype(jnp.int32)


def merge_dots(place_ref, upper, lower, mine_ref, pair_ref, x_ref, x_pair_ref, y_ref, y_pair_ref, refs):
    half, block = x_ref.shape
    at = [pl.ds(pl.multiple_of((place_ref[1] + k) % 2 * block, block), block) for k in range(2)]
    own, x, y = refs
    for k, ref in enumerate((mine_ref, pair_ref)):
        own(at[k], dot(upper, ref[:half, :]), dot(lower, ref[half:, :]))
    for k, ref in enumerate((x_ref, x_pair_ref)):
        x(at[k], dot(upper, ref[...]))
    for k, ref in enumerate((y_ref, y_pair_ref)):
        y(at[k], dot(lower, ref[...]))


def merge_own_kernel(place_ref, upper_ref, lower_ref, *refs):
    weights, (own_ref, x_ref, y_ref) = refs[:6], refs[6:]

    def own(at, a, b):
        own_ref[:, at] = a + b

    def x(at, a):
        x_ref[:, at] = a

    def y(at, b):
        y_ref[:, at] = b

    merge_dots(place_ref, upper_ref[...], lower_ref[...], *weights, (own, x, y))


def merge_other_kernel(place_ref, upper_ref, lower_ref, *refs):
    weights, (to_y_ref, to_x_ref) = refs[:6], refs[6:]
    wide = to_x_ref.shape[1] // 2

    def own(at, a, b):
        to_y_ref[:, at] = a.astype(BF16)
        to_x_ref[:, at] = b.astype(BF16)

    def x(at, a):
        to_y_ref[:, pl.ds(pl.multiple_of(wide + at.start, at.size), at.size)] = a.astype(BF16)

    def y(at, b):
        to_x_ref[:, pl.ds(pl.multiple_of(wide + at.start, at.size), at.size)] = b.astype(BF16)

    merge_dots(place_ref, upper_ref[...], lower_ref[...], *weights, (own, x, y))


def combine_kernel(place_ref, own_ref, x_ref, y_ref, from_y_ref, from_x_ref, out_ref):
    wide = own_ref.shape[1]
    chip = place_ref[0]
    from_x, from_y = from_x_ref[...].astype(F32), from_y_ref[...].astype(F32)
    parts = [
        own_ref[...],
        x_ref[...] + from_x[:, :wide],
        y_ref[...] + from_y[:, :wide],
        from_x[:, wide:] + from_y[:, wide:],
    ]
    for m, part in enumerate(parts):
        out_ref[:, pl.ds(pl.multiple_of((chip ^ m) * wide, wide), wide)] = part.astype(BF16)


def local_call(kernel, out, place, args, flops, name, mib=16):
    vmem = pl.BlockSpec(memory_space=pltpu.VMEM)
    return pl.pallas_call(
        kernel,
        in_specs=[pl.BlockSpec(memory_space=pltpu.SMEM)] + [vmem] * len(args),
        out_specs=[vmem] * len(out),
        out_shape=out,
        compiler_params=params(mib),
        cost_estimate=pl.CostEstimate(flops=flops, bytes_accessed=2**20, transcendentals=0),
        name=name,
    )(place, *args)


def merge_by_squares(upper, lower, merge_weight):
    half = merge_weight.shape[0] // 2
    block = merge_weight.shape[1]
    count = upper.shape[0]
    x = chip_swap(merge_weight[:half], 1)
    y = chip_swap(merge_weight[half:], 2)
    x_pair, y_pair, _ = lax.optimization_barrier((x, y, upper))
    weights = [merge_weight, core_swap(merge_weight), x, core_swap(x_pair), y, core_swap(y_pair)]
    place = place_index()
    from_y = chip_swap(upper, 2)
    from_x = chip_swap(lower, 1)
    flops = 16 * count * half * block
    wide = jax.ShapeDtypeStruct((count, 2 * block), F32)
    own = local_call(merge_own_kernel, [wide] * 3, place, [upper, lower] + weights, flops, "merge_own")
    pair = jax.ShapeDtypeStruct((count, 4 * block), BF16)
    to_y, to_x = local_call(merge_other_kernel, [pair] * 2, place, [from_y, from_x] + weights, flops, "merge_other")
    back_y, back_x = chip_swap(to_y, 2), chip_swap(to_x, 1)
    out = jax.ShapeDtypeStruct((count, 8 * block), BF16)
    return local_call(combine_kernel, [out], place, [*own, back_y, back_x], 0, "combine")[0]


def ffn_kernel(mine_ref, theirs_ref, up_ref, down_ref, out_mine_ref, low_ref, high_ref, normed_ref, hidden_ref):
    count = mine_ref.shape[0]
    for k, ref in enumerate((mine_ref, theirs_ref)):
        normed_ref[k * count : (k + 1) * count, :] = normalize(ref[...].astype(F32)).astype(BF16)
    hidden = hidden_ref.shape[1]
    step = 256
    for at in range(0, hidden, step):
        raw = dot(normed_ref[...], up_ref[:, at : at + step])
        active = 0.5 * raw * (1.0 + lax.erf(raw * np.float32(np.sqrt(0.5))))
        hidden_ref[:, at : at + step] = active.astype(BF16)
    half = low_ref.shape[1]
    for at in range(0, 2 * half, step):
        out = dot(hidden_ref[...], down_ref[:, at : at + step]).astype(BF16)
        out_mine_ref[:, at : at + step] = out[:count]
        ref = low_ref if at < half else high_ref
        ref[:, at % half : at % half + step] = out[count:]


def feed_forward(mine, theirs, up, down):
    count = mine.shape[0]
    width, hidden = up.shape
    vmem = pl.BlockSpec(memory_space=pltpu.VMEM)
    return pl.pallas_call(
        ffn_kernel,
        in_specs=[vmem] * 4,
        out_specs=[vmem] * 3,
        out_shape=[jax.ShapeDtypeStruct((count, width // n), BF16) for n in (1, 2, 2)],
        scratch_shapes=[pltpu.VMEM((2 * count, width), BF16), pltpu.VMEM((2 * count, hidden), BF16)],
        compiler_params=params(20),
        cost_estimate=pl.CostEstimate(
            flops=8 * count * width * hidden, bytes_accessed=4 * width * hidden, transcendentals=2 * count * hidden
        ),
        name="feed_forward",
    )(mine, theirs, up, down)


def added(mine, low, high):
    return (mine.astype(F32) + jnp.concatenate([low, high], axis=1).astype(F32)).astype(BF16)


def summed(mine, low, high):
    return added(mine, core_swap(low), core_swap(high))


def core_swap(value):
    size = lax.axis_size("lon")
    return lax.ppermute(value, "lon", [(i, i ^ 1) for i in range(size)])


def chip_swap(value, offset):
    size = lax.axis_size("lon")
    return lax.ppermute(value, "lon", [(i, i ^ (2 * offset)) for i in range(size)])


def cross(value, first, second):
    size = lax.axis_size("lon")
    return lax.ppermute(value, "lon", [(i, i ^ (2 * (second if i % 2 else first))) for i in range(size)])


def coarse_by_squares(upper, lower, merge_weight, up, down):
    own = merge_by_squares(upper, lower, merge_weight)
    near = cross(own, 1, 2)
    next_near = cross(own, 2, 1)
    first = feed_forward(own, core_swap(own), up, down)
    near, next_near, *first = lax.optimization_barrier((near, next_near, *first))
    far = cross(near, 2, 1)
    sums = [summed(*first)]
    for chunk in (near, next_near):
        sums.append(summed(*feed_forward(chunk, core_swap(chunk), up, down)))
    pair, *sums = lax.optimization_barrier((core_swap(far), *sums))
    back = [cross(sums[1], 1, 2), cross(sums[2], 2, 1)]
    mine, low, high = feed_forward(far, pair, up, down)
    low, high, *back = lax.optimization_barrier((core_swap(low), core_swap(high), *back))
    back.append(chip_swap(added(mine, low, high), 3))
    return sum(part.astype(F32) for part in (own, sums[0], *back))


def coarse_by_chips(upper, lower, merge_weight, up, down):
    weight = lax.all_gather(merge_weight, "lon", axis=1, tiled=True)
    patches = jnp.concatenate([upper, lower], axis=1)
    coarse = jnp.dot(patches, weight, preferred_element_type=F32).astype(BF16)
    chips = lax.axis_size("lon") // 2
    arrived = [coarse] + [chip_swap(coarse, m) for m in range(1, chips)]
    total = coarse.astype(F32)
    for m in range(chips):
        part = summed(*feed_forward(arrived[m], core_swap(arrived[m]), up, down))
        total = total + (chip_swap(part, m) if m else part).astype(F32)
    return total


def per_device(tokens, qkv_weight, out_weight, merge_weight, up_weight, down_weight):
    rows, columns, width = tokens.shape
    bands = Bands(rows, columns)
    cells = rows * columns // 4
    middle_out, upper, lower = attention(bands, tokens, qkv_weight, out_weight)
    coarse = coarse_by_squares if lax.axis_size("lon") == 8 else coarse_by_chips
    total = coarse(upper, lower, merge_weight, up_weight, down_weight)
    coarse_out = total[:cells].astype(jnp.bfloat16)
    return (middle_out, coarse_out.reshape(rows // 2, columns // 2, -1))


def solution(mesh):
    return jax.shard_map(
        per_device,
        mesh=mesh,
        in_specs=(P("lat", "lon", None), P(), P(), P(None, "lon"), P(None, "lon"), P("lon", None)),
        out_specs=(P("lat", "lon", None), P("lat", "lon", None)),
        check_vma=False,
    )
```

```python
import functools

import jax
import jax.numpy as jnp
import numpy as np
from jax import lax
from jax.experimental import pallas as pl
from jax.experimental.pallas import tpu as pltpu
from jax.sharding import PartitionSpec as P

HEADS = 16
WLAT = 6
WLON = 12
RIM_LAT = WLAT // 2
RIM_LON = WLON // 2
SIDE = 8
GROUP = 4
F32 = jnp.float32
BF16 = jnp.bfloat16


def up16(n):
    return -(-n // 16) * 16


def params(mib=48, **kw):
    return pltpu.CompilerParams(vmem_limit_bytes=mib * 2**20, **kw)


class Bands:
    def __init__(self, rows, columns):
        assert (rows - WLAT) % WLAT == 0 and (columns - WLON) % WLON == 0
        self.rows, self.columns = rows, columns
        inner = (rows - WLAT) // WLAT
        self.height = [RIM_LAT] + [WLAT] * inner + [RIM_LAT]
        self.count = len(self.height)
        self.first = [sum(self.height[:b]) for b in range(self.count)]
        self.widths = [RIM_LON] + [WLON] * ((columns - WLON) // WLON) + [RIM_LON]
        self.own = [h * columns for h in self.height]
        self.own_padded = [up16(n) for n in self.own]
        self.own_at = [sum(self.own_padded[:b]) for b in range(self.count)]
        self.own_total = sum(self.own_padded)
        self.side = [2 * h * SIDE for h in self.height]
        assert all(n % 16 == 0 for n in self.side)
        self.side_at = [sum(self.side[:b]) for b in range(self.count)]
        self.side_total = sum(self.side)
        self.slab = columns + 2 * SIDE
        self.slab_padded = up16(RIM_LAT * self.slab)
        self.window = up16(WLAT * WLON)
        self.counts = [[GROUP * h * w for w in self.widths] for h in self.height]
        self.counts_padded = [[up16(n) for n in row] for row in self.counts]

    def edge(self, b):
        return b in (0, self.count - 1)

    def sources(self, b):
        return self.own_padded[b] + self.side[b] + (self.slab_padded if self.edge(b) else 0)

    def source(self, b, i, j):
        columns, h, first = self.columns, self.height[b], self.first[b]
        at = self.own_padded[b]
        if not 0 <= i < self.rows:
            i = i + RIM_LAT if i < 0 else i - self.rows
            return at + self.side[b] + i * self.slab + j + SIDE
        if 0 <= j < columns:
            return (i - first) * columns + j
        at += (i - first) * SIDE
        return at + (j + SIDE if j < 0 else h * SIDE + j - columns)

    def key_matrix(self, b):
        g = np.zeros((len(self.widths) * self.window, self.sources(b)), np.float32)
        top = self.first[b] - (RIM_LAT if b == 0 else 0)
        for c in range(len(self.widths)):
            for i in range(WLAT):
                for j in range(WLON):
                    at = c * self.window + i * WLON + j
                    g[at, self.source(b, top + i, c * WLON - RIM_LON + j)] = 1
        return g.astype(BF16)

    def query_matrix(self, b):
        total = sum(self.counts_padded[b])
        g = np.zeros((total, self.own_padded[b]), np.float32)
        head = np.zeros((total,), np.int32)
        start = left = 0
        for width, padded in zip(self.widths, self.counts_padded[b]):
            at = start
            for k in range(GROUP):
                for i in range(self.height[b]):
                    for j in range(width):
                        g[at, i * self.columns + left + j] = 1
                        head[at] = k
                        at += 1
            left += width
            start += padded
        return g.astype(BF16), head

    def patch_matrix(self):
        cells = self.rows * self.columns // 4
        padded = up16(cells)
        g = np.zeros((4 * padded, self.rows * self.columns), np.float32)
        for r in range(self.rows // 2):
            for c in range(self.columns // 2):
                for k in range(4):
                    to = k * padded + r * (self.columns // 2) + c
                    g[to, (2 * r + k // 2) * self.columns + 2 * c + k % 2] = 1
        return g.astype(BF16)

    def constants(self, some, block):
        distinct, kinds, consts = [], [], []
        for b in some:
            kind = (self.height[b], b == 0, b == self.count - 1)
            if kind not in distinct:
                distinct.append(kind)
                query, head = self.query_matrix(b)
                mask = head[:, None] == (np.arange(block) // (block // GROUP))[None, :]
                scale = np.float32((block // GROUP) ** -0.5)
                scaled = (query.astype(np.float32) * scale).astype(BF16)
                consts += [self.key_matrix(b), scaled, mask.astype(BF16), np.ascontiguousarray(query.T)]
            kinds.append(4 * distinct.index(kind))
        return kinds, consts


def normalize(values):
    center = values - jnp.mean(values, axis=-1, keepdims=True)
    spread = jnp.mean(center * center, axis=-1, keepdims=True)
    return center * lax.rsqrt(spread + 1e-05)


def dot(a, b, dims=((1,), (0,))):
    return lax.dot_general(a, b, (dims, ((), ())), preferred_element_type=F32)


def flat_normed(ref):
    values = ref[...].astype(F32)
    return normalize(values.reshape(-1, values.shape[-1]))


def project(normed_ref, weight_ref, out_ref):
    step = 256
    for at in range(0, out_ref.shape[1], step):
        out_ref[:, at : at + step] = dot(normed_ref[...], weight_ref[:, at : at + step]).astype(BF16)


def padded_rows(values, total):
    if values.shape[0] == total:
        return values
    return jnp.concatenate([values, jnp.zeros((total - values.shape[0], values.shape[1]), values.dtype)], axis=0)


def prepare_kernel(tokens_ref, weight_ref, east_ref, west_ref, upper_ref, lower_ref, sems):
    half = upper_ref.shape[0]
    copies = [
        pltpu.make_async_copy(weight_ref.at[k * half : (k + 1) * half], ref, sems.at[k])
        for k, ref in enumerate((upper_ref, lower_ref))
    ]
    for copy in copies:
        copy.start()
    columns = tokens_ref.shape[1]
    east_ref[...] = tokens_ref[:, columns - SIDE :]
    west_ref[...] = tokens_ref[:, :SIDE]
    for copy in copies:
        copy.wait()


def prepare(tokens, merge_weight):
    rows, _, width = tokens.shape
    depth, block = merge_weight.shape
    vmem, anywhere = pl.BlockSpec(memory_space=pltpu.VMEM), pl.BlockSpec(memory_space=pl.ANY)
    return pl.pallas_call(
        prepare_kernel,
        in_specs=[vmem, anywhere],
        out_specs=[vmem] * 4,
        out_shape=[jax.ShapeDtypeStruct((rows, SIDE, width), BF16)] * 2
        + [jax.ShapeDtypeStruct((depth // 2, block), BF16)] * 2,
        scratch_shapes=[pltpu.SemaphoreType.DMA((2,))],
        compiler_params=params(52),
        name="prepare",
    )(tokens, merge_weight)


def own_kernel(bands, tokens_ref, weight_ref, out_ref, kv_ref, normed_ref, q_ref, sems):
    width = q_ref.shape[1]
    chunk = weight_ref.shape[1] // sems.shape[0]
    places = []
    for n in range(sems.shape[0]):
        at = n * chunk
        places.append((q_ref, at) if at < width else (kv_ref, at - width))
    copies = [
        pltpu.make_async_copy(weight_ref.at[:, pl.ds(n * chunk, chunk)], ref.at[:, pl.ds(at, chunk)], sems.at[n])
        for n, (ref, at) in enumerate(places)
    ]
    for copy in copies:
        copy.start()
    normed = flat_normed(tokens_ref)
    for b in range(bands.count):
        at = bands.first[b] * bands.columns
        part = padded_rows(normed[at : at + bands.own[b]], bands.own_padded[b])
        normed_ref[bands.own_at[b] : bands.own_at[b] + bands.own_padded[b], :] = part.astype(BF16)
    step = 256
    for n, (ref, first) in enumerate(places):
        copies[n].wait()
        for at in range(0, chunk, step):
            part = ref[:, first + at : first + at + step]
            out_ref[:, n * chunk + at : n * chunk + at + step] = dot(normed_ref[...], part).astype(BF16)


def own_projection(bands, tokens, weight):
    width, out = weight.shape
    vmem = pl.BlockSpec(memory_space=pltpu.VMEM)
    return pl.pallas_call(
        functools.partial(own_kernel, bands),
        in_specs=[vmem, pl.BlockSpec(memory_space=pl.ANY)],
        out_specs=[vmem, vmem],
        out_shape=[
            jax.ShapeDtypeStruct((bands.own_total, out), BF16),
            jax.ShapeDtypeStruct((width, out - width), BF16),
        ],
        scratch_shapes=[
            pltpu.VMEM((bands.own_total, width), BF16),
            pltpu.VMEM((width, width), BF16),
            pltpu.SemaphoreType.DMA((6,)),
        ],
        compiler_params=params(42),
        cost_estimate=pl.CostEstimate(
            flops=2 * bands.own_total * width * out, bytes_accessed=2 * width * out, transcendentals=0
        ),
        name="own_projection",
    )(tokens, weight)


def attend(bands, some, kinds, consts, own_ref, outer, bias_ref, put, scratch):
    k_ref, v_ref, q_ref, p_ref, r_ref = scratch
    width = own_ref.shape[1] // 3
    block = width * GROUP // HEADS
    window = WLAT * WLON
    units = [(n, b, g) for n, b in enumerate(some) for g in range(HEADS // GROUP)]
    for u, (n, b, g) in enumerate(units):
        keys, query, mask, _ = consts[kinds[n] : kinds[n] + 4]
        own = slice(bands.own_at[b], bands.own_at[b] + bands.own_padded[b])
        for ref, skip in ((k_ref, 0), (v_ref, width)):
            parts = [own_ref[own, width + skip + g * block : width + skip + (g + 1) * block]]
            for out_ref, at, size in outer(b):
                parts.append(out_ref[at : at + size, skip + g * block : skip + (g + 1) * block])
            ref[u] = dot(keys[...], jnp.concatenate(parts, axis=0)).astype(BF16)
        total = query.shape[0]
        q_ref[u, :total] = dot(query[...], own_ref[own, g * block : (g + 1) * block]).astype(BF16) * mask[...]
    for u, (n, b, g) in enumerate(units):
        at = 0
        for c, count in enumerate(bands.counts_padded[b]):
            scores = dot(
                q_ref[u, at : at + count], k_ref[u, c * bands.window : c * bands.window + window], ((1,), (1,))
            )
            if b == 0:
                scores = scores + bias_ref[0:1, :window]
            if b == bands.count - 1:
                scores = scores + bias_ref[1:2, :window]
            raised = jnp.exp(scores - jnp.max(scores, axis=-1, keepdims=True))
            weights = raised * (1.0 / jnp.sum(raised, axis=-1, keepdims=True))
            p_ref[u, at : at + count, :window] = weights.astype(BF16)
            at += count
    for u, (n, b, g) in enumerate(units):
        mask = consts[kinds[n] + 2]
        at = 0
        for c, count in enumerate(bands.counts_padded[b]):
            mixed = dot(
                p_ref[u, at : at + count, :window], v_ref[u, c * bands.window : c * bands.window + window]
            )
            r_ref[u, at : at + count] = mixed.astype(BF16) * mask[at : at + count]
            at += count
    for u, (n, b, g) in enumerate(units):
        back = consts[kinds[n] + 3]
        put(b, g, dot(back[...], r_ref[u, : back.shape[1]]).astype(BF16))


def attend_scratch(bands, some, block):
    units = len(some) * HEADS // GROUP
    keys = len(bands.widths) * bands.window
    rows = max(sum(bands.counts_padded[b]) for b in some)
    return [
        pltpu.VMEM((units, keys, block), BF16),
        pltpu.VMEM((units, keys, block), BF16),
        pltpu.VMEM((units, rows, block), BF16),
        pltpu.VMEM((units, rows, 128), BF16),
        pltpu.VMEM((units, rows, block), BF16),
    ]


def middle_kernel(bands, some, kinds, west_ref, east_ref, own_ref, weight_ref, *rest):
    consts, (side_ref, out_ref, normed_ref, *scratch) = rest[:-8], rest[-8:]
    west, east = flat_normed(west_ref), flat_normed(east_ref)
    for b in range(bands.count):
        at, size = bands.first[b] * SIDE, bands.height[b] * SIDE
        part = jnp.concatenate([west[at : at + size], east[at : at + size]], axis=0)
        normed_ref[bands.side_at[b] : bands.side_at[b] + bands.side[b], :] = part.astype(BF16)
    project(normed_ref, weight_ref, side_ref)

    def outer(b):
        return [(side_ref, bands.side_at[b], bands.side[b])]

    def put(b, g, value):
        at = bands.own_at[b] - bands.own_at[1]
        block = value.shape[1]
        out_ref[at : at + bands.own_padded[b], g * block : (g + 1) * block] = value

    attend(bands, some, kinds, consts, own_ref, outer, None, put, scratch)


def edge_kernel(bands, some, kinds, tokens_ref, north_ref, south_ref, bias_ref, own_ref, side_ref, inner_ref, weight_ref, out_w_ref, patch_ref, *rest):
    consts, rest = rest[:-11], rest[-11:]
    middle_ref, upper_ref, lower_ref, normed_ref, slab_ref, attended_ref, *scratch = rest
    rows, columns, width = tokens_ref.shape
    slab = bands.slab_padded
    for k, ref in enumerate((north_ref, south_ref)):
        normed_ref[k * slab : (k + 1) * slab, :] = padded_rows(flat_normed(ref), slab).astype(BF16)
    project(normed_ref, weight_ref, slab_ref)

    def outer(b):
        return [
            (side_ref, bands.side_at[b], bands.side[b]),
            (slab_ref, 0 if b == 0 else slab, slab),
        ]

    def put(b, g, value):
        block = value.shape[1]
        attended_ref[bands.own_at[b] : bands.own_at[b] + bands.own_padded[b], g * block : (g + 1) * block] = value

    attended_ref[bands.own_at[1] : bands.own_at[-1], :] = inner_ref[...]
    attend(bands, some, kinds, consts, own_ref, outer, bias_ref, put, scratch)
    mixed = dot(attended_ref[...], out_w_ref[...])
    mixed = jnp.concatenate([mixed[at : at + n] for at, n in zip(bands.own_at, bands.own)], axis=0)
    middle = tokens_ref[...].astype(F32) + mixed.reshape(rows, columns, width)
    middle_ref[...] = middle.astype(BF16)
    middle = middle.reshape(rows * columns, width).astype(BF16)
    padded = patch_ref.shape[0] // 4
    parts = [dot(patch_ref[k * padded : (k + 1) * padded, :], middle) for k in range(4)]
    total = sum(jnp.sum(p, axis=-1, keepdims=True) for p in parts)
    mean = total * (1.0 / (4 * width))
    parts = [p - mean for p in parts]
    spread = sum(jnp.sum(p * p, axis=-1, keepdims=True) for p in parts)
    factor = lax.rsqrt(spread * (1.0 / (4 * width)) + 1e-05)
    for k in range(4):
        ref = (upper_ref, lower_ref)[k // 2]
        ref[:, k % 2 * width : (k % 2 + 1) * width] = (parts[k] * factor).astype(BF16)


def vmem_call(kernel, out, args, scratch, flops, name, mib=24, exps=0):
    vmem = pl.BlockSpec(memory_space=pltpu.VMEM)
    return pl.pallas_call(
        kernel,
        in_specs=[vmem] * len(args),
        out_specs=[vmem] * len(out),
        out_shape=[jax.ShapeDtypeStruct(shape, BF16) for shape in out],
        scratch_shapes=scratch,
        compiler_params=params(mib),
        cost_estimate=pl.CostEstimate(flops=flops, bytes_accessed=2**20, transcendentals=exps),
        name=name,
    )(*args)


def attention(bands, tokens, rims, qkv_weight, out_weight):
    rows, columns, width = tokens.shape
    block = width * GROUP // HEADS
    west = shift(rims[0], "lon", 1, True)
    east = shift(rims[1], "lon", -1, True)
    own, kv_weight = own_projection(bands, tokens, qkv_weight)

    def slab(part):
        return jnp.concatenate([west[part], tokens[part], east[part]], axis=1)

    north = shift(slab(slice(rows - RIM_LAT, rows)), "lat", 1, False)
    south = shift(slab(slice(0, RIM_LAT)), "lat", -1, False)
    inner = list(range(1, bands.count - 1))
    edges = [0, bands.count - 1]
    kinds, consts = bands.constants(inner, block)
    side, attended = vmem_call(
        functools.partial(middle_kernel, bands, inner, kinds),
        [(bands.side_total, 2 * width), (bands.own_at[-1] - bands.own_at[1], width)],
        [west, east, own, kv_weight] + consts,
        [pltpu.VMEM((bands.side_total, width), BF16)] + attend_scratch(bands, inner, block),
        5 * 10**9,
        "middle_attention",
        exps=500000,
    )
    kinds, consts = bands.constants(edges, block)
    padded = up16(rows * columns // 4)
    return vmem_call(
        functools.partial(edge_kernel, bands, edges, kinds),
        [tokens.shape, (padded, 2 * width), (padded, 2 * width)],
        [tokens, north, south, key_bias(), own, side, attended, kv_weight, out_weight, bands.patch_matrix()] + consts,
        [
            pltpu.VMEM((2 * bands.slab_padded, width), BF16),
            pltpu.VMEM((2 * bands.slab_padded, 2 * width), BF16),
            pltpu.VMEM((bands.own_total, width), BF16),
        ]
        + attend_scratch(bands, edges, block),
        6 * 10**9,
        "edge_attention",
        exps=300000,
    )


def shift(part, axis, step, wrap):
    size = lax.axis_size(axis)
    pairs = [(i, (i + step) % size) for i in range(size) if wrap or 0 <= i + step < size]
    return lax.ppermute(part, axis, pairs)


def key_bias():
    row = jnp.arange(8, dtype=jnp.int32)[:, None]
    key = jnp.arange(128, dtype=jnp.int32)[None, :] // WLON
    north = (row == 0) & (key < RIM_LAT) & (lax.axis_index("lat") == 0)
    south = (row == 1) & (key >= RIM_LAT) & (lax.axis_index("lat") == lax.axis_size("lat") - 1)
    return jnp.where(north | south, F32(-1e30), F32(0.0))


def place_index():
    me = lax.axis_index("lon")
    return jnp.stack([me // 2, me % 2]).astype(jnp.int32)


def merge_dots(place_ref, upper, lower, mine_ref, pair_ref, x_ref, x_pair_ref, y_ref, y_pair_ref, refs):
    half, block = x_ref.shape
    at = [pl.ds(pl.multiple_of((place_ref[1] + k) % 2 * block, block), block) for k in range(2)]
    own, x, y = refs
    for k, ref in enumerate((mine_ref, pair_ref)):
        own(at[k], dot(upper, ref[:half, :]), dot(lower, ref[half:, :]))
    for k, ref in enumerate((x_ref, x_pair_ref)):
        x(at[k], dot(upper, ref[...]))
    for k, ref in enumerate((y_ref, y_pair_ref)):
        y(at[k], dot(lower, ref[...]))


def merge_own_kernel(place_ref, upper_ref, lower_ref, *refs):
    weights, (own_ref, x_ref, y_ref), kept = refs[:6], refs[6:9], refs[9:]
    for ref, to in zip(weights, kept):
        to[...] = ref[...]

    def own(at, a, b):
        own_ref[:, at] = a + b

    def x(at, a):
        x_ref[:, at] = a

    def y(at, b):
        y_ref[:, at] = b

    merge_dots(place_ref, upper_ref[...], lower_ref[...], *weights, (own, x, y))


def merge_other_kernel(place_ref, upper_ref, lower_ref, *refs):
    weights, (to_y_ref, to_x_ref) = refs[:6], refs[6:]
    wide = to_x_ref.shape[1] // 2

    def own(at, a, b):
        to_y_ref[:, at] = a.astype(BF16)
        to_x_ref[:, at] = b.astype(BF16)

    def x(at, a):
        to_y_ref[:, pl.ds(pl.multiple_of(wide + at.start, at.size), at.size)] = a.astype(BF16)

    def y(at, b):
        to_x_ref[:, pl.ds(pl.multiple_of(wide + at.start, at.size), at.size)] = b.astype(BF16)

    merge_dots(place_ref, upper_ref[...], lower_ref[...], *weights, (own, x, y))


def combine_kernel(place_ref, own_ref, x_ref, y_ref, from_y_ref, from_x_ref, out_ref):
    wide = own_ref.shape[1]
    chip = place_ref[0]
    from_x, from_y = from_x_ref[...].astype(F32), from_y_ref[...].astype(F32)
    parts = [
        own_ref[...],
        x_ref[...] + from_x[:, :wide],
        y_ref[...] + from_y[:, :wide],
        from_x[:, wide:] + from_y[:, wide:],
    ]
    for m, part in enumerate(parts):
        out_ref[:, pl.ds(pl.multiple_of((chip ^ m) * wide, wide), wide)] = part.astype(BF16)


def local_call(kernel, out, place, args, flops, name, mib=16):
    vmem = pl.BlockSpec(memory_space=pltpu.VMEM)
    return pl.pallas_call(
        kernel,
        in_specs=[pl.BlockSpec(memory_space=pltpu.SMEM)] + [vmem] * len(args),
        out_specs=[vmem] * len(out),
        out_shape=out,
        compiler_params=params(mib),
        cost_estimate=pl.CostEstimate(flops=flops, bytes_accessed=2**20, transcendentals=0),
        name=name,
    )(place, *args)


def merge_by_squares(upper, lower, merge_weight, halves):
    half = merge_weight.shape[0] // 2
    block = merge_weight.shape[1]
    count = upper.shape[0]
    x = chip_swap(halves[0], 1)
    y = chip_swap(halves[1], 2)
    x_pair, y_pair, _ = lax.optimization_barrier((x, y, upper))
    weights = [merge_weight, core_swap(merge_weight), x, core_swap(x_pair), y, core_swap(y_pair)]
    place = place_index()
    from_y = chip_swap(upper, 2)
    from_x = chip_swap(lower, 1)
    flops = 16 * count * half * block
    wide = jax.ShapeDtypeStruct((count, 2 * block), F32)
    kept = [jax.ShapeDtypeStruct(w.shape, BF16) for w in weights]
    *own, a, b, c, d, e, f = local_call(
        merge_own_kernel, [wide] * 3 + kept, place, [upper, lower] + weights, flops, "merge_own", 28
    )
    weights = [a, b, c, d, e, f]
    pair = jax.ShapeDtypeStruct((count, 4 * block), BF16)
    to_y, to_x = local_call(merge_other_kernel, [pair] * 2, place, [from_y, from_x] + weights, flops, "merge_other")
    back_y, back_x = chip_swap(to_y, 2), chip_swap(to_x, 1)
    out = jax.ShapeDtypeStruct((count, 8 * block), BF16)
    return local_call(combine_kernel, [out], place, [*own, back_y, back_x], 0, "combine")[0]


def ffn_kernel(mine_ref, theirs_ref, up_ref, down_ref, out_mine_ref, low_ref, high_ref, normed_ref, hidden_ref):
    count = mine_ref.shape[0]
    for k, ref in enumerate((mine_ref, theirs_ref)):
        normed_ref[k * count : (k + 1) * count, :] = normalize(ref[...].astype(F32)).astype(BF16)
    hidden = hidden_ref.shape[1]
    step = 256
    for at in range(0, hidden, step):
        raw = dot(normed_ref[...], up_ref[:, at : at + step])
        active = 0.5 * raw * (1.0 + lax.erf(raw * np.float32(np.sqrt(0.5))))
        hidden_ref[:, at : at + step] = active.astype(BF16)
    half = low_ref.shape[1]
    for at in range(0, 2 * half, step):
        out = dot(hidden_ref[...], down_ref[:, at : at + step]).astype(BF16)
        out_mine_ref[:, at : at + step] = out[:count]
        ref = low_ref if at < half else high_ref
        ref[:, at % half : at % half + step] = out[count:]


def feed_forward(mine, theirs, up, down):
    count = mine.shape[0]
    width, hidden = up.shape
    vmem = pl.BlockSpec(memory_space=pltpu.VMEM)
    return pl.pallas_call(
        ffn_kernel,
        in_specs=[vmem] * 4,
        out_specs=[vmem] * 3,
        out_shape=[jax.ShapeDtypeStruct((count, width // n), BF16) for n in (1, 2, 2)],
        scratch_shapes=[pltpu.VMEM((2 * count, width), BF16), pltpu.VMEM((2 * count, hidden), BF16)],
        compiler_params=params(20),
        cost_estimate=pl.CostEstimate(
            flops=8 * count * width * hidden, bytes_accessed=4 * width * hidden, transcendentals=2 * count * hidden
        ),
        name="feed_forward",
    )(mine, theirs, up, down)


def added(mine, low, high):
    return (mine.astype(F32) + jnp.concatenate([low, high], axis=1).astype(F32)).astype(BF16)


def summed(mine, low, high):
    return added(mine, core_swap(low), core_swap(high))


def core_swap(value):
    size = lax.axis_size("lon")
    return lax.ppermute(value, "lon", [(i, i ^ 1) for i in range(size)])


def chip_swap(value, offset):
    size = lax.axis_size("lon")
    return lax.ppermute(value, "lon", [(i, i ^ (2 * offset)) for i in range(size)])


def cross(value, first, second):
    size = lax.axis_size("lon")
    return lax.ppermute(value, "lon", [(i, i ^ (2 * (second if i % 2 else first))) for i in range(size)])


def coarse_by_squares(upper, lower, merge_weight, halves, up, down):
    own = merge_by_squares(upper, lower, merge_weight, halves)
    near = cross(own, 1, 2)
    next_near = cross(own, 2, 1)
    first = feed_forward(own, core_swap(own), up, down)
    near, next_near, *first = lax.optimization_barrier((near, next_near, *first))
    far = cross(near, 2, 1)
    sums = [summed(*first)]
    for chunk in (near, next_near):
        sums.append(summed(*feed_forward(chunk, core_swap(chunk), up, down)))
    pair, *sums = lax.optimization_barrier((core_swap(far), *sums))
    back = [cross(sums[1], 1, 2), cross(sums[2], 2, 1)]
    mine, low, high = feed_forward(far, pair, up, down)
    low, high, *back = lax.optimization_barrier((core_swap(low), core_swap(high), *back))
    back.append(chip_swap(added(mine, low, high), 3))
    return sum(part.astype(F32) for part in (own, sums[0], *back))


def coarse_by_chips(upper, lower, merge_weight, halves, up, down):
    weight = lax.all_gather(merge_weight, "lon", axis=1, tiled=True)
    patches = jnp.concatenate([upper, lower], axis=1)
    coarse = jnp.dot(patches, weight, preferred_element_type=F32).astype(BF16)
    chips = lax.axis_size("lon") // 2
    arrived = [coarse] + [chip_swap(coarse, m) for m in range(1, chips)]
    total = coarse.astype(F32)
    for m in range(chips):
        part = summed(*feed_forward(arrived[m], core_swap(arrived[m]), up, down))
        total = total + (chip_swap(part, m) if m else part).astype(F32)
    return total


def per_device(tokens, qkv_weight, out_weight, merge_weight, up_weight, down_weight):
    rows, columns, width = tokens.shape
    bands = Bands(rows, columns)
    cells = rows * columns // 4
    *rims, upper_weight, lower_weight = prepare(tokens, merge_weight)
    middle_out, upper, lower = attention(bands, tokens, rims, qkv_weight, out_weight)
    coarse = coarse_by_squares if lax.axis_size("lon") == 8 else coarse_by_chips
    halves = [upper_weight, lower_weight]
    total = coarse(upper, lower, merge_weight, halves, up_weight, down_weight)
    coarse_out = total[:cells].astype(jnp.bfloat16)
    return (middle_out, coarse_out.reshape(rows // 2, columns // 2, -1))


def solution(mesh):
    return jax.shard_map(
        per_device,
        mesh=mesh,
        in_specs=(P("lat", "lon", None), P(), P(), P(None, "lon"), P(None, "lon"), P("lon", None)),
        out_specs=(P("lat", "lon", None), P("lat", "lon", None)),
        check_vma=False,
    )
```

```python
import functools

import jax
import jax.numpy as jnp
import numpy as np
from jax import lax
from jax.experimental import pallas as pl
from jax.experimental.pallas import tpu as pltpu
from jax.sharding import PartitionSpec as P

HEADS = 16
WLAT = 6
WLON = 12
RIM_LAT = WLAT // 2
RIM_LON = WLON // 2
SIDE = 8
GROUP = 4
F32 = jnp.float32
BF16 = jnp.bfloat16


def up16(n):
    return -(-n // 16) * 16


def params(mib=48, **kw):
    return pltpu.CompilerParams(vmem_limit_bytes=mib * 2**20, **kw)


class Bands:
    def __init__(self, rows, columns):
        assert (rows - WLAT) % WLAT == 0 and (columns - WLON) % WLON == 0
        self.rows, self.columns = rows, columns
        inner = (rows - WLAT) // WLAT
        self.height = [RIM_LAT] + [WLAT] * inner + [RIM_LAT]
        self.count = len(self.height)
        self.first = [sum(self.height[:b]) for b in range(self.count)]
        self.widths = [RIM_LON] + [WLON] * ((columns - WLON) // WLON) + [RIM_LON]
        self.own = [h * columns for h in self.height]
        self.own_padded = [up16(n) for n in self.own]
        self.own_at = [sum(self.own_padded[:b]) for b in range(self.count)]
        self.own_total = sum(self.own_padded)
        self.side = [2 * h * SIDE for h in self.height]
        assert all(n % 16 == 0 for n in self.side)
        self.side_at = [sum(self.side[:b]) for b in range(self.count)]
        self.side_total = sum(self.side)
        self.slab = columns + 2 * SIDE
        self.slab_padded = up16(RIM_LAT * self.slab)
        self.window = up16(WLAT * WLON)
        self.counts = [[GROUP * h * w for w in self.widths] for h in self.height]
        self.counts_padded = [[up16(n) for n in row] for row in self.counts]

    def edge(self, b):
        return b in (0, self.count - 1)

    def sources(self, b):
        return self.own_padded[b] + self.side[b] + (self.slab_padded if self.edge(b) else 0)

    def source(self, b, i, j):
        columns, h, first = self.columns, self.height[b], self.first[b]
        at = self.own_padded[b]
        if not 0 <= i < self.rows:
            i = i + RIM_LAT if i < 0 else i - self.rows
            return at + self.side[b] + i * self.slab + j + SIDE
        if 0 <= j < columns:
            return (i - first) * columns + j
        at += (i - first) * SIDE
        return at + (j + SIDE if j < 0 else h * SIDE + j - columns)

    def key_matrix(self, b):
        g = np.zeros((len(self.widths) * self.window, self.sources(b)), np.float32)
        top = self.first[b] - (RIM_LAT if b == 0 else 0)
        for c in range(len(self.widths)):
            for i in range(WLAT):
                for j in range(WLON):
                    at = c * self.window + i * WLON + j
                    g[at, self.source(b, top + i, c * WLON - RIM_LON + j)] = 1
        return g.astype(BF16)

    def query_matrix(self, b):
        total = sum(self.counts_padded[b])
        g = np.zeros((total, self.own_padded[b]), np.float32)
        head = np.zeros((total,), np.int32)
        start = left = 0
        for width, padded in zip(self.widths, self.counts_padded[b]):
            at = start
            for k in range(GROUP):
                for i in range(self.height[b]):
                    for j in range(width):
                        g[at, i * self.columns + left + j] = 1
                        head[at] = k
                        at += 1
            left += width
            start += padded
        return g.astype(BF16), head

    def patch_matrix(self):
        cells = self.rows * self.columns // 4
        padded = up16(cells)
        g = np.zeros((4 * padded, self.rows * self.columns), np.float32)
        for r in range(self.rows // 2):
            for c in range(self.columns // 2):
                for k in range(4):
                    to = k * padded + r * (self.columns // 2) + c
                    g[to, (2 * r + k // 2) * self.columns + 2 * c + k % 2] = 1
        return g.astype(BF16)

    def constants(self, some, block):
        distinct, kinds, consts = [], [], []
        for b in some:
            kind = (self.height[b], b == 0, b == self.count - 1)
            if kind not in distinct:
                distinct.append(kind)
                query, head = self.query_matrix(b)
                mask = head[:, None] == (np.arange(block) // (block // GROUP))[None, :]
                scale = np.float32((block // GROUP) ** -0.5)
                scaled = (query.astype(np.float32) * scale).astype(BF16)
                consts += [self.key_matrix(b), scaled, mask.astype(BF16), np.ascontiguousarray(query.T)]
            kinds.append(4 * distinct.index(kind))
        return kinds, consts


def normalize(values):
    center = values - jnp.mean(values, axis=-1, keepdims=True)
    spread = jnp.mean(center * center, axis=-1, keepdims=True)
    return center * lax.rsqrt(spread + 1e-05)


def dot(a, b, dims=((1,), (0,))):
    return lax.dot_general(a, b, (dims, ((), ())), preferred_element_type=F32)


def flat_normed(ref):
    values = ref[...].astype(F32)
    return normalize(values.reshape(-1, values.shape[-1]))


def project(normed_ref, weight_ref, out_ref):
    step = 256
    for at in range(0, out_ref.shape[1], step):
        out_ref[:, at : at + step] = dot(normed_ref[...], weight_ref[:, at : at + step]).astype(BF16)


def padded_rows(values, total):
    if values.shape[0] == total:
        return values
    return jnp.concatenate([values, jnp.zeros((total - values.shape[0], values.shape[1]), values.dtype)], axis=0)


def prepare_kernel(tokens_ref, weight_ref, east_ref, west_ref, upper_ref, lower_ref, sems):
    half = upper_ref.shape[0]
    copies = [
        pltpu.make_async_copy(weight_ref.at[k * half : (k + 1) * half], ref, sems.at[k])
        for k, ref in enumerate((upper_ref, lower_ref))
    ]
    for copy in copies:
        copy.start()
    columns = tokens_ref.shape[1]
    east_ref[...] = tokens_ref[:, columns - SIDE :]
    west_ref[...] = tokens_ref[:, :SIDE]
    for copy in copies:
        copy.wait()


def prepare(tokens, merge_weight):
    rows, _, width = tokens.shape
    depth, block = merge_weight.shape
    vmem, anywhere = pl.BlockSpec(memory_space=pltpu.VMEM), pl.BlockSpec(memory_space=pl.ANY)
    return pl.pallas_call(
        prepare_kernel,
        in_specs=[vmem, anywhere],
        out_specs=[vmem] * 4,
        out_shape=[jax.ShapeDtypeStruct((rows, SIDE, width), BF16)] * 2
        + [jax.ShapeDtypeStruct((depth // 2, block), BF16)] * 2,
        scratch_shapes=[pltpu.SemaphoreType.DMA((2,))],
        compiler_params=params(52),
        name="prepare",
    )(tokens, merge_weight)


def own_kernel(bands, tokens_ref, weight_ref, out_ref, kv_ref, normed_ref, q_ref, sems):
    width = q_ref.shape[1]
    chunk = weight_ref.shape[1] // sems.shape[0]
    places = []
    for n in range(sems.shape[0]):
        at = n * chunk
        places.append((q_ref, at) if at < width else (kv_ref, at - width))
    copies = [
        pltpu.make_async_copy(weight_ref.at[:, pl.ds(n * chunk, chunk)], ref.at[:, pl.ds(at, chunk)], sems.at[n])
        for n, (ref, at) in enumerate(places)
    ]
    for copy in copies:
        copy.start()
    normed = flat_normed(tokens_ref)
    for b in range(bands.count):
        at = bands.first[b] * bands.columns
        part = padded_rows(normed[at : at + bands.own[b]], bands.own_padded[b])
        normed_ref[bands.own_at[b] : bands.own_at[b] + bands.own_padded[b], :] = part.astype(BF16)
    step = 256
    for n, (ref, first) in enumerate(places):
        copies[n].wait()
        for at in range(0, chunk, step):
            part = ref[:, first + at : first + at + step]
            out_ref[:, n * chunk + at : n * chunk + at + step] = dot(normed_ref[...], part).astype(BF16)


def own_projection(bands, tokens, weight):
    width, out = weight.shape
    vmem = pl.BlockSpec(memory_space=pltpu.VMEM)
    return pl.pallas_call(
        functools.partial(own_kernel, bands),
        in_specs=[vmem, pl.BlockSpec(memory_space=pl.ANY)],
        out_specs=[vmem, vmem],
        out_shape=[
            jax.ShapeDtypeStruct((bands.own_total, out), BF16),
            jax.ShapeDtypeStruct((width, out - width), BF16),
        ],
        scratch_shapes=[
            pltpu.VMEM((bands.own_total, width), BF16),
            pltpu.VMEM((width, width), BF16),
            pltpu.SemaphoreType.DMA((6,)),
        ],
        compiler_params=params(42),
        cost_estimate=pl.CostEstimate(
            flops=2 * bands.own_total * width * out, bytes_accessed=2 * width * out, transcendentals=0
        ),
        name="own_projection",
    )(tokens, weight)


def attend(bands, some, kinds, consts, own_ref, outer, bias_ref, put, scratch):
    k_ref, v_ref, q_ref, p_ref, r_ref = scratch
    width = own_ref.shape[1] // 3
    block = width * GROUP // HEADS
    window = WLAT * WLON
    units = [(n, b, g) for n, b in enumerate(some) for g in range(HEADS // GROUP)]
    for u, (n, b, g) in enumerate(units):
        keys, query, mask, _ = consts[kinds[n] : kinds[n] + 4]
        own = slice(bands.own_at[b], bands.own_at[b] + bands.own_padded[b])
        for ref, skip in ((k_ref, 0), (v_ref, width)):
            parts = [own_ref[own, width + skip + g * block : width + skip + (g + 1) * block]]
            for out_ref, at, size in outer(b):
                parts.append(out_ref[at : at + size, skip + g * block : skip + (g + 1) * block])
            ref[u] = dot(keys[...], jnp.concatenate(parts, axis=0)).astype(BF16)
        total = query.shape[0]
        q_ref[u, :total] = dot(query[...], own_ref[own, g * block : (g + 1) * block]).astype(BF16) * mask[...]
    for u, (n, b, g) in enumerate(units):
        at = 0
        for c, count in enumerate(bands.counts_padded[b]):
            scores = dot(
                q_ref[u, at : at + count], k_ref[u, c * bands.window : c * bands.window + window], ((1,), (1,))
            )
            if b == 0:
                scores = scores + bias_ref[0:1, :window]
            if b == bands.count - 1:
                scores = scores + bias_ref[1:2, :window]
            raised = jnp.exp(scores - jnp.max(scores, axis=-1, keepdims=True))
            weights = raised * (1.0 / jnp.sum(raised, axis=-1, keepdims=True))
            p_ref[u, at : at + count, :window] = weights.astype(BF16)
            at += count
    for u, (n, b, g) in enumerate(units):
        mask = consts[kinds[n] + 2]
        at = 0
        for c, count in enumerate(bands.counts_padded[b]):
            mixed = dot(
                p_ref[u, at : at + count, :window], v_ref[u, c * bands.window : c * bands.window + window]
            )
            r_ref[u, at : at + count] = mixed.astype(BF16) * mask[at : at + count]
            at += count
    for u, (n, b, g) in enumerate(units):
        back = consts[kinds[n] + 3]
        put(b, g, dot(back[...], r_ref[u, : back.shape[1]]).astype(BF16))


def attend_scratch(bands, some, block):
    units = len(some) * HEADS // GROUP
    keys = len(bands.widths) * bands.window
    rows = max(sum(bands.counts_padded[b]) for b in some)
    return [
        pltpu.VMEM((units, keys, block), BF16),
        pltpu.VMEM((units, keys, block), BF16),
        pltpu.VMEM((units, rows, block), BF16),
        pltpu.VMEM((units, rows, 128), BF16),
        pltpu.VMEM((units, rows, block), BF16),
    ]


def middle_kernel(bands, some, kinds, west_ref, east_ref, own_ref, weight_ref, *rest):
    consts, (side_ref, out_ref, normed_ref, *scratch) = rest[:-8], rest[-8:]
    west, east = flat_normed(west_ref), flat_normed(east_ref)
    for b in range(bands.count):
        at, size = bands.first[b] * SIDE, bands.height[b] * SIDE
        part = jnp.concatenate([west[at : at + size], east[at : at + size]], axis=0)
        normed_ref[bands.side_at[b] : bands.side_at[b] + bands.side[b], :] = part.astype(BF16)
    project(normed_ref, weight_ref, side_ref)

    def outer(b):
        return [(side_ref, bands.side_at[b], bands.side[b])]

    def put(b, g, value):
        at = bands.own_at[b] - bands.own_at[1]
        block = value.shape[1]
        out_ref[at : at + bands.own_padded[b], g * block : (g + 1) * block] = value

    attend(bands, some, kinds, consts, own_ref, outer, None, put, scratch)


def edge_kernel(bands, some, kinds, tokens_ref, north_ref, south_ref, bias_ref, own_ref, side_ref, inner_ref, weight_ref, out_w_ref, patch_ref, *rest):
    consts, rest = rest[:-11], rest[-11:]
    middle_ref, upper_ref, lower_ref, normed_ref, slab_ref, attended_ref, *scratch = rest
    rows, columns, width = tokens_ref.shape
    slab = bands.slab_padded
    for k, ref in enumerate((north_ref, south_ref)):
        normed_ref[k * slab : (k + 1) * slab, :] = padded_rows(flat_normed(ref), slab).astype(BF16)
    project(normed_ref, weight_ref, slab_ref)

    def outer(b):
        return [
            (side_ref, bands.side_at[b], bands.side[b]),
            (slab_ref, 0 if b == 0 else slab, slab),
        ]

    def put(b, g, value):
        block = value.shape[1]
        attended_ref[bands.own_at[b] : bands.own_at[b] + bands.own_padded[b], g * block : (g + 1) * block] = value

    attended_ref[bands.own_at[1] : bands.own_at[-1], :] = inner_ref[...]
    attend(bands, some, kinds, consts, own_ref, outer, bias_ref, put, scratch)
    mixed = dot(attended_ref[...], out_w_ref[...])
    mixed = jnp.concatenate([mixed[at : at + n] for at, n in zip(bands.own_at, bands.own)], axis=0)
    middle = tokens_ref[...].astype(F32) + mixed.reshape(rows, columns, width)
    middle_ref[...] = middle.astype(BF16)
    middle = middle.reshape(rows * columns, width).astype(BF16)
    padded = patch_ref.shape[0] // 4
    parts = [dot(patch_ref[k * padded : (k + 1) * padded, :], middle) for k in range(4)]
    total = sum(jnp.sum(p, axis=-1, keepdims=True) for p in parts)
    mean = total * (1.0 / (4 * width))
    parts = [p - mean for p in parts]
    spread = sum(jnp.sum(p * p, axis=-1, keepdims=True) for p in parts)
    factor = lax.rsqrt(spread * (1.0 / (4 * width)) + 1e-05)
    for k in range(4):
        ref = (upper_ref, lower_ref)[k // 2]
        ref[:, k % 2 * width : (k % 2 + 1) * width] = (parts[k] * factor).astype(BF16)


def vmem_call(kernel, out, args, scratch, flops, name, mib=24, exps=0):
    vmem = pl.BlockSpec(memory_space=pltpu.VMEM)
    return pl.pallas_call(
        kernel,
        in_specs=[vmem] * len(args),
        out_specs=[vmem] * len(out),
        out_shape=[jax.ShapeDtypeStruct(shape, BF16) for shape in out],
        scratch_shapes=scratch,
        compiler_params=params(mib),
        cost_estimate=pl.CostEstimate(flops=flops, bytes_accessed=2**20, transcendentals=exps),
        name=name,
    )(*args)


def attention(bands, tokens, rims, qkv_weight, out_weight):
    rows, columns, width = tokens.shape
    block = width * GROUP // HEADS
    west = shift(rims[0], "lon", 1, True)
    east = shift(rims[1], "lon", -1, True)
    own, kv_weight = own_projection(bands, tokens, qkv_weight)

    def slab(part):
        return jnp.concatenate([west[part], tokens[part], east[part]], axis=1)

    north = shift(slab(slice(rows - RIM_LAT, rows)), "lat", 1, False)
    south = shift(slab(slice(0, RIM_LAT)), "lat", -1, False)
    inner = list(range(1, bands.count - 1))
    edges = [0, bands.count - 1]
    kinds, consts = bands.constants(inner, block)
    side, attended = vmem_call(
        functools.partial(middle_kernel, bands, inner, kinds),
        [(bands.side_total, 2 * width), (bands.own_at[-1] - bands.own_at[1], width)],
        [west, east, own, kv_weight] + consts,
        [pltpu.VMEM((bands.side_total, width), BF16)] + attend_scratch(bands, inner, block),
        5 * 10**9,
        "middle_attention",
        exps=500000,
    )
    kinds, consts = bands.constants(edges, block)
    padded = up16(rows * columns // 4)
    return vmem_call(
        functools.partial(edge_kernel, bands, edges, kinds),
        [tokens.shape, (padded, 2 * width), (padded, 2 * width)],
        [tokens, north, south, key_bias(), own, side, attended, kv_weight, out_weight, bands.patch_matrix()] + consts,
        [
            pltpu.VMEM((2 * bands.slab_padded, width), BF16),
            pltpu.VMEM((2 * bands.slab_padded, 2 * width), BF16),
            pltpu.VMEM((bands.own_total, width), BF16),
        ]
        + attend_scratch(bands, edges, block),
        6 * 10**9,
        "edge_attention",
        exps=300000,
    )


def shift(part, axis, step, wrap):
    size = lax.axis_size(axis)
    pairs = [(i, (i + step) % size) for i in range(size) if wrap or 0 <= i + step < size]
    return lax.ppermute(part, axis, pairs)


def key_bias():
    row = jnp.arange(8, dtype=jnp.int32)[:, None]
    key = jnp.arange(128, dtype=jnp.int32)[None, :] // WLON
    north = (row == 0) & (key < RIM_LAT) & (lax.axis_index("lat") == 0)
    south = (row == 1) & (key >= RIM_LAT) & (lax.axis_index("lat") == lax.axis_size("lat") - 1)
    return jnp.where(north | south, F32(-1e30), F32(0.0))


def place_index():
    me = lax.axis_index("lon")
    return jnp.stack([me // 2, me % 2]).astype(jnp.int32)


def merge_dots(place_ref, upper, lower, mine_ref, pair_ref, x_ref, x_pair_ref, y_ref, y_pair_ref, refs):
    half, block = x_ref.shape
    at = [pl.ds(pl.multiple_of((place_ref[1] + k) % 2 * block, block), block) for k in range(2)]
    own, x, y = refs
    for k, ref in enumerate((mine_ref, pair_ref)):
        own(at[k], dot(upper, ref[:half, :]), dot(lower, ref[half:, :]))
    for k, ref in enumerate((x_ref, x_pair_ref)):
        x(at[k], dot(upper, ref[...]))
    for k, ref in enumerate((y_ref, y_pair_ref)):
        y(at[k], dot(lower, ref[...]))


def merge_own_kernel(place_ref, upper_ref, lower_ref, *refs):
    weights, (own_ref, x_ref, y_ref), kept = refs[:6], refs[6:9], refs[9:]
    for ref, to in zip(weights, kept):
        to[...] = ref[...]

    def own(at, a, b):
        own_ref[:, at] = a + b

    def x(at, a):
        x_ref[:, at] = a

    def y(at, b):
        y_ref[:, at] = b

    merge_dots(place_ref, upper_ref[...], lower_ref[...], *weights, (own, x, y))


def merge_other_kernel(place_ref, upper_ref, lower_ref, *refs):
    weights, (to_y_ref, to_x_ref) = refs[:6], refs[6:]
    wide = to_x_ref.shape[1] // 2

    def own(at, a, b):
        to_y_ref[:, at] = a.astype(BF16)
        to_x_ref[:, at] = b.astype(BF16)

    def x(at, a):
        to_y_ref[:, pl.ds(pl.multiple_of(wide + at.start, at.size), at.size)] = a.astype(BF16)

    def y(at, b):
        to_x_ref[:, pl.ds(pl.multiple_of(wide + at.start, at.size), at.size)] = b.astype(BF16)

    merge_dots(place_ref, upper_ref[...], lower_ref[...], *weights, (own, x, y))


def combine_kernel(place_ref, own_ref, x_ref, y_ref, from_y_ref, from_x_ref, out_ref):
    wide = own_ref.shape[1]
    chip = place_ref[0]
    from_x, from_y = from_x_ref[...].astype(F32), from_y_ref[...].astype(F32)
    parts = [
        own_ref[...],
        x_ref[...] + from_x[:, :wide],
        y_ref[...] + from_y[:, :wide],
        from_x[:, wide:] + from_y[:, wide:],
    ]
    for m, part in enumerate(parts):
        out_ref[:, pl.ds(pl.multiple_of((chip ^ m) * wide, wide), wide)] = part.astype(BF16)


def local_call(kernel, out, place, args, flops, name, mib=16):
    vmem = pl.BlockSpec(memory_space=pltpu.VMEM)
    return pl.pallas_call(
        kernel,
        in_specs=[pl.BlockSpec(memory_space=pltpu.SMEM)] + [vmem] * len(args),
        out_specs=[vmem] * len(out),
        out_shape=out,
        compiler_params=params(mib),
        cost_estimate=pl.CostEstimate(flops=flops, bytes_accessed=2**20, transcendentals=0),
        name=name,
    )(place, *args)


def merge_by_squares(upper, lower, merge_weight, halves):
    half = merge_weight.shape[0] // 2
    block = merge_weight.shape[1]
    count = upper.shape[0]
    x = chip_swap(halves[0], 1)
    y = chip_swap(halves[1], 2)
    x_pair, y_pair, _ = lax.optimization_barrier((x, y, upper))
    weights = [merge_weight, core_swap(merge_weight), x, core_swap(x_pair), y, core_swap(y_pair)]
    place = place_index()
    from_y = chip_swap(upper, 2)
    from_x = chip_swap(lower, 1)
    flops = 16 * count * half * block
    wide = jax.ShapeDtypeStruct((count, 2 * block), F32)
    kept = [jax.ShapeDtypeStruct(w.shape, BF16) for w in weights]
    *own, a, b, c, d, e, f = local_call(
        merge_own_kernel, [wide] * 3 + kept, place, [upper, lower] + weights, flops, "merge_own", 28
    )
    weights = [a, b, c, d, e, f]
    pair = jax.ShapeDtypeStruct((count, 4 * block), BF16)
    to_y, to_x = local_call(merge_other_kernel, [pair] * 2, place, [from_y, from_x] + weights, flops, "merge_other")
    back_y, back_x = chip_swap(to_y, 2), chip_swap(to_x, 1)
    out = jax.ShapeDtypeStruct((count, 8 * block), BF16)
    return local_call(combine_kernel, [out], place, [*own, back_y, back_x], 0, "combine")[0]


def ffn_kernel(mine_ref, theirs_ref, up_ref, down_ref, out_mine_ref, low_ref, high_ref, normed_ref, hidden_ref):
    count = mine_ref.shape[0]
    for k, ref in enumerate((mine_ref, theirs_ref)):
        normed_ref[k * count : (k + 1) * count, :] = normalize(ref[...].astype(F32)).astype(BF16)
    hidden = hidden_ref.shape[1]
    step = 256
    for at in range(0, hidden, step):
        raw = dot(normed_ref[...], up_ref[:, at : at + step])
        active = 0.5 * raw * (1.0 + lax.erf(raw * np.float32(np.sqrt(0.5))))
        hidden_ref[:, at : at + step] = active.astype(BF16)
    half = low_ref.shape[1]
    for at in range(0, 2 * half, step):
        out = dot(hidden_ref[...], down_ref[:, at : at + step]).astype(BF16)
        out_mine_ref[:, at : at + step] = out[:count]
        ref = low_ref if at < half else high_ref
        ref[:, at % half : at % half + step] = out[count:]


def feed_forward(mine, theirs, up, down):
    count = mine.shape[0]
    width, hidden = up.shape
    vmem = pl.BlockSpec(memory_space=pltpu.VMEM)
    return pl.pallas_call(
        ffn_kernel,
        in_specs=[vmem] * 4,
        out_specs=[vmem] * 3,
        out_shape=[jax.ShapeDtypeStruct((count, width // n), BF16) for n in (1, 2, 2)],
        scratch_shapes=[pltpu.VMEM((2 * count, width), BF16), pltpu.VMEM((2 * count, hidden), BF16)],
        compiler_params=params(20),
        cost_estimate=pl.CostEstimate(
            flops=8 * count * width * hidden, bytes_accessed=4 * width * hidden, transcendentals=2 * count * hidden
        ),
        name="feed_forward",
    )(mine, theirs, up, down)


def added(mine, low, high, more=None):
    total = mine.astype(F32) + jnp.concatenate([low, high], axis=1).astype(F32)
    return (total if more is None else total + more.astype(F32)).astype(BF16)


def summed(mine, low, high):
    return added(mine, core_swap(low), core_swap(high))


def core_swap(value):
    size = lax.axis_size("lon")
    return lax.ppermute(value, "lon", [(i, i ^ 1) for i in range(size)])


def chip_swap(value, offset):
    size = lax.axis_size("lon")
    return lax.ppermute(value, "lon", [(i, i ^ (2 * offset)) for i in range(size)])


def cross(value, first, second):
    size = lax.axis_size("lon")
    return lax.ppermute(value, "lon", [(i, i ^ (2 * (second if i % 2 else first))) for i in range(size)])


def coarse_by_squares(upper, lower, merge_weight, halves, up, down):
    own = merge_by_squares(upper, lower, merge_weight, halves)
    near = cross(own, 1, 2)
    first = feed_forward(own, core_swap(own), up, down)
    near, *first = lax.optimization_barrier((near, *first))
    far = cross(near, 2, 1)
    near_sums = feed_forward(near, core_swap(near), up, down)
    later, *near_sums = lax.optimization_barrier((own, *near_sums))
    other = cross(later, 2, 1)
    far_sums = feed_forward(far, core_swap(far), up, down)
    other, *far_sums = lax.optimization_barrier((other, *far_sums))
    relayed = cross(summed(*far_sums), 2, 1)
    other_back = cross(summed(*feed_forward(other, core_swap(other), up, down)), 2, 1)
    near_back = cross(added(*near_sums[:1], core_swap(near_sums[1]), core_swap(near_sums[2]), relayed), 1, 2)
    return sum(part.astype(F32) for part in (own, summed(*first), other_back, near_back))


def coarse_by_chips(upper, lower, merge_weight, halves, up, down):
    weight = lax.all_gather(merge_weight, "lon", axis=1, tiled=True)
    patches = jnp.concatenate([upper, lower], axis=1)
    coarse = jnp.dot(patches, weight, preferred_element_type=F32).astype(BF16)
    chips = lax.axis_size("lon") // 2
    arrived = [coarse] + [chip_swap(coarse, m) for m in range(1, chips)]
    total = coarse.astype(F32)
    for m in range(chips):
        part = summed(*feed_forward(arrived[m], core_swap(arrived[m]), up, down))
        total = total + (chip_swap(part, m) if m else part).astype(F32)
    return total


def per_device(tokens, qkv_weight, out_weight, merge_weight, up_weight, down_weight):
    rows, columns, width = tokens.shape
    bands = Bands(rows, columns)
    cells = rows * columns // 4
    *rims, upper_weight, lower_weight = prepare(tokens, merge_weight)
    middle_out, upper, lower = attention(bands, tokens, rims, qkv_weight, out_weight)
    coarse = coarse_by_squares if lax.axis_size("lon") == 8 else coarse_by_chips
    halves = [upper_weight, lower_weight]
    total = coarse(upper, lower, merge_weight, halves, up_weight, down_weight)
    coarse_out = total[:cells].astype(jnp.bfloat16)
    return (middle_out, coarse_out.reshape(rows // 2, columns // 2, -1))


def solution(mesh):
    return jax.shard_map(
        per_device,
        mesh=mesh,
        in_specs=(P("lat", "lon", None), P(), P(), P(None, "lon"), P(None, "lon"), P("lon", None)),
        out_specs=(P("lat", "lon", None), P("lat", "lon", None)),
        check_vma=False,
    )
```

```python
import functools

import jax
import jax.numpy as jnp
import numpy as np
from jax import lax
from jax.experimental import pallas as pl
from jax.experimental.pallas import tpu as pltpu
from jax.sharding import PartitionSpec as P

HEADS = 16
WLAT = 6
WLON = 12
RIM_LAT = WLAT // 2
RIM_LON = WLON // 2
SIDE = 8
GROUP = 4
F32 = jnp.float32
BF16 = jnp.bfloat16


def up16(n):
    return -(-n // 16) * 16


def params(mib=48, **kw):
    return pltpu.CompilerParams(vmem_limit_bytes=mib * 2**20, **kw)


class Bands:
    def __init__(self, rows, columns):
        assert (rows - WLAT) % WLAT == 0 and (columns - WLON) % WLON == 0
        self.rows, self.columns = rows, columns
        inner = (rows - WLAT) // WLAT
        self.height = [RIM_LAT] + [WLAT] * inner + [RIM_LAT]
        self.count = len(self.height)
        self.first = [sum(self.height[:b]) for b in range(self.count)]
        self.widths = [RIM_LON] + [WLON] * ((columns - WLON) // WLON) + [RIM_LON]
        self.own = [h * columns for h in self.height]
        self.own_padded = [up16(n) for n in self.own]
        self.own_at = [sum(self.own_padded[:b]) for b in range(self.count)]
        self.own_total = sum(self.own_padded)
        self.side = [2 * h * SIDE for h in self.height]
        assert all(n % 16 == 0 for n in self.side)
        self.side_at = [sum(self.side[:b]) for b in range(self.count)]
        self.side_total = sum(self.side)
        self.slab = columns + 2 * SIDE
        self.slab_padded = up16(RIM_LAT * self.slab)
        self.window = up16(WLAT * WLON)
        self.counts = [[GROUP * h * w for w in self.widths] for h in self.height]
        self.counts_padded = [[up16(n) for n in row] for row in self.counts]

    def edge(self, b):
        return b in (0, self.count - 1)

    def sources(self, b):
        return self.own_padded[b] + self.side[b] + (self.slab_padded if self.edge(b) else 0)

    def source(self, b, i, j):
        columns, h, first = self.columns, self.height[b], self.first[b]
        at = self.own_padded[b]
        if not 0 <= i < self.rows:
            i = i + RIM_LAT if i < 0 else i - self.rows
            return at + self.side[b] + i * self.slab + j + SIDE
        if 0 <= j < columns:
            return (i - first) * columns + j
        at += (i - first) * SIDE
        return at + (j + SIDE if j < 0 else h * SIDE + j - columns)

    def key_matrix(self, b):
        g = np.zeros((len(self.widths) * self.window, self.sources(b)), np.float32)
        top = self.first[b] - (RIM_LAT if b == 0 else 0)
        for c in range(len(self.widths)):
            for i in range(WLAT):
                for j in range(WLON):
                    at = c * self.window + i * WLON + j
                    g[at, self.source(b, top + i, c * WLON - RIM_LON + j)] = 1
        return g.astype(BF16)

    def query_matrix(self, b):
        total = sum(self.counts_padded[b])
        g = np.zeros((total, self.own_padded[b]), np.float32)
        head = np.zeros((total,), np.int32)
        start = left = 0
        for width, padded in zip(self.widths, self.counts_padded[b]):
            at = start
            for k in range(GROUP):
                for i in range(self.height[b]):
                    for j in range(width):
                        g[at, i * self.columns + left + j] = 1
                        head[at] = k
                        at += 1
            left += width
            start += padded
        return g.astype(BF16), head

    def patch_matrix(self):
        cells = self.rows * self.columns // 4
        padded = up16(cells)
        g = np.zeros((4 * padded, self.rows * self.columns), np.float32)
        for r in range(self.rows // 2):
            for c in range(self.columns // 2):
                for k in range(4):
                    to = k * padded + r * (self.columns // 2) + c
                    g[to, (2 * r + k // 2) * self.columns + 2 * c + k % 2] = 1
        return g.astype(BF16)

    def constants(self, some, block):
        distinct, kinds, consts = [], [], []
        for b in some:
            kind = (self.height[b], b == 0, b == self.count - 1)
            if kind not in distinct:
                distinct.append(kind)
                query, head = self.query_matrix(b)
                mask = head[:, None] == (np.arange(block) // (block // GROUP))[None, :]
                scale = np.float32((block // GROUP) ** -0.5)
                scaled = (query.astype(np.float32) * scale).astype(BF16)
                consts += [self.key_matrix(b), scaled, mask.astype(BF16), np.ascontiguousarray(query.T)]
            kinds.append(4 * distinct.index(kind))
        return kinds, consts


def normalize(values):
    center = values - jnp.mean(values, axis=-1, keepdims=True)
    spread = jnp.mean(center * center, axis=-1, keepdims=True)
    return center * lax.rsqrt(spread + 1e-05)


def dot(a, b, dims=((1,), (0,))):
    return lax.dot_general(a, b, (dims, ((), ())), preferred_element_type=F32)


def flat_normed(ref):
    values = ref[...].astype(F32)
    return normalize(values.reshape(-1, values.shape[-1]))


def project(normed_ref, weight_ref, out_ref):
    step = 256
    for at in range(0, out_ref.shape[1], step):
        out_ref[:, at : at + step] = dot(normed_ref[...], weight_ref[:, at : at + step]).astype(BF16)


def padded_rows(values, total):
    if values.shape[0] == total:
        return values
    return jnp.concatenate([values, jnp.zeros((total - values.shape[0], values.shape[1]), values.dtype)], axis=0)


def prepare_kernel(tokens_ref, weight_ref, east_ref, west_ref, upper_ref, lower_ref, sems):
    half = upper_ref.shape[0]
    copies = [
        pltpu.make_async_copy(weight_ref.at[k * half : (k + 1) * half], ref, sems.at[k])
        for k, ref in enumerate((upper_ref, lower_ref))
    ]
    for copy in copies:
        copy.start()
    columns = tokens_ref.shape[1]
    east_ref[...] = tokens_ref[:, columns - SIDE :]
    west_ref[...] = tokens_ref[:, :SIDE]
    for copy in copies:
        copy.wait()


def prepare(tokens, merge_weight):
    rows, _, width = tokens.shape
    depth, block = merge_weight.shape
    vmem, anywhere = pl.BlockSpec(memory_space=pltpu.VMEM), pl.BlockSpec(memory_space=pl.ANY)
    return pl.pallas_call(
        prepare_kernel,
        in_specs=[vmem, anywhere],
        out_specs=[vmem] * 4,
        out_shape=[jax.ShapeDtypeStruct((rows, SIDE, width), BF16)] * 2
        + [jax.ShapeDtypeStruct((depth // 2, block), BF16)] * 2,
        scratch_shapes=[pltpu.SemaphoreType.DMA((2,))],
        compiler_params=params(52),
        name="prepare",
    )(tokens, merge_weight)


def own_kernel(bands, tokens_ref, weight_ref, out_ref, kv_ref, normed_ref, q_ref, sems):
    width = q_ref.shape[1]
    chunk = weight_ref.shape[1] // sems.shape[0]
    places = []
    for n in range(sems.shape[0]):
        at = n * chunk
        places.append((q_ref, at) if at < width else (kv_ref, at - width))
    copies = [
        pltpu.make_async_copy(weight_ref.at[:, pl.ds(n * chunk, chunk)], ref.at[:, pl.ds(at, chunk)], sems.at[n])
        for n, (ref, at) in enumerate(places)
    ]
    for copy in copies:
        copy.start()
    normed = flat_normed(tokens_ref)
    for b in range(bands.count):
        at = bands.first[b] * bands.columns
        part = padded_rows(normed[at : at + bands.own[b]], bands.own_padded[b])
        normed_ref[bands.own_at[b] : bands.own_at[b] + bands.own_padded[b], :] = part.astype(BF16)
    step = 256
    for n, (ref, first) in enumerate(places):
        copies[n].wait()
        for at in range(0, chunk, step):
            part = ref[:, first + at : first + at + step]
            out_ref[:, n * chunk + at : n * chunk + at + step] = dot(normed_ref[...], part).astype(BF16)


def own_projection(bands, tokens, weight):
    width, out = weight.shape
    vmem = pl.BlockSpec(memory_space=pltpu.VMEM)
    return pl.pallas_call(
        functools.partial(own_kernel, bands),
        in_specs=[vmem, pl.BlockSpec(memory_space=pl.ANY)],
        out_specs=[vmem, vmem],
        out_shape=[
            jax.ShapeDtypeStruct((bands.own_total, out), BF16),
            jax.ShapeDtypeStruct((width, out - width), BF16),
        ],
        scratch_shapes=[
            pltpu.VMEM((bands.own_total, width), BF16),
            pltpu.VMEM((width, width), BF16),
            pltpu.SemaphoreType.DMA((6,)),
        ],
        compiler_params=params(42),
        cost_estimate=pl.CostEstimate(
            flops=2 * bands.own_total * width * out, bytes_accessed=2 * width * out, transcendentals=0
        ),
        name="own_projection",
    )(tokens, weight)


def attend(bands, some, kinds, consts, own_ref, outer, bias_ref, put, scratch):
    k_ref, v_ref, q_ref, p_ref, r_ref = scratch
    width = own_ref.shape[1] // 3
    block = width * GROUP // HEADS
    window = WLAT * WLON
    units = [(n, b, g) for n, b in enumerate(some) for g in range(HEADS // GROUP)]
    for u, (n, b, g) in enumerate(units):
        keys, query, mask, _ = consts[kinds[n] : kinds[n] + 4]
        own = slice(bands.own_at[b], bands.own_at[b] + bands.own_padded[b])
        for ref, skip in ((k_ref, 0), (v_ref, width)):
            parts = [own_ref[own, width + skip + g * block : width + skip + (g + 1) * block]]
            for out_ref, at, size in outer(b):
                parts.append(out_ref[at : at + size, skip + g * block : skip + (g + 1) * block])
            ref[u] = dot(keys[...], jnp.concatenate(parts, axis=0)).astype(BF16)
        total = query.shape[0]
        q_ref[u, :total] = dot(query[...], own_ref[own, g * block : (g + 1) * block]).astype(BF16) * mask[...]
    for u, (n, b, g) in enumerate(units):
        at = 0
        for c, count in enumerate(bands.counts_padded[b]):
            scores = dot(
                q_ref[u, at : at + count], k_ref[u, c * bands.window : c * bands.window + window], ((1,), (1,))
            )
            if b == 0:
                scores = scores + bias_ref[0:1, :window]
            if b == bands.count - 1:
                scores = scores + bias_ref[1:2, :window]
            raised = jnp.exp(scores - jnp.max(scores, axis=-1, keepdims=True))
            weights = raised * (1.0 / jnp.sum(raised, axis=-1, keepdims=True))
            p_ref[u, at : at + count, :window] = weights.astype(BF16)
            at += count
    for u, (n, b, g) in enumerate(units):
        mask = consts[kinds[n] + 2]
        at = 0
        for c, count in enumerate(bands.counts_padded[b]):
            mixed = dot(
                p_ref[u, at : at + count, :window], v_ref[u, c * bands.window : c * bands.window + window]
            )
            r_ref[u, at : at + count] = mixed.astype(BF16) * mask[at : at + count]
            at += count
    for u, (n, b, g) in enumerate(units):
        back = consts[kinds[n] + 3]
        put(b, g, dot(back[...], r_ref[u, : back.shape[1]]).astype(BF16))


def attend_scratch(bands, some, block):
    units = len(some) * HEADS // GROUP
    keys = len(bands.widths) * bands.window
    rows = max(sum(bands.counts_padded[b]) for b in some)
    return [
        pltpu.VMEM((units, keys, block), BF16),
        pltpu.VMEM((units, keys, block), BF16),
        pltpu.VMEM((units, rows, block), BF16),
        pltpu.VMEM((units, rows, 128), BF16),
        pltpu.VMEM((units, rows, block), BF16),
    ]


def middle_kernel(bands, some, kinds, west_ref, east_ref, own_ref, weight_ref, *rest):
    consts, (side_ref, out_ref, normed_ref, *scratch) = rest[:-8], rest[-8:]
    west, east = flat_normed(west_ref), flat_normed(east_ref)
    for b in range(bands.count):
        at, size = bands.first[b] * SIDE, bands.height[b] * SIDE
        part = jnp.concatenate([west[at : at + size], east[at : at + size]], axis=0)
        normed_ref[bands.side_at[b] : bands.side_at[b] + bands.side[b], :] = part.astype(BF16)
    project(normed_ref, weight_ref, side_ref)

    def outer(b):
        return [(side_ref, bands.side_at[b], bands.side[b])]

    def put(b, g, value):
        at = bands.own_at[b] - bands.own_at[1]
        block = value.shape[1]
        out_ref[at : at + bands.own_padded[b], g * block : (g + 1) * block] = value

    attend(bands, some, kinds, consts, own_ref, outer, None, put, scratch)


def edge_kernel(bands, some, kinds, tokens_ref, north_ref, south_ref, bias_ref, own_ref, side_ref, inner_ref, weight_ref, out_w_ref, patch_ref, *rest):
    consts, rest = rest[:-11], rest[-11:]
    middle_ref, upper_ref, lower_ref, normed_ref, slab_ref, attended_ref, *scratch = rest
    rows, columns, width = tokens_ref.shape
    slab = bands.slab_padded
    for k, ref in enumerate((north_ref, south_ref)):
        normed_ref[k * slab : (k + 1) * slab, :] = padded_rows(flat_normed(ref), slab).astype(BF16)
    project(normed_ref, weight_ref, slab_ref)

    def outer(b):
        return [
            (side_ref, bands.side_at[b], bands.side[b]),
            (slab_ref, 0 if b == 0 else slab, slab),
        ]

    def put(b, g, value):
        block = value.shape[1]
        attended_ref[bands.own_at[b] : bands.own_at[b] + bands.own_padded[b], g * block : (g + 1) * block] = value

    attended_ref[bands.own_at[1] : bands.own_at[-1], :] = inner_ref[...]
    attend(bands, some, kinds, consts, own_ref, outer, bias_ref, put, scratch)
    mixed = dot(attended_ref[...], out_w_ref[...])
    mixed = jnp.concatenate([mixed[at : at + n] for at, n in zip(bands.own_at, bands.own)], axis=0)
    middle = tokens_ref[...].astype(F32) + mixed.reshape(rows, columns, width)
    middle_ref[...] = middle.astype(BF16)
    middle = middle.reshape(rows * columns, width).astype(BF16)
    padded = patch_ref.shape[0] // 4
    parts = [dot(patch_ref[k * padded : (k + 1) * padded, :], middle) for k in range(4)]
    total = sum(jnp.sum(p, axis=-1, keepdims=True) for p in parts)
    mean = total * (1.0 / (4 * width))
    parts = [p - mean for p in parts]
    spread = sum(jnp.sum(p * p, axis=-1, keepdims=True) for p in parts)
    factor = lax.rsqrt(spread * (1.0 / (4 * width)) + 1e-05)
    for k in range(4):
        ref = (upper_ref, lower_ref)[k // 2]
        ref[:, k % 2 * width : (k % 2 + 1) * width] = (parts[k] * factor).astype(BF16)


def vmem_call(kernel, out, args, scratch, flops, name, mib=24, exps=0):
    vmem = pl.BlockSpec(memory_space=pltpu.VMEM)
    return pl.pallas_call(
        kernel,
        in_specs=[vmem] * len(args),
        out_specs=[vmem] * len(out),
        out_shape=[jax.ShapeDtypeStruct(shape, BF16) for shape in out],
        scratch_shapes=scratch,
        compiler_params=params(mib),
        cost_estimate=pl.CostEstimate(flops=flops, bytes_accessed=2**20, transcendentals=exps),
        name=name,
    )(*args)


def attention(bands, tokens, rims, qkv_weight, out_weight):
    rows, columns, width = tokens.shape
    block = width * GROUP // HEADS
    west = shift(rims[0], "lon", 1, True)
    east = shift(rims[1], "lon", -1, True)
    own, kv_weight = own_projection(bands, tokens, qkv_weight)

    def slab(part):
        return jnp.concatenate([west[part], tokens[part], east[part]], axis=1)

    north = shift(slab(slice(rows - RIM_LAT, rows)), "lat", 1, False)
    south = shift(slab(slice(0, RIM_LAT)), "lat", -1, False)
    inner = list(range(1, bands.count - 1))
    edges = [0, bands.count - 1]
    kinds, consts = bands.constants(inner, block)
    side, attended = vmem_call(
        functools.partial(middle_kernel, bands, inner, kinds),
        [(bands.side_total, 2 * width), (bands.own_at[-1] - bands.own_at[1], width)],
        [west, east, own, kv_weight] + consts,
        [pltpu.VMEM((bands.side_total, width), BF16)] + attend_scratch(bands, inner, block),
        5 * 10**9,
        "middle_attention",
        exps=500000,
    )
    kinds, consts = bands.constants(edges, block)
    padded = up16(rows * columns // 4)
    return vmem_call(
        functools.partial(edge_kernel, bands, edges, kinds),
        [tokens.shape, (padded, 2 * width), (padded, 2 * width)],
        [tokens, north, south, key_bias(), own, side, attended, kv_weight, out_weight, bands.patch_matrix()] + consts,
        [
            pltpu.VMEM((2 * bands.slab_padded, width), BF16),
            pltpu.VMEM((2 * bands.slab_padded, 2 * width), BF16),
            pltpu.VMEM((bands.own_total, width), BF16),
        ]
        + attend_scratch(bands, edges, block),
        6 * 10**9,
        "edge_attention",
        exps=300000,
    )


def shift(part, axis, step, wrap):
    size = lax.axis_size(axis)
    pairs = [(i, (i + step) % size) for i in range(size) if wrap or 0 <= i + step < size]
    return lax.ppermute(part, axis, pairs)


def key_bias():
    row = jnp.arange(8, dtype=jnp.int32)[:, None]
    key = jnp.arange(128, dtype=jnp.int32)[None, :] // WLON
    north = (row == 0) & (key < RIM_LAT) & (lax.axis_index("lat") == 0)
    south = (row == 1) & (key >= RIM_LAT) & (lax.axis_index("lat") == lax.axis_size("lat") - 1)
    return jnp.where(north | south, F32(-1e30), F32(0.0))


def place_index():
    me = lax.axis_index("lon")
    return jnp.stack([me // 2, me % 2]).astype(jnp.int32)


def merge_dots(place_ref, upper, lower, mine_ref, pair_ref, x_ref, x_pair_ref, y_ref, y_pair_ref, refs):
    half, block = x_ref.shape
    at = [pl.ds(pl.multiple_of((place_ref[1] + k) % 2 * block, block), block) for k in range(2)]
    own, x, y = refs
    for k, ref in enumerate((mine_ref, pair_ref)):
        own(at[k], dot(upper, ref[:half, :]), dot(lower, ref[half:, :]))
    for k, ref in enumerate((x_ref, x_pair_ref)):
        x(at[k], dot(upper, ref[...]))
    for k, ref in enumerate((y_ref, y_pair_ref)):
        y(at[k], dot(lower, ref[...]))


def merge_own_kernel(place_ref, upper_ref, lower_ref, *refs):
    weights, (own_ref, x_ref, y_ref), kept = refs[:6], refs[6:9], refs[9:]
    for ref, to in zip(weights, kept):
        to[...] = ref[...]

    def own(at, a, b):
        own_ref[:, at] = a + b

    def x(at, a):
        x_ref[:, at] = a

    def y(at, b):
        y_ref[:, at] = b

    merge_dots(place_ref, upper_ref[...], lower_ref[...], *weights, (own, x, y))


def merge_other_kernel(place_ref, upper_ref, lower_ref, *refs):
    weights, (to_y_ref, to_x_ref) = refs[:6], refs[6:]
    wide = to_x_ref.shape[1] // 2

    def own(at, a, b):
        to_y_ref[:, at] = a.astype(BF16)
        to_x_ref[:, at] = b.astype(BF16)

    def x(at, a):
        to_y_ref[:, pl.ds(pl.multiple_of(wide + at.start, at.size), at.size)] = a.astype(BF16)

    def y(at, b):
        to_x_ref[:, pl.ds(pl.multiple_of(wide + at.start, at.size), at.size)] = b.astype(BF16)

    merge_dots(place_ref, upper_ref[...], lower_ref[...], *weights, (own, x, y))


def combine_kernel(place_ref, own_ref, x_ref, y_ref, from_y_ref, from_x_ref, out_ref):
    wide = own_ref.shape[1]
    chip = place_ref[0]
    from_x, from_y = from_x_ref[...].astype(F32), from_y_ref[...].astype(F32)
    parts = [
        own_ref[...],
        x_ref[...] + from_x[:, :wide],
        y_ref[...] + from_y[:, :wide],
        from_x[:, wide:] + from_y[:, wide:],
    ]
    for m, part in enumerate(parts):
        out_ref[:, pl.ds(pl.multiple_of((chip ^ m) * wide, wide), wide)] = part.astype(BF16)


def local_call(kernel, out, place, args, flops, name, mib=16):
    vmem = pl.BlockSpec(memory_space=pltpu.VMEM)
    return pl.pallas_call(
        kernel,
        in_specs=[pl.BlockSpec(memory_space=pltpu.SMEM)] + [vmem] * len(args),
        out_specs=[vmem] * len(out),
        out_shape=out,
        compiler_params=params(mib),
        cost_estimate=pl.CostEstimate(flops=flops, bytes_accessed=2**20, transcendentals=0),
        name=name,
    )(place, *args)


def merge_by_squares(upper, lower, merge_weight, halves):
    half = merge_weight.shape[0] // 2
    block = merge_weight.shape[1]
    count = upper.shape[0]
    x = chip_swap(halves[0], 1)
    y = chip_swap(halves[1], 2)
    x_pair, y_pair, _ = lax.optimization_barrier((x, y, upper))
    weights = [merge_weight, core_swap(merge_weight), x, core_swap(x_pair), y, core_swap(y_pair)]
    place = place_index()
    from_y = chip_swap(upper, 2)
    from_x = chip_swap(lower, 1)
    flops = 16 * count * half * block
    wide = jax.ShapeDtypeStruct((count, 2 * block), F32)
    kept = [jax.ShapeDtypeStruct(w.shape, BF16) for w in weights]
    *own, a, b, c, d, e, f = local_call(
        merge_own_kernel, [wide] * 3 + kept, place, [upper, lower] + weights, flops, "merge_own", 28
    )
    weights = [a, b, c, d, e, f]
    pair = jax.ShapeDtypeStruct((count, 4 * block), BF16)
    to_y, to_x = local_call(merge_other_kernel, [pair] * 2, place, [from_y, from_x] + weights, flops, "merge_other")
    back_y, back_x = chip_swap(to_y, 2), chip_swap(to_x, 1)
    out = jax.ShapeDtypeStruct((count, 8 * block), BF16)
    return local_call(combine_kernel, [out], place, [*own, back_y, back_x], 0, "combine")[0]


def ffn_kernel(mine_ref, theirs_ref, up_ref, down_ref, out_mine_ref, low_ref, high_ref, normed_ref, hidden_ref):
    count = mine_ref.shape[0]
    for k, ref in enumerate((mine_ref, theirs_ref)):
        normed_ref[k * count : (k + 1) * count, :] = normalize(ref[...].astype(F32)).astype(BF16)
    hidden = hidden_ref.shape[1]
    step = 256
    for at in range(0, hidden, step):
        raw = dot(normed_ref[...], up_ref[:, at : at + step])
        active = 0.5 * raw * (1.0 + lax.erf(raw * np.float32(np.sqrt(0.5))))
        hidden_ref[:, at : at + step] = active.astype(BF16)
    half = low_ref.shape[1]
    for at in range(0, 2 * half, step):
        out = dot(hidden_ref[...], down_ref[:, at : at + step]).astype(BF16)
        out_mine_ref[:, at : at + step] = out[:count]
        ref = low_ref if at < half else high_ref
        ref[:, at % half : at % half + step] = out[count:]


def feed_forward(mine, theirs, up, down):
    count = mine.shape[0]
    width, hidden = up.shape
    vmem = pl.BlockSpec(memory_space=pltpu.VMEM)
    return pl.pallas_call(
        ffn_kernel,
        in_specs=[vmem] * 4,
        out_specs=[vmem] * 3,
        out_shape=[jax.ShapeDtypeStruct((count, width // n), BF16) for n in (1, 2, 2)],
        scratch_shapes=[pltpu.VMEM((2 * count, width), BF16), pltpu.VMEM((2 * count, hidden), BF16)],
        compiler_params=params(20),
        cost_estimate=pl.CostEstimate(
            flops=8 * count * width * hidden, bytes_accessed=4 * width * hidden, transcendentals=2 * count * hidden
        ),
        name="feed_forward",
    )(mine, theirs, up, down)


def added(mine, low, high):
    return (mine.astype(F32) + jnp.concatenate([low, high], axis=1).astype(F32)).astype(BF16)


def summed(mine, low, high):
    return added(mine, core_swap(low), core_swap(high))


def core_swap(value):
    size = lax.axis_size("lon")
    return lax.ppermute(value, "lon", [(i, i ^ 1) for i in range(size)])


def chip_swap(value, offset):
    size = lax.axis_size("lon")
    return lax.ppermute(value, "lon", [(i, i ^ (2 * offset)) for i in range(size)])


def cross(value, first, second):
    size = lax.axis_size("lon")
    return lax.ppermute(value, "lon", [(i, i ^ (2 * (second if i % 2 else first))) for i in range(size)])


def coarse_by_squares(upper, lower, merge_weight, halves, up, down):
    own = merge_by_squares(upper, lower, merge_weight, halves)
    near = cross(own, 1, 2)
    first = feed_forward(own, core_swap(own), up, down)
    near, *first = lax.optimization_barrier((near, *first))
    far = cross(near, 2, 1)
    near_mine, near_low, near_high = feed_forward(near, core_swap(near), up, down)
    later, near_mine = lax.optimization_barrier((own, near_mine))
    other = cross(later, 2, 1)
    near_low, far = lax.optimization_barrier((core_swap(near_low), far))
    mine, low, high = feed_forward(far, core_swap(far), up, down)
    low, other = lax.optimization_barrier((core_swap(low), other))
    relayed = cross(added(mine, low, core_swap(high)), 2, 1)
    other_back = cross(summed(*feed_forward(other, core_swap(other), up, down)), 2, 1)
    half = low.shape[1]
    near_back = []
    for part, at in ((near_low, 0), (core_swap(near_high), half)):
        columns = slice(at, at + half)
        total = near_mine[:, columns].astype(F32) + part.astype(F32) + relayed[:, columns].astype(F32)
        near_back.append(cross(total.astype(BF16), 1, 2))
    near_back = jnp.concatenate(near_back, axis=1)
    return sum(part.astype(F32) for part in (own, summed(*first), other_back, near_back))


def coarse_by_chips(upper, lower, merge_weight, halves, up, down):
    weight = lax.all_gather(merge_weight, "lon", axis=1, tiled=True)
    patches = jnp.concatenate([upper, lower], axis=1)
    coarse = jnp.dot(patches, weight, preferred_element_type=F32).astype(BF16)
    chips = lax.axis_size("lon") // 2
    arrived = [coarse] + [chip_swap(coarse, m) for m in range(1, chips)]
    total = coarse.astype(F32)
    for m in range(chips):
        part = summed(*feed_forward(arrived[m], core_swap(arrived[m]), up, down))
        total = total + (chip_swap(part, m) if m else part).astype(F32)
    return total


def per_device(tokens, qkv_weight, out_weight, merge_weight, up_weight, down_weight):
    rows, columns, width = tokens.shape
    bands = Bands(rows, columns)
    cells = rows * columns // 4
    *rims, upper_weight, lower_weight = prepare(tokens, merge_weight)
    middle_out, upper, lower = attention(bands, tokens, rims, qkv_weight, out_weight)
    coarse = coarse_by_squares if lax.axis_size("lon") == 8 else coarse_by_chips
    halves = [upper_weight, lower_weight]
    total = coarse(upper, lower, merge_weight, halves, up_weight, down_weight)
    coarse_out = total[:cells].astype(jnp.bfloat16)
    return (middle_out, coarse_out.reshape(rows // 2, columns // 2, -1))


def solution(mesh):
    return jax.shard_map(
        per_device,
        mesh=mesh,
        in_specs=(P("lat", "lon", None), P(), P(), P(None, "lon"), P(None, "lon"), P("lon", None)),
        out_specs=(P("lat", "lon", None), P("lat", "lon", None)),
        check_vma=False,
    )
```

```python
import functools

import jax
import jax.numpy as jnp
import numpy as np
from jax import lax
from jax.experimental import pallas as pl
from jax.experimental.pallas import tpu as pltpu
from jax.sharding import PartitionSpec as P

HEADS = 16
WLAT = 6
WLON = 12
RIM_LAT = WLAT // 2
RIM_LON = WLON // 2
SIDE = 8
GROUP = 4
F32 = jnp.float32
BF16 = jnp.bfloat16


def up16(n):
    return -(-n // 16) * 16


def params(mib=48, **kw):
    return pltpu.CompilerParams(vmem_limit_bytes=mib * 2**20, **kw)


class Bands:
    def __init__(self, rows, columns):
        assert (rows - WLAT) % WLAT == 0 and (columns - WLON) % WLON == 0
        self.rows, self.columns = rows, columns
        inner = (rows - WLAT) // WLAT
        self.height = [RIM_LAT] + [WLAT] * inner + [RIM_LAT]
        self.count = len(self.height)
        self.first = [sum(self.height[:b]) for b in range(self.count)]
        self.widths = [RIM_LON] + [WLON] * ((columns - WLON) // WLON) + [RIM_LON]
        self.own = [h * columns for h in self.height]
        self.own_padded = [up16(n) for n in self.own]
        self.own_at = [sum(self.own_padded[:b]) for b in range(self.count)]
        self.own_total = sum(self.own_padded)
        self.side = [2 * h * SIDE for h in self.height]
        assert all(n % 16 == 0 for n in self.side)
        self.side_at = [sum(self.side[:b]) for b in range(self.count)]
        self.side_total = sum(self.side)
        self.slab = columns + 2 * SIDE
        self.slab_padded = up16(RIM_LAT * self.slab)
        self.window = up16(WLAT * WLON)
        self.counts = [[GROUP * h * w for w in self.widths] for h in self.height]
        self.counts_padded = [[up16(n) for n in row] for row in self.counts]

    def edge(self, b):
        return b in (0, self.count - 1)

    def sources(self, b):
        return self.own_padded[b] + self.side[b] + (self.slab_padded if self.edge(b) else 0)

    def source(self, b, i, j):
        columns, h, first = self.columns, self.height[b], self.first[b]
        at = self.own_padded[b]
        if not 0 <= i < self.rows:
            i = i + RIM_LAT if i < 0 else i - self.rows
            return at + self.side[b] + i * self.slab + j + SIDE
        if 0 <= j < columns:
            return (i - first) * columns + j
        at += (i - first) * SIDE
        return at + (j + SIDE if j < 0 else h * SIDE + j - columns)

    def key_matrix(self, b):
        g = np.zeros((len(self.widths) * self.window, self.sources(b)), np.float32)
        top = self.first[b] - (RIM_LAT if b == 0 else 0)
        for c in range(len(self.widths)):
            for i in range(WLAT):
                for j in range(WLON):
                    at = c * self.window + i * WLON + j
                    g[at, self.source(b, top + i, c * WLON - RIM_LON + j)] = 1
        return g.astype(BF16)

    def query_matrix(self, b):
        total = sum(self.counts_padded[b])
        g = np.zeros((total, self.own_padded[b]), np.float32)
        head = np.zeros((total,), np.int32)
        start = left = 0
        for width, padded in zip(self.widths, self.counts_padded[b]):
            at = start
            for k in range(GROUP):
                for i in range(self.height[b]):
                    for j in range(width):
                        g[at, i * self.columns + left + j] = 1
                        head[at] = k
                        at += 1
            left += width
            start += padded
        return g.astype(BF16), head

    def patch_matrix(self):
        cells = self.rows * self.columns // 4
        padded = up16(cells)
        g = np.zeros((4 * padded, self.rows * self.columns), np.float32)
        for r in range(self.rows // 2):
            for c in range(self.columns // 2):
                for k in range(4):
                    to = k * padded + r * (self.columns // 2) + c
                    g[to, (2 * r + k // 2) * self.columns + 2 * c + k % 2] = 1
        return g.astype(BF16)

    def constants(self, some, block):
        distinct, kinds, consts = [], [], []
        for b in some:
            kind = (self.height[b], b == 0, b == self.count - 1)
            if kind not in distinct:
                distinct.append(kind)
                query, head = self.query_matrix(b)
                mask = head[:, None] == (np.arange(block) // (block // GROUP))[None, :]
                scale = np.float32((block // GROUP) ** -0.5)
                scaled = (query.astype(np.float32) * scale).astype(BF16)
                consts += [self.key_matrix(b), scaled, mask.astype(BF16), np.ascontiguousarray(query.T)]
            kinds.append(4 * distinct.index(kind))
        return kinds, consts


def normalize(values):
    center = values - jnp.mean(values, axis=-1, keepdims=True)
    spread = jnp.mean(center * center, axis=-1, keepdims=True)
    return center * lax.rsqrt(spread + 1e-05)


def dot(a, b, dims=((1,), (0,))):
    return lax.dot_general(a, b, (dims, ((), ())), preferred_element_type=F32)


def flat_normed(ref):
    values = ref[...].astype(F32)
    return normalize(values.reshape(-1, values.shape[-1]))


def project(normed_ref, weight_ref, out_ref):
    step = 256
    for at in range(0, out_ref.shape[1], step):
        out_ref[:, at : at + step] = dot(normed_ref[...], weight_ref[:, at : at + step]).astype(BF16)


def padded_rows(values, total):
    if values.shape[0] == total:
        return values
    return jnp.concatenate([values, jnp.zeros((total - values.shape[0], values.shape[1]), values.dtype)], axis=0)


def rims_kernel(tokens_ref, east_ref, west_ref):
    columns = tokens_ref.shape[1]
    east_ref[...] = tokens_ref[:, columns - SIDE :]
    west_ref[...] = tokens_ref[:, :SIDE]


def rims(tokens):
    rows, _, width = tokens.shape
    vmem = pl.BlockSpec(memory_space=pltpu.VMEM)
    return pl.pallas_call(
        rims_kernel,
        in_specs=[vmem],
        out_specs=[vmem] * 2,
        out_shape=[jax.ShapeDtypeStruct((rows, SIDE, width), BF16)] * 2,
        compiler_params=params(16),
        name="rims",
    )(tokens)


def halves_kernel(weight_ref, upper_ref, lower_ref, sems):
    half = upper_ref.shape[0]
    copies = [
        pltpu.make_async_copy(weight_ref.at[k * half : (k + 1) * half], ref, sems.at[k])
        for k, ref in enumerate((upper_ref, lower_ref))
    ]
    for copy in copies:
        copy.start()
    for copy in copies:
        copy.wait()


def halves_of(weight):
    depth, block = weight.shape
    return pl.pallas_call(
        halves_kernel,
        in_specs=[pl.BlockSpec(memory_space=pl.ANY)],
        out_specs=[pl.BlockSpec(memory_space=pltpu.VMEM)] * 2,
        out_shape=[jax.ShapeDtypeStruct((depth // 2, block), BF16)] * 2,
        scratch_shapes=[pltpu.SemaphoreType.DMA((2,))],
        compiler_params=params(52),
        name="halves",
    )(weight)


def own_kernel(bands, tokens_ref, weight_ref, out_ref, kv_ref, normed_ref, q_ref, sems):
    width = q_ref.shape[1]
    chunk = weight_ref.shape[1] // sems.shape[0]
    places = []
    for n in range(sems.shape[0]):
        at = n * chunk
        places.append((q_ref, at) if at < width else (kv_ref, at - width))
    copies = [
        pltpu.make_async_copy(weight_ref.at[:, pl.ds(n * chunk, chunk)], ref.at[:, pl.ds(at, chunk)], sems.at[n])
        for n, (ref, at) in enumerate(places)
    ]
    for copy in copies:
        copy.start()
    normed = flat_normed(tokens_ref)
    for b in range(bands.count):
        at = bands.first[b] * bands.columns
        part = padded_rows(normed[at : at + bands.own[b]], bands.own_padded[b])
        normed_ref[bands.own_at[b] : bands.own_at[b] + bands.own_padded[b], :] = part.astype(BF16)
    step = 256
    for n, (ref, first) in enumerate(places):
        copies[n].wait()
        for at in range(0, chunk, step):
            part = ref[:, first + at : first + at + step]
            out_ref[:, n * chunk + at : n * chunk + at + step] = dot(normed_ref[...], part).astype(BF16)


def own_projection(bands, tokens, weight):
    width, out = weight.shape
    vmem = pl.BlockSpec(memory_space=pltpu.VMEM)
    return pl.pallas_call(
        functools.partial(own_kernel, bands),
        in_specs=[vmem, pl.BlockSpec(memory_space=pl.ANY)],
        out_specs=[vmem, vmem],
        out_shape=[
            jax.ShapeDtypeStruct((bands.own_total, out), BF16),
            jax.ShapeDtypeStruct((width, out - width), BF16),
        ],
        scratch_shapes=[
            pltpu.VMEM((bands.own_total, width), BF16),
            pltpu.VMEM((width, width), BF16),
            pltpu.SemaphoreType.DMA((6,)),
        ],
        compiler_params=params(42),
        cost_estimate=pl.CostEstimate(
            flops=2 * bands.own_total * width * out, bytes_accessed=2 * width * out, transcendentals=0
        ),
        name="own_projection",
    )(tokens, weight)


def attend(bands, some, kinds, consts, own_ref, outer, bias_ref, put, scratch):
    k_ref, v_ref, q_ref, p_ref, r_ref = scratch
    width = own_ref.shape[1] // 3
    block = width * GROUP // HEADS
    window = WLAT * WLON
    units = [(n, b, g) for n, b in enumerate(some) for g in range(HEADS // GROUP)]
    for u, (n, b, g) in enumerate(units):
        keys, query, mask, _ = consts[kinds[n] : kinds[n] + 4]
        own = slice(bands.own_at[b], bands.own_at[b] + bands.own_padded[b])
        for ref, skip in ((k_ref, 0), (v_ref, width)):
            parts = [own_ref[own, width + skip + g * block : width + skip + (g + 1) * block]]
            for out_ref, at, size in outer(b):
                parts.append(out_ref[at : at + size, skip + g * block : skip + (g + 1) * block])
            ref[u] = dot(keys[...], jnp.concatenate(parts, axis=0)).astype(BF16)
        total = query.shape[0]
        q_ref[u, :total] = dot(query[...], own_ref[own, g * block : (g + 1) * block]).astype(BF16) * mask[...]
    for u, (n, b, g) in enumerate(units):
        at = 0
        for c, count in enumerate(bands.counts_padded[b]):
            scores = dot(
                q_ref[u, at : at + count], k_ref[u, c * bands.window : c * bands.window + window], ((1,), (1,))
            )
            if b == 0:
                scores = scores + bias_ref[0:1, :window]
            if b == bands.count - 1:
                scores = scores + bias_ref[1:2, :window]
            raised = jnp.exp(scores - jnp.max(scores, axis=-1, keepdims=True))
            weights = raised * (1.0 / jnp.sum(raised, axis=-1, keepdims=True))
            p_ref[u, at : at + count, :window] = weights.astype(BF16)
            at += count
    for u, (n, b, g) in enumerate(units):
        mask = consts[kinds[n] + 2]
        at = 0
        for c, count in enumerate(bands.counts_padded[b]):
            mixed = dot(
                p_ref[u, at : at + count, :window], v_ref[u, c * bands.window : c * bands.window + window]
            )
            r_ref[u, at : at + count] = mixed.astype(BF16) * mask[at : at + count]
            at += count
    for u, (n, b, g) in enumerate(units):
        back = consts[kinds[n] + 3]
        put(b, g, dot(back[...], r_ref[u, : back.shape[1]]).astype(BF16))


def attend_scratch(bands, some, block):
    units = len(some) * HEADS // GROUP
    keys = len(bands.widths) * bands.window
    rows = max(sum(bands.counts_padded[b]) for b in some)
    return [
        pltpu.VMEM((units, keys, block), BF16),
        pltpu.VMEM((units, keys, block), BF16),
        pltpu.VMEM((units, rows, block), BF16),
        pltpu.VMEM((units, rows, 128), BF16),
        pltpu.VMEM((units, rows, block), BF16),
    ]


def middle_kernel(bands, some, kinds, west_ref, east_ref, own_ref, weight_ref, *rest):
    consts, (side_ref, out_ref, normed_ref, *scratch) = rest[:-8], rest[-8:]
    west, east = flat_normed(west_ref), flat_normed(east_ref)
    for b in range(bands.count):
        at, size = bands.first[b] * SIDE, bands.height[b] * SIDE
        part = jnp.concatenate([west[at : at + size], east[at : at + size]], axis=0)
        normed_ref[bands.side_at[b] : bands.side_at[b] + bands.side[b], :] = part.astype(BF16)
    project(normed_ref, weight_ref, side_ref)

    def outer(b):
        return [(side_ref, bands.side_at[b], bands.side[b])]

    def put(b, g, value):
        at = bands.own_at[b] - bands.own_at[1]
        block = value.shape[1]
        out_ref[at : at + bands.own_padded[b], g * block : (g + 1) * block] = value

    attend(bands, some, kinds, consts, own_ref, outer, None, put, scratch)


def edge_kernel(bands, some, kinds, tokens_ref, north_ref, south_ref, bias_ref, own_ref, side_ref, inner_ref, weight_ref, out_w_ref, patch_ref, *rest):
    consts, rest = rest[:-11], rest[-11:]
    middle_ref, upper_ref, lower_ref, normed_ref, slab_ref, attended_ref, *scratch = rest
    rows, columns, width = tokens_ref.shape
    slab = bands.slab_padded
    for k, ref in enumerate((north_ref, south_ref)):
        normed_ref[k * slab : (k + 1) * slab, :] = padded_rows(flat_normed(ref), slab).astype(BF16)
    project(normed_ref, weight_ref, slab_ref)

    def outer(b):
        return [
            (side_ref, bands.side_at[b], bands.side[b]),
            (slab_ref, 0 if b == 0 else slab, slab),
        ]

    def put(b, g, value):
        block = value.shape[1]
        attended_ref[bands.own_at[b] : bands.own_at[b] + bands.own_padded[b], g * block : (g + 1) * block] = value

    attended_ref[bands.own_at[1] : bands.own_at[-1], :] = inner_ref[...]
    attend(bands, some, kinds, consts, own_ref, outer, bias_ref, put, scratch)
    mixed = dot(attended_ref[...], out_w_ref[...])
    mixed = jnp.concatenate([mixed[at : at + n] for at, n in zip(bands.own_at, bands.own)], axis=0)
    middle = tokens_ref[...].astype(F32) + mixed.reshape(rows, columns, width)
    middle_ref[...] = middle.astype(BF16)
    middle = middle.reshape(rows * columns, width).astype(BF16)
    padded = patch_ref.shape[0] // 4
    parts = [dot(patch_ref[k * padded : (k + 1) * padded, :], middle) for k in range(4)]
    total = sum(jnp.sum(p, axis=-1, keepdims=True) for p in parts)
    mean = total * (1.0 / (4 * width))
    parts = [p - mean for p in parts]
    spread = sum(jnp.sum(p * p, axis=-1, keepdims=True) for p in parts)
    factor = lax.rsqrt(spread * (1.0 / (4 * width)) + 1e-05)
    for k in range(4):
        ref = (upper_ref, lower_ref)[k // 2]
        ref[:, k % 2 * width : (k % 2 + 1) * width] = (parts[k] * factor).astype(BF16)


def vmem_call(kernel, out, args, scratch, flops, name, mib=24, exps=0):
    vmem = pl.BlockSpec(memory_space=pltpu.VMEM)
    return pl.pallas_call(
        kernel,
        in_specs=[vmem] * len(args),
        out_specs=[vmem] * len(out),
        out_shape=[jax.ShapeDtypeStruct(shape, BF16) for shape in out],
        scratch_shapes=scratch,
        compiler_params=params(mib),
        cost_estimate=pl.CostEstimate(flops=flops, bytes_accessed=2**20, transcendentals=exps),
        name=name,
    )(*args)


def attention(bands, tokens, sides, qkv_weight, out_weight):
    rows, columns, width = tokens.shape
    block = width * GROUP // HEADS
    west = shift(sides[0], "lon", 1, True)
    east = shift(sides[1], "lon", -1, True)
    own, kv_weight = own_projection(bands, tokens, qkv_weight)

    def slab(part):
        return jnp.concatenate([west[part], tokens[part], east[part]], axis=1)

    north = shift(slab(slice(rows - RIM_LAT, rows)), "lat", 1, False)
    south = shift(slab(slice(0, RIM_LAT)), "lat", -1, False)
    inner = list(range(1, bands.count - 1))
    edges = [0, bands.count - 1]
    kinds, consts = bands.constants(inner, block)
    side, attended = vmem_call(
        functools.partial(middle_kernel, bands, inner, kinds),
        [(bands.side_total, 2 * width), (bands.own_at[-1] - bands.own_at[1], width)],
        [west, east, own, kv_weight] + consts,
        [pltpu.VMEM((bands.side_total, width), BF16)] + attend_scratch(bands, inner, block),
        5 * 10**9,
        "middle_attention",
        exps=500000,
    )
    kinds, consts = bands.constants(edges, block)
    padded = up16(rows * columns // 4)
    return vmem_call(
        functools.partial(edge_kernel, bands, edges, kinds),
        [tokens.shape, (padded, 2 * width), (padded, 2 * width)],
        [tokens, north, south, key_bias(), own, side, attended, kv_weight, out_weight, bands.patch_matrix()] + consts,
        [
            pltpu.VMEM((2 * bands.slab_padded, width), BF16),
            pltpu.VMEM((2 * bands.slab_padded, 2 * width), BF16),
            pltpu.VMEM((bands.own_total, width), BF16),
        ]
        + attend_scratch(bands, edges, block),
        6 * 10**9,
        "edge_attention",
        exps=300000,
    )


def shift(part, axis, step, wrap):
    size = lax.axis_size(axis)
    pairs = [(i, (i + step) % size) for i in range(size) if wrap or 0 <= i + step < size]
    return lax.ppermute(part, axis, pairs)


def key_bias():
    row = jnp.arange(8, dtype=jnp.int32)[:, None]
    key = jnp.arange(128, dtype=jnp.int32)[None, :] // WLON
    north = (row == 0) & (key < RIM_LAT) & (lax.axis_index("lat") == 0)
    south = (row == 1) & (key >= RIM_LAT) & (lax.axis_index("lat") == lax.axis_size("lat") - 1)
    return jnp.where(north | south, F32(-1e30), F32(0.0))


def place_index():
    me = lax.axis_index("lon")
    return jnp.stack([me // 2, me % 2]).astype(jnp.int32)


def merge_dots(place_ref, upper, lower, mine_ref, pair_ref, x_ref, x_pair_ref, y_ref, y_pair_ref, refs):
    half, block = x_ref.shape
    at = [pl.ds(pl.multiple_of((place_ref[1] + k) % 2 * block, block), block) for k in range(2)]
    own, x, y = refs
    for k, ref in enumerate((mine_ref, pair_ref)):
        own(at[k], dot(upper, ref[:half, :]), dot(lower, ref[half:, :]))
    for k, ref in enumerate((x_ref, x_pair_ref)):
        x(at[k], dot(upper, ref[...]))
    for k, ref in enumerate((y_ref, y_pair_ref)):
        y(at[k], dot(lower, ref[...]))


def merge_own_kernel(place_ref, upper_ref, lower_ref, *refs):
    weights, (own_ref, x_ref, y_ref), kept = refs[:6], refs[6:9], refs[9:]
    for ref, to in zip(weights, kept):
        to[...] = ref[...]

    def own(at, a, b):
        own_ref[:, at] = a + b

    def x(at, a):
        x_ref[:, at] = a

    def y(at, b):
        y_ref[:, at] = b

    merge_dots(place_ref, upper_ref[...], lower_ref[...], *weights, (own, x, y))


def merge_other_kernel(place_ref, upper_ref, lower_ref, *refs):
    weights, (to_y_ref, to_x_ref) = refs[:6], refs[6:]
    wide = to_x_ref.shape[1] // 2

    def own(at, a, b):
        to_y_ref[:, at] = a.astype(BF16)
        to_x_ref[:, at] = b.astype(BF16)

    def x(at, a):
        to_y_ref[:, pl.ds(pl.multiple_of(wide + at.start, at.size), at.size)] = a.astype(BF16)

    def y(at, b):
        to_x_ref[:, pl.ds(pl.multiple_of(wide + at.start, at.size), at.size)] = b.astype(BF16)

    merge_dots(place_ref, upper_ref[...], lower_ref[...], *weights, (own, x, y))


def combine_kernel(place_ref, own_ref, x_ref, y_ref, from_y_ref, from_x_ref, out_ref):
    wide = own_ref.shape[1]
    chip = place_ref[0]
    from_x, from_y = from_x_ref[...].astype(F32), from_y_ref[...].astype(F32)
    parts = [
        own_ref[...],
        x_ref[...] + from_x[:, :wide],
        y_ref[...] + from_y[:, :wide],
        from_x[:, wide:] + from_y[:, wide:],
    ]
    for m, part in enumerate(parts):
        out_ref[:, pl.ds(pl.multiple_of((chip ^ m) * wide, wide), wide)] = part.astype(BF16)


def local_call(kernel, out, place, args, flops, name, mib=16):
    vmem = pl.BlockSpec(memory_space=pltpu.VMEM)
    return pl.pallas_call(
        kernel,
        in_specs=[pl.BlockSpec(memory_space=pltpu.SMEM)] + [vmem] * len(args),
        out_specs=[vmem] * len(out),
        out_shape=out,
        compiler_params=params(mib),
        cost_estimate=pl.CostEstimate(flops=flops, bytes_accessed=2**20, transcendentals=0),
        name=name,
    )(place, *args)


def merge_by_squares(upper, lower, merge_weight, halves):
    half = merge_weight.shape[0] // 2
    block = merge_weight.shape[1]
    count = upper.shape[0]
    x = chip_swap(halves[0], 1)
    y = chip_swap(halves[1], 2)
    x_pair, y_pair, _ = lax.optimization_barrier((x, y, upper))
    weights = [merge_weight, core_swap(merge_weight), x, core_swap(x_pair), y, core_swap(y_pair)]
    place = place_index()
    from_y = chip_swap(upper, 2)
    from_x = chip_swap(lower, 1)
    flops = 16 * count * half * block
    wide = jax.ShapeDtypeStruct((count, 2 * block), F32)
    kept = [jax.ShapeDtypeStruct(w.shape, BF16) for w in weights]
    *own, a, b, c, d, e, f = local_call(
        merge_own_kernel, [wide] * 3 + kept, place, [upper, lower] + weights, flops, "merge_own", 28
    )
    weights = [a, b, c, d, e, f]
    pair = jax.ShapeDtypeStruct((count, 4 * block), BF16)
    to_y, to_x = local_call(merge_other_kernel, [pair] * 2, place, [from_y, from_x] + weights, flops, "merge_other")
    back_y, back_x = chip_swap(to_y, 2), chip_swap(to_x, 1)
    out = jax.ShapeDtypeStruct((count, 8 * block), BF16)
    return local_call(combine_kernel, [out], place, [*own, back_y, back_x], 0, "combine")[0]


def ffn_kernel(mine_ref, theirs_ref, up_ref, down_ref, out_mine_ref, low_ref, high_ref, normed_ref, hidden_ref):
    count = mine_ref.shape[0]
    for k, ref in enumerate((mine_ref, theirs_ref)):
        normed_ref[k * count : (k + 1) * count, :] = normalize(ref[...].astype(F32)).astype(BF16)
    hidden = hidden_ref.shape[1]
    step = 256
    for at in range(0, hidden, step):
        raw = dot(normed_ref[...], up_ref[:, at : at + step])
        active = 0.5 * raw * (1.0 + lax.erf(raw * np.float32(np.sqrt(0.5))))
        hidden_ref[:, at : at + step] = active.astype(BF16)
    half = low_ref.shape[1]
    for at in range(0, 2 * half, step):
        out = dot(hidden_ref[...], down_ref[:, at : at + step]).astype(BF16)
        out_mine_ref[:, at : at + step] = out[:count]
        ref = low_ref if at < half else high_ref
        ref[:, at % half : at % half + step] = out[count:]


def feed_forward(mine, theirs, up, down):
    count = mine.shape[0]
    width, hidden = up.shape
    vmem = pl.BlockSpec(memory_space=pltpu.VMEM)
    return pl.pallas_call(
        ffn_kernel,
        in_specs=[vmem] * 4,
        out_specs=[vmem] * 3,
        out_shape=[jax.ShapeDtypeStruct((count, width // n), BF16) for n in (1, 2, 2)],
        scratch_shapes=[pltpu.VMEM((2 * count, width), BF16), pltpu.VMEM((2 * count, hidden), BF16)],
        compiler_params=params(20),
        cost_estimate=pl.CostEstimate(
            flops=8 * count * width * hidden, bytes_accessed=4 * width * hidden, transcendentals=2 * count * hidden
        ),
        name="feed_forward",
    )(mine, theirs, up, down)


def added(mine, low, high):
    return (mine.astype(F32) + jnp.concatenate([low, high], axis=1).astype(F32)).astype(BF16)


def summed(mine, low, high):
    return added(mine, core_swap(low), core_swap(high))


def core_swap(value):
    size = lax.axis_size("lon")
    return lax.ppermute(value, "lon", [(i, i ^ 1) for i in range(size)])


def chip_swap(value, offset):
    size = lax.axis_size("lon")
    return lax.ppermute(value, "lon", [(i, i ^ (2 * offset)) for i in range(size)])


def cross(value, first, second):
    size = lax.axis_size("lon")
    return lax.ppermute(value, "lon", [(i, i ^ (2 * (second if i % 2 else first))) for i in range(size)])


def coarse_by_squares(upper, lower, merge_weight, halves, up, down):
    own = merge_by_squares(upper, lower, merge_weight, halves)
    near = cross(own, 1, 2)
    first = feed_forward(own, core_swap(own), up, down)
    near, *first = lax.optimization_barrier((near, *first))
    far = cross(near, 2, 1)
    near_mine, near_low, near_high = feed_forward(near, core_swap(near), up, down)
    later, near_mine = lax.optimization_barrier((own, near_mine))
    other = cross(later, 2, 1)
    near_low, far = lax.optimization_barrier((core_swap(near_low), far))
    mine, low, high = feed_forward(far, core_swap(far), up, down)
    low, other = lax.optimization_barrier((core_swap(low), other))
    relayed = cross(added(mine, low, core_swap(high)), 2, 1)
    other_back = cross(summed(*feed_forward(other, core_swap(other), up, down)), 2, 1)
    half = low.shape[1]
    near_back = []
    for part, at in ((near_low, 0), (core_swap(near_high), half)):
        columns = slice(at, at + half)
        total = near_mine[:, columns].astype(F32) + part.astype(F32) + relayed[:, columns].astype(F32)
        near_back.append(cross(total.astype(BF16), 1, 2))
    near_back = jnp.concatenate(near_back, axis=1)
    return sum(part.astype(F32) for part in (own, summed(*first), other_back, near_back))


def coarse_by_chips(upper, lower, merge_weight, halves, up, down):
    weight = lax.all_gather(merge_weight, "lon", axis=1, tiled=True)
    patches = jnp.concatenate([upper, lower], axis=1)
    coarse = jnp.dot(patches, weight, preferred_element_type=F32).astype(BF16)
    chips = lax.axis_size("lon") // 2
    arrived = [coarse] + [chip_swap(coarse, m) for m in range(1, chips)]
    total = coarse.astype(F32)
    for m in range(chips):
        part = summed(*feed_forward(arrived[m], core_swap(arrived[m]), up, down))
        total = total + (chip_swap(part, m) if m else part).astype(F32)
    return total


def per_device(tokens, qkv_weight, out_weight, merge_weight, up_weight, down_weight):
    rows, columns, width = tokens.shape
    bands = Bands(rows, columns)
    cells = rows * columns // 4
    sides = rims(tokens)
    *sides, later = lax.optimization_barrier((*sides, merge_weight))
    halves = halves_of(later)
    middle_out, upper, lower = attention(bands, tokens, sides, qkv_weight, out_weight)
    coarse = coarse_by_squares if lax.axis_size("lon") == 8 else coarse_by_chips
    total = coarse(upper, lower, merge_weight, halves, up_weight, down_weight)
    coarse_out = total[:cells].astype(jnp.bfloat16)
    return (middle_out, coarse_out.reshape(rows // 2, columns // 2, -1))


def solution(mesh):
    return jax.shard_map(
        per_device,
        mesh=mesh,
        in_specs=(P("lat", "lon", None), P(), P(), P(None, "lon"), P(None, "lon"), P("lon", None)),
        out_specs=(P("lat", "lon", None), P("lat", "lon", None)),
        check_vma=False,
    )
```

```python
import functools

import jax
import jax.numpy as jnp
import numpy as np
from jax import lax
from jax.experimental import pallas as pl
from jax.experimental.pallas import tpu as pltpu
from jax.sharding import PartitionSpec as P

HEADS = 16
WLAT = 6
WLON = 12
RIM_LAT = WLAT // 2
RIM_LON = WLON // 2
SIDE = 8
GROUP = 4
F32 = jnp.float32
BF16 = jnp.bfloat16


def up16(n):
    return -(-n // 16) * 16


def params(mib=48, **kw):
    return pltpu.CompilerParams(vmem_limit_bytes=mib * 2**20, **kw)


class Bands:
    def __init__(self, rows, columns):
        assert (rows - WLAT) % WLAT == 0 and (columns - WLON) % WLON == 0
        self.rows, self.columns = rows, columns
        inner = (rows - WLAT) // WLAT
        self.height = [RIM_LAT] + [WLAT] * inner + [RIM_LAT]
        self.count = len(self.height)
        self.first = [sum(self.height[:b]) for b in range(self.count)]
        self.widths = [RIM_LON] + [WLON] * ((columns - WLON) // WLON) + [RIM_LON]
        self.own = [h * columns for h in self.height]
        self.own_padded = [up16(n) for n in self.own]
        self.own_at = [sum(self.own_padded[:b]) for b in range(self.count)]
        self.own_total = sum(self.own_padded)
        self.side = [2 * h * SIDE for h in self.height]
        assert all(n % 16 == 0 for n in self.side)
        self.side_at = [sum(self.side[:b]) for b in range(self.count)]
        self.side_total = sum(self.side)
        self.slab = columns + 2 * SIDE
        self.slab_padded = up16(RIM_LAT * self.slab)
        self.window = up16(WLAT * WLON)
        self.counts = [[GROUP * h * w for w in self.widths] for h in self.height]
        self.counts_padded = [[up16(n) for n in row] for row in self.counts]

    def edge(self, b):
        return b in (0, self.count - 1)

    def sources(self, b):
        return self.own_padded[b] + self.side[b] + (self.slab_padded if self.edge(b) else 0)

    def source(self, b, i, j):
        columns, h, first = self.columns, self.height[b], self.first[b]
        at = self.own_padded[b]
        if not 0 <= i < self.rows:
            i = i + RIM_LAT if i < 0 else i - self.rows
            return at + self.side[b] + i * self.slab + j + SIDE
        if 0 <= j < columns:
            return (i - first) * columns + j
        at += (i - first) * SIDE
        return at + (j + SIDE if j < 0 else h * SIDE + j - columns)

    def key_matrix(self, b):
        g = np.zeros((len(self.widths) * self.window, self.sources(b)), np.float32)
        top = self.first[b] - (RIM_LAT if b == 0 else 0)
        for c in range(len(self.widths)):
            for i in range(WLAT):
                for j in range(WLON):
                    at = c * self.window + i * WLON + j
                    g[at, self.source(b, top + i, c * WLON - RIM_LON + j)] = 1
        return g.astype(BF16)

    def query_matrix(self, b):
        total = sum(self.counts_padded[b])
        g = np.zeros((total, self.own_padded[b]), np.float32)
        head = np.zeros((total,), np.int32)
        start = left = 0
        for width, padded in zip(self.widths, self.counts_padded[b]):
            at = start
            for k in range(GROUP):
                for i in range(self.height[b]):
                    for j in range(width):
                        g[at, i * self.columns + left + j] = 1
                        head[at] = k
                        at += 1
            left += width
            start += padded
        return g.astype(BF16), head

    def patch_matrix(self):
        cells = self.rows * self.columns // 4
        padded = up16(cells)
        g = np.zeros((4 * padded, self.rows * self.columns), np.float32)
        for r in range(self.rows // 2):
            for c in range(self.columns // 2):
                for k in range(4):
                    to = k * padded + r * (self.columns // 2) + c
                    g[to, (2 * r + k // 2) * self.columns + 2 * c + k % 2] = 1
        return g.astype(BF16)

    def constants(self, some, block):
        distinct, kinds, consts = [], [], []
        for b in some:
            kind = (self.height[b], b == 0, b == self.count - 1)
            if kind not in distinct:
                distinct.append(kind)
                query, head = self.query_matrix(b)
                mask = head[:, None] == (np.arange(block) // (block // GROUP))[None, :]
                scale = np.float32((block // GROUP) ** -0.5)
                scaled = (query.astype(np.float32) * scale).astype(BF16)
                consts += [self.key_matrix(b), scaled, mask.astype(BF16), np.ascontiguousarray(query.T)]
            kinds.append(4 * distinct.index(kind))
        return kinds, consts


def normalize(values):
    center = values - jnp.mean(values, axis=-1, keepdims=True)
    spread = jnp.mean(center * center, axis=-1, keepdims=True)
    return center * lax.rsqrt(spread + 1e-05)


def dot(a, b, dims=((1,), (0,))):
    return lax.dot_general(a, b, (dims, ((), ())), preferred_element_type=F32)


def flat_normed(ref):
    values = ref[...].astype(F32)
    return normalize(values.reshape(-1, values.shape[-1]))


def project(normed_ref, weight_ref, out_ref):
    step = 256
    for at in range(0, out_ref.shape[1], step):
        out_ref[:, at : at + step] = dot(normed_ref[...], weight_ref[:, at : at + step]).astype(BF16)


def padded_rows(values, total):
    if values.shape[0] == total:
        return values
    return jnp.concatenate([values, jnp.zeros((total - values.shape[0], values.shape[1]), values.dtype)], axis=0)


def rims_kernel(tokens_ref, east_ref, west_ref):
    columns = tokens_ref.shape[1]
    east_ref[...] = tokens_ref[:, columns - SIDE :]
    west_ref[...] = tokens_ref[:, :SIDE]


def rims(tokens):
    rows, _, width = tokens.shape
    vmem = pl.BlockSpec(memory_space=pltpu.VMEM)
    return pl.pallas_call(
        rims_kernel,
        in_specs=[vmem],
        out_specs=[vmem] * 2,
        out_shape=[jax.ShapeDtypeStruct((rows, SIDE, width), BF16)] * 2,
        compiler_params=params(16),
        name="rims",
    )(tokens)


def halves_kernel(weight_ref, upper_ref, lower_ref, sems):
    half = upper_ref.shape[0]
    pieces = sems.shape[0] // 2
    size = half // pieces
    copies = []
    for k, ref in enumerate((upper_ref, lower_ref)):
        for n in range(pieces):
            rows = weight_ref.at[k * half + n * size : k * half + (n + 1) * size]
            to = ref.at[n * size : (n + 1) * size]
            copies.append(pltpu.make_async_copy(rows, to, sems.at[k * pieces + n]))
    for copy in copies:
        copy.start()
    for copy in copies:
        copy.wait()


def halves_of(weight):
    depth, block = weight.shape
    return pl.pallas_call(
        halves_kernel,
        in_specs=[pl.BlockSpec(memory_space=pl.ANY)],
        out_specs=[pl.BlockSpec(memory_space=pltpu.VMEM)] * 2,
        out_shape=[jax.ShapeDtypeStruct((depth // 2, block), BF16)] * 2,
        scratch_shapes=[pltpu.SemaphoreType.DMA((8,))],
        compiler_params=params(52),
        name="halves",
    )(weight)


def own_kernel(bands, tokens_ref, weight_ref, out_ref, kv_ref, normed_ref, q_ref, sems):
    width = q_ref.shape[1]
    chunk = weight_ref.shape[1] // sems.shape[0]
    places = []
    for n in range(sems.shape[0]):
        at = n * chunk
        places.append((q_ref, at) if at < width else (kv_ref, at - width))
    copies = [
        pltpu.make_async_copy(weight_ref.at[:, pl.ds(n * chunk, chunk)], ref.at[:, pl.ds(at, chunk)], sems.at[n])
        for n, (ref, at) in enumerate(places)
    ]
    for copy in copies:
        copy.start()
    normed = flat_normed(tokens_ref)
    for b in range(bands.count):
        at = bands.first[b] * bands.columns
        part = padded_rows(normed[at : at + bands.own[b]], bands.own_padded[b])
        normed_ref[bands.own_at[b] : bands.own_at[b] + bands.own_padded[b], :] = part.astype(BF16)
    step = 256
    for n, (ref, first) in enumerate(places):
        copies[n].wait()
        for at in range(0, chunk, step):
            part = ref[:, first + at : first + at + step]
            out_ref[:, n * chunk + at : n * chunk + at + step] = dot(normed_ref[...], part).astype(BF16)


def own_projection(bands, tokens, weight):
    width, out = weight.shape
    vmem = pl.BlockSpec(memory_space=pltpu.VMEM)
    return pl.pallas_call(
        functools.partial(own_kernel, bands),
        in_specs=[vmem, pl.BlockSpec(memory_space=pl.ANY)],
        out_specs=[vmem, vmem],
        out_shape=[
            jax.ShapeDtypeStruct((bands.own_total, out), BF16),
            jax.ShapeDtypeStruct((width, out - width), BF16),
        ],
        scratch_shapes=[
            pltpu.VMEM((bands.own_total, width), BF16),
            pltpu.VMEM((width, width), BF16),
            pltpu.SemaphoreType.DMA((12,)),
        ],
        compiler_params=params(42),
        cost_estimate=pl.CostEstimate(
            flops=2 * bands.own_total * width * out, bytes_accessed=2 * width * out, transcendentals=0
        ),
        name="own_projection",
    )(tokens, weight)


def attend(bands, some, kinds, consts, own_ref, outer, bias_ref, put, scratch):
    k_ref, v_ref, q_ref, p_ref, r_ref = scratch
    width = own_ref.shape[1] // 3
    block = width * GROUP // HEADS
    window = WLAT * WLON
    units = [(n, b, g) for n, b in enumerate(some) for g in range(HEADS // GROUP)]
    for u, (n, b, g) in enumerate(units):
        keys, query, mask, _ = consts[kinds[n] : kinds[n] + 4]
        own = slice(bands.own_at[b], bands.own_at[b] + bands.own_padded[b])
        for ref, skip in ((k_ref, 0), (v_ref, width)):
            parts = [own_ref[own, width + skip + g * block : width + skip + (g + 1) * block]]
            for out_ref, at, size in outer(b):
                parts.append(out_ref[at : at + size, skip + g * block : skip + (g + 1) * block])
            ref[u] = dot(keys[...], jnp.concatenate(parts, axis=0)).astype(BF16)
        total = query.shape[0]
        q_ref[u, :total] = dot(query[...], own_ref[own, g * block : (g + 1) * block]).astype(BF16) * mask[...]
    for u, (n, b, g) in enumerate(units):
        at = 0
        for c, count in enumerate(bands.counts_padded[b]):
            scores = dot(
                q_ref[u, at : at + count], k_ref[u, c * bands.window : c * bands.window + window], ((1,), (1,))
            )
            if b == 0:
                scores = scores + bias_ref[0:1, :window]
            if b == bands.count - 1:
                scores = scores + bias_ref[1:2, :window]
            raised = jnp.exp(scores - jnp.max(scores, axis=-1, keepdims=True))
            weights = raised * (1.0 / jnp.sum(raised, axis=-1, keepdims=True))
            p_ref[u, at : at + count, :window] = weights.astype(BF16)
            at += count
    for u, (n, b, g) in enumerate(units):
        mask = consts[kinds[n] + 2]
        at = 0
        for c, count in enumerate(bands.counts_padded[b]):
            mixed = dot(
                p_ref[u, at : at + count, :window], v_ref[u, c * bands.window : c * bands.window + window]
            )
            r_ref[u, at : at + count] = mixed.astype(BF16) * mask[at : at + count]
            at += count
    for u, (n, b, g) in enumerate(units):
        back = consts[kinds[n] + 3]
        put(b, g, dot(back[...], r_ref[u, : back.shape[1]]).astype(BF16))


def attend_scratch(bands, some, block):
    units = len(some) * HEADS // GROUP
    keys = len(bands.widths) * bands.window
    rows = max(sum(bands.counts_padded[b]) for b in some)
    return [
        pltpu.VMEM((units, keys, block), BF16),
        pltpu.VMEM((units, keys, block), BF16),
        pltpu.VMEM((units, rows, block), BF16),
        pltpu.VMEM((units, rows, 128), BF16),
        pltpu.VMEM((units, rows, block), BF16),
    ]


def middle_kernel(bands, some, kinds, west_ref, east_ref, own_ref, weight_ref, *rest):
    consts, (side_ref, out_ref, normed_ref, *scratch) = rest[:-8], rest[-8:]
    west, east = flat_normed(west_ref), flat_normed(east_ref)
    for b in range(bands.count):
        at, size = bands.first[b] * SIDE, bands.height[b] * SIDE
        part = jnp.concatenate([west[at : at + size], east[at : at + size]], axis=0)
        normed_ref[bands.side_at[b] : bands.side_at[b] + bands.side[b], :] = part.astype(BF16)
    project(normed_ref, weight_ref, side_ref)

    def outer(b):
        return [(side_ref, bands.side_at[b], bands.side[b])]

    def put(b, g, value):
        at = bands.own_at[b] - bands.own_at[1]
        block = value.shape[1]
        out_ref[at : at + bands.own_padded[b], g * block : (g + 1) * block] = value

    attend(bands, some, kinds, consts, own_ref, outer, None, put, scratch)


def edge_kernel(bands, some, kinds, tokens_ref, north_ref, south_ref, bias_ref, own_ref, side_ref, inner_ref, weight_ref, out_w_ref, patch_ref, *rest):
    consts, rest = rest[:-11], rest[-11:]
    middle_ref, upper_ref, lower_ref, normed_ref, slab_ref, attended_ref, *scratch = rest
    rows, columns, width = tokens_ref.shape
    slab = bands.slab_padded
    for k, ref in enumerate((north_ref, south_ref)):
        normed_ref[k * slab : (k + 1) * slab, :] = padded_rows(flat_normed(ref), slab).astype(BF16)
    project(normed_ref, weight_ref, slab_ref)

    def outer(b):
        return [
            (side_ref, bands.side_at[b], bands.side[b]),
            (slab_ref, 0 if b == 0 else slab, slab),
        ]

    def put(b, g, value):
        block = value.shape[1]
        attended_ref[bands.own_at[b] : bands.own_at[b] + bands.own_padded[b], g * block : (g + 1) * block] = value

    attended_ref[bands.own_at[1] : bands.own_at[-1], :] = inner_ref[...]
    attend(bands, some, kinds, consts, own_ref, outer, bias_ref, put, scratch)
    mixed = dot(attended_ref[...], out_w_ref[...])
    mixed = jnp.concatenate([mixed[at : at + n] for at, n in zip(bands.own_at, bands.own)], axis=0)
    middle = tokens_ref[...].astype(F32) + mixed.reshape(rows, columns, width)
    middle_ref[...] = middle.astype(BF16)
    middle = middle.reshape(rows * columns, width).astype(BF16)
    padded = patch_ref.shape[0] // 4
    parts = [dot(patch_ref[k * padded : (k + 1) * padded, :], middle) for k in range(4)]
    total = sum(jnp.sum(p, axis=-1, keepdims=True) for p in parts)
    mean = total * (1.0 / (4 * width))
    parts = [p - mean for p in parts]
    spread = sum(jnp.sum(p * p, axis=-1, keepdims=True) for p in parts)
    factor = lax.rsqrt(spread * (1.0 / (4 * width)) + 1e-05)
    for k in range(4):
        ref = (upper_ref, lower_ref)[k // 2]
        ref[:, k % 2 * width : (k % 2 + 1) * width] = (parts[k] * factor).astype(BF16)


def vmem_call(kernel, out, args, scratch, flops, name, mib=24, exps=0):
    vmem = pl.BlockSpec(memory_space=pltpu.VMEM)
    return pl.pallas_call(
        kernel,
        in_specs=[vmem] * len(args),
        out_specs=[vmem] * len(out),
        out_shape=[jax.ShapeDtypeStruct(shape, BF16) for shape in out],
        scratch_shapes=scratch,
        compiler_params=params(mib),
        cost_estimate=pl.CostEstimate(flops=flops, bytes_accessed=2**20, transcendentals=exps),
        name=name,
    )(*args)


def attention(bands, tokens, sides, qkv_weight, out_weight):
    rows, columns, width = tokens.shape
    block = width * GROUP // HEADS
    west = shift(sides[0], "lon", 1, True)
    east = shift(sides[1], "lon", -1, True)
    own, kv_weight = own_projection(bands, tokens, qkv_weight)

    def slab(part):
        return jnp.concatenate([west[part], tokens[part], east[part]], axis=1)

    north = shift(slab(slice(rows - RIM_LAT, rows)), "lat", 1, False)
    south = shift(slab(slice(0, RIM_LAT)), "lat", -1, False)
    inner = list(range(1, bands.count - 1))
    edges = [0, bands.count - 1]
    kinds, consts = bands.constants(inner, block)
    side, attended = vmem_call(
        functools.partial(middle_kernel, bands, inner, kinds),
        [(bands.side_total, 2 * width), (bands.own_at[-1] - bands.own_at[1], width)],
        [west, east, own, kv_weight] + consts,
        [pltpu.VMEM((bands.side_total, width), BF16)] + attend_scratch(bands, inner, block),
        5 * 10**9,
        "middle_attention",
        exps=500000,
    )
    kinds, consts = bands.constants(edges, block)
    padded = up16(rows * columns // 4)
    return vmem_call(
        functools.partial(edge_kernel, bands, edges, kinds),
        [tokens.shape, (padded, 2 * width), (padded, 2 * width)],
        [tokens, north, south, key_bias(), own, side, attended, kv_weight, out_weight, bands.patch_matrix()] + consts,
        [
            pltpu.VMEM((2 * bands.slab_padded, width), BF16),
            pltpu.VMEM((2 * bands.slab_padded, 2 * width), BF16),
            pltpu.VMEM((bands.own_total, width), BF16),
        ]
        + attend_scratch(bands, edges, block),
        6 * 10**9,
        "edge_attention",
        exps=300000,
    )


def shift(part, axis, step, wrap):
    size = lax.axis_size(axis)
    pairs = [(i, (i + step) % size) for i in range(size) if wrap or 0 <= i + step < size]
    return lax.ppermute(part, axis, pairs)


def key_bias():
    row = jnp.arange(8, dtype=jnp.int32)[:, None]
    key = jnp.arange(128, dtype=jnp.int32)[None, :] // WLON
    north = (row == 0) & (key < RIM_LAT) & (lax.axis_index("lat") == 0)
    south = (row == 1) & (key >= RIM_LAT) & (lax.axis_index("lat") == lax.axis_size("lat") - 1)
    return jnp.where(north | south, F32(-1e30), F32(0.0))


def place_index():
    me = lax.axis_index("lon")
    return jnp.stack([me // 2, me % 2]).astype(jnp.int32)


def merge_dots(place_ref, upper, lower, mine_ref, pair_ref, x_ref, x_pair_ref, y_ref, y_pair_ref, refs):
    half, block = x_ref.shape
    at = [pl.ds(pl.multiple_of((place_ref[1] + k) % 2 * block, block), block) for k in range(2)]
    own, x, y = refs
    for k, ref in enumerate((mine_ref, pair_ref)):
        own(at[k], dot(upper, ref[:half, :]), dot(lower, ref[half:, :]))
    for k, ref in enumerate((x_ref, x_pair_ref)):
        x(at[k], dot(upper, ref[...]))
    for k, ref in enumerate((y_ref, y_pair_ref)):
        y(at[k], dot(lower, ref[...]))


def merge_own_kernel(place_ref, upper_ref, lower_ref, *refs):
    weights, (own_ref, x_ref, y_ref), kept = refs[:6], refs[6:9], refs[9:]
    for ref, to in zip(weights, kept):
        to[...] = ref[...]

    def own(at, a, b):
        own_ref[:, at] = a + b

    def x(at, a):
        x_ref[:, at] = a

    def y(at, b):
        y_ref[:, at] = b

    merge_dots(place_ref, upper_ref[...], lower_ref[...], *weights, (own, x, y))


def merge_other_kernel(place_ref, upper_ref, lower_ref, *refs):
    weights, (to_y_ref, to_x_ref) = refs[:6], refs[6:]
    wide = to_x_ref.shape[1] // 2

    def own(at, a, b):
        to_y_ref[:, at] = a.astype(BF16)
        to_x_ref[:, at] = b.astype(BF16)

    def x(at, a):
        to_y_ref[:, pl.ds(pl.multiple_of(wide + at.start, at.size), at.size)] = a.astype(BF16)

    def y(at, b):
        to_x_ref[:, pl.ds(pl.multiple_of(wide + at.start, at.size), at.size)] = b.astype(BF16)

    merge_dots(place_ref, upper_ref[...], lower_ref[...], *weights, (own, x, y))


def combine_kernel(place_ref, own_ref, x_ref, y_ref, from_y_ref, from_x_ref, out_ref):
    wide = own_ref.shape[1]
    chip = place_ref[0]
    from_x, from_y = from_x_ref[...].astype(F32), from_y_ref[...].astype(F32)
    parts = [
        own_ref[...],
        x_ref[...] + from_x[:, :wide],
        y_ref[...] + from_y[:, :wide],
        from_x[:, wide:] + from_y[:, wide:],
    ]
    for m, part in enumerate(parts):
        out_ref[:, pl.ds(pl.multiple_of((chip ^ m) * wide, wide), wide)] = part.astype(BF16)


def local_call(kernel, out, place, args, flops, name, mib=16):
    vmem = pl.BlockSpec(memory_space=pltpu.VMEM)
    return pl.pallas_call(
        kernel,
        in_specs=[pl.BlockSpec(memory_space=pltpu.SMEM)] + [vmem] * len(args),
        out_specs=[vmem] * len(out),
        out_shape=out,
        compiler_params=params(mib),
        cost_estimate=pl.CostEstimate(flops=flops, bytes_accessed=2**20, transcendentals=0),
        name=name,
    )(place, *args)


def merge_by_squares(upper, lower, merge_weight, halves):
    half = merge_weight.shape[0] // 2
    block = merge_weight.shape[1]
    count = upper.shape[0]
    x = chip_swap(halves[0], 1)
    y = chip_swap(halves[1], 2)
    x_pair, y_pair, _ = lax.optimization_barrier((x, y, upper))
    weights = [merge_weight, core_swap(merge_weight), x, core_swap(x_pair), y, core_swap(y_pair)]
    place = place_index()
    from_y = chip_swap(upper, 2)
    from_x = chip_swap(lower, 1)
    flops = 16 * count * half * block
    wide = jax.ShapeDtypeStruct((count, 2 * block), F32)
    kept = [jax.ShapeDtypeStruct(w.shape, BF16) for w in weights]
    *own, a, b, c, d, e, f = local_call(
        merge_own_kernel, [wide] * 3 + kept, place, [upper, lower] + weights, flops, "merge_own", 28
    )
    weights = [a, b, c, d, e, f]
    pair = jax.ShapeDtypeStruct((count, 4 * block), BF16)
    to_y, to_x = local_call(merge_other_kernel, [pair] * 2, place, [from_y, from_x] + weights, flops, "merge_other")
    back_y, back_x = chip_swap(to_y, 2), chip_swap(to_x, 1)
    out = jax.ShapeDtypeStruct((count, 8 * block), BF16)
    return local_call(combine_kernel, [out], place, [*own, back_y, back_x], 0, "combine")[0]


def ffn_kernel(mine_ref, theirs_ref, up_ref, down_ref, out_mine_ref, low_ref, high_ref, normed_ref, hidden_ref):
    count = mine_ref.shape[0]
    for k, ref in enumerate((mine_ref, theirs_ref)):
        normed_ref[k * count : (k + 1) * count, :] = normalize(ref[...].astype(F32)).astype(BF16)
    hidden = hidden_ref.shape[1]
    step = 256
    for at in range(0, hidden, step):
        raw = dot(normed_ref[...], up_ref[:, at : at + step])
        active = 0.5 * raw * (1.0 + lax.erf(raw * np.float32(np.sqrt(0.5))))
        hidden_ref[:, at : at + step] = active.astype(BF16)
    half = low_ref.shape[1]
    for at in range(0, 2 * half, step):
        out = dot(hidden_ref[...], down_ref[:, at : at + step]).astype(BF16)
        out_mine_ref[:, at : at + step] = out[:count]
        ref = low_ref if at < half else high_ref
        ref[:, at % half : at % half + step] = out[count:]


def feed_forward(mine, theirs, up, down):
    count = mine.shape[0]
    width, hidden = up.shape
    vmem = pl.BlockSpec(memory_space=pltpu.VMEM)
    return pl.pallas_call(
        ffn_kernel,
        in_specs=[vmem] * 4,
        out_specs=[vmem] * 3,
        out_shape=[jax.ShapeDtypeStruct((count, width // n), BF16) for n in (1, 2, 2)],
        scratch_shapes=[pltpu.VMEM((2 * count, width), BF16), pltpu.VMEM((2 * count, hidden), BF16)],
        compiler_params=params(20),
        cost_estimate=pl.CostEstimate(
            flops=8 * count * width * hidden, bytes_accessed=4 * width * hidden, transcendentals=2 * count * hidden
        ),
        name="feed_forward",
    )(mine, theirs, up, down)


def added(mine, low, high):
    return (mine.astype(F32) + jnp.concatenate([low, high], axis=1).astype(F32)).astype(BF16)


def summed(mine, low, high):
    return added(mine, core_swap(low), core_swap(high))


def core_swap(value):
    size = lax.axis_size("lon")
    return lax.ppermute(value, "lon", [(i, i ^ 1) for i in range(size)])


def chip_swap(value, offset):
    size = lax.axis_size("lon")
    return lax.ppermute(value, "lon", [(i, i ^ (2 * offset)) for i in range(size)])


def cross(value, first, second):
    size = lax.axis_size("lon")
    return lax.ppermute(value, "lon", [(i, i ^ (2 * (second if i % 2 else first))) for i in range(size)])


def coarse_by_squares(upper, lower, merge_weight, halves, up, down):
    own = merge_by_squares(upper, lower, merge_weight, halves)
    near = cross(own, 1, 2)
    first = feed_forward(own, core_swap(own), up, down)
    near, *first = lax.optimization_barrier((near, *first))
    far = cross(near, 2, 1)
    near_mine, near_low, near_high = feed_forward(near, core_swap(near), up, down)
    later, near_mine = lax.optimization_barrier((own, near_mine))
    other = cross(later, 2, 1)
    near_low, far = lax.optimization_barrier((core_swap(near_low), far))
    mine, low, high = feed_forward(far, core_swap(far), up, down)
    low, high, other = lax.optimization_barrier((core_swap(low), core_swap(high), other))
    relayed = cross(added(mine, low, high), 2, 1)
    other_back = cross(summed(*feed_forward(other, core_swap(other), up, down)), 2, 1)
    half = low.shape[1]
    near_back = []
    for part, at in ((near_low, 0), (core_swap(near_high), half)):
        columns = slice(at, at + half)
        total = near_mine[:, columns].astype(F32) + part.astype(F32) + relayed[:, columns].astype(F32)
        near_back.append(cross(total.astype(BF16), 1, 2))
    near_back = jnp.concatenate(near_back, axis=1)
    return sum(part.astype(F32) for part in (own, summed(*first), other_back, near_back))


def coarse_by_chips(upper, lower, merge_weight, halves, up, down):
    weight = lax.all_gather(merge_weight, "lon", axis=1, tiled=True)
    patches = jnp.concatenate([upper, lower], axis=1)
    coarse = jnp.dot(patches, weight, preferred_element_type=F32).astype(BF16)
    chips = lax.axis_size("lon") // 2
    arrived = [coarse] + [chip_swap(coarse, m) for m in range(1, chips)]
    total = coarse.astype(F32)
    for m in range(chips):
        part = summed(*feed_forward(arrived[m], core_swap(arrived[m]), up, down))
        total = total + (chip_swap(part, m) if m else part).astype(F32)
    return total


def per_device(tokens, qkv_weight, out_weight, merge_weight, up_weight, down_weight):
    rows, columns, width = tokens.shape
    bands = Bands(rows, columns)
    cells = rows * columns // 4
    sides = rims(tokens)
    *sides, later = lax.optimization_barrier((*sides, merge_weight))
    halves = halves_of(later)
    middle_out, upper, lower = attention(bands, tokens, sides, qkv_weight, out_weight)
    coarse = coarse_by_squares if lax.axis_size("lon") == 8 else coarse_by_chips
    total = coarse(upper, lower, merge_weight, halves, up_weight, down_weight)
    coarse_out = total[:cells].astype(jnp.bfloat16)
    return (middle_out, coarse_out.reshape(rows // 2, columns // 2, -1))


def solution(mesh):
    return jax.shard_map(
        per_device,
        mesh=mesh,
        in_specs=(P("lat", "lon", None), P(), P(), P(None, "lon"), P(None, "lon"), P("lon", None)),
        out_specs=(P("lat", "lon", None), P("lat", "lon", None)),
        check_vma=False,
    )
```

```python
import functools

import jax
import jax.numpy as jnp
import numpy as np
from jax import lax
from jax.experimental import pallas as pl
from jax.experimental.pallas import tpu as pltpu
from jax.sharding import PartitionSpec as P

HEADS = 16
WLAT = 6
WLON = 12
RIM_LAT = WLAT // 2
RIM_LON = WLON // 2
SIDE = 8
GROUP = 4
F32 = jnp.float32
BF16 = jnp.bfloat16


def up16(n):
    return -(-n // 16) * 16


def params(mib=48, **kw):
    return pltpu.CompilerParams(vmem_limit_bytes=mib * 2**20, **kw)


class Bands:
    def __init__(self, rows, columns):
        assert (rows - WLAT) % WLAT == 0 and (columns - WLON) % WLON == 0
        self.rows, self.columns = rows, columns
        inner = (rows - WLAT) // WLAT
        self.height = [RIM_LAT] + [WLAT] * inner + [RIM_LAT]
        self.count = len(self.height)
        self.first = [sum(self.height[:b]) for b in range(self.count)]
        self.widths = [RIM_LON] + [WLON] * ((columns - WLON) // WLON) + [RIM_LON]
        self.own = [h * columns for h in self.height]
        self.own_padded = [up16(n) for n in self.own]
        self.own_at = [sum(self.own_padded[:b]) for b in range(self.count)]
        self.own_total = sum(self.own_padded)
        self.side = [2 * h * SIDE for h in self.height]
        assert all(n % 16 == 0 for n in self.side)
        self.side_at = [sum(self.side[:b]) for b in range(self.count)]
        self.side_total = sum(self.side)
        self.slab = columns + 2 * SIDE
        self.slab_padded = up16(RIM_LAT * self.slab)
        self.window = up16(WLAT * WLON)
        self.counts = [[GROUP * h * w for w in self.widths] for h in self.height]
        self.counts_padded = [[up16(n) for n in row] for row in self.counts]

    def edge(self, b):
        return b in (0, self.count - 1)

    def sources(self, b):
        return self.own_padded[b] + self.side[b] + (self.slab_padded if self.edge(b) else 0)

    def source(self, b, i, j):
        columns, h, first = self.columns, self.height[b], self.first[b]
        at = self.own_padded[b]
        if not 0 <= i < self.rows:
            i = i + RIM_LAT if i < 0 else i - self.rows
            return at + self.side[b] + i * self.slab + j + SIDE
        if 0 <= j < columns:
            return (i - first) * columns + j
        at += (i - first) * SIDE
        return at + (j + SIDE if j < 0 else h * SIDE + j - columns)

    def key_matrix(self, b):
        g = np.zeros((len(self.widths) * self.window, self.sources(b)), np.float32)
        top = self.first[b] - (RIM_LAT if b == 0 else 0)
        for c in range(len(self.widths)):
            for i in range(WLAT):
                for j in range(WLON):
                    at = c * self.window + i * WLON + j
                    g[at, self.source(b, top + i, c * WLON - RIM_LON + j)] = 1
        return g.astype(BF16)

    def query_matrix(self, b):
        total = sum(self.counts_padded[b])
        g = np.zeros((total, self.own_padded[b]), np.float32)
        head = np.zeros((total,), np.int32)
        start = left = 0
        for width, padded in zip(self.widths, self.counts_padded[b]):
            at = start
            for k in range(GROUP):
                for i in range(self.height[b]):
                    for j in range(width):
                        g[at, i * self.columns + left + j] = 1
                        head[at] = k
                        at += 1
            left += width
            start += padded
        return g.astype(BF16), head

    def inner_patches(self):
        rows = range(self.rows // 2)
        inner = [r for r in rows if 2 * r >= RIM_LAT and 2 * r + 1 < self.rows - RIM_LAT]
        return inner, [r for r in rows if r not in inner]

    def patch_matrix(self, patch_rows, place, sources):
        half = self.columns // 2
        padded = up16(len(patch_rows) * half)
        g = np.zeros((4 * padded, sources), np.float32)
        for n, r in enumerate(patch_rows):
            for c in range(half):
                for k in range(4):
                    g[k * padded + n * half + c, place(2 * r + k // 2) + 2 * c + k % 2] = 1
        return g.astype(BF16)

    def inner_patch_matrix(self):
        return self.patch_matrix(
            self.inner_patches()[0],
            lambda i: (i - RIM_LAT) * self.columns,
            (self.rows - 2 * RIM_LAT) * self.columns,
        )

    def edge_patch_matrix(self):
        last = self.rows - RIM_LAT - 1
        return self.patch_matrix(
            self.inner_patches()[1],
            lambda i: (i if i <= RIM_LAT else RIM_LAT + 1 + i - last) * self.columns,
            2 * (RIM_LAT + 1) * self.columns,
        )

    def constants(self, some, block):
        distinct, kinds, consts = [], [], []
        for b in some:
            kind = (self.height[b], b == 0, b == self.count - 1)
            if kind not in distinct:
                distinct.append(kind)
                query, head = self.query_matrix(b)
                mask = head[:, None] == (np.arange(block) // (block // GROUP))[None, :]
                scale = np.float32((block // GROUP) ** -0.5)
                scaled = (query.astype(np.float32) * scale).astype(BF16)
                consts += [self.key_matrix(b), scaled, mask.astype(BF16), np.ascontiguousarray(query.T)]
            kinds.append(4 * distinct.index(kind))
        return kinds, consts


def normalize(values):
    center = values - jnp.mean(values, axis=-1, keepdims=True)
    spread = jnp.mean(center * center, axis=-1, keepdims=True)
    return center * lax.rsqrt(spread + 1e-05)


def dot(a, b, dims=((1,), (0,))):
    return lax.dot_general(a, b, (dims, ((), ())), preferred_element_type=F32)


def flat_normed(ref):
    values = ref[...].astype(F32)
    return normalize(values.reshape(-1, values.shape[-1]))


def project(normed_ref, weight_ref, out_ref):
    step = 256
    for at in range(0, out_ref.shape[1], step):
        out_ref[:, at : at + step] = dot(normed_ref[...], weight_ref[:, at : at + step]).astype(BF16)


def padded_rows(values, total):
    if values.shape[0] == total:
        return values
    return jnp.concatenate([values, jnp.zeros((total - values.shape[0], values.shape[1]), values.dtype)], axis=0)


def rims_kernel(tokens_ref, east_ref, west_ref):
    columns = tokens_ref.shape[1]
    east_ref[...] = tokens_ref[:, columns - SIDE :]
    west_ref[...] = tokens_ref[:, :SIDE]


def rims(tokens):
    rows, _, width = tokens.shape
    vmem = pl.BlockSpec(memory_space=pltpu.VMEM)
    return pl.pallas_call(
        rims_kernel,
        in_specs=[vmem],
        out_specs=[vmem] * 2,
        out_shape=[jax.ShapeDtypeStruct((rows, SIDE, width), BF16)] * 2,
        compiler_params=params(16),
        name="rims",
    )(tokens)


def halves_kernel(weight_ref, upper_ref, lower_ref, sems):
    half = upper_ref.shape[0]
    copies = [
        pltpu.make_async_copy(weight_ref.at[k * half : (k + 1) * half], ref, sems.at[k])
        for k, ref in enumerate((upper_ref, lower_ref))
    ]
    for copy in copies:
        copy.start()
    for copy in copies:
        copy.wait()


def halves_of(weight):
    depth, block = weight.shape
    return pl.pallas_call(
        halves_kernel,
        in_specs=[pl.BlockSpec(memory_space=pl.ANY)],
        out_specs=[pl.BlockSpec(memory_space=pltpu.VMEM)] * 2,
        out_shape=[jax.ShapeDtypeStruct((depth // 2, block), BF16)] * 2,
        scratch_shapes=[pltpu.SemaphoreType.DMA((2,))],
        compiler_params=params(52),
        name="halves",
    )(weight)


def own_kernel(bands, tokens_ref, weight_ref, out_ref, kv_ref, normed_ref, q_ref, sems):
    width = q_ref.shape[1]
    chunk = weight_ref.shape[1] // sems.shape[0]
    places = []
    for n in range(sems.shape[0]):
        at = n * chunk
        places.append((q_ref, at) if at < width else (kv_ref, at - width))
    copies = [
        pltpu.make_async_copy(weight_ref.at[:, pl.ds(n * chunk, chunk)], ref.at[:, pl.ds(at, chunk)], sems.at[n])
        for n, (ref, at) in enumerate(places)
    ]
    for copy in copies:
        copy.start()
    normed = flat_normed(tokens_ref)
    for b in range(bands.count):
        at = bands.first[b] * bands.columns
        part = padded_rows(normed[at : at + bands.own[b]], bands.own_padded[b])
        normed_ref[bands.own_at[b] : bands.own_at[b] + bands.own_padded[b], :] = part.astype(BF16)
    step = 256
    for n, (ref, first) in enumerate(places):
        copies[n].wait()
        for at in range(0, chunk, step):
            part = ref[:, first + at : first + at + step]
            out_ref[:, n * chunk + at : n * chunk + at + step] = dot(normed_ref[...], part).astype(BF16)


def own_projection(bands, tokens, weight):
    width, out = weight.shape
    vmem = pl.BlockSpec(memory_space=pltpu.VMEM)
    return pl.pallas_call(
        functools.partial(own_kernel, bands),
        in_specs=[vmem, pl.BlockSpec(memory_space=pl.ANY)],
        out_specs=[vmem, vmem],
        out_shape=[
            jax.ShapeDtypeStruct((bands.own_total, out), BF16),
            jax.ShapeDtypeStruct((width, out - width), BF16),
        ],
        scratch_shapes=[
            pltpu.VMEM((bands.own_total, width), BF16),
            pltpu.VMEM((width, width), BF16),
            pltpu.SemaphoreType.DMA((3,)),
        ],
        compiler_params=params(42),
        cost_estimate=pl.CostEstimate(
            flops=2 * bands.own_total * width * out, bytes_accessed=2 * width * out, transcendentals=0
        ),
        name="own_projection",
    )(tokens, weight)


def attend(bands, some, kinds, consts, own_ref, outer, bias_ref, put, scratch):
    k_ref, v_ref, q_ref, p_ref, r_ref = scratch
    width = own_ref.shape[1] // 3
    block = width * GROUP // HEADS
    window = WLAT * WLON
    units = [(n, b, g) for n, b in enumerate(some) for g in range(HEADS // GROUP)]
    for u, (n, b, g) in enumerate(units):
        keys, query, mask, _ = consts[kinds[n] : kinds[n] + 4]
        own = slice(bands.own_at[b], bands.own_at[b] + bands.own_padded[b])
        for ref, skip in ((k_ref, 0), (v_ref, width)):
            parts = [own_ref[own, width + skip + g * block : width + skip + (g + 1) * block]]
            for out_ref, at, size in outer(b):
                parts.append(out_ref[at : at + size, skip + g * block : skip + (g + 1) * block])
            ref[u] = dot(keys[...], jnp.concatenate(parts, axis=0)).astype(BF16)
        total = query.shape[0]
        q_ref[u, :total] = dot(query[...], own_ref[own, g * block : (g + 1) * block]).astype(BF16) * mask[...]
    for u, (n, b, g) in enumerate(units):
        at = 0
        for c, count in enumerate(bands.counts_padded[b]):
            scores = dot(
                q_ref[u, at : at + count], k_ref[u, c * bands.window : c * bands.window + window], ((1,), (1,))
            )
            if b == 0:
                scores = scores + bias_ref[0:1, :window]
            if b == bands.count - 1:
                scores = scores + bias_ref[1:2, :window]
            raised = jnp.exp(scores - jnp.max(scores, axis=-1, keepdims=True))
            weights = raised * (1.0 / jnp.sum(raised, axis=-1, keepdims=True))
            p_ref[u, at : at + count, :window] = weights.astype(BF16)
            at += count
    for u, (n, b, g) in enumerate(units):
        mask = consts[kinds[n] + 2]
        at = 0
        for c, count in enumerate(bands.counts_padded[b]):
            mixed = dot(
                p_ref[u, at : at + count, :window], v_ref[u, c * bands.window : c * bands.window + window]
            )
            r_ref[u, at : at + count] = mixed.astype(BF16) * mask[at : at + count]
            at += count
    for u, (n, b, g) in enumerate(units):
        back = consts[kinds[n] + 3]
        put(b, g, dot(back[...], r_ref[u, : back.shape[1]]).astype(BF16))


def attend_scratch(bands, some, block):
    units = len(some) * HEADS // GROUP
    keys = len(bands.widths) * bands.window
    rows = max(sum(bands.counts_padded[b]) for b in some)
    return [
        pltpu.VMEM((units, keys, block), BF16),
        pltpu.VMEM((units, keys, block), BF16),
        pltpu.VMEM((units, rows, block), BF16),
        pltpu.VMEM((units, rows, 128), BF16),
        pltpu.VMEM((units, rows, block), BF16),
    ]


def merge_rows(patch_ref, cells, upper_ref, lower_ref, first):
    width = cells.shape[1]
    padded = patch_ref.shape[0] // 4
    parts = [dot(patch_ref[k * padded : (k + 1) * padded, :], cells) for k in range(4)]
    total = sum(jnp.sum(p, axis=-1, keepdims=True) for p in parts)
    mean = total * (1.0 / (4 * width))
    parts = [p - mean for p in parts]
    spread = sum(jnp.sum(p * p, axis=-1, keepdims=True) for p in parts)
    factor = lax.rsqrt(spread * (1.0 / (4 * width)) + 1e-05)
    for k in range(4):
        ref = (upper_ref, lower_ref)[k // 2]
        ref[first : first + padded, k % 2 * width : (k % 2 + 1) * width] = (parts[k] * factor).astype(BF16)


def middle_kernel(bands, some, kinds, tokens_ref, west_ref, east_ref, own_ref, weight_ref, out_w_ref, patch_ref, *rest):
    consts, rest = rest[:-11], rest[-11:]
    side_ref, middle_ref, upper_ref, lower_ref, normed_ref, attended_ref, *scratch = rest
    rows, columns, width = tokens_ref.shape
    west, east = flat_normed(west_ref), flat_normed(east_ref)
    for b in range(bands.count):
        at, size = bands.first[b] * SIDE, bands.height[b] * SIDE
        part = jnp.concatenate([west[at : at + size], east[at : at + size]], axis=0)
        normed_ref[bands.side_at[b] : bands.side_at[b] + bands.side[b], :] = part.astype(BF16)
    project(normed_ref, weight_ref, side_ref)

    def outer(b):
        return [(side_ref, bands.side_at[b], bands.side[b])]

    def put(b, g, value):
        at = bands.own_at[b] - bands.own_at[1]
        block = value.shape[1]
        attended_ref[at : at + bands.own_padded[b], g * block : (g + 1) * block] = value

    attend(bands, some, kinds, consts, own_ref, outer, None, put, scratch)
    mixed = dot(attended_ref[...], out_w_ref[...])
    middle = tokens_ref[RIM_LAT : rows - RIM_LAT].astype(F32) + mixed.reshape(-1, columns, width)
    middle_ref[...] = middle.astype(BF16)
    merge_rows(patch_ref, middle.reshape(-1, width).astype(BF16), upper_ref, lower_ref, 0)


def edge_kernel(bands, some, kinds, tokens_ref, north_ref, south_ref, bias_ref, own_ref, side_ref, inner_ref, inner_upper_ref, inner_lower_ref, weight_ref, out_w_ref, patch_ref, *rest):
    consts, rest = rest[:-11], rest[-11:]
    middle_ref, upper_ref, lower_ref, normed_ref, slab_ref, attended_ref, *scratch = rest
    rows, columns, width = tokens_ref.shape
    slab = bands.slab_padded
    for k, ref in enumerate((north_ref, south_ref)):
        normed_ref[k * slab : (k + 1) * slab, :] = padded_rows(flat_normed(ref), slab).astype(BF16)
    project(normed_ref, weight_ref, slab_ref)

    def outer(b):
        return [
            (side_ref, bands.side_at[b], bands.side[b]),
            (slab_ref, 0 if b == 0 else slab, slab),
        ]

    def put(b, g, value):
        block = value.shape[1]
        at = 0 if b == 0 else bands.own_padded[0]
        attended_ref[at : at + bands.own_padded[b], g * block : (g + 1) * block] = value

    attend(bands, some, kinds, consts, own_ref, outer, bias_ref, put, scratch)
    mixed = dot(attended_ref[...], out_w_ref[...])
    low = bands.own_padded[0]
    top = tokens_ref[:RIM_LAT].astype(F32) + mixed[: bands.own[0]].reshape(-1, columns, width)
    bottom = tokens_ref[rows - RIM_LAT :].astype(F32) + mixed[low : low + bands.own[-1]].reshape(-1, columns, width)
    middle_ref[:RIM_LAT] = top.astype(BF16)
    middle_ref[RIM_LAT : rows - RIM_LAT] = inner_ref[...]
    middle_ref[rows - RIM_LAT :] = bottom.astype(BF16)
    first, last = inner_ref[0].astype(F32), inner_ref[rows - 2 * RIM_LAT - 1].astype(F32)
    cells = jnp.concatenate([top.reshape(-1, width), first, last, bottom.reshape(-1, width)], axis=0)
    inner_count = inner_upper_ref.shape[0]
    upper_ref[:inner_count, :] = inner_upper_ref[...]
    lower_ref[:inner_count, :] = inner_lower_ref[...]
    merge_rows(patch_ref, cells.astype(BF16), upper_ref, lower_ref, inner_count)


def vmem_call(kernel, out, args, scratch, flops, name, mib=24, exps=0):
    vmem = pl.BlockSpec(memory_space=pltpu.VMEM)
    return pl.pallas_call(
        kernel,
        in_specs=[vmem] * len(args),
        out_specs=[vmem] * len(out),
        out_shape=[jax.ShapeDtypeStruct(shape, BF16) for shape in out],
        scratch_shapes=scratch,
        compiler_params=params(mib),
        cost_estimate=pl.CostEstimate(flops=flops, bytes_accessed=2**20, transcendentals=exps),
        name=name,
    )(*args)


def attention(bands, tokens, sides, qkv_weight, out_weight):
    rows, columns, width = tokens.shape
    block = width * GROUP // HEADS
    west = shift(sides[0], "lon", 1, True)
    east = shift(sides[1], "lon", -1, True)
    own, kv_weight = own_projection(bands, tokens, qkv_weight)

    def slab(part):
        return jnp.concatenate([west[part], tokens[part], east[part]], axis=1)

    north = shift(slab(slice(rows - RIM_LAT, rows)), "lat", 1, False)
    south = shift(slab(slice(0, RIM_LAT)), "lat", -1, False)
    inner = list(range(1, bands.count - 1))
    edges = [0, bands.count - 1]
    kinds, consts = bands.constants(inner, block)
    patch = bands.inner_patch_matrix()
    inner_count = patch.shape[0] // 4
    side, middle, upper, lower = vmem_call(
        functools.partial(middle_kernel, bands, inner, kinds),
        [
            (bands.side_total, 2 * width),
            (rows - 2 * RIM_LAT, columns, width),
            (inner_count, 2 * width),
            (inner_count, 2 * width),
        ],
        [tokens, west, east, own, kv_weight, out_weight, patch] + consts,
        [
            pltpu.VMEM((bands.side_total, width), BF16),
            pltpu.VMEM((bands.own_at[-1] - bands.own_at[1], width), BF16),
        ]
        + attend_scratch(bands, inner, block),
        5 * 10**9,
        "middle_attention",
        exps=500000,
    )
    kinds, consts = bands.constants(edges, block)
    patch = bands.edge_patch_matrix()
    count = inner_count + patch.shape[0] // 4
    return vmem_call(
        functools.partial(edge_kernel, bands, edges, kinds),
        [tokens.shape, (count, 2 * width), (count, 2 * width)],
        [tokens, north, south, key_bias(), own, side, middle, upper, lower, kv_weight, out_weight, patch] + consts,
        [
            pltpu.VMEM((2 * bands.slab_padded, width), BF16),
            pltpu.VMEM((2 * bands.slab_padded, 2 * width), BF16),
            pltpu.VMEM((bands.own_padded[0] + bands.own_padded[-1], width), BF16),
        ]
        + attend_scratch(bands, edges, block),
        6 * 10**9,
        "edge_attention",
        exps=300000,
    )


def shift(part, axis, step, wrap):
    size = lax.axis_size(axis)
    pairs = [(i, (i + step) % size) for i in range(size) if wrap or 0 <= i + step < size]
    return lax.ppermute(part, axis, pairs)


def key_bias():
    row = jnp.arange(8, dtype=jnp.int32)[:, None]
    key = jnp.arange(128, dtype=jnp.int32)[None, :] // WLON
    north = (row == 0) & (key < RIM_LAT) & (lax.axis_index("lat") == 0)
    south = (row == 1) & (key >= RIM_LAT) & (lax.axis_index("lat") == lax.axis_size("lat") - 1)
    return jnp.where(north | south, F32(-1e30), F32(0.0))


def place_index():
    me = lax.axis_index("lon")
    return jnp.stack([me // 2, me % 2]).astype(jnp.int32)


def merge_dots(place_ref, upper, lower, mine_ref, pair_ref, x_ref, x_pair_ref, y_ref, y_pair_ref, refs):
    half, block = x_ref.shape
    at = [pl.ds(pl.multiple_of((place_ref[1] + k) % 2 * block, block), block) for k in range(2)]
    own, x, y = refs
    for k, ref in enumerate((mine_ref, pair_ref)):
        own(at[k], dot(upper, ref[:half, :]), dot(lower, ref[half:, :]))
    for k, ref in enumerate((x_ref, x_pair_ref)):
        x(at[k], dot(upper, ref[...]))
    for k, ref in enumerate((y_ref, y_pair_ref)):
        y(at[k], dot(lower, ref[...]))


def merge_own_kernel(place_ref, upper_ref, lower_ref, *refs):
    weights, (own_ref, x_ref, y_ref), kept = refs[:6], refs[6:9], refs[9:]
    for ref, to in zip(weights, kept):
        to[...] = ref[...]

    def own(at, a, b):
        own_ref[:, at] = a + b

    def x(at, a):
        x_ref[:, at] = a

    def y(at, b):
        y_ref[:, at] = b

    merge_dots(place_ref, upper_ref[...], lower_ref[...], *weights, (own, x, y))


def merge_other_kernel(place_ref, upper_ref, lower_ref, *refs):
    weights, (to_y_ref, to_x_ref) = refs[:6], refs[6:]
    wide = to_x_ref.shape[1] // 2

    def own(at, a, b):
        to_y_ref[:, at] = a.astype(BF16)
        to_x_ref[:, at] = b.astype(BF16)

    def x(at, a):
        to_y_ref[:, pl.ds(pl.multiple_of(wide + at.start, at.size), at.size)] = a.astype(BF16)

    def y(at, b):
        to_x_ref[:, pl.ds(pl.multiple_of(wide + at.start, at.size), at.size)] = b.astype(BF16)

    merge_dots(place_ref, upper_ref[...], lower_ref[...], *weights, (own, x, y))


def combine_kernel(place_ref, own_ref, x_ref, y_ref, from_y_ref, from_x_ref, out_ref):
    wide = own_ref.shape[1]
    chip = place_ref[0]
    from_x, from_y = from_x_ref[...].astype(F32), from_y_ref[...].astype(F32)
    parts = [
        own_ref[...],
        x_ref[...] + from_x[:, :wide],
        y_ref[...] + from_y[:, :wide],
        from_x[:, wide:] + from_y[:, wide:],
    ]
    for m, part in enumerate(parts):
        out_ref[:, pl.ds(pl.multiple_of((chip ^ m) * wide, wide), wide)] = part.astype(BF16)


def local_call(kernel, out, place, args, flops, name, mib=16):
    vmem = pl.BlockSpec(memory_space=pltpu.VMEM)
    return pl.pallas_call(
        kernel,
        in_specs=[pl.BlockSpec(memory_space=pltpu.SMEM)] + [vmem] * len(args),
        out_specs=[vmem] * len(out),
        out_shape=out,
        compiler_params=params(mib),
        cost_estimate=pl.CostEstimate(flops=flops, bytes_accessed=2**20, transcendentals=0),
        name=name,
    )(place, *args)


def merge_by_squares(upper, lower, merge_weight, halves):
    half = merge_weight.shape[0] // 2
    block = merge_weight.shape[1]
    count = upper.shape[0]
    x = chip_swap(halves[0], 1)
    y = chip_swap(halves[1], 2)
    x_pair, y_pair, _ = lax.optimization_barrier((x, y, upper))
    weights = [merge_weight, core_swap(merge_weight), x, core_swap(x_pair), y, core_swap(y_pair)]
    place = place_index()
    from_y = chip_swap(upper, 2)
    from_x = chip_swap(lower, 1)
    flops = 16 * count * half * block
    wide = jax.ShapeDtypeStruct((count, 2 * block), F32)
    kept = [jax.ShapeDtypeStruct(w.shape, BF16) for w in weights]
    *own, a, b, c, d, e, f = local_call(
        merge_own_kernel, [wide] * 3 + kept, place, [upper, lower] + weights, flops, "merge_own", 28
    )
    weights = [a, b, c, d, e, f]
    pair = jax.ShapeDtypeStruct((count, 4 * block), BF16)
    to_y, to_x = local_call(merge_other_kernel, [pair] * 2, place, [from_y, from_x] + weights, flops, "merge_other")
    back_y, back_x = chip_swap(to_y, 2), chip_swap(to_x, 1)
    out = jax.ShapeDtypeStruct((count, 8 * block), BF16)
    return local_call(combine_kernel, [out], place, [*own, back_y, back_x], 0, "combine")[0]


def ffn_kernel(mine_ref, theirs_ref, up_ref, down_ref, out_mine_ref, low_ref, high_ref, normed_ref, hidden_ref):
    count = mine_ref.shape[0]
    for k, ref in enumerate((mine_ref, theirs_ref)):
        normed_ref[k * count : (k + 1) * count, :] = normalize(ref[...].astype(F32)).astype(BF16)
    hidden = hidden_ref.shape[1]
    step = 256
    for at in range(0, hidden, step):
        raw = dot(normed_ref[...], up_ref[:, at : at + step])
        active = 0.5 * raw * (1.0 + lax.erf(raw * np.float32(np.sqrt(0.5))))
        hidden_ref[:, at : at + step] = active.astype(BF16)
    half = low_ref.shape[1]
    for at in range(0, 2 * half, step):
        out = dot(hidden_ref[...], down_ref[:, at : at + step]).astype(BF16)
        out_mine_ref[:, at : at + step] = out[:count]
        ref = low_ref if at < half else high_ref
        ref[:, at % half : at % half + step] = out[count:]


def feed_forward(mine, theirs, up, down):
    count = mine.shape[0]
    width, hidden = up.shape
    vmem = pl.BlockSpec(memory_space=pltpu.VMEM)
    return pl.pallas_call(
        ffn_kernel,
        in_specs=[vmem] * 4,
        out_specs=[vmem] * 3,
        out_shape=[jax.ShapeDtypeStruct((count, width // n), BF16) for n in (1, 2, 2)],
        scratch_shapes=[pltpu.VMEM((2 * count, width), BF16), pltpu.VMEM((2 * count, hidden), BF16)],
        compiler_params=params(20),
        cost_estimate=pl.CostEstimate(
            flops=8 * count * width * hidden, bytes_accessed=4 * width * hidden, transcendentals=2 * count * hidden
        ),
        name="feed_forward",
    )(mine, theirs, up, down)


def added(mine, low, high):
    return (mine.astype(F32) + jnp.concatenate([low, high], axis=1).astype(F32)).astype(BF16)


def summed(mine, low, high):
    return added(mine, core_swap(low), core_swap(high))


def core_swap(value):
    size = lax.axis_size("lon")
    return lax.ppermute(value, "lon", [(i, i ^ 1) for i in range(size)])


def chip_swap(value, offset):
    size = lax.axis_size("lon")
    return lax.ppermute(value, "lon", [(i, i ^ (2 * offset)) for i in range(size)])


def cross(value, first, second):
    size = lax.axis_size("lon")
    return lax.ppermute(value, "lon", [(i, i ^ (2 * (second if i % 2 else first))) for i in range(size)])


def coarse_by_squares(upper, lower, merge_weight, halves, up, down):
    own = merge_by_squares(upper, lower, merge_weight, halves)
    near = cross(own, 1, 2)
    first = feed_forward(own, core_swap(own), up, down)
    near, *first = lax.optimization_barrier((near, *first))
    far = cross(near, 2, 1)
    near_mine, near_low, near_high = feed_forward(near, core_swap(near), up, down)
    later, near_mine = lax.optimization_barrier((own, near_mine))
    other = cross(later, 2, 1)
    near_low, far = lax.optimization_barrier((core_swap(near_low), far))
    mine, low, high = feed_forward(far, core_swap(far), up, down)
    low, other = lax.optimization_barrier((core_swap(low), other))
    relayed = cross(added(mine, low, core_swap(high)), 2, 1)
    other_back = cross(summed(*feed_forward(other, core_swap(other), up, down)), 2, 1)
    half = low.shape[1]
    near_back = []
    for part, at in ((near_low, 0), (core_swap(near_high), half)):
        columns = slice(at, at + half)
        total = near_mine[:, columns].astype(F32) + part.astype(F32) + relayed[:, columns].astype(F32)
        near_back.append(cross(total.astype(BF16), 1, 2))
    near_back = jnp.concatenate(near_back, axis=1)
    return sum(part.astype(F32) for part in (own, summed(*first), other_back, near_back))


def coarse_by_chips(upper, lower, merge_weight, halves, up, down):
    weight = lax.all_gather(merge_weight, "lon", axis=1, tiled=True)
    patches = jnp.concatenate([upper, lower], axis=1)
    coarse = jnp.dot(patches, weight, preferred_element_type=F32).astype(BF16)
    chips = lax.axis_size("lon") // 2
    arrived = [coarse] + [chip_swap(coarse, m) for m in range(1, chips)]
    total = coarse.astype(F32)
    for m in range(chips):
        part = summed(*feed_forward(arrived[m], core_swap(arrived[m]), up, down))
        total = total + (chip_swap(part, m) if m else part).astype(F32)
    return total


def per_device(tokens, qkv_weight, out_weight, merge_weight, up_weight, down_weight):
    rows, columns, width = tokens.shape
    bands = Bands(rows, columns)
    sides = rims(tokens)
    *sides, later = lax.optimization_barrier((*sides, merge_weight))
    halves = halves_of(later)
    middle_out, upper, lower = attention(bands, tokens, sides, qkv_weight, out_weight)
    coarse = coarse_by_squares if lax.axis_size("lon") == 8 else coarse_by_chips
    total = coarse(upper, lower, merge_weight, halves, up_weight, down_weight)
    inner, edge = bands.inner_patches()
    half = columns // 2
    above = half * sum(r < inner[0] for r in edge)
    start = up16(half * len(inner))
    below = start + half * len(edge)
    ordered = [total[start : start + above], total[: half * len(inner)], total[start + above : below]]
    coarse_out = jnp.concatenate(ordered, axis=0).astype(jnp.bfloat16)
    return (middle_out, coarse_out.reshape(rows // 2, columns // 2, -1))


def solution(mesh):
    return jax.shard_map(
        per_device,
        mesh=mesh,
        in_specs=(P("lat", "lon", None), P(), P(), P(None, "lon"), P(None, "lon"), P("lon", None)),
        out_specs=(P("lat", "lon", None), P("lat", "lon", None)),
        check_vma=False,
    )
```

```python
import functools

import jax
import jax.numpy as jnp
import numpy as np
from jax import lax
from jax.experimental import pallas as pl
from jax.experimental.pallas import tpu as pltpu
from jax.sharding import PartitionSpec as P

HEADS = 16
WLAT = 6
WLON = 12
RIM_LAT = WLAT // 2
RIM_LON = WLON // 2
SIDE = 8
GROUP = 4
F32 = jnp.float32
BF16 = jnp.bfloat16


def up16(n):
    return -(-n // 16) * 16


def params(mib=48, **kw):
    return pltpu.CompilerParams(vmem_limit_bytes=mib * 2**20, **kw)


class Bands:
    def __init__(self, rows, columns):
        assert (rows - WLAT) % WLAT == 0 and (columns - WLON) % WLON == 0
        self.rows, self.columns = rows, columns
        inner = (rows - WLAT) // WLAT
        self.height = [RIM_LAT] + [WLAT] * inner + [RIM_LAT]
        self.count = len(self.height)
        self.first = [sum(self.height[:b]) for b in range(self.count)]
        self.widths = [RIM_LON] + [WLON] * ((columns - WLON) // WLON) + [RIM_LON]
        self.own = [h * columns for h in self.height]
        self.own_padded = [up16(n) for n in self.own]
        self.own_at = [sum(self.own_padded[:b]) for b in range(self.count)]
        self.own_total = sum(self.own_padded)
        self.side = [2 * h * SIDE for h in self.height]
        assert all(n % 16 == 0 for n in self.side)
        self.side_at = [sum(self.side[:b]) for b in range(self.count)]
        self.side_total = sum(self.side)
        self.slab = columns + 2 * SIDE
        self.slab_padded = up16(RIM_LAT * self.slab)
        self.window = up16(WLAT * WLON)
        self.counts = [[GROUP * h * w for w in self.widths] for h in self.height]
        self.counts_padded = [[up16(n) for n in row] for row in self.counts]

    def edge(self, b):
        return b in (0, self.count - 1)

    def sources(self, b):
        return self.own_padded[b] + self.side[b] + (self.slab_padded if self.edge(b) else 0)

    def source(self, b, i, j):
        columns, h, first = self.columns, self.height[b], self.first[b]
        at = self.own_padded[b]
        if not 0 <= i < self.rows:
            i = i + RIM_LAT if i < 0 else i - self.rows
            return at + self.side[b] + i * self.slab + j + SIDE
        if 0 <= j < columns:
            return (i - first) * columns + j
        at += (i - first) * SIDE
        return at + (j + SIDE if j < 0 else h * SIDE + j - columns)

    def key_matrix(self, b):
        g = np.zeros((len(self.widths) * self.window, self.sources(b)), np.float32)
        top = self.first[b] - (RIM_LAT if b == 0 else 0)
        for c in range(len(self.widths)):
            for i in range(WLAT):
                for j in range(WLON):
                    at = c * self.window + i * WLON + j
                    g[at, self.source(b, top + i, c * WLON - RIM_LON + j)] = 1
        return g.astype(BF16)

    def query_matrix(self, b):
        total = sum(self.counts_padded[b])
        g = np.zeros((total, self.own_padded[b]), np.float32)
        head = np.zeros((total,), np.int32)
        start = left = 0
        for width, padded in zip(self.widths, self.counts_padded[b]):
            at = start
            for k in range(GROUP):
                for i in range(self.height[b]):
                    for j in range(width):
                        g[at, i * self.columns + left + j] = 1
                        head[at] = k
                        at += 1
            left += width
            start += padded
        return g.astype(BF16), head

    def inner_patches(self):
        rows = range(self.rows // 2)
        inner = [r for r in rows if 2 * r >= RIM_LAT and 2 * r + 1 < self.rows - RIM_LAT]
        return inner, [r for r in rows if r not in inner]

    def patch_matrix(self, patch_rows, place, sources):
        half = self.columns // 2
        padded = up16(len(patch_rows) * half)
        g = np.zeros((4 * padded, sources), np.float32)
        for n, r in enumerate(patch_rows):
            for c in range(half):
                for k in range(4):
                    g[k * padded + n * half + c, place(2 * r + k // 2) + 2 * c + k % 2] = 1
        return g.astype(BF16)

    def inner_patch_matrix(self):
        return self.patch_matrix(
            self.inner_patches()[0],
            lambda i: (i - RIM_LAT) * self.columns,
            (self.rows - 2 * RIM_LAT) * self.columns,
        )

    def edge_patch_matrix(self):
        last = self.rows - RIM_LAT - 1
        return self.patch_matrix(
            self.inner_patches()[1],
            lambda i: (i if i <= RIM_LAT else RIM_LAT + 1 + i - last) * self.columns,
            2 * (RIM_LAT + 1) * self.columns,
        )

    def constants(self, some, block):
        distinct, kinds, consts = [], [], []
        for b in some:
            kind = (self.height[b], b == 0, b == self.count - 1)
            if kind not in distinct:
                distinct.append(kind)
                query, head = self.query_matrix(b)
                mask = head[:, None] == (np.arange(block) // (block // GROUP))[None, :]
                scale = np.float32((block // GROUP) ** -0.5)
                scaled = (query.astype(np.float32) * scale).astype(BF16)
                consts += [self.key_matrix(b), scaled, mask.astype(BF16), np.ascontiguousarray(query.T)]
            kinds.append(4 * distinct.index(kind))
        return kinds, consts


def normalize(values):
    center = values - jnp.mean(values, axis=-1, keepdims=True)
    spread = jnp.mean(center * center, axis=-1, keepdims=True)
    return center * lax.rsqrt(spread + 1e-05)


def dot(a, b, dims=((1,), (0,))):
    return lax.dot_general(a, b, (dims, ((), ())), preferred_element_type=F32)


def flat_normed(ref):
    values = ref[...].astype(F32)
    return normalize(values.reshape(-1, values.shape[-1]))


def project(normed_ref, weight_ref, out_ref):
    step = 256
    for at in range(0, out_ref.shape[1], step):
        out_ref[:, at : at + step] = dot(normed_ref[...], weight_ref[:, at : at + step]).astype(BF16)


def padded_rows(values, total):
    if values.shape[0] == total:
        return values
    return jnp.concatenate([values, jnp.zeros((total - values.shape[0], values.shape[1]), values.dtype)], axis=0)


def rims_kernel(tokens_ref, east_ref, west_ref):
    columns = tokens_ref.shape[1]
    east_ref[...] = tokens_ref[:, columns - SIDE :]
    west_ref[...] = tokens_ref[:, :SIDE]


def rims(tokens):
    rows, _, width = tokens.shape
    vmem = pl.BlockSpec(memory_space=pltpu.VMEM)
    return pl.pallas_call(
        rims_kernel,
        in_specs=[vmem],
        out_specs=[vmem] * 2,
        out_shape=[jax.ShapeDtypeStruct((rows, SIDE, width), BF16)] * 2,
        compiler_params=params(16),
        name="rims",
    )(tokens)


def halves_kernel(weight_ref, upper_ref, lower_ref, sems):
    half = upper_ref.shape[0]
    copies = [
        pltpu.make_async_copy(weight_ref.at[k * half : (k + 1) * half], ref, sems.at[k])
        for k, ref in enumerate((upper_ref, lower_ref))
    ]
    for copy in copies:
        copy.start()
    for copy in copies:
        copy.wait()


def halves_of(weight):
    depth, block = weight.shape
    return pl.pallas_call(
        halves_kernel,
        in_specs=[pl.BlockSpec(memory_space=pl.ANY)],
        out_specs=[pl.BlockSpec(memory_space=pltpu.VMEM)] * 2,
        out_shape=[jax.ShapeDtypeStruct((depth // 2, block), BF16)] * 2,
        scratch_shapes=[pltpu.SemaphoreType.DMA((2,))],
        compiler_params=params(52),
        name="halves",
    )(weight)


def own_kernel(bands, tokens_ref, weight_ref, out_ref, kv_ref, normed_ref, q_ref, sems):
    width = q_ref.shape[1]
    chunk = weight_ref.shape[1] // sems.shape[0]
    places = []
    for n in range(sems.shape[0]):
        at = n * chunk
        places.append((q_ref, at) if at < width else (kv_ref, at - width))
    copies = [
        pltpu.make_async_copy(weight_ref.at[:, pl.ds(n * chunk, chunk)], ref.at[:, pl.ds(at, chunk)], sems.at[n])
        for n, (ref, at) in enumerate(places)
    ]
    for copy in copies:
        copy.start()
    normed = flat_normed(tokens_ref)
    for b in range(bands.count):
        at = bands.first[b] * bands.columns
        part = padded_rows(normed[at : at + bands.own[b]], bands.own_padded[b])
        normed_ref[bands.own_at[b] : bands.own_at[b] + bands.own_padded[b], :] = part.astype(BF16)
    step = 256
    for n, (ref, first) in enumerate(places):
        copies[n].wait()
        for at in range(0, chunk, step):
            part = ref[:, first + at : first + at + step]
            out_ref[:, n * chunk + at : n * chunk + at + step] = dot(normed_ref[...], part).astype(BF16)


def own_projection(bands, tokens, weight):
    width, out = weight.shape
    vmem = pl.BlockSpec(memory_space=pltpu.VMEM)
    return pl.pallas_call(
        functools.partial(own_kernel, bands),
        in_specs=[vmem, pl.BlockSpec(memory_space=pl.ANY)],
        out_specs=[vmem, vmem],
        out_shape=[
            jax.ShapeDtypeStruct((bands.own_total, out), BF16),
            jax.ShapeDtypeStruct((width, out - width), BF16),
        ],
        scratch_shapes=[
            pltpu.VMEM((bands.own_total, width), BF16),
            pltpu.VMEM((width, width), BF16),
            pltpu.SemaphoreType.DMA((3,)),
        ],
        compiler_params=params(42),
        cost_estimate=pl.CostEstimate(
            flops=2 * bands.own_total * width * out, bytes_accessed=2 * width * out, transcendentals=0
        ),
        name="own_projection",
    )(tokens, weight)


def attend(bands, some, kinds, consts, own_ref, outer, bias_ref, put, scratch):
    k_ref, v_ref, q_ref, p_ref, r_ref = scratch
    width = own_ref.shape[1] // 3
    block = width * GROUP // HEADS
    window = WLAT * WLON
    units = [(n, b, g) for n, b in enumerate(some) for g in range(HEADS // GROUP)]
    for u, (n, b, g) in enumerate(units):
        keys, query, mask, _ = consts[kinds[n] : kinds[n] + 4]
        own = slice(bands.own_at[b], bands.own_at[b] + bands.own_padded[b])
        for ref, skip in ((k_ref, 0), (v_ref, width)):
            parts = [own_ref[own, width + skip + g * block : width + skip + (g + 1) * block]]
            for out_ref, at, size in outer(b):
                parts.append(out_ref[at : at + size, skip + g * block : skip + (g + 1) * block])
            ref[u] = dot(keys[...], jnp.concatenate(parts, axis=0)).astype(BF16)
        total = query.shape[0]
        q_ref[u, :total] = dot(query[...], own_ref[own, g * block : (g + 1) * block]).astype(BF16) * mask[...]
    for u, (n, b, g) in enumerate(units):
        at = 0
        for c, count in enumerate(bands.counts_padded[b]):
            scores = dot(
                q_ref[u, at : at + count], k_ref[u, c * bands.window : c * bands.window + window], ((1,), (1,))
            )
            if b == 0:
                scores = scores + bias_ref[0:1, :window]
            if b == bands.count - 1:
                scores = scores + bias_ref[1:2, :window]
            raised = jnp.exp(scores - jnp.max(scores, axis=-1, keepdims=True))
            weights = raised * (1.0 / jnp.sum(raised, axis=-1, keepdims=True))
            p_ref[u, at : at + count, :window] = weights.astype(BF16)
            at += count
    for u, (n, b, g) in enumerate(units):
        mask = consts[kinds[n] + 2]
        at = 0
        for c, count in enumerate(bands.counts_padded[b]):
            mixed = dot(
                p_ref[u, at : at + count, :window], v_ref[u, c * bands.window : c * bands.window + window]
            )
            r_ref[u, at : at + count] = mixed.astype(BF16) * mask[at : at + count]
            at += count
    for u, (n, b, g) in enumerate(units):
        back = consts[kinds[n] + 3]
        put(b, g, dot(back[...], r_ref[u, : back.shape[1]]).astype(BF16))


def attend_scratch(bands, some, block):
    units = len(some) * HEADS // GROUP
    keys = len(bands.widths) * bands.window
    rows = max(sum(bands.counts_padded[b]) for b in some)
    return [
        pltpu.VMEM((units, keys, block), BF16),
        pltpu.VMEM((units, keys, block), BF16),
        pltpu.VMEM((units, rows, block), BF16),
        pltpu.VMEM((units, rows, 128), BF16),
        pltpu.VMEM((units, rows, block), BF16),
    ]


def merge_rows(patch_ref, cells, upper_ref, lower_ref, first):
    width = cells.shape[1]
    padded = patch_ref.shape[0] // 4
    parts = [dot(patch_ref[k * padded : (k + 1) * padded, :], cells) for k in range(4)]
    total = sum(jnp.sum(p, axis=-1, keepdims=True) for p in parts)
    mean = total * (1.0 / (4 * width))
    parts = [p - mean for p in parts]
    spread = sum(jnp.sum(p * p, axis=-1, keepdims=True) for p in parts)
    factor = lax.rsqrt(spread * (1.0 / (4 * width)) + 1e-05)
    for k in range(4):
        ref = (upper_ref, lower_ref)[k // 2]
        ref[first : first + padded, k % 2 * width : (k % 2 + 1) * width] = (parts[k] * factor).astype(BF16)


def middle_kernel(bands, some, kinds, tokens_ref, west_ref, east_ref, own_ref, weight_ref, out_w_ref, patch_ref, *rest):
    consts, rest = rest[:-11], rest[-11:]
    side_ref, middle_ref, upper_ref, lower_ref, normed_ref, attended_ref, *scratch = rest
    rows, columns, width = tokens_ref.shape
    west, east = flat_normed(west_ref), flat_normed(east_ref)
    for b in range(bands.count):
        at, size = bands.first[b] * SIDE, bands.height[b] * SIDE
        part = jnp.concatenate([west[at : at + size], east[at : at + size]], axis=0)
        normed_ref[bands.side_at[b] : bands.side_at[b] + bands.side[b], :] = part.astype(BF16)
    project(normed_ref, weight_ref, side_ref)

    def outer(b):
        return [(side_ref, bands.side_at[b], bands.side[b])]

    def put(b, g, value):
        at = bands.own_at[b] - bands.own_at[1]
        block = value.shape[1]
        attended_ref[at : at + bands.own_padded[b], g * block : (g + 1) * block] = value

    attend(bands, some, kinds, consts, own_ref, outer, None, put, scratch)
    mixed = dot(attended_ref[...], out_w_ref[...])
    middle = tokens_ref[RIM_LAT : rows - RIM_LAT].astype(F32) + mixed.reshape(-1, columns, width)
    middle_ref[...] = middle.astype(BF16)
    merge_rows(patch_ref, middle.reshape(-1, width).astype(BF16), upper_ref, lower_ref, 0)


def edge_kernel(bands, some, kinds, tokens_ref, north_ref, south_ref, bias_ref, own_ref, side_ref, inner_ref, inner_upper_ref, inner_lower_ref, weight_ref, out_w_ref, patch_ref, *rest):
    consts, rest = rest[:-11], rest[-11:]
    middle_ref, upper_ref, lower_ref, normed_ref, slab_ref, attended_ref, *scratch = rest
    rows, columns, width = tokens_ref.shape
    slab = bands.slab_padded
    for k, ref in enumerate((north_ref, south_ref)):
        normed_ref[k * slab : (k + 1) * slab, :] = padded_rows(flat_normed(ref), slab).astype(BF16)
    project(normed_ref, weight_ref, slab_ref)

    def outer(b):
        return [
            (side_ref, bands.side_at[b], bands.side[b]),
            (slab_ref, 0 if b == 0 else slab, slab),
        ]

    def put(b, g, value):
        block = value.shape[1]
        at = 0 if b == 0 else bands.own_padded[0]
        attended_ref[at : at + bands.own_padded[b], g * block : (g + 1) * block] = value

    attend(bands, some, kinds, consts, own_ref, outer, bias_ref, put, scratch)
    mixed = dot(attended_ref[...], out_w_ref[...])
    low = bands.own_padded[0]
    top = tokens_ref[:RIM_LAT].astype(F32) + mixed[: bands.own[0]].reshape(-1, columns, width)
    bottom = tokens_ref[rows - RIM_LAT :].astype(F32) + mixed[low : low + bands.own[-1]].reshape(-1, columns, width)
    middle_ref[:RIM_LAT] = top.astype(BF16)
    middle_ref[RIM_LAT : rows - RIM_LAT] = inner_ref[...]
    middle_ref[rows - RIM_LAT :] = bottom.astype(BF16)
    first, last = inner_ref[0].astype(F32), inner_ref[rows - 2 * RIM_LAT - 1].astype(F32)
    cells = jnp.concatenate([top.reshape(-1, width), first, last, bottom.reshape(-1, width)], axis=0)
    inner_count = inner_upper_ref.shape[0]
    upper_ref[:inner_count, :] = inner_upper_ref[...]
    lower_ref[:inner_count, :] = inner_lower_ref[...]
    merge_rows(patch_ref, cells.astype(BF16), upper_ref, lower_ref, inner_count)


def vmem_call(kernel, out, args, scratch, flops, name, mib=24, exps=0):
    vmem = pl.BlockSpec(memory_space=pltpu.VMEM)
    return pl.pallas_call(
        kernel,
        in_specs=[vmem] * len(args),
        out_specs=[vmem] * len(out),
        out_shape=[jax.ShapeDtypeStruct(shape, BF16) for shape in out],
        scratch_shapes=scratch,
        compiler_params=params(mib),
        cost_estimate=pl.CostEstimate(flops=flops, bytes_accessed=2**20, transcendentals=exps),
        name=name,
    )(*args)


def attention(bands, tokens, sides, qkv_weight, out_weight):
    rows, columns, width = tokens.shape
    block = width * GROUP // HEADS
    west = shift(sides[0], "lon", 1, True)
    east = shift(sides[1], "lon", -1, True)
    own, kv_weight = own_projection(bands, tokens, qkv_weight)

    def slab(part):
        return jnp.concatenate([west[part], tokens[part], east[part]], axis=1)

    north = shift(slab(slice(rows - RIM_LAT, rows)), "lat", 1, False)
    south = shift(slab(slice(0, RIM_LAT)), "lat", -1, False)
    inner = list(range(1, bands.count - 1))
    edges = [0, bands.count - 1]
    kinds, consts = bands.constants(inner, block)
    patch = bands.inner_patch_matrix()
    inner_count = patch.shape[0] // 4
    side, middle, upper, lower = vmem_call(
        functools.partial(middle_kernel, bands, inner, kinds),
        [
            (bands.side_total, 2 * width),
            (rows - 2 * RIM_LAT, columns, width),
            (inner_count, 2 * width),
            (inner_count, 2 * width),
        ],
        [tokens, west, east, own, kv_weight, out_weight, patch] + consts,
        [
            pltpu.VMEM((bands.side_total, width), BF16),
            pltpu.VMEM((bands.own_at[-1] - bands.own_at[1], width), BF16),
        ]
        + attend_scratch(bands, inner, block),
        5 * 10**9,
        "middle_attention",
        exps=500000,
    )
    kinds, consts = bands.constants(edges, block)
    patch = bands.edge_patch_matrix()
    count = inner_count + patch.shape[0] // 4
    return vmem_call(
        functools.partial(edge_kernel, bands, edges, kinds),
        [tokens.shape, (count, 2 * width), (count, 2 * width)],
        [tokens, north, south, key_bias(), own, side, middle, upper, lower, kv_weight, out_weight, patch] + consts,
        [
            pltpu.VMEM((2 * bands.slab_padded, width), BF16),
            pltpu.VMEM((2 * bands.slab_padded, 2 * width), BF16),
            pltpu.VMEM((bands.own_padded[0] + bands.own_padded[-1], width), BF16),
        ]
        + attend_scratch(bands, edges, block),
        6 * 10**9,
        "edge_attention",
        exps=300000,
    )


def shift(part, axis, step, wrap):
    size = lax.axis_size(axis)
    pairs = [(i, (i + step) % size) for i in range(size) if wrap or 0 <= i + step < size]
    return lax.ppermute(part, axis, pairs)


def key_bias():
    row = jnp.arange(8, dtype=jnp.int32)[:, None]
    key = jnp.arange(128, dtype=jnp.int32)[None, :] // WLON
    north = (row == 0) & (key < RIM_LAT) & (lax.axis_index("lat") == 0)
    south = (row == 1) & (key >= RIM_LAT) & (lax.axis_index("lat") == lax.axis_size("lat") - 1)
    return jnp.where(north | south, F32(-1e30), F32(0.0))


def place_index():
    me = lax.axis_index("lon")
    return jnp.stack([me // 2, me % 2]).astype(jnp.int32)


def merge_dots(place_ref, upper, lower, mine_ref, pair_ref, x_ref, x_pair_ref, y_ref, y_pair_ref, refs):
    half, block = x_ref.shape
    at = [pl.ds(pl.multiple_of((place_ref[1] + k) % 2 * block, block), block) for k in range(2)]
    own, x, y = refs
    for k, ref in enumerate((mine_ref, pair_ref)):
        own(at[k], dot(upper, ref[:half, :]), dot(lower, ref[half:, :]))
    for k, ref in enumerate((x_ref, x_pair_ref)):
        x(at[k], dot(upper, ref[...]))
    for k, ref in enumerate((y_ref, y_pair_ref)):
        y(at[k], dot(lower, ref[...]))


def merge_own_kernel(place_ref, upper_ref, lower_ref, *refs):
    weights, (own_ref, x_ref, y_ref), kept = refs[:6], refs[6:9], refs[9:]
    for ref, to in zip(weights, kept):
        to[...] = ref[...]

    def own(at, a, b):
        own_ref[:, at] = a + b

    def x(at, a):
        x_ref[:, at] = a

    def y(at, b):
        y_ref[:, at] = b

    merge_dots(place_ref, upper_ref[...], lower_ref[...], *weights, (own, x, y))


def merge_other_kernel(place_ref, upper_ref, lower_ref, *refs):
    weights, (to_y_ref, to_x_ref) = refs[:6], refs[6:]
    wide = to_x_ref.shape[1] // 2

    def own(at, a, b):
        to_y_ref[:, at] = a.astype(BF16)
        to_x_ref[:, at] = b.astype(BF16)

    def x(at, a):
        to_y_ref[:, pl.ds(pl.multiple_of(wide + at.start, at.size), at.size)] = a.astype(BF16)

    def y(at, b):
        to_x_ref[:, pl.ds(pl.multiple_of(wide + at.start, at.size), at.size)] = b.astype(BF16)

    merge_dots(place_ref, upper_ref[...], lower_ref[...], *weights, (own, x, y))


def combine_kernel(place_ref, own_ref, x_ref, y_ref, from_y_ref, from_x_ref, out_ref):
    wide = own_ref.shape[1]
    chip = place_ref[0]
    from_x, from_y = from_x_ref[...].astype(F32), from_y_ref[...].astype(F32)
    parts = [
        own_ref[...],
        x_ref[...] + from_x[:, :wide],
        y_ref[...] + from_y[:, :wide],
        from_x[:, wide:] + from_y[:, wide:],
    ]
    for m, part in enumerate(parts):
        out_ref[:, pl.ds(pl.multiple_of((chip ^ m) * wide, wide), wide)] = part.astype(BF16)


def local_call(kernel, out, place, args, flops, name, mib=16):
    vmem = pl.BlockSpec(memory_space=pltpu.VMEM)
    return pl.pallas_call(
        kernel,
        in_specs=[pl.BlockSpec(memory_space=pltpu.SMEM)] + [vmem] * len(args),
        out_specs=[vmem] * len(out),
        out_shape=out,
        compiler_params=params(mib),
        cost_estimate=pl.CostEstimate(flops=flops, bytes_accessed=2**20, transcendentals=0),
        name=name,
    )(place, *args)


def merge_by_squares(upper, lower, merge_weight, halves):
    half = merge_weight.shape[0] // 2
    block = merge_weight.shape[1]
    count = upper.shape[0]
    x = chip_swap(halves[0], 1)
    y = chip_swap(halves[1], 2)
    x_pair, y_pair, _ = lax.optimization_barrier((x, y, upper))
    weights = [merge_weight, core_swap(merge_weight), x, core_swap(x_pair), y, core_swap(y_pair)]
    place = place_index()
    from_y = chip_swap(upper, 2)
    from_x = chip_swap(lower, 1)
    flops = 16 * count * half * block
    wide = jax.ShapeDtypeStruct((count, 2 * block), F32)
    kept = [jax.ShapeDtypeStruct(w.shape, BF16) for w in weights]
    *own, a, b, c, d, e, f = local_call(
        merge_own_kernel, [wide] * 3 + kept, place, [upper, lower] + weights, flops, "merge_own", 28
    )
    weights = [a, b, c, d, e, f]
    pair = jax.ShapeDtypeStruct((count, 4 * block), BF16)
    to_y, to_x = local_call(merge_other_kernel, [pair] * 2, place, [from_y, from_x] + weights, flops, "merge_other")
    back_y, back_x = chip_swap(to_y, 2), chip_swap(to_x, 1)
    out = jax.ShapeDtypeStruct((count, 8 * block), BF16)
    return local_call(combine_kernel, [out], place, [*own, back_y, back_x], 0, "combine")[0]


def ffn_kernel(mine_ref, theirs_ref, up_ref, down_ref, out_mine_ref, low_ref, high_ref, normed_ref, hidden_ref):
    count = mine_ref.shape[0]
    for k, ref in enumerate((mine_ref, theirs_ref)):
        normed_ref[k * count : (k + 1) * count, :] = normalize(ref[...].astype(F32)).astype(BF16)
    hidden = hidden_ref.shape[1]
    step = 256
    for at in range(0, hidden, step):
        raw = dot(normed_ref[...], up_ref[:, at : at + step])
        active = 0.5 * raw * (1.0 + lax.erf(raw * np.float32(np.sqrt(0.5))))
        hidden_ref[:, at : at + step] = active.astype(BF16)
    half = low_ref.shape[1]
    for at in range(0, 2 * half, step):
        out = dot(hidden_ref[...], down_ref[:, at : at + step]).astype(BF16)
        out_mine_ref[:, at : at + step] = out[:count]
        ref = low_ref if at < half else high_ref
        ref[:, at % half : at % half + step] = out[count:]


def feed_forward(mine, theirs, up, down):
    count = mine.shape[0]
    width, hidden = up.shape
    vmem = pl.BlockSpec(memory_space=pltpu.VMEM)
    return pl.pallas_call(
        ffn_kernel,
        in_specs=[vmem] * 4,
        out_specs=[vmem] * 3,
        out_shape=[jax.ShapeDtypeStruct((count, width // n), BF16) for n in (1, 2, 2)],
        scratch_shapes=[pltpu.VMEM((2 * count, width), BF16), pltpu.VMEM((2 * count, hidden), BF16)],
        compiler_params=params(20),
        cost_estimate=pl.CostEstimate(
            flops=8 * count * width * hidden, bytes_accessed=4 * width * hidden, transcendentals=2 * count * hidden
        ),
        name="feed_forward",
    )(mine, theirs, up, down)


def added(mine, low, high):
    return (mine.astype(F32) + jnp.concatenate([low, high], axis=1).astype(F32)).astype(BF16)


def summed(mine, low, high):
    return added(mine, core_swap(low), core_swap(high))


def core_swap(value):
    size = lax.axis_size("lon")
    return lax.ppermute(value, "lon", [(i, i ^ 1) for i in range(size)])


def chip_swap(value, offset):
    size = lax.axis_size("lon")
    return lax.ppermute(value, "lon", [(i, i ^ (2 * offset)) for i in range(size)])


def cross(value, first, second):
    size = lax.axis_size("lon")
    return lax.ppermute(value, "lon", [(i, i ^ (2 * (second if i % 2 else first))) for i in range(size)])


def coarse_by_squares(upper, lower, merge_weight, halves, up, down):
    own = merge_by_squares(upper, lower, merge_weight, halves)
    near = cross(own, 1, 2)
    first = feed_forward(own, core_swap(own), up, down)
    near, *first = lax.optimization_barrier((near, *first))
    far = cross(near, 2, 1)
    near_mine, near_low, near_high = feed_forward(near, core_swap(near), up, down)
    later, near_mine = lax.optimization_barrier((own, near_mine))
    other = cross(later, 2, 1)
    near_low, far = lax.optimization_barrier((core_swap(near_low), far))
    mine, low, high = feed_forward(far, core_swap(far), up, down)
    low, other = lax.optimization_barrier((core_swap(low), other))
    far_sum = added(mine, low, core_swap(high))
    pair, far_sum = lax.optimization_barrier((core_swap(other), far_sum))
    relayed = cross(far_sum, 2, 1)
    mine, low, high = feed_forward(other, pair, up, down)
    relayed, low = lax.optimization_barrier((relayed, core_swap(low)))
    other_back = cross(added(mine, low, core_swap(high)), 2, 1)
    half = low.shape[1]
    near_back = []
    for part, at in ((near_low, 0), (core_swap(near_high), half)):
        columns = slice(at, at + half)
        total = near_mine[:, columns].astype(F32) + part.astype(F32) + relayed[:, columns].astype(F32)
        near_back.append(cross(total.astype(BF16), 1, 2))
    near_back = jnp.concatenate(near_back, axis=1)
    return sum(part.astype(F32) for part in (own, summed(*first), other_back, near_back))


def coarse_by_chips(upper, lower, merge_weight, halves, up, down):
    weight = lax.all_gather(merge_weight, "lon", axis=1, tiled=True)
    patches = jnp.concatenate([upper, lower], axis=1)
    coarse = jnp.dot(patches, weight, preferred_element_type=F32).astype(BF16)
    chips = lax.axis_size("lon") // 2
    arrived = [coarse] + [chip_swap(coarse, m) for m in range(1, chips)]
    total = coarse.astype(F32)
    for m in range(chips):
        part = summed(*feed_forward(arrived[m], core_swap(arrived[m]), up, down))
        total = total + (chip_swap(part, m) if m else part).astype(F32)
    return total


def per_device(tokens, qkv_weight, out_weight, merge_weight, up_weight, down_weight):
    rows, columns, width = tokens.shape
    bands = Bands(rows, columns)
    sides = rims(tokens)
    *sides, later = lax.optimization_barrier((*sides, merge_weight))
    halves = halves_of(later)
    middle_out, upper, lower = attention(bands, tokens, sides, qkv_weight, out_weight)
    coarse = coarse_by_squares if lax.axis_size("lon") == 8 else coarse_by_chips
    total = coarse(upper, lower, merge_weight, halves, up_weight, down_weight)
    inner, edge = bands.inner_patches()
    half = columns // 2
    above = half * sum(r < inner[0] for r in edge)
    start = up16(half * len(inner))
    below = start + half * len(edge)
    ordered = [total[start : start + above], total[: half * len(inner)], total[start + above : below]]
    coarse_out = jnp.concatenate(ordered, axis=0).astype(jnp.bfloat16)
    return (middle_out, coarse_out.reshape(rows // 2, columns // 2, -1))


def solution(mesh):
    return jax.shard_map(
        per_device,
        mesh=mesh,
        in_specs=(P("lat", "lon", None), P(), P(), P(None, "lon"), P(None, "lon"), P("lon", None)),
        out_specs=(P("lat", "lon", None), P("lat", "lon", None)),
        check_vma=False,
    )
```

```python
import functools

import jax
import jax.numpy as jnp
import numpy as np
from jax import lax
from jax.experimental import pallas as pl
from jax.experimental.pallas import tpu as pltpu
from jax.sharding import PartitionSpec as P

HEADS = 16
WLAT = 6
WLON = 12
RIM_LAT = WLAT // 2
RIM_LON = WLON // 2
SIDE = 8
GROUP = 4
F32 = jnp.float32
BF16 = jnp.bfloat16


def up16(n):
    return -(-n // 16) * 16


def params(mib=48, **kw):
    return pltpu.CompilerParams(vmem_limit_bytes=mib * 2**20, **kw)


class Bands:
    def __init__(self, rows, columns):
        assert (rows - WLAT) % WLAT == 0 and (columns - WLON) % WLON == 0
        self.rows, self.columns = rows, columns
        inner = (rows - WLAT) // WLAT
        self.height = [RIM_LAT] + [WLAT] * inner + [RIM_LAT]
        self.count = len(self.height)
        self.first = [sum(self.height[:b]) for b in range(self.count)]
        self.widths = [RIM_LON] + [WLON] * ((columns - WLON) // WLON) + [RIM_LON]
        self.own = [h * columns for h in self.height]
        self.own_padded = [up16(n) for n in self.own]
        self.own_at = [sum(self.own_padded[:b]) for b in range(self.count)]
        self.own_total = sum(self.own_padded)
        self.side = [2 * h * SIDE for h in self.height]
        assert all(n % 16 == 0 for n in self.side)
        self.side_at = [sum(self.side[:b]) for b in range(self.count)]
        self.side_total = sum(self.side)
        self.slab = columns + 2 * SIDE
        self.slab_padded = up16(RIM_LAT * self.slab)
        self.window = up16(WLAT * WLON)
        self.counts = [[GROUP * h * w for w in self.widths] for h in self.height]
        self.counts_padded = [[up16(n) for n in row] for row in self.counts]

    def edge(self, b):
        return b in (0, self.count - 1)

    def sources(self, b):
        return self.own_padded[b] + self.side[b] + (self.slab_padded if self.edge(b) else 0)

    def source(self, b, i, j):
        columns, h, first = self.columns, self.height[b], self.first[b]
        at = self.own_padded[b]
        if not 0 <= i < self.rows:
            i = i + RIM_LAT if i < 0 else i - self.rows
            return at + self.side[b] + i * self.slab + j + SIDE
        if 0 <= j < columns:
            return (i - first) * columns + j
        at += (i - first) * SIDE
        return at + (j + SIDE if j < 0 else h * SIDE + j - columns)

    def key_matrix(self, b):
        g = np.zeros((len(self.widths) * self.window, self.sources(b)), np.float32)
        top = self.first[b] - (RIM_LAT if b == 0 else 0)
        for c in range(len(self.widths)):
            for i in range(WLAT):
                for j in range(WLON):
                    at = c * self.window + i * WLON + j
                    g[at, self.source(b, top + i, c * WLON - RIM_LON + j)] = 1
        return g.astype(BF16)

    def query_matrix(self, b):
        total = sum(self.counts_padded[b])
        g = np.zeros((total, self.own_padded[b]), np.float32)
        head = np.zeros((total,), np.int32)
        start = left = 0
        for width, padded in zip(self.widths, self.counts_padded[b]):
            at = start
            for k in range(GROUP):
                for i in range(self.height[b]):
                    for j in range(width):
                        g[at, i * self.columns + left + j] = 1
                        head[at] = k
                        at += 1
            left += width
            start += padded
        return g.astype(BF16), head

    def inner_patches(self):
        rows = range(self.rows // 2)
        inner = [r for r in rows if 2 * r >= RIM_LAT and 2 * r + 1 < self.rows - RIM_LAT]
        return inner, [r for r in rows if r not in inner]

    def patch_matrix(self, patch_rows, place, sources):
        half = self.columns // 2
        padded = up16(len(patch_rows) * half)
        g = np.zeros((4 * padded, sources), np.float32)
        for n, r in enumerate(patch_rows):
            for c in range(half):
                for k in range(4):
                    g[k * padded + n * half + c, place(2 * r + k // 2) + 2 * c + k % 2] = 1
        return g.astype(BF16)

    def inner_patch_matrix(self):
        return self.patch_matrix(
            self.inner_patches()[0],
            lambda i: (i - RIM_LAT) * self.columns,
            (self.rows - 2 * RIM_LAT) * self.columns,
        )

    def edge_patch_matrix(self):
        last = self.rows - RIM_LAT - 1
        return self.patch_matrix(
            self.inner_patches()[1],
            lambda i: (i if i <= RIM_LAT else RIM_LAT + 1 + i - last) * self.columns,
            2 * (RIM_LAT + 1) * self.columns,
        )

    def constants(self, some, block):
        distinct, kinds, consts = [], [], []
        for b in some:
            kind = (self.height[b], b == 0, b == self.count - 1)
            if kind not in distinct:
                distinct.append(kind)
                query, head = self.query_matrix(b)
                mask = head[:, None] == (np.arange(block) // (block // GROUP))[None, :]
                scale = np.float32((block // GROUP) ** -0.5)
                scaled = (query.astype(np.float32) * scale).astype(BF16)
                consts += [self.key_matrix(b), scaled, mask.astype(BF16), np.ascontiguousarray(query.T)]
            kinds.append(4 * distinct.index(kind))
        return kinds, consts


def normalize(values):
    center = values - jnp.mean(values, axis=-1, keepdims=True)
    spread = jnp.mean(center * center, axis=-1, keepdims=True)
    return center * lax.rsqrt(spread + 1e-05)


def dot(a, b, dims=((1,), (0,))):
    return lax.dot_general(a, b, (dims, ((), ())), preferred_element_type=F32)


def flat_normed(ref):
    values = ref[...].astype(F32)
    return normalize(values.reshape(-1, values.shape[-1]))


def project(normed_ref, weight_ref, out_ref):
    step = 256
    for at in range(0, out_ref.shape[1], step):
        out_ref[:, at : at + step] = dot(normed_ref[...], weight_ref[:, at : at + step]).astype(BF16)


def padded_rows(values, total):
    if values.shape[0] == total:
        return values
    return jnp.concatenate([values, jnp.zeros((total - values.shape[0], values.shape[1]), values.dtype)], axis=0)


def rims_kernel(tokens_ref, east_ref, west_ref):
    columns = tokens_ref.shape[1]
    east_ref[...] = tokens_ref[:, columns - SIDE :]
    west_ref[...] = tokens_ref[:, :SIDE]


def rims(tokens):
    rows, _, width = tokens.shape
    vmem = pl.BlockSpec(memory_space=pltpu.VMEM)
    return pl.pallas_call(
        rims_kernel,
        in_specs=[vmem],
        out_specs=[vmem] * 2,
        out_shape=[jax.ShapeDtypeStruct((rows, SIDE, width), BF16)] * 2,
        compiler_params=params(16),
        name="rims",
    )(tokens)


def halves_kernel(weight_ref, upper_ref, lower_ref, sems):
    half = upper_ref.shape[0]
    copies = [
        pltpu.make_async_copy(weight_ref.at[k * half : (k + 1) * half], ref, sems.at[k])
        for k, ref in enumerate((upper_ref, lower_ref))
    ]
    for copy in copies:
        copy.start()
    for copy in copies:
        copy.wait()


def halves_of(weight):
    depth, block = weight.shape
    return pl.pallas_call(
        halves_kernel,
        in_specs=[pl.BlockSpec(memory_space=pl.ANY)],
        out_specs=[pl.BlockSpec(memory_space=pltpu.VMEM)] * 2,
        out_shape=[jax.ShapeDtypeStruct((depth // 2, block), BF16)] * 2,
        scratch_shapes=[pltpu.SemaphoreType.DMA((2,))],
        compiler_params=params(52),
        name="halves",
    )(weight)


def own_kernel(bands, tokens_ref, weight_ref, out_ref, kv_ref, normed_ref, q_ref, sems):
    width = q_ref.shape[1]
    chunk = weight_ref.shape[1] // sems.shape[0]
    places = []
    for n in range(sems.shape[0]):
        at = n * chunk
        places.append((q_ref, at) if at < width else (kv_ref, at - width))
    copies = [
        pltpu.make_async_copy(weight_ref.at[:, pl.ds(n * chunk, chunk)], ref.at[:, pl.ds(at, chunk)], sems.at[n])
        for n, (ref, at) in enumerate(places)
    ]
    for copy in copies:
        copy.start()
    normed = flat_normed(tokens_ref)
    for b in range(bands.count):
        at = bands.first[b] * bands.columns
        part = padded_rows(normed[at : at + bands.own[b]], bands.own_padded[b])
        normed_ref[bands.own_at[b] : bands.own_at[b] + bands.own_padded[b], :] = part.astype(BF16)
    step = 256
    for n, (ref, first) in enumerate(places):
        copies[n].wait()
        for at in range(0, chunk, step):
            part = ref[:, first + at : first + at + step]
            out_ref[:, n * chunk + at : n * chunk + at + step] = dot(normed_ref[...], part).astype(BF16)


def own_projection(bands, tokens, weight):
    width, out = weight.shape
    vmem = pl.BlockSpec(memory_space=pltpu.VMEM)
    return pl.pallas_call(
        functools.partial(own_kernel, bands),
        in_specs=[vmem, pl.BlockSpec(memory_space=pl.ANY)],
        out_specs=[vmem, vmem],
        out_shape=[
            jax.ShapeDtypeStruct((bands.own_total, out), BF16),
            jax.ShapeDtypeStruct((width, out - width), BF16),
        ],
        scratch_shapes=[
            pltpu.VMEM((bands.own_total, width), BF16),
            pltpu.VMEM((width, width), BF16),
            pltpu.SemaphoreType.DMA((3,)),
        ],
        compiler_params=params(42),
        cost_estimate=pl.CostEstimate(
            flops=2 * bands.own_total * width * out, bytes_accessed=2 * width * out, transcendentals=0
        ),
        name="own_projection",
    )(tokens, weight)


def attend(bands, some, kinds, consts, own_ref, outer, bias_ref, put, scratch):
    k_ref, v_ref, q_ref, p_ref, r_ref = scratch
    width = own_ref.shape[1] // 3
    block = width * GROUP // HEADS
    window = WLAT * WLON
    units = [(n, b, g) for n, b in enumerate(some) for g in range(HEADS // GROUP)]
    for u, (n, b, g) in enumerate(units):
        keys, query, mask, _ = consts[kinds[n] : kinds[n] + 4]
        own = slice(bands.own_at[b], bands.own_at[b] + bands.own_padded[b])
        for ref, skip in ((k_ref, 0), (v_ref, width)):
            parts = [own_ref[own, width + skip + g * block : width + skip + (g + 1) * block]]
            for out_ref, at, size in outer(b):
                parts.append(out_ref[at : at + size, skip + g * block : skip + (g + 1) * block])
            ref[u] = dot(keys[...], jnp.concatenate(parts, axis=0)).astype(BF16)
        total = query.shape[0]
        q_ref[u, :total] = dot(query[...], own_ref[own, g * block : (g + 1) * block]).astype(BF16) * mask[...]
    for u, (n, b, g) in enumerate(units):
        at = 0
        for c, count in enumerate(bands.counts_padded[b]):
            scores = dot(
                q_ref[u, at : at + count], k_ref[u, c * bands.window : c * bands.window + window], ((1,), (1,))
            )
            if b == 0:
                scores = scores + bias_ref[0:1, :window]
            if b == bands.count - 1:
                scores = scores + bias_ref[1:2, :window]
            raised = jnp.exp(scores - jnp.max(scores, axis=-1, keepdims=True))
            weights = raised * (1.0 / jnp.sum(raised, axis=-1, keepdims=True))
            p_ref[u, at : at + count, :window] = weights.astype(BF16)
            at += count
    for u, (n, b, g) in enumerate(units):
        mask = consts[kinds[n] + 2]
        at = 0
        for c, count in enumerate(bands.counts_padded[b]):
            mixed = dot(
                p_ref[u, at : at + count, :window], v_ref[u, c * bands.window : c * bands.window + window]
            )
            r_ref[u, at : at + count] = mixed.astype(BF16) * mask[at : at + count]
            at += count
    for u, (n, b, g) in enumerate(units):
        back = consts[kinds[n] + 3]
        put(b, g, dot(back[...], r_ref[u, : back.shape[1]]).astype(BF16))


def attend_scratch(bands, some, block):
    units = len(some) * HEADS // GROUP
    keys = len(bands.widths) * bands.window
    rows = max(sum(bands.counts_padded[b]) for b in some)
    return [
        pltpu.VMEM((units, keys, block), BF16),
        pltpu.VMEM((units, keys, block), BF16),
        pltpu.VMEM((units, rows, block), BF16),
        pltpu.VMEM((units, rows, 128), BF16),
        pltpu.VMEM((units, rows, block), BF16),
    ]


def merge_rows(patch_ref, cells, upper_ref, lower_ref, first):
    width = cells.shape[1]
    padded = patch_ref.shape[0] // 4
    parts = [dot(patch_ref[k * padded : (k + 1) * padded, :], cells) for k in range(4)]
    total = sum(jnp.sum(p, axis=-1, keepdims=True) for p in parts)
    mean = total * (1.0 / (4 * width))
    parts = [p - mean for p in parts]
    spread = sum(jnp.sum(p * p, axis=-1, keepdims=True) for p in parts)
    factor = lax.rsqrt(spread * (1.0 / (4 * width)) + 1e-05)
    for k in range(4):
        ref = (upper_ref, lower_ref)[k // 2]
        ref[first : first + padded, k % 2 * width : (k % 2 + 1) * width] = (parts[k] * factor).astype(BF16)


def middle_kernel(bands, some, kinds, tokens_ref, west_ref, east_ref, own_ref, weight_ref, out_w_ref, patch_ref, *rest):
    consts, rest = rest[:-11], rest[-11:]
    side_ref, middle_ref, upper_ref, lower_ref, normed_ref, attended_ref, *scratch = rest
    rows, columns, width = tokens_ref.shape
    west, east = flat_normed(west_ref), flat_normed(east_ref)
    for b in range(bands.count):
        at, size = bands.first[b] * SIDE, bands.height[b] * SIDE
        part = jnp.concatenate([west[at : at + size], east[at : at + size]], axis=0)
        normed_ref[bands.side_at[b] : bands.side_at[b] + bands.side[b], :] = part.astype(BF16)
    project(normed_ref, weight_ref, side_ref)

    def outer(b):
        return [(side_ref, bands.side_at[b], bands.side[b])]

    def put(b, g, value):
        at = bands.own_at[b] - bands.own_at[1]
        block = value.shape[1]
        attended_ref[at : at + bands.own_padded[b], g * block : (g + 1) * block] = value

    attend(bands, some, kinds, consts, own_ref, outer, None, put, scratch)
    mixed = dot(attended_ref[...], out_w_ref[...])
    middle = tokens_ref[RIM_LAT : rows - RIM_LAT].astype(F32) + mixed.reshape(-1, columns, width)
    middle_ref[...] = middle.astype(BF16)
    merge_rows(patch_ref, middle.reshape(-1, width).astype(BF16), upper_ref, lower_ref, 0)


def edge_kernel(bands, some, kinds, tokens_ref, north_ref, south_ref, bias_ref, own_ref, side_ref, inner_ref, inner_upper_ref, inner_lower_ref, weight_ref, out_w_ref, patch_ref, *rest):
    consts, rest = rest[:-11], rest[-11:]
    middle_ref, upper_ref, lower_ref, normed_ref, slab_ref, attended_ref, *scratch = rest
    rows, columns, width = tokens_ref.shape
    slab = bands.slab_padded
    for k, ref in enumerate((north_ref, south_ref)):
        normed_ref[k * slab : (k + 1) * slab, :] = padded_rows(flat_normed(ref), slab).astype(BF16)
    project(normed_ref, weight_ref, slab_ref)

    def outer(b):
        return [
            (side_ref, bands.side_at[b], bands.side[b]),
            (slab_ref, 0 if b == 0 else slab, slab),
        ]

    def put(b, g, value):
        block = value.shape[1]
        at = 0 if b == 0 else bands.own_padded[0]
        attended_ref[at : at + bands.own_padded[b], g * block : (g + 1) * block] = value

    attend(bands, some, kinds, consts, own_ref, outer, bias_ref, put, scratch)
    mixed = dot(attended_ref[...], out_w_ref[...])
    low = bands.own_padded[0]
    top = tokens_ref[:RIM_LAT].astype(F32) + mixed[: bands.own[0]].reshape(-1, columns, width)
    bottom = tokens_ref[rows - RIM_LAT :].astype(F32) + mixed[low : low + bands.own[-1]].reshape(-1, columns, width)
    middle_ref[:RIM_LAT] = top.astype(BF16)
    middle_ref[RIM_LAT : rows - RIM_LAT] = inner_ref[...]
    middle_ref[rows - RIM_LAT :] = bottom.astype(BF16)
    first, last = inner_ref[0].astype(F32), inner_ref[rows - 2 * RIM_LAT - 1].astype(F32)
    cells = jnp.concatenate([top.reshape(-1, width), first, last, bottom.reshape(-1, width)], axis=0)
    inner_count = inner_upper_ref.shape[0]
    upper_ref[:inner_count, :] = inner_upper_ref[...]
    lower_ref[:inner_count, :] = inner_lower_ref[...]
    merge_rows(patch_ref, cells.astype(BF16), upper_ref, lower_ref, inner_count)


def vmem_call(kernel, out, args, scratch, flops, name, mib=24, exps=0):
    vmem = pl.BlockSpec(memory_space=pltpu.VMEM)
    return pl.pallas_call(
        kernel,
        in_specs=[vmem] * len(args),
        out_specs=[vmem] * len(out),
        out_shape=[jax.ShapeDtypeStruct(shape, BF16) for shape in out],
        scratch_shapes=scratch,
        compiler_params=params(mib),
        cost_estimate=pl.CostEstimate(flops=flops, bytes_accessed=2**20, transcendentals=exps),
        name=name,
    )(*args)


def attention(bands, tokens, sides, qkv_weight, out_weight):
    rows, columns, width = tokens.shape
    block = width * GROUP // HEADS
    west = shift(sides[0], "lon", 1, True)
    east = shift(sides[1], "lon", -1, True)
    own, kv_weight = own_projection(bands, tokens, qkv_weight)

    def slab(part):
        return jnp.concatenate([west[part], tokens[part], east[part]], axis=1)

    north = shift(slab(slice(rows - RIM_LAT, rows)), "lat", 1, False)
    south = shift(slab(slice(0, RIM_LAT)), "lat", -1, False)
    inner = list(range(1, bands.count - 1))
    edges = [0, bands.count - 1]
    kinds, consts = bands.constants(inner, block)
    patch = bands.inner_patch_matrix()
    inner_count = patch.shape[0] // 4
    side, middle, upper, lower = vmem_call(
        functools.partial(middle_kernel, bands, inner, kinds),
        [
            (bands.side_total, 2 * width),
            (rows - 2 * RIM_LAT, columns, width),
            (inner_count, 2 * width),
            (inner_count, 2 * width),
        ],
        [tokens, west, east, own, kv_weight, out_weight, patch] + consts,
        [
            pltpu.VMEM((bands.side_total, width), BF16),
            pltpu.VMEM((bands.own_at[-1] - bands.own_at[1], width), BF16),
        ]
        + attend_scratch(bands, inner, block),
        5 * 10**9,
        "middle_attention",
        exps=500000,
    )
    kinds, consts = bands.constants(edges, block)
    patch = bands.edge_patch_matrix()
    count = inner_count + patch.shape[0] // 4
    return vmem_call(
        functools.partial(edge_kernel, bands, edges, kinds),
        [tokens.shape, (count, 2 * width), (count, 2 * width)],
        [tokens, north, south, key_bias(), own, side, middle, upper, lower, kv_weight, out_weight, patch] + consts,
        [
            pltpu.VMEM((2 * bands.slab_padded, width), BF16),
            pltpu.VMEM((2 * bands.slab_padded, 2 * width), BF16),
            pltpu.VMEM((bands.own_padded[0] + bands.own_padded[-1], width), BF16),
        ]
        + attend_scratch(bands, edges, block),
        6 * 10**9,
        "edge_attention",
        exps=300000,
    )


def shift(part, axis, step, wrap):
    size = lax.axis_size(axis)
    pairs = [(i, (i + step) % size) for i in range(size) if wrap or 0 <= i + step < size]
    return lax.ppermute(part, axis, pairs)


def key_bias():
    row = jnp.arange(8, dtype=jnp.int32)[:, None]
    key = jnp.arange(128, dtype=jnp.int32)[None, :] // WLON
    north = (row == 0) & (key < RIM_LAT) & (lax.axis_index("lat") == 0)
    south = (row == 1) & (key >= RIM_LAT) & (lax.axis_index("lat") == lax.axis_size("lat") - 1)
    return jnp.where(north | south, F32(-1e30), F32(0.0))


def place_index():
    me = lax.axis_index("lon")
    return jnp.stack([me // 2, me % 2]).astype(jnp.int32)


def merge_dots(place_ref, upper, lower, mine_ref, pair_ref, x_ref, x_pair_ref, y_ref, y_pair_ref, refs):
    half, block = x_ref.shape
    at = [pl.ds(pl.multiple_of((place_ref[1] + k) % 2 * block, block), block) for k in range(2)]
    own, x, y = refs
    for k, ref in enumerate((mine_ref, pair_ref)):
        own(at[k], dot(upper, ref[:half, :]), dot(lower, ref[half:, :]))
    for k, ref in enumerate((x_ref, x_pair_ref)):
        x(at[k], dot(upper, ref[...]))
    for k, ref in enumerate((y_ref, y_pair_ref)):
        y(at[k], dot(lower, ref[...]))


def merge_own_kernel(place_ref, upper_ref, lower_ref, *refs):
    weights, (own_ref, x_ref, y_ref), kept = refs[:6], refs[6:9], refs[9:]
    for ref, to in zip(weights, kept):
        to[...] = ref[...]

    def own(at, a, b):
        own_ref[:, at] = a + b

    def x(at, a):
        x_ref[:, at] = a

    def y(at, b):
        y_ref[:, at] = b

    merge_dots(place_ref, upper_ref[...], lower_ref[...], *weights, (own, x, y))


def merge_other_kernel(place_ref, upper_ref, lower_ref, *refs):
    weights, (to_y_ref, to_x_ref) = refs[:6], refs[6:]
    wide = to_x_ref.shape[1] // 2

    def own(at, a, b):
        to_y_ref[:, at] = a.astype(BF16)
        to_x_ref[:, at] = b.astype(BF16)

    def x(at, a):
        to_y_ref[:, pl.ds(pl.multiple_of(wide + at.start, at.size), at.size)] = a.astype(BF16)

    def y(at, b):
        to_x_ref[:, pl.ds(pl.multiple_of(wide + at.start, at.size), at.size)] = b.astype(BF16)

    merge_dots(place_ref, upper_ref[...], lower_ref[...], *weights, (own, x, y))


def combine_kernel(place_ref, own_ref, x_ref, y_ref, from_y_ref, from_x_ref, out_ref):
    wide = own_ref.shape[1]
    chip = place_ref[0]
    from_x, from_y = from_x_ref[...].astype(F32), from_y_ref[...].astype(F32)
    parts = [
        own_ref[...],
        x_ref[...] + from_x[:, :wide],
        y_ref[...] + from_y[:, :wide],
        from_x[:, wide:] + from_y[:, wide:],
    ]
    for m, part in enumerate(parts):
        out_ref[:, pl.ds(pl.multiple_of((chip ^ m) * wide, wide), wide)] = part.astype(BF16)


def local_call(kernel, out, place, args, flops, name, mib=16):
    vmem = pl.BlockSpec(memory_space=pltpu.VMEM)
    return pl.pallas_call(
        kernel,
        in_specs=[pl.BlockSpec(memory_space=pltpu.SMEM)] + [vmem] * len(args),
        out_specs=[vmem] * len(out),
        out_shape=out,
        compiler_params=params(mib),
        cost_estimate=pl.CostEstimate(flops=flops, bytes_accessed=2**20, transcendentals=0),
        name=name,
    )(place, *args)


def merge_by_squares(upper, lower, merge_weight, halves):
    half = merge_weight.shape[0] // 2
    block = merge_weight.shape[1]
    count = upper.shape[0]
    x = chip_swap(halves[0], 1)
    y = chip_swap(halves[1], 2)
    x_pair, y_pair, _ = lax.optimization_barrier((x, y, upper))
    weights = [merge_weight, core_swap(merge_weight), x, core_swap(x_pair), y, core_swap(y_pair)]
    place = place_index()
    from_y = chip_swap(upper, 2)
    from_x = chip_swap(lower, 1)
    flops = 16 * count * half * block
    wide = jax.ShapeDtypeStruct((count, 2 * block), F32)
    kept = [jax.ShapeDtypeStruct(w.shape, BF16) for w in weights]
    *own, a, b, c, d, e, f = local_call(
        merge_own_kernel, [wide] * 3 + kept, place, [upper, lower] + weights, flops, "merge_own", 28
    )
    weights = [a, b, c, d, e, f]
    pair = jax.ShapeDtypeStruct((count, 4 * block), BF16)
    to_y, to_x = local_call(merge_other_kernel, [pair] * 2, place, [from_y, from_x] + weights, flops, "merge_other")
    back_y, back_x = chip_swap(to_y, 2), chip_swap(to_x, 1)
    out = jax.ShapeDtypeStruct((count, 8 * block), BF16)
    return local_call(combine_kernel, [out], place, [*own, back_y, back_x], 0, "combine")[0]


def ffn_kernel(mine_ref, theirs_ref, up_ref, down_ref, out_mine_ref, low_ref, high_ref, normed_ref, hidden_ref):
    count = mine_ref.shape[0]
    for k, ref in enumerate((mine_ref, theirs_ref)):
        normed_ref[k * count : (k + 1) * count, :] = normalize(ref[...].astype(F32)).astype(BF16)
    hidden = hidden_ref.shape[1]
    step = 256
    for at in range(0, hidden, step):
        raw = dot(normed_ref[...], up_ref[:, at : at + step])
        active = 0.5 * raw * (1.0 + lax.erf(raw * np.float32(np.sqrt(0.5))))
        hidden_ref[:, at : at + step] = active.astype(BF16)
    half = low_ref.shape[1]
    for at in range(0, 2 * half, step):
        out = dot(hidden_ref[...], down_ref[:, at : at + step]).astype(BF16)
        out_mine_ref[:, at : at + step] = out[:count]
        ref = low_ref if at < half else high_ref
        ref[:, at % half : at % half + step] = out[count:]


def feed_forward(mine, theirs, up, down):
    count = mine.shape[0]
    width, hidden = up.shape
    vmem = pl.BlockSpec(memory_space=pltpu.VMEM)
    return pl.pallas_call(
        ffn_kernel,
        in_specs=[vmem] * 4,
        out_specs=[vmem] * 3,
        out_shape=[jax.ShapeDtypeStruct((count, width // n), BF16) for n in (1, 2, 2)],
        scratch_shapes=[pltpu.VMEM((2 * count, width), BF16), pltpu.VMEM((2 * count, hidden), BF16)],
        compiler_params=params(20),
        cost_estimate=pl.CostEstimate(
            flops=8 * count * width * hidden, bytes_accessed=4 * width * hidden, transcendentals=2 * count * hidden
        ),
        name="feed_forward",
    )(mine, theirs, up, down)


def added(mine, low, high):
    return (mine.astype(F32) + jnp.concatenate([low, high], axis=1).astype(F32)).astype(BF16)


def summed(mine, low, high):
    return added(mine, core_swap(low), core_swap(high))


def core_swap(value):
    size = lax.axis_size("lon")
    return lax.ppermute(value, "lon", [(i, i ^ 1) for i in range(size)])


def chip_swap(value, offset):
    size = lax.axis_size("lon")
    return lax.ppermute(value, "lon", [(i, i ^ (2 * offset)) for i in range(size)])


def cross(value, first, second):
    size = lax.axis_size("lon")
    return lax.ppermute(value, "lon", [(i, i ^ (2 * (second if i % 2 else first))) for i in range(size)])


def coarse_by_squares(upper, lower, merge_weight, halves, up, down):
    own = merge_by_squares(upper, lower, merge_weight, halves)
    near = cross(own, 1, 2)
    first = feed_forward(own, core_swap(own), up, down)
    near, *first = lax.optimization_barrier((near, *first))
    far = cross(near, 2, 1)
    near_mine, near_low, near_high = feed_forward(near, core_swap(near), up, down)
    later, near_mine = lax.optimization_barrier((own, near_mine))
    other = cross(later, 2, 1)
    near_low, far = lax.optimization_barrier((core_swap(near_low), far))
    mine, low, high = feed_forward(far, core_swap(far), up, down)
    low, other = lax.optimization_barrier((core_swap(low), other))
    far_sum = added(mine, low, core_swap(high))
    pair, far_sum = lax.optimization_barrier((core_swap(other), far_sum))
    relayed = cross(far_sum, 2, 1)
    mine, low, high = feed_forward(other, pair, up, down)
    relayed, low = lax.optimization_barrier((relayed, core_swap(low)))
    other_back = cross(added(mine, low, core_swap(high)), 2, 1)
    half = low.shape[1]
    near_back = []
    for part, at in ((near_low, 0), (core_swap(near_high), half)):
        columns = slice(at, at + half)
        total = near_mine[:, columns].astype(F32) + part.astype(F32) + relayed[:, columns].astype(F32)
        near_back.append(cross(total.astype(BF16), 1, 2))
    return [own, summed(*first), other_back], near_back


def coarse_by_chips(upper, lower, merge_weight, halves, up, down):
    weight = lax.all_gather(merge_weight, "lon", axis=1, tiled=True)
    patches = jnp.concatenate([upper, lower], axis=1)
    coarse = jnp.dot(patches, weight, preferred_element_type=F32).astype(BF16)
    chips = lax.axis_size("lon") // 2
    arrived = [coarse] + [chip_swap(coarse, m) for m in range(1, chips)]
    total = coarse.astype(F32)
    for m in range(chips):
        part = summed(*feed_forward(arrived[m], core_swap(arrived[m]), up, down))
        total = total + (chip_swap(part, m) if m else part).astype(F32)
    return [total.astype(BF16)], []


def finish_kernel(spans, *refs):
    *parts, low_ref, high_ref, out_ref = refs
    total = sum(ref[...].astype(F32) for ref in parts)
    if low_ref is not None:
        total = total + jnp.concatenate([low_ref[...], high_ref[...]], axis=1).astype(F32)
    for r, at in enumerate(spans):
        out_ref[r] = total[at : at + out_ref.shape[1]].astype(BF16)


def finish(bands, whole, halves):
    inner, edge = bands.inner_patches()
    half = bands.columns // 2
    start = up16(half * len(inner))
    place = {r: n * half for n, r in enumerate(inner)} | {r: start + n * half for n, r in enumerate(edge)}
    spans = [place[r] for r in range(bands.rows // 2)]
    vmem = pl.BlockSpec(memory_space=pltpu.VMEM)

    def kernel(*refs):
        finish_kernel(spans, *(refs if halves else (*refs[:-1], None, None, refs[-1])))

    return pl.pallas_call(
        kernel,
        in_specs=[vmem] * (len(whole) + len(halves)),
        out_specs=vmem,
        out_shape=jax.ShapeDtypeStruct((bands.rows // 2, half, whole[0].shape[1]), BF16),
        compiler_params=params(16),
        name="finish",
    )(*whole, *halves)


def per_device(tokens, qkv_weight, out_weight, merge_weight, up_weight, down_weight):
    rows, columns, width = tokens.shape
    bands = Bands(rows, columns)
    sides = rims(tokens)
    *sides, later = lax.optimization_barrier((*sides, merge_weight))
    halves = halves_of(later)
    middle_out, upper, lower = attention(bands, tokens, sides, qkv_weight, out_weight)
    coarse = coarse_by_squares if lax.axis_size("lon") == 8 else coarse_by_chips
    parts = coarse(upper, lower, merge_weight, halves, up_weight, down_weight)
    return (middle_out, finish(bands, *parts))


def solution(mesh):
    return jax.shard_map(
        per_device,
        mesh=mesh,
        in_specs=(P("lat", "lon", None), P(), P(), P(None, "lon"), P(None, "lon"), P("lon", None)),
        out_specs=(P("lat", "lon", None), P("lat", "lon", None)),
        check_vma=False,
    )
```

```python
import functools

import jax
import jax.numpy as jnp
import numpy as np
from jax import lax
from jax.experimental import pallas as pl
from jax.experimental.pallas import tpu as pltpu
from jax.sharding import PartitionSpec as P

HEADS = 16
WLAT = 6
WLON = 12
RIM_LAT = WLAT // 2
RIM_LON = WLON // 2
SIDE = 8
GROUP = 4
F32 = jnp.float32
BF16 = jnp.bfloat16


def up16(n):
    return -(-n // 16) * 16


def params(mib=48, **kw):
    return pltpu.CompilerParams(vmem_limit_bytes=mib * 2**20, **kw)


class Bands:
    def __init__(self, rows, columns):
        assert (rows - WLAT) % WLAT == 0 and (columns - WLON) % WLON == 0
        self.rows, self.columns = rows, columns
        inner = (rows - WLAT) // WLAT
        self.height = [RIM_LAT] + [WLAT] * inner + [RIM_LAT]
        self.count = len(self.height)
        self.first = [sum(self.height[:b]) for b in range(self.count)]
        self.widths = [RIM_LON] + [WLON] * ((columns - WLON) // WLON) + [RIM_LON]
        self.own = [h * columns for h in self.height]
        self.own_padded = [up16(n) for n in self.own]
        self.own_at = [sum(self.own_padded[:b]) for b in range(self.count)]
        self.own_total = sum(self.own_padded)
        self.side = [2 * h * SIDE for h in self.height]
        assert all(n % 16 == 0 for n in self.side)
        self.side_at = [sum(self.side[:b]) for b in range(self.count)]
        self.side_total = sum(self.side)
        self.slab = columns + 2 * SIDE
        self.slab_padded = up16(RIM_LAT * self.slab)
        self.window = up16(WLAT * WLON)
        self.counts = [[GROUP * h * w for w in self.widths] for h in self.height]
        self.counts_padded = [[up16(n) for n in row] for row in self.counts]

    def edge(self, b):
        return b in (0, self.count - 1)

    def sources(self, b):
        return self.own_padded[b] + self.side[b] + (self.slab_padded if self.edge(b) else 0)

    def source(self, b, i, j):
        columns, h, first = self.columns, self.height[b], self.first[b]
        at = self.own_padded[b]
        if not 0 <= i < self.rows:
            i = i + RIM_LAT if i < 0 else i - self.rows
            return at + self.side[b] + i * self.slab + j + SIDE
        if 0 <= j < columns:
            return (i - first) * columns + j
        at += (i - first) * SIDE
        return at + (j + SIDE if j < 0 else h * SIDE + j - columns)

    def key_matrix(self, b):
        g = np.zeros((len(self.widths) * self.window, self.sources(b)), np.float32)
        top = self.first[b] - (RIM_LAT if b == 0 else 0)
        for c in range(len(self.widths)):
            for i in range(WLAT):
                for j in range(WLON):
                    at = c * self.window + i * WLON + j
                    g[at, self.source(b, top + i, c * WLON - RIM_LON + j)] = 1
        return g.astype(BF16)

    def query_matrix(self, b):
        total = sum(self.counts_padded[b])
        g = np.zeros((total, self.own_padded[b]), np.float32)
        head = np.zeros((total,), np.int32)
        start = left = 0
        for width, padded in zip(self.widths, self.counts_padded[b]):
            at = start
            for k in range(GROUP):
                for i in range(self.height[b]):
                    for j in range(width):
                        g[at, i * self.columns + left + j] = 1
                        head[at] = k
                        at += 1
            left += width
            start += padded
        return g.astype(BF16), head

    def inner_patches(self):
        rows = range(self.rows // 2)
        inner = [r for r in rows if 2 * r >= RIM_LAT and 2 * r + 1 < self.rows - RIM_LAT]
        return inner, [r for r in rows if r not in inner]

    def patch_matrix(self, patch_rows, place, sources):
        half = self.columns // 2
        padded = up16(len(patch_rows) * half)
        g = np.zeros((4 * padded, sources), np.float32)
        for n, r in enumerate(patch_rows):
            for c in range(half):
                for k in range(4):
                    g[k * padded + n * half + c, place(2 * r + k // 2) + 2 * c + k % 2] = 1
        return g.astype(BF16)

    def inner_patch_matrix(self):
        return self.patch_matrix(
            self.inner_patches()[0],
            lambda i: (i - RIM_LAT) * self.columns,
            (self.rows - 2 * RIM_LAT) * self.columns,
        )

    def edge_patch_matrix(self):
        last = self.rows - RIM_LAT - 1
        return self.patch_matrix(
            self.inner_patches()[1],
            lambda i: (i if i <= RIM_LAT else RIM_LAT + 1 + i - last) * self.columns,
            2 * (RIM_LAT + 1) * self.columns,
        )

    def constants(self, some, block):
        distinct, kinds, consts = [], [], []
        for b in some:
            kind = (self.height[b], b == 0, b == self.count - 1)
            if kind not in distinct:
                distinct.append(kind)
                query, head = self.query_matrix(b)
                mask = head[:, None] == (np.arange(block) // (block // GROUP))[None, :]
                scale = np.float32((block // GROUP) ** -0.5)
                scaled = (query.astype(np.float32) * scale).astype(BF16)
                consts += [self.key_matrix(b), scaled, mask.astype(BF16), np.ascontiguousarray(query.T)]
            kinds.append(4 * distinct.index(kind))
        return kinds, consts


def normalize(values):
    center = values - jnp.mean(values, axis=-1, keepdims=True)
    spread = jnp.mean(center * center, axis=-1, keepdims=True)
    return center * lax.rsqrt(spread + 1e-05)


def dot(a, b, dims=((1,), (0,))):
    return lax.dot_general(a, b, (dims, ((), ())), preferred_element_type=F32)


def flat_normed(ref):
    values = ref[...].astype(F32)
    return normalize(values.reshape(-1, values.shape[-1]))


def project(normed_ref, weight_ref, out_ref):
    step = 256
    for at in range(0, out_ref.shape[1], step):
        out_ref[:, at : at + step] = dot(normed_ref[...], weight_ref[:, at : at + step]).astype(BF16)


def padded_rows(values, total):
    if values.shape[0] == total:
        return values
    return jnp.concatenate([values, jnp.zeros((total - values.shape[0], values.shape[1]), values.dtype)], axis=0)


def rims_kernel(tokens_ref, east_ref, west_ref):
    columns = tokens_ref.shape[1]
    east_ref[...] = tokens_ref[:, columns - SIDE :]
    west_ref[...] = tokens_ref[:, :SIDE]


def rims(tokens):
    rows, _, width = tokens.shape
    vmem = pl.BlockSpec(memory_space=pltpu.VMEM)
    return pl.pallas_call(
        rims_kernel,
        in_specs=[vmem],
        out_specs=[vmem] * 2,
        out_shape=[jax.ShapeDtypeStruct((rows, SIDE, width), BF16)] * 2,
        compiler_params=params(16),
        name="rims",
    )(tokens)


def halves_kernel(weight_ref, upper_ref, lower_ref):
    half = upper_ref.shape[0]
    upper_ref[...] = weight_ref[:half, :]
    lower_ref[...] = weight_ref[half:, :]


def halves_of(weight):
    depth, block = weight.shape
    vmem = pl.BlockSpec(memory_space=pltpu.VMEM)
    return pl.pallas_call(
        halves_kernel,
        in_specs=[vmem],
        out_specs=[vmem] * 2,
        out_shape=[jax.ShapeDtypeStruct((depth // 2, block), BF16)] * 2,
        compiler_params=params(16),
        name="halves",
    )(weight)


def own_kernel(bands, tokens_ref, weight_ref, out_ref, kv_ref, normed_ref, q_ref, sems):
    width = q_ref.shape[1]
    chunk = weight_ref.shape[1] // sems.shape[0]
    places = []
    for n in range(sems.shape[0]):
        at = n * chunk
        places.append((q_ref, at) if at < width else (kv_ref, at - width))
    copies = [
        pltpu.make_async_copy(weight_ref.at[:, pl.ds(n * chunk, chunk)], ref.at[:, pl.ds(at, chunk)], sems.at[n])
        for n, (ref, at) in enumerate(places)
    ]
    for copy in copies:
        copy.start()
    normed = flat_normed(tokens_ref)
    for b in range(bands.count):
        at = bands.first[b] * bands.columns
        part = padded_rows(normed[at : at + bands.own[b]], bands.own_padded[b])
        normed_ref[bands.own_at[b] : bands.own_at[b] + bands.own_padded[b], :] = part.astype(BF16)
    step = 256
    for n, (ref, first) in enumerate(places):
        copies[n].wait()
        for at in range(0, chunk, step):
            part = ref[:, first + at : first + at + step]
            out_ref[:, n * chunk + at : n * chunk + at + step] = dot(normed_ref[...], part).astype(BF16)


def own_projection(bands, tokens, weight):
    width, out = weight.shape
    vmem = pl.BlockSpec(memory_space=pltpu.VMEM)
    return pl.pallas_call(
        functools.partial(own_kernel, bands),
        in_specs=[vmem, pl.BlockSpec(memory_space=pl.ANY)],
        out_specs=[vmem, vmem],
        out_shape=[
            jax.ShapeDtypeStruct((bands.own_total, out), BF16),
            jax.ShapeDtypeStruct((width, out - width), BF16),
        ],
        scratch_shapes=[
            pltpu.VMEM((bands.own_total, width), BF16),
            pltpu.VMEM((width, width), BF16),
            pltpu.SemaphoreType.DMA((3,)),
        ],
        compiler_params=params(42),
        cost_estimate=pl.CostEstimate(
            flops=2 * bands.own_total * width * out, bytes_accessed=2 * width * out, transcendentals=0
        ),
        name="own_projection",
    )(tokens, weight)


def attend(bands, some, kinds, consts, own_ref, outer, bias_ref, put, scratch):
    k_ref, v_ref, q_ref, p_ref, r_ref = scratch
    width = own_ref.shape[1] // 3
    block = width * GROUP // HEADS
    window = WLAT * WLON
    units = [(n, b, g) for n, b in enumerate(some) for g in range(HEADS // GROUP)]
    for u, (n, b, g) in enumerate(units):
        keys, query, mask, _ = consts[kinds[n] : kinds[n] + 4]
        own = slice(bands.own_at[b], bands.own_at[b] + bands.own_padded[b])
        for ref, skip in ((k_ref, 0), (v_ref, width)):
            parts = [own_ref[own, width + skip + g * block : width + skip + (g + 1) * block]]
            for out_ref, at, size in outer(b):
                parts.append(out_ref[at : at + size, skip + g * block : skip + (g + 1) * block])
            ref[u] = dot(keys[...], jnp.concatenate(parts, axis=0)).astype(BF16)
        total = query.shape[0]
        q_ref[u, :total] = dot(query[...], own_ref[own, g * block : (g + 1) * block]).astype(BF16) * mask[...]
    for u, (n, b, g) in enumerate(units):
        at = 0
        for c, count in enumerate(bands.counts_padded[b]):
            scores = dot(
                q_ref[u, at : at + count], k_ref[u, c * bands.window : c * bands.window + window], ((1,), (1,))
            )
            if b == 0:
                scores = scores + bias_ref[0:1, :window]
            if b == bands.count - 1:
                scores = scores + bias_ref[1:2, :window]
            raised = jnp.exp(scores - jnp.max(scores, axis=-1, keepdims=True))
            weights = raised * (1.0 / jnp.sum(raised, axis=-1, keepdims=True))
            p_ref[u, at : at + count, :window] = weights.astype(BF16)
            at += count
    for u, (n, b, g) in enumerate(units):
        mask = consts[kinds[n] + 2]
        at = 0
        for c, count in enumerate(bands.counts_padded[b]):
            mixed = dot(
                p_ref[u, at : at + count, :window], v_ref[u, c * bands.window : c * bands.window + window]
            )
            r_ref[u, at : at + count] = mixed.astype(BF16) * mask[at : at + count]
            at += count
    for u, (n, b, g) in enumerate(units):
        back = consts[kinds[n] + 3]
        put(b, g, dot(back[...], r_ref[u, : back.shape[1]]).astype(BF16))


def attend_scratch(bands, some, block):
    units = len(some) * HEADS // GROUP
    keys = len(bands.widths) * bands.window
    rows = max(sum(bands.counts_padded[b]) for b in some)
    return [
        pltpu.VMEM((units, keys, block), BF16),
        pltpu.VMEM((units, keys, block), BF16),
        pltpu.VMEM((units, rows, block), BF16),
        pltpu.VMEM((units, rows, 128), BF16),
        pltpu.VMEM((units, rows, block), BF16),
    ]


def merge_rows(patch_ref, cells, upper_ref, lower_ref, first):
    width = cells.shape[1]
    padded = patch_ref.shape[0] // 4
    parts = [dot(patch_ref[k * padded : (k + 1) * padded, :], cells) for k in range(4)]
    total = sum(jnp.sum(p, axis=-1, keepdims=True) for p in parts)
    mean = total * (1.0 / (4 * width))
    parts = [p - mean for p in parts]
    spread = sum(jnp.sum(p * p, axis=-1, keepdims=True) for p in parts)
    factor = lax.rsqrt(spread * (1.0 / (4 * width)) + 1e-05)
    for k in range(4):
        ref = (upper_ref, lower_ref)[k // 2]
        ref[first : first + padded, k % 2 * width : (k % 2 + 1) * width] = (parts[k] * factor).astype(BF16)


def middle_kernel(bands, some, kinds, tokens_ref, west_ref, east_ref, own_ref, weight_ref, out_w_ref, patch_ref, *rest):
    consts, rest = rest[:-11], rest[-11:]
    side_ref, middle_ref, upper_ref, lower_ref, normed_ref, attended_ref, *scratch = rest
    rows, columns, width = tokens_ref.shape
    west, east = flat_normed(west_ref), flat_normed(east_ref)
    for b in range(bands.count):
        at, size = bands.first[b] * SIDE, bands.height[b] * SIDE
        part = jnp.concatenate([west[at : at + size], east[at : at + size]], axis=0)
        normed_ref[bands.side_at[b] : bands.side_at[b] + bands.side[b], :] = part.astype(BF16)
    project(normed_ref, weight_ref, side_ref)

    def outer(b):
        return [(side_ref, bands.side_at[b], bands.side[b])]

    def put(b, g, value):
        at = bands.own_at[b] - bands.own_at[1]
        block = value.shape[1]
        attended_ref[at : at + bands.own_padded[b], g * block : (g + 1) * block] = value

    attend(bands, some, kinds, consts, own_ref, outer, None, put, scratch)
    mixed = dot(attended_ref[...], out_w_ref[...])
    middle = tokens_ref[RIM_LAT : rows - RIM_LAT].astype(F32) + mixed.reshape(-1, columns, width)
    middle_ref[...] = middle.astype(BF16)
    merge_rows(patch_ref, middle.reshape(-1, width).astype(BF16), upper_ref, lower_ref, 0)


def edge_kernel(bands, some, kinds, tokens_ref, north_ref, south_ref, bias_ref, own_ref, side_ref, inner_ref, inner_upper_ref, inner_lower_ref, weight_ref, out_w_ref, patch_ref, *rest):
    consts, rest = rest[:-11], rest[-11:]
    middle_ref, upper_ref, lower_ref, normed_ref, slab_ref, attended_ref, *scratch = rest
    rows, columns, width = tokens_ref.shape
    slab = bands.slab_padded
    for k, ref in enumerate((north_ref, south_ref)):
        normed_ref[k * slab : (k + 1) * slab, :] = padded_rows(flat_normed(ref), slab).astype(BF16)
    project(normed_ref, weight_ref, slab_ref)

    def outer(b):
        return [
            (side_ref, bands.side_at[b], bands.side[b]),
            (slab_ref, 0 if b == 0 else slab, slab),
        ]

    def put(b, g, value):
        block = value.shape[1]
        at = 0 if b == 0 else bands.own_padded[0]
        attended_ref[at : at + bands.own_padded[b], g * block : (g + 1) * block] = value

    attend(bands, some, kinds, consts, own_ref, outer, bias_ref, put, scratch)
    mixed = dot(attended_ref[...], out_w_ref[...])
    low = bands.own_padded[0]
    top = tokens_ref[:RIM_LAT].astype(F32) + mixed[: bands.own[0]].reshape(-1, columns, width)
    bottom = tokens_ref[rows - RIM_LAT :].astype(F32) + mixed[low : low + bands.own[-1]].reshape(-1, columns, width)
    middle_ref[:RIM_LAT] = top.astype(BF16)
    middle_ref[RIM_LAT : rows - RIM_LAT] = inner_ref[...]
    middle_ref[rows - RIM_LAT :] = bottom.astype(BF16)
    first, last = inner_ref[0].astype(F32), inner_ref[rows - 2 * RIM_LAT - 1].astype(F32)
    cells = jnp.concatenate([top.reshape(-1, width), first, last, bottom.reshape(-1, width)], axis=0)
    inner_count = inner_upper_ref.shape[0]
    upper_ref[:inner_count, :] = inner_upper_ref[...]
    lower_ref[:inner_count, :] = inner_lower_ref[...]
    merge_rows(patch_ref, cells.astype(BF16), upper_ref, lower_ref, inner_count)


def vmem_call(kernel, out, args, scratch, flops, name, mib=24, exps=0):
    vmem = pl.BlockSpec(memory_space=pltpu.VMEM)
    return pl.pallas_call(
        kernel,
        in_specs=[vmem] * len(args),
        out_specs=[vmem] * len(out),
        out_shape=[jax.ShapeDtypeStruct(shape, BF16) for shape in out],
        scratch_shapes=scratch,
        compiler_params=params(mib),
        cost_estimate=pl.CostEstimate(flops=flops, bytes_accessed=2**20, transcendentals=exps),
        name=name,
    )(*args)


def attention(bands, tokens, sides, qkv_weight, out_weight):
    rows, columns, width = tokens.shape
    block = width * GROUP // HEADS
    west = shift(sides[0], "lon", 1, True)
    east = shift(sides[1], "lon", -1, True)
    own, kv_weight = own_projection(bands, tokens, qkv_weight)

    def slab(part):
        return jnp.concatenate([west[part], tokens[part], east[part]], axis=1)

    north = shift(slab(slice(rows - RIM_LAT, rows)), "lat", 1, False)
    south = shift(slab(slice(0, RIM_LAT)), "lat", -1, False)
    inner = list(range(1, bands.count - 1))
    edges = [0, bands.count - 1]
    kinds, consts = bands.constants(inner, block)
    patch = bands.inner_patch_matrix()
    inner_count = patch.shape[0] // 4
    side, middle, upper, lower = vmem_call(
        functools.partial(middle_kernel, bands, inner, kinds),
        [
            (bands.side_total, 2 * width),
            (rows - 2 * RIM_LAT, columns, width),
            (inner_count, 2 * width),
            (inner_count, 2 * width),
        ],
        [tokens, west, east, own, kv_weight, out_weight, patch] + consts,
        [
            pltpu.VMEM((bands.side_total, width), BF16),
            pltpu.VMEM((bands.own_at[-1] - bands.own_at[1], width), BF16),
        ]
        + attend_scratch(bands, inner, block),
        5 * 10**9,
        "middle_attention",
        exps=500000,
    )
    kinds, consts = bands.constants(edges, block)
    patch = bands.edge_patch_matrix()
    count = inner_count + patch.shape[0] // 4
    return vmem_call(
        functools.partial(edge_kernel, bands, edges, kinds),
        [tokens.shape, (count, 2 * width), (count, 2 * width)],
        [tokens, north, south, key_bias(), own, side, middle, upper, lower, kv_weight, out_weight, patch] + consts,
        [
            pltpu.VMEM((2 * bands.slab_padded, width), BF16),
            pltpu.VMEM((2 * bands.slab_padded, 2 * width), BF16),
            pltpu.VMEM((bands.own_padded[0] + bands.own_padded[-1], width), BF16),
        ]
        + attend_scratch(bands, edges, block),
        6 * 10**9,
        "edge_attention",
        exps=300000,
    )


def shift(part, axis, step, wrap):
    size = lax.axis_size(axis)
    pairs = [(i, (i + step) % size) for i in range(size) if wrap or 0 <= i + step < size]
    return lax.ppermute(part, axis, pairs)


def key_bias():
    row = jnp.arange(8, dtype=jnp.int32)[:, None]
    key = jnp.arange(128, dtype=jnp.int32)[None, :] // WLON
    north = (row == 0) & (key < RIM_LAT) & (lax.axis_index("lat") == 0)
    south = (row == 1) & (key >= RIM_LAT) & (lax.axis_index("lat") == lax.axis_size("lat") - 1)
    return jnp.where(north | south, F32(-1e30), F32(0.0))


def place_index():
    me = lax.axis_index("lon")
    return jnp.stack([me // 2, me % 2]).astype(jnp.int32)


def merge_dots(place_ref, upper, lower, mine_ref, pair_ref, x_ref, x_pair_ref, y_ref, y_pair_ref, refs):
    half, block = x_ref.shape
    at = [pl.ds(pl.multiple_of((place_ref[1] + k) % 2 * block, block), block) for k in range(2)]
    own, x, y = refs
    for k, ref in enumerate((mine_ref, pair_ref)):
        own(at[k], dot(upper, ref[:half, :]), dot(lower, ref[half:, :]))
    for k, ref in enumerate((x_ref, x_pair_ref)):
        x(at[k], dot(upper, ref[...]))
    for k, ref in enumerate((y_ref, y_pair_ref)):
        y(at[k], dot(lower, ref[...]))


def merge_own_kernel(place_ref, upper_ref, lower_ref, *refs):
    weights, (own_ref, x_ref, y_ref), kept = refs[:6], refs[6:9], refs[9:]
    for ref, to in zip(weights, kept):
        to[...] = ref[...]

    def own(at, a, b):
        own_ref[:, at] = a + b

    def x(at, a):
        x_ref[:, at] = a

    def y(at, b):
        y_ref[:, at] = b

    merge_dots(place_ref, upper_ref[...], lower_ref[...], *weights, (own, x, y))


def merge_other_kernel(place_ref, upper_ref, lower_ref, *refs):
    weights, (to_y_ref, to_x_ref) = refs[:6], refs[6:]
    wide = to_x_ref.shape[1] // 2

    def own(at, a, b):
        to_y_ref[:, at] = a.astype(BF16)
        to_x_ref[:, at] = b.astype(BF16)

    def x(at, a):
        to_y_ref[:, pl.ds(pl.multiple_of(wide + at.start, at.size), at.size)] = a.astype(BF16)

    def y(at, b):
        to_x_ref[:, pl.ds(pl.multiple_of(wide + at.start, at.size), at.size)] = b.astype(BF16)

    merge_dots(place_ref, upper_ref[...], lower_ref[...], *weights, (own, x, y))


def combine_kernel(place_ref, own_ref, x_ref, y_ref, from_y_ref, from_x_ref, out_ref):
    wide = own_ref.shape[1]
    chip = place_ref[0]
    from_x, from_y = from_x_ref[...].astype(F32), from_y_ref[...].astype(F32)
    parts = [
        own_ref[...],
        x_ref[...] + from_x[:, :wide],
        y_ref[...] + from_y[:, :wide],
        from_x[:, wide:] + from_y[:, wide:],
    ]
    for m, part in enumerate(parts):
        out_ref[:, pl.ds(pl.multiple_of((chip ^ m) * wide, wide), wide)] = part.astype(BF16)


def local_call(kernel, out, place, args, flops, name, mib=16):
    vmem = pl.BlockSpec(memory_space=pltpu.VMEM)
    return pl.pallas_call(
        kernel,
        in_specs=[pl.BlockSpec(memory_space=pltpu.SMEM)] + [vmem] * len(args),
        out_specs=[vmem] * len(out),
        out_shape=out,
        compiler_params=params(mib),
        cost_estimate=pl.CostEstimate(flops=flops, bytes_accessed=2**20, transcendentals=0),
        name=name,
    )(place, *args)


def merge_by_squares(upper, lower, merge_weight, halves):
    half = merge_weight.shape[0] // 2
    block = merge_weight.shape[1]
    count = upper.shape[0]
    x = chip_swap(halves[0], 1)
    y = chip_swap(halves[1], 2)
    x_pair, y_pair, _ = lax.optimization_barrier((x, y, upper))
    weights = [merge_weight, core_swap(merge_weight), x, core_swap(x_pair), y, core_swap(y_pair)]
    place = place_index()
    from_y = chip_swap(upper, 2)
    from_x = chip_swap(lower, 1)
    flops = 16 * count * half * block
    wide = jax.ShapeDtypeStruct((count, 2 * block), F32)
    kept = [jax.ShapeDtypeStruct(w.shape, BF16) for w in weights]
    *own, a, b, c, d, e, f = local_call(
        merge_own_kernel, [wide] * 3 + kept, place, [upper, lower] + weights, flops, "merge_own", 28
    )
    weights = [a, b, c, d, e, f]
    pair = jax.ShapeDtypeStruct((count, 4 * block), BF16)
    to_y, to_x = local_call(merge_other_kernel, [pair] * 2, place, [from_y, from_x] + weights, flops, "merge_other")
    back_y, back_x = chip_swap(to_y, 2), chip_swap(to_x, 1)
    out = jax.ShapeDtypeStruct((count, 8 * block), BF16)
    return local_call(combine_kernel, [out], place, [*own, back_y, back_x], 0, "combine")[0]


def ffn_kernel(mine_ref, theirs_ref, up_ref, down_ref, out_mine_ref, low_ref, high_ref, normed_ref, hidden_ref):
    count = mine_ref.shape[0]
    for k, ref in enumerate((mine_ref, theirs_ref)):
        normed_ref[k * count : (k + 1) * count, :] = normalize(ref[...].astype(F32)).astype(BF16)
    hidden = hidden_ref.shape[1]
    step = 256
    for at in range(0, hidden, step):
        raw = dot(normed_ref[...], up_ref[:, at : at + step])
        active = 0.5 * raw * (1.0 + lax.erf(raw * np.float32(np.sqrt(0.5))))
        hidden_ref[:, at : at + step] = active.astype(BF16)
    half = low_ref.shape[1]
    for at in range(0, 2 * half, step):
        out = dot(hidden_ref[...], down_ref[:, at : at + step]).astype(BF16)
        out_mine_ref[:, at : at + step] = out[:count]
        ref = low_ref if at < half else high_ref
        ref[:, at % half : at % half + step] = out[count:]


def feed_forward(mine, theirs, up, down):
    count = mine.shape[0]
    width, hidden = up.shape
    vmem = pl.BlockSpec(memory_space=pltpu.VMEM)
    return pl.pallas_call(
        ffn_kernel,
        in_specs=[vmem] * 4,
        out_specs=[vmem] * 3,
        out_shape=[jax.ShapeDtypeStruct((count, width // n), BF16) for n in (1, 2, 2)],
        scratch_shapes=[pltpu.VMEM((2 * count, width), BF16), pltpu.VMEM((2 * count, hidden), BF16)],
        compiler_params=params(20),
        cost_estimate=pl.CostEstimate(
            flops=8 * count * width * hidden, bytes_accessed=4 * width * hidden, transcendentals=2 * count * hidden
        ),
        name="feed_forward",
    )(mine, theirs, up, down)


def added(mine, low, high):
    return (mine.astype(F32) + jnp.concatenate([low, high], axis=1).astype(F32)).astype(BF16)


def summed(mine, low, high):
    return added(mine, core_swap(low), core_swap(high))


def core_swap(value):
    size = lax.axis_size("lon")
    return lax.ppermute(value, "lon", [(i, i ^ 1) for i in range(size)])


def chip_swap(value, offset):
    size = lax.axis_size("lon")
    return lax.ppermute(value, "lon", [(i, i ^ (2 * offset)) for i in range(size)])


def cross(value, first, second):
    size = lax.axis_size("lon")
    return lax.ppermute(value, "lon", [(i, i ^ (2 * (second if i % 2 else first))) for i in range(size)])


def coarse_by_squares(upper, lower, merge_weight, halves, up, down):
    own = merge_by_squares(upper, lower, merge_weight, halves)
    near = cross(own, 1, 2)
    first = feed_forward(own, core_swap(own), up, down)
    near, *first = lax.optimization_barrier((near, *first))
    far = cross(near, 2, 1)
    near_mine, near_low, near_high = feed_forward(near, core_swap(near), up, down)
    later, near_mine = lax.optimization_barrier((own, near_mine))
    other = cross(later, 2, 1)
    near_low, far = lax.optimization_barrier((core_swap(near_low), far))
    mine, low, high = feed_forward(far, core_swap(far), up, down)
    low, other = lax.optimization_barrier((core_swap(low), other))
    far_sum = added(mine, low, core_swap(high))
    pair, far_sum = lax.optimization_barrier((core_swap(other), far_sum))
    relayed = cross(far_sum, 2, 1)
    mine, low, high = feed_forward(other, pair, up, down)
    relayed, low = lax.optimization_barrier((relayed, core_swap(low)))
    other_back = cross(added(mine, low, core_swap(high)), 2, 1)
    half = low.shape[1]
    near_back = []
    for part, at in ((near_low, 0), (core_swap(near_high), half)):
        columns = slice(at, at + half)
        total = near_mine[:, columns].astype(F32) + part.astype(F32) + relayed[:, columns].astype(F32)
        near_back.append(cross(total.astype(BF16), 1, 2))
    return [own, summed(*first), other_back], near_back


def coarse_by_chips(upper, lower, merge_weight, halves, up, down):
    weight = lax.all_gather(merge_weight, "lon", axis=1, tiled=True)
    patches = jnp.concatenate([upper, lower], axis=1)
    coarse = jnp.dot(patches, weight, preferred_element_type=F32).astype(BF16)
    chips = lax.axis_size("lon") // 2
    arrived = [coarse] + [chip_swap(coarse, m) for m in range(1, chips)]
    total = coarse.astype(F32)
    for m in range(chips):
        part = summed(*feed_forward(arrived[m], core_swap(arrived[m]), up, down))
        total = total + (chip_swap(part, m) if m else part).astype(F32)
    return [total.astype(BF16)], []


def finish_kernel(spans, *refs):
    *parts, low_ref, high_ref, out_ref = refs
    total = sum(ref[...].astype(F32) for ref in parts)
    if low_ref is not None:
        total = total + jnp.concatenate([low_ref[...], high_ref[...]], axis=1).astype(F32)
    for r, at in enumerate(spans):
        out_ref[r] = total[at : at + out_ref.shape[1]].astype(BF16)


def finish(bands, whole, halves):
    inner, edge = bands.inner_patches()
    half = bands.columns // 2
    start = up16(half * len(inner))
    place = {r: n * half for n, r in enumerate(inner)} | {r: start + n * half for n, r in enumerate(edge)}
    spans = [place[r] for r in range(bands.rows // 2)]
    vmem = pl.BlockSpec(memory_space=pltpu.VMEM)

    def kernel(*refs):
        finish_kernel(spans, *(refs if halves else (*refs[:-1], None, None, refs[-1])))

    return pl.pallas_call(
        kernel,
        in_specs=[vmem] * (len(whole) + len(halves)),
        out_specs=vmem,
        out_shape=jax.ShapeDtypeStruct((bands.rows // 2, half, whole[0].shape[1]), BF16),
        compiler_params=params(16),
        name="finish",
    )(*whole, *halves)


def per_device(tokens, qkv_weight, out_weight, merge_weight, up_weight, down_weight):
    rows, columns, width = tokens.shape
    bands = Bands(rows, columns)
    sides = rims(tokens)
    *sides, later = lax.optimization_barrier((*sides, merge_weight))
    halves = halves_of(later)
    middle_out, upper, lower = attention(bands, tokens, sides, qkv_weight, out_weight)
    coarse = coarse_by_squares if lax.axis_size("lon") == 8 else coarse_by_chips
    parts = coarse(upper, lower, merge_weight, halves, up_weight, down_weight)
    return (middle_out, finish(bands, *parts))


def solution(mesh):
    return jax.shard_map(
        per_device,
        mesh=mesh,
        in_specs=(P("lat", "lon", None), P(), P(), P(None, "lon"), P(None, "lon"), P("lon", None)),
        out_specs=(P("lat", "lon", None), P("lat", "lon", None)),
        check_vma=False,
    )
```

```python
import functools

import jax
import jax.numpy as jnp
import numpy as np
from jax import lax
from jax.experimental import pallas as pl
from jax.experimental.pallas import tpu as pltpu
from jax.sharding import PartitionSpec as P

HEADS = 16
WLAT = 6
WLON = 12
RIM_LAT = WLAT // 2
RIM_LON = WLON // 2
SIDE = 8
GROUP = 4
F32 = jnp.float32
BF16 = jnp.bfloat16


def up16(n):
    return -(-n // 16) * 16


def params(mib=48, **kw):
    return pltpu.CompilerParams(vmem_limit_bytes=mib * 2**20, **kw)


class Bands:
    def __init__(self, rows, columns):
        assert (rows - WLAT) % WLAT == 0 and (columns - WLON) % WLON == 0
        self.rows, self.columns = rows, columns
        inner = (rows - WLAT) // WLAT
        self.height = [RIM_LAT] + [WLAT] * inner + [RIM_LAT]
        self.count = len(self.height)
        self.first = [sum(self.height[:b]) for b in range(self.count)]
        self.widths = [RIM_LON] + [WLON] * ((columns - WLON) // WLON) + [RIM_LON]
        self.own = [h * columns for h in self.height]
        self.own_padded = [up16(n) for n in self.own]
        self.own_at = [sum(self.own_padded[:b]) for b in range(self.count)]
        self.own_total = sum(self.own_padded)
        self.side = [2 * h * SIDE for h in self.height]
        assert all(n % 16 == 0 for n in self.side)
        self.side_at = [sum(self.side[:b]) for b in range(self.count)]
        self.side_total = sum(self.side)
        self.slab = columns + 2 * SIDE
        self.slab_padded = up16(RIM_LAT * self.slab)
        self.window = up16(WLAT * WLON)
        self.counts = [[GROUP * h * w for w in self.widths] for h in self.height]
        self.counts_padded = [[up16(n) for n in row] for row in self.counts]

    def edge(self, b):
        return b in (0, self.count - 1)

    def sources(self, b):
        return self.own_padded[b] + self.side[b] + (self.slab_padded if self.edge(b) else 0)

    def source(self, b, i, j):
        columns, h, first = self.columns, self.height[b], self.first[b]
        at = self.own_padded[b]
        if not 0 <= i < self.rows:
            i = i + RIM_LAT if i < 0 else i - self.rows
            return at + self.side[b] + i * self.slab + j + SIDE
        if 0 <= j < columns:
            return (i - first) * columns + j
        at += (i - first) * SIDE
        return at + (j + SIDE if j < 0 else h * SIDE + j - columns)

    def key_matrix(self, b):
        g = np.zeros((len(self.widths) * self.window, self.sources(b)), np.float32)
        top = self.first[b] - (RIM_LAT if b == 0 else 0)
        for c in range(len(self.widths)):
            for i in range(WLAT):
                for j in range(WLON):
                    at = c * self.window + i * WLON + j
                    g[at, self.source(b, top + i, c * WLON - RIM_LON + j)] = 1
        return g.astype(BF16)

    def query_matrix(self, b):
        total = sum(self.counts_padded[b])
        g = np.zeros((total, self.own_padded[b]), np.float32)
        head = np.zeros((total,), np.int32)
        start = left = 0
        for width, padded in zip(self.widths, self.counts_padded[b]):
            at = start
            for k in range(GROUP):
                for i in range(self.height[b]):
                    for j in range(width):
                        g[at, i * self.columns + left + j] = 1
                        head[at] = k
                        at += 1
            left += width
            start += padded
        return g.astype(BF16), head

    def inner_patches(self):
        rows = range(self.rows // 2)
        inner = [r for r in rows if 2 * r >= RIM_LAT and 2 * r + 1 < self.rows - RIM_LAT]
        return inner, [r for r in rows if r not in inner]

    def patch_matrix(self, patch_rows, place, sources):
        half = self.columns // 2
        padded = up16(len(patch_rows) * half)
        g = np.zeros((4 * padded, sources), np.float32)
        for n, r in enumerate(patch_rows):
            for c in range(half):
                for k in range(4):
                    g[k * padded + n * half + c, place(2 * r + k // 2) + 2 * c + k % 2] = 1
        return g.astype(BF16)

    def inner_patch_matrix(self):
        return self.patch_matrix(
            self.inner_patches()[0],
            lambda i: (i - RIM_LAT) * self.columns,
            (self.rows - 2 * RIM_LAT) * self.columns,
        )

    def edge_patch_matrix(self):
        last = self.rows - RIM_LAT - 1
        return self.patch_matrix(
            self.inner_patches()[1],
            lambda i: (i if i <= RIM_LAT else RIM_LAT + 1 + i - last) * self.columns,
            2 * (RIM_LAT + 1) * self.columns,
        )

    def constants(self, some, block):
        distinct, kinds, consts = [], [], []
        for b in some:
            kind = (self.height[b], b == 0, b == self.count - 1)
            if kind not in distinct:
                distinct.append(kind)
                query, head = self.query_matrix(b)
                mask = head[:, None] == (np.arange(block) // (block // GROUP))[None, :]
                scale = np.float32((block // GROUP) ** -0.5)
                scaled = (query.astype(np.float32) * scale).astype(BF16)
                consts += [self.key_matrix(b), scaled, mask.astype(BF16), np.ascontiguousarray(query.T)]
            kinds.append(4 * distinct.index(kind))
        return kinds, consts


def normalize(values):
    center = values - jnp.mean(values, axis=-1, keepdims=True)
    spread = jnp.mean(center * center, axis=-1, keepdims=True)
    return center * lax.rsqrt(spread + 1e-05)


def dot(a, b, dims=((1,), (0,))):
    return lax.dot_general(a, b, (dims, ((), ())), preferred_element_type=F32)


def flat_normed(ref):
    values = ref[...].astype(F32)
    return normalize(values.reshape(-1, values.shape[-1]))


def project(normed_ref, weight_ref, out_ref):
    step = 256
    for at in range(0, out_ref.shape[1], step):
        out_ref[:, at : at + step] = dot(normed_ref[...], weight_ref[:, at : at + step]).astype(BF16)


def padded_rows(values, total):
    if values.shape[0] == total:
        return values
    return jnp.concatenate([values, jnp.zeros((total - values.shape[0], values.shape[1]), values.dtype)], axis=0)


def rims_kernel(tokens_ref, east_ref, west_ref):
    columns = tokens_ref.shape[1]
    east_ref[...] = tokens_ref[:, columns - SIDE :]
    west_ref[...] = tokens_ref[:, :SIDE]


def rims(tokens):
    rows, _, width = tokens.shape
    vmem = pl.BlockSpec(memory_space=pltpu.VMEM)
    return pl.pallas_call(
        rims_kernel,
        in_specs=[vmem],
        out_specs=[vmem] * 2,
        out_shape=[jax.ShapeDtypeStruct((rows, SIDE, width), BF16)] * 2,
        compiler_params=params(16),
        name="rims",
    )(tokens)


def halves_kernel(weight_ref, upper_ref, lower_ref, sems):
    half = upper_ref.shape[0]
    copies = [
        pltpu.make_async_copy(weight_ref.at[k * half : (k + 1) * half], ref, sems.at[k])
        for k, ref in enumerate((upper_ref, lower_ref))
    ]
    for copy in copies:
        copy.start()
    for copy in copies:
        copy.wait()


def halves_of(weight):
    depth, block = weight.shape
    return pl.pallas_call(
        halves_kernel,
        in_specs=[pl.BlockSpec(memory_space=pl.ANY)],
        out_specs=[pl.BlockSpec(memory_space=pltpu.VMEM)] * 2,
        out_shape=[jax.ShapeDtypeStruct((depth // 2, block), BF16)] * 2,
        scratch_shapes=[pltpu.SemaphoreType.DMA((2,))],
        compiler_params=params(52),
        name="halves",
    )(weight)


def own_kernel(bands, tokens_ref, weight_ref, out_ref, kv_ref, normed_ref, q_ref, sems):
    width = q_ref.shape[1]
    chunk = weight_ref.shape[1] // sems.shape[0]
    places = []
    for n in range(sems.shape[0]):
        at = n * chunk
        places.append((q_ref, at) if at < width else (kv_ref, at - width))
    copies = [
        pltpu.make_async_copy(weight_ref.at[:, pl.ds(n * chunk, chunk)], ref.at[:, pl.ds(at, chunk)], sems.at[n])
        for n, (ref, at) in enumerate(places)
    ]
    for copy in copies:
        copy.start()
    normed = flat_normed(tokens_ref)
    for b in range(bands.count):
        at = bands.first[b] * bands.columns
        part = padded_rows(normed[at : at + bands.own[b]], bands.own_padded[b])
        normed_ref[bands.own_at[b] : bands.own_at[b] + bands.own_padded[b], :] = part.astype(BF16)
    step = 256
    for n, (ref, first) in enumerate(places):
        copies[n].wait()
        for at in range(0, chunk, step):
            part = ref[:, first + at : first + at + step]
            out_ref[:, n * chunk + at : n * chunk + at + step] = dot(normed_ref[...], part).astype(BF16)


def own_projection(bands, tokens, weight):
    width, out = weight.shape
    vmem = pl.BlockSpec(memory_space=pltpu.VMEM)
    return pl.pallas_call(
        functools.partial(own_kernel, bands),
        in_specs=[vmem, pl.BlockSpec(memory_space=pl.ANY)],
        out_specs=[vmem, vmem],
        out_shape=[
            jax.ShapeDtypeStruct((bands.own_total, out), BF16),
            jax.ShapeDtypeStruct((width, out - width), BF16),
        ],
        scratch_shapes=[
            pltpu.VMEM((bands.own_total, width), BF16),
            pltpu.VMEM((width, width), BF16),
            pltpu.SemaphoreType.DMA((3,)),
        ],
        compiler_params=params(42),
        cost_estimate=pl.CostEstimate(
            flops=2 * bands.own_total * width * out, bytes_accessed=2 * width * out, transcendentals=0
        ),
        name="own_projection",
    )(tokens, weight)


def attend(bands, some, kinds, consts, own_ref, outer, bias_ref, put, scratch):
    k_ref, v_ref, q_ref, p_ref, r_ref = scratch
    width = own_ref.shape[1] // 3
    block = width * GROUP // HEADS
    window = WLAT * WLON
    units = [(n, b, g) for n, b in enumerate(some) for g in range(HEADS // GROUP)]
    for u, (n, b, g) in enumerate(units):
        keys, query, mask, _ = consts[kinds[n] : kinds[n] + 4]
        own = slice(bands.own_at[b], bands.own_at[b] + bands.own_padded[b])
        for ref, skip in ((k_ref, 0), (v_ref, width)):
            parts = [own_ref[own, width + skip + g * block : width + skip + (g + 1) * block]]
            for out_ref, at, size in outer(b):
                parts.append(out_ref[at : at + size, skip + g * block : skip + (g + 1) * block])
            ref[u] = dot(keys[...], jnp.concatenate(parts, axis=0)).astype(BF16)
        total = query.shape[0]
        q_ref[u, :total] = dot(query[...], own_ref[own, g * block : (g + 1) * block]).astype(BF16) * mask[...]
    for u, (n, b, g) in enumerate(units):
        at = 0
        for c, count in enumerate(bands.counts_padded[b]):
            scores = dot(
                q_ref[u, at : at + count], k_ref[u, c * bands.window : c * bands.window + window], ((1,), (1,))
            )
            if b == 0:
                scores = scores + bias_ref[0:1, :window]
            if b == bands.count - 1:
                scores = scores + bias_ref[1:2, :window]
            raised = jnp.exp(scores - jnp.max(scores, axis=-1, keepdims=True))
            weights = raised * (1.0 / jnp.sum(raised, axis=-1, keepdims=True))
            p_ref[u, at : at + count, :window] = weights.astype(BF16)
            at += count
    for u, (n, b, g) in enumerate(units):
        mask = consts[kinds[n] + 2]
        at = 0
        for c, count in enumerate(bands.counts_padded[b]):
            mixed = dot(
                p_ref[u, at : at + count, :window], v_ref[u, c * bands.window : c * bands.window + window]
            )
            r_ref[u, at : at + count] = mixed.astype(BF16) * mask[at : at + count]
            at += count
    for u, (n, b, g) in enumerate(units):
        back = consts[kinds[n] + 3]
        put(b, g, dot(back[...], r_ref[u, : back.shape[1]]).astype(BF16))


def attend_scratch(bands, some, block):
    units = len(some) * HEADS // GROUP
    keys = len(bands.widths) * bands.window
    rows = max(sum(bands.counts_padded[b]) for b in some)
    return [
        pltpu.VMEM((units, keys, block), BF16),
        pltpu.VMEM((units, keys, block), BF16),
        pltpu.VMEM((units, rows, block), BF16),
        pltpu.VMEM((units, rows, 128), BF16),
        pltpu.VMEM((units, rows, block), BF16),
    ]


def merge_rows(patch_ref, cells, upper_ref, lower_ref):
    width = cells.shape[1]
    padded = patch_ref.shape[0] // 4
    parts = [dot(patch_ref[k * padded : (k + 1) * padded, :], cells) for k in range(4)]
    total = sum(jnp.sum(p, axis=-1, keepdims=True) for p in parts)
    mean = total * (1.0 / (4 * width))
    parts = [p - mean for p in parts]
    spread = sum(jnp.sum(p * p, axis=-1, keepdims=True) for p in parts)
    factor = lax.rsqrt(spread * (1.0 / (4 * width)) + 1e-05)
    for k in range(4):
        ref = (upper_ref, lower_ref)[k // 2]
        ref[:, k % 2 * width : (k % 2 + 1) * width] = (parts[k] * factor).astype(BF16)


def middle_kernel(bands, some, kinds, tokens_ref, west_ref, east_ref, own_ref, weight_ref, out_w_ref, patch_ref, *rest):
    consts, rest = rest[:-11], rest[-11:]
    side_ref, middle_ref, upper_ref, lower_ref, normed_ref, attended_ref, *scratch = rest
    rows, columns, width = tokens_ref.shape
    west, east = flat_normed(west_ref), flat_normed(east_ref)
    for b in range(bands.count):
        at, size = bands.first[b] * SIDE, bands.height[b] * SIDE
        part = jnp.concatenate([west[at : at + size], east[at : at + size]], axis=0)
        normed_ref[bands.side_at[b] : bands.side_at[b] + bands.side[b], :] = part.astype(BF16)
    project(normed_ref, weight_ref, side_ref)

    def outer(b):
        return [(side_ref, bands.side_at[b], bands.side[b])]

    def put(b, g, value):
        at = bands.own_at[b] - bands.own_at[1]
        block = value.shape[1]
        attended_ref[at : at + bands.own_padded[b], g * block : (g + 1) * block] = value

    attend(bands, some, kinds, consts, own_ref, outer, None, put, scratch)
    mixed = dot(attended_ref[...], out_w_ref[...])
    middle = tokens_ref[RIM_LAT : rows - RIM_LAT].astype(F32) + mixed.reshape(-1, columns, width)
    middle_ref[...] = middle.astype(BF16)
    merge_rows(patch_ref, middle.reshape(-1, width).astype(BF16), upper_ref, lower_ref)


def edge_kernel(bands, some, kinds, tokens_ref, north_ref, south_ref, bias_ref, own_ref, side_ref, inner_ref, weight_ref, out_w_ref, patch_ref, *rest):
    consts, rest = rest[:-11], rest[-11:]
    middle_ref, upper_ref, lower_ref, normed_ref, slab_ref, attended_ref, *scratch = rest
    rows, columns, width = tokens_ref.shape
    slab = bands.slab_padded
    for k, ref in enumerate((north_ref, south_ref)):
        normed_ref[k * slab : (k + 1) * slab, :] = padded_rows(flat_normed(ref), slab).astype(BF16)
    project(normed_ref, weight_ref, slab_ref)

    def outer(b):
        return [
            (side_ref, bands.side_at[b], bands.side[b]),
            (slab_ref, 0 if b == 0 else slab, slab),
        ]

    def put(b, g, value):
        block = value.shape[1]
        at = 0 if b == 0 else bands.own_padded[0]
        attended_ref[at : at + bands.own_padded[b], g * block : (g + 1) * block] = value

    attend(bands, some, kinds, consts, own_ref, outer, bias_ref, put, scratch)
    mixed = dot(attended_ref[...], out_w_ref[...])
    low = bands.own_padded[0]
    top = tokens_ref[:RIM_LAT].astype(F32) + mixed[: bands.own[0]].reshape(-1, columns, width)
    bottom = tokens_ref[rows - RIM_LAT :].astype(F32) + mixed[low : low + bands.own[-1]].reshape(-1, columns, width)
    middle_ref[:RIM_LAT] = top.astype(BF16)
    middle_ref[RIM_LAT : rows - RIM_LAT] = inner_ref[...]
    middle_ref[rows - RIM_LAT :] = bottom.astype(BF16)
    first, last = inner_ref[0].astype(F32), inner_ref[rows - 2 * RIM_LAT - 1].astype(F32)
    cells = jnp.concatenate([top.reshape(-1, width), first, last, bottom.reshape(-1, width)], axis=0)
    merge_rows(patch_ref, cells.astype(BF16), upper_ref, lower_ref)


def vmem_call(kernel, out, args, scratch, flops, name, mib=24, exps=0):
    vmem = pl.BlockSpec(memory_space=pltpu.VMEM)
    return pl.pallas_call(
        kernel,
        in_specs=[vmem] * len(args),
        out_specs=[vmem] * len(out),
        out_shape=[jax.ShapeDtypeStruct(shape, BF16) for shape in out],
        scratch_shapes=scratch,
        compiler_params=params(mib),
        cost_estimate=pl.CostEstimate(flops=flops, bytes_accessed=2**20, transcendentals=exps),
        name=name,
    )(*args)


def attention(bands, tokens, sides, qkv_weight, out_weight):
    rows, columns, width = tokens.shape
    block = width * GROUP // HEADS
    west = shift(sides[0], "lon", 1, True)
    east = shift(sides[1], "lon", -1, True)
    own, kv_weight = own_projection(bands, tokens, qkv_weight)

    def slab(part):
        return jnp.concatenate([west[part], tokens[part], east[part]], axis=1)

    north = shift(slab(slice(rows - RIM_LAT, rows)), "lat", 1, False)
    south = shift(slab(slice(0, RIM_LAT)), "lat", -1, False)
    inner = list(range(1, bands.count - 1))
    edges = [0, bands.count - 1]
    kinds, consts = bands.constants(inner, block)
    patch = bands.inner_patch_matrix()
    inner_count = patch.shape[0] // 4
    side, middle, upper, lower = vmem_call(
        functools.partial(middle_kernel, bands, inner, kinds),
        [
            (bands.side_total, 2 * width),
            (rows - 2 * RIM_LAT, columns, width),
            (inner_count, 2 * width),
            (inner_count, 2 * width),
        ],
        [tokens, west, east, own, kv_weight, out_weight, patch] + consts,
        [
            pltpu.VMEM((bands.side_total, width), BF16),
            pltpu.VMEM((bands.own_at[-1] - bands.own_at[1], width), BF16),
        ]
        + attend_scratch(bands, inner, block),
        5 * 10**9,
        "middle_attention",
        exps=500000,
    )
    kinds, consts = bands.constants(edges, block)
    patch = bands.edge_patch_matrix()
    count = patch.shape[0] // 4
    middle_out, upper_edge, lower_edge = vmem_call(
        functools.partial(edge_kernel, bands, edges, kinds),
        [tokens.shape, (count, 2 * width), (count, 2 * width)],
        [tokens, north, south, key_bias(), own, side, middle, kv_weight, out_weight, patch] + consts,
        [
            pltpu.VMEM((2 * bands.slab_padded, width), BF16),
            pltpu.VMEM((2 * bands.slab_padded, 2 * width), BF16),
            pltpu.VMEM((bands.own_padded[0] + bands.own_padded[-1], width), BF16),
        ]
        + attend_scratch(bands, edges, block),
        6 * 10**9,
        "edge_attention",
        exps=300000,
    )
    return middle_out, [upper, upper_edge], [lower, lower_edge]


def shift(part, axis, step, wrap):
    size = lax.axis_size(axis)
    pairs = [(i, (i + step) % size) for i in range(size) if wrap or 0 <= i + step < size]
    return lax.ppermute(part, axis, pairs)


def key_bias():
    row = jnp.arange(8, dtype=jnp.int32)[:, None]
    key = jnp.arange(128, dtype=jnp.int32)[None, :] // WLON
    north = (row == 0) & (key < RIM_LAT) & (lax.axis_index("lat") == 0)
    south = (row == 1) & (key >= RIM_LAT) & (lax.axis_index("lat") == lax.axis_size("lat") - 1)
    return jnp.where(north | south, F32(-1e30), F32(0.0))


def place_index():
    me = lax.axis_index("lon")
    return jnp.stack([me // 2, me % 2]).astype(jnp.int32)


def merge_dots(place_ref, upper, lower, mine_ref, pair_ref, x_ref, x_pair_ref, y_ref, y_pair_ref, refs):
    half, block = x_ref.shape
    at = [pl.ds(pl.multiple_of((place_ref[1] + k) % 2 * block, block), block) for k in range(2)]
    own, x, y = refs
    for k, ref in enumerate((mine_ref, pair_ref)):
        own(at[k], dot(upper, ref[:half, :]), dot(lower, ref[half:, :]))
    for k, ref in enumerate((x_ref, x_pair_ref)):
        x(at[k], dot(upper, ref[...]))
    for k, ref in enumerate((y_ref, y_pair_ref)):
        y(at[k], dot(lower, ref[...]))


def stacked(refs):
    return jnp.concatenate([ref[...] for ref in refs], axis=0)


def merge_own_kernel(place_ref, *refs):
    rows, refs = refs[:4], refs[4:]
    weights, (own_ref, x_ref, y_ref), kept = refs[:6], refs[6:9], refs[9:]
    for ref, to in zip(weights, kept):
        to[...] = ref[...]

    def own(at, a, b):
        own_ref[:, at] = a + b

    def x(at, a):
        x_ref[:, at] = a

    def y(at, b):
        y_ref[:, at] = b

    merge_dots(place_ref, stacked(rows[:2]), stacked(rows[2:]), *weights, (own, x, y))


def merge_other_kernel(place_ref, *refs):
    rows, refs = refs[:4], refs[4:]
    weights, (to_y_ref, to_x_ref) = refs[:6], refs[6:]
    wide = to_x_ref.shape[1] // 2

    def own(at, a, b):
        to_y_ref[:, at] = a.astype(BF16)
        to_x_ref[:, at] = b.astype(BF16)

    def x(at, a):
        to_y_ref[:, pl.ds(pl.multiple_of(wide + at.start, at.size), at.size)] = a.astype(BF16)

    def y(at, b):
        to_x_ref[:, pl.ds(pl.multiple_of(wide + at.start, at.size), at.size)] = b.astype(BF16)

    merge_dots(place_ref, stacked(rows[:2]), stacked(rows[2:]), *weights, (own, x, y))


def combine_kernel(place_ref, own_ref, x_ref, y_ref, from_y_ref, from_x_ref, out_ref):
    wide = own_ref.shape[1]
    chip = place_ref[0]
    from_x, from_y = from_x_ref[...].astype(F32), from_y_ref[...].astype(F32)
    parts = [
        own_ref[...],
        x_ref[...] + from_x[:, :wide],
        y_ref[...] + from_y[:, :wide],
        from_x[:, wide:] + from_y[:, wide:],
    ]
    for m, part in enumerate(parts):
        out_ref[:, pl.ds(pl.multiple_of((chip ^ m) * wide, wide), wide)] = part.astype(BF16)


def local_call(kernel, out, place, args, flops, name, mib=16):
    vmem = pl.BlockSpec(memory_space=pltpu.VMEM)
    return pl.pallas_call(
        kernel,
        in_specs=[pl.BlockSpec(memory_space=pltpu.SMEM)] + [vmem] * len(args),
        out_specs=[vmem] * len(out),
        out_shape=out,
        compiler_params=params(mib),
        cost_estimate=pl.CostEstimate(flops=flops, bytes_accessed=2**20, transcendentals=0),
        name=name,
    )(place, *args)


def merge_by_squares(upper, lower, merge_weight, halves):
    half = merge_weight.shape[0] // 2
    block = merge_weight.shape[1]
    count = sum(part.shape[0] for part in upper)
    x = chip_swap(halves[0], 1)
    y = chip_swap(halves[1], 2)
    from_y = [chip_swap(part, 2) for part in upper]
    from_x = [chip_swap(part, 1) for part in lower]
    x_pair, y_pair, from_y[0], from_x[0], _ = lax.optimization_barrier((x, y, from_y[0], from_x[0], upper[1]))
    weights = [merge_weight, core_swap(merge_weight), x, core_swap(x_pair), y, core_swap(y_pair)]
    place = place_index()
    flops = 16 * count * half * block
    wide = jax.ShapeDtypeStruct((count, 2 * block), F32)
    kept = [jax.ShapeDtypeStruct(w.shape, BF16) for w in weights]
    *own, a, b, c, d, e, f = local_call(
        merge_own_kernel, [wide] * 3 + kept, place, [*upper, *lower] + weights, flops, "merge_own", 28
    )
    weights = [a, b, c, d, e, f]
    pair = jax.ShapeDtypeStruct((count, 4 * block), BF16)
    to_y, to_x = local_call(merge_other_kernel, [pair] * 2, place, [*from_y, *from_x] + weights, flops, "merge_other")
    back_y, back_x = chip_swap(to_y, 2), chip_swap(to_x, 1)
    out = jax.ShapeDtypeStruct((count, 8 * block), BF16)
    return local_call(combine_kernel, [out], place, [*own, back_y, back_x], 0, "combine")[0]


def ffn_kernel(mine_ref, theirs_ref, up_ref, down_ref, out_mine_ref, low_ref, high_ref, normed_ref, hidden_ref):
    count = mine_ref.shape[0]
    for k, ref in enumerate((mine_ref, theirs_ref)):
        normed_ref[k * count : (k + 1) * count, :] = normalize(ref[...].astype(F32)).astype(BF16)
    hidden = hidden_ref.shape[1]
    step = 256
    for at in range(0, hidden, step):
        raw = dot(normed_ref[...], up_ref[:, at : at + step])
        active = 0.5 * raw * (1.0 + lax.erf(raw * np.float32(np.sqrt(0.5))))
        hidden_ref[:, at : at + step] = active.astype(BF16)
    half = low_ref.shape[1]
    for at in range(0, 2 * half, step):
        out = dot(hidden_ref[...], down_ref[:, at : at + step]).astype(BF16)
        out_mine_ref[:, at : at + step] = out[:count]
        ref = low_ref if at < half else high_ref
        ref[:, at % half : at % half + step] = out[count:]


def feed_forward(mine, theirs, up, down):
    count = mine.shape[0]
    width, hidden = up.shape
    vmem = pl.BlockSpec(memory_space=pltpu.VMEM)
    return pl.pallas_call(
        ffn_kernel,
        in_specs=[vmem] * 4,
        out_specs=[vmem] * 3,
        out_shape=[jax.ShapeDtypeStruct((count, width // n), BF16) for n in (1, 2, 2)],
        scratch_shapes=[pltpu.VMEM((2 * count, width), BF16), pltpu.VMEM((2 * count, hidden), BF16)],
        compiler_params=params(20),
        cost_estimate=pl.CostEstimate(
            flops=8 * count * width * hidden, bytes_accessed=4 * width * hidden, transcendentals=2 * count * hidden
        ),
        name="feed_forward",
    )(mine, theirs, up, down)


def added(mine, low, high):
    return (mine.astype(F32) + jnp.concatenate([low, high], axis=1).astype(F32)).astype(BF16)


def summed(mine, low, high):
    return added(mine, core_swap(low), core_swap(high))


def core_swap(value):
    size = lax.axis_size("lon")
    return lax.ppermute(value, "lon", [(i, i ^ 1) for i in range(size)])


def chip_swap(value, offset):
    size = lax.axis_size("lon")
    return lax.ppermute(value, "lon", [(i, i ^ (2 * offset)) for i in range(size)])


def cross(value, first, second):
    size = lax.axis_size("lon")
    return lax.ppermute(value, "lon", [(i, i ^ (2 * (second if i % 2 else first))) for i in range(size)])


def coarse_by_squares(upper, lower, merge_weight, halves, up, down):
    own = merge_by_squares(upper, lower, merge_weight, halves)
    near = cross(own, 1, 2)
    first = feed_forward(own, core_swap(own), up, down)
    near, *first = lax.optimization_barrier((near, *first))
    far = cross(near, 2, 1)
    near_mine, near_low, near_high = feed_forward(near, core_swap(near), up, down)
    later, near_mine = lax.optimization_barrier((own, near_mine))
    other = cross(later, 2, 1)
    near_low, far = lax.optimization_barrier((core_swap(near_low), far))
    mine, low, high = feed_forward(far, core_swap(far), up, down)
    low, other = lax.optimization_barrier((core_swap(low), other))
    far_sum = added(mine, low, core_swap(high))
    pair, far_sum = lax.optimization_barrier((core_swap(other), far_sum))
    relayed = cross(far_sum, 2, 1)
    mine, low, high = feed_forward(other, pair, up, down)
    relayed, low = lax.optimization_barrier((relayed, core_swap(low)))
    other_back = cross(added(mine, low, core_swap(high)), 2, 1)
    half = low.shape[1]
    near_back = []
    for part, at in ((near_low, 0), (core_swap(near_high), half)):
        columns = slice(at, at + half)
        total = near_mine[:, columns].astype(F32) + part.astype(F32) + relayed[:, columns].astype(F32)
        near_back.append(cross(total.astype(BF16), 1, 2))
    return [own, summed(*first), other_back], near_back


def coarse_by_chips(upper, lower, merge_weight, halves, up, down):
    weight = lax.all_gather(merge_weight, "lon", axis=1, tiled=True)
    patches = jnp.concatenate([jnp.concatenate(upper, axis=0), jnp.concatenate(lower, axis=0)], axis=1)
    coarse = jnp.dot(patches, weight, preferred_element_type=F32).astype(BF16)
    chips = lax.axis_size("lon") // 2
    arrived = [coarse] + [chip_swap(coarse, m) for m in range(1, chips)]
    total = coarse.astype(F32)
    for m in range(chips):
        part = summed(*feed_forward(arrived[m], core_swap(arrived[m]), up, down))
        total = total + (chip_swap(part, m) if m else part).astype(F32)
    return [total.astype(BF16)], []


def finish_kernel(spans, *refs):
    *parts, low_ref, high_ref, out_ref = refs
    total = sum(ref[...].astype(F32) for ref in parts)
    if low_ref is not None:
        total = total + jnp.concatenate([low_ref[...], high_ref[...]], axis=1).astype(F32)
    for r, at in enumerate(spans):
        out_ref[r] = total[at : at + out_ref.shape[1]].astype(BF16)


def finish(bands, whole, halves):
    inner, edge = bands.inner_patches()
    half = bands.columns // 2
    start = up16(half * len(inner))
    place = {r: n * half for n, r in enumerate(inner)} | {r: start + n * half for n, r in enumerate(edge)}
    spans = [place[r] for r in range(bands.rows // 2)]
    vmem = pl.BlockSpec(memory_space=pltpu.VMEM)

    def kernel(*refs):
        finish_kernel(spans, *(refs if halves else (*refs[:-1], None, None, refs[-1])))

    return pl.pallas_call(
        kernel,
        in_specs=[vmem] * (len(whole) + len(halves)),
        out_specs=vmem,
        out_shape=jax.ShapeDtypeStruct((bands.rows // 2, half, whole[0].shape[1]), BF16),
        compiler_params=params(16),
        name="finish",
    )(*whole, *halves)


def per_device(tokens, qkv_weight, out_weight, merge_weight, up_weight, down_weight):
    rows, columns, width = tokens.shape
    bands = Bands(rows, columns)
    sides = rims(tokens)
    *sides, later = lax.optimization_barrier((*sides, merge_weight))
    halves = halves_of(later)
    middle_out, upper, lower = attention(bands, tokens, sides, qkv_weight, out_weight)
    coarse = coarse_by_squares if lax.axis_size("lon") == 8 else coarse_by_chips
    parts = coarse(upper, lower, merge_weight, halves, up_weight, down_weight)
    return (middle_out, finish(bands, *parts))


def solution(mesh):
    return jax.shard_map(
        per_device,
        mesh=mesh,
        in_specs=(P("lat", "lon", None), P(), P(), P(None, "lon"), P(None, "lon"), P("lon", None)),
        out_specs=(P("lat", "lon", None), P("lat", "lon", None)),
        check_vma=False,
    )
```

```python
import functools

import jax
import jax.numpy as jnp
import numpy as np
from jax import lax
from jax.experimental import pallas as pl
from jax.experimental.pallas import tpu as pltpu
from jax.sharding import PartitionSpec as P

HEADS = 16
WLAT = 6
WLON = 12
RIM_LAT = WLAT // 2
RIM_LON = WLON // 2
SIDE = 8
GROUP = 4
F32 = jnp.float32
BF16 = jnp.bfloat16


def up16(n):
    return -(-n // 16) * 16


def params(mib=48, **kw):
    return pltpu.CompilerParams(vmem_limit_bytes=mib * 2**20, **kw)


class Bands:
    def __init__(self, rows, columns):
        assert (rows - WLAT) % WLAT == 0 and (columns - WLON) % WLON == 0
        self.rows, self.columns = rows, columns
        inner = (rows - WLAT) // WLAT
        self.height = [RIM_LAT] + [WLAT] * inner + [RIM_LAT]
        self.count = len(self.height)
        self.first = [sum(self.height[:b]) for b in range(self.count)]
        self.widths = [RIM_LON] + [WLON] * ((columns - WLON) // WLON) + [RIM_LON]
        self.own = [h * columns for h in self.height]
        self.own_padded = [up16(n) for n in self.own]
        self.own_at = [sum(self.own_padded[:b]) for b in range(self.count)]
        self.own_total = sum(self.own_padded)
        self.side = [2 * h * SIDE for h in self.height]
        assert all(n % 16 == 0 for n in self.side)
        self.side_at = [sum(self.side[:b]) for b in range(self.count)]
        self.side_total = sum(self.side)
        self.slab = columns + 2 * SIDE
        self.slab_padded = up16(RIM_LAT * self.slab)
        self.window = up16(WLAT * WLON)
        self.counts = [[GROUP * h * w for w in self.widths] for h in self.height]
        self.counts_padded = [[up16(n) for n in row] for row in self.counts]

    def edge(self, b):
        return b in (0, self.count - 1)

    def sources(self, b):
        return self.own_padded[b] + self.side[b] + (self.slab_padded if self.edge(b) else 0)

    def source(self, b, i, j):
        columns, h, first = self.columns, self.height[b], self.first[b]
        at = self.own_padded[b]
        if not 0 <= i < self.rows:
            i = i + RIM_LAT if i < 0 else i - self.rows
            return at + self.side[b] + i * self.slab + j + SIDE
        if 0 <= j < columns:
            return (i - first) * columns + j
        at += (i - first) * SIDE
        return at + (j + SIDE if j < 0 else h * SIDE + j - columns)

    def key_matrix(self, b):
        g = np.zeros((len(self.widths) * self.window, self.sources(b)), np.float32)
        top = self.first[b] - (RIM_LAT if b == 0 else 0)
        for c in range(len(self.widths)):
            for i in range(WLAT):
                for j in range(WLON):
                    at = c * self.window + i * WLON + j
                    g[at, self.source(b, top + i, c * WLON - RIM_LON + j)] = 1
        return g.astype(BF16)

    def query_matrix(self, b):
        total = sum(self.counts_padded[b])
        g = np.zeros((total, self.own_padded[b]), np.float32)
        head = np.zeros((total,), np.int32)
        start = left = 0
        for width, padded in zip(self.widths, self.counts_padded[b]):
            at = start
            for k in range(GROUP):
                for i in range(self.height[b]):
                    for j in range(width):
                        g[at, i * self.columns + left + j] = 1
                        head[at] = k
                        at += 1
            left += width
            start += padded
        return g.astype(BF16), head

    def inner_patches(self):
        rows = range(self.rows // 2)
        inner = [r for r in rows if 2 * r >= RIM_LAT and 2 * r + 1 < self.rows - RIM_LAT]
        return inner, [r for r in rows if r not in inner]

    def patch_matrix(self, patch_rows, place, sources):
        half = self.columns // 2
        padded = up16(len(patch_rows) * half)
        g = np.zeros((4 * padded, sources), np.float32)
        for n, r in enumerate(patch_rows):
            for c in range(half):
                for k in range(4):
                    g[k * padded + n * half + c, place(2 * r + k // 2) + 2 * c + k % 2] = 1
        return g.astype(BF16)

    def inner_patch_matrix(self):
        return self.patch_matrix(
            self.inner_patches()[0],
            lambda i: (i - RIM_LAT) * self.columns,
            (self.rows - 2 * RIM_LAT) * self.columns,
        )

    def edge_patch_matrix(self):
        last = self.rows - RIM_LAT - 1
        return self.patch_matrix(
            self.inner_patches()[1],
            lambda i: (i if i <= RIM_LAT else RIM_LAT + 1 + i - last) * self.columns,
            2 * (RIM_LAT + 1) * self.columns,
        )

    def constants(self, some, block):
        distinct, kinds, consts = [], [], []
        for b in some:
            kind = (self.height[b], b == 0, b == self.count - 1)
            if kind not in distinct:
                distinct.append(kind)
                query, head = self.query_matrix(b)
                mask = head[:, None] == (np.arange(block) // (block // GROUP))[None, :]
                scale = np.float32((block // GROUP) ** -0.5)
                scaled = (query.astype(np.float32) * scale).astype(BF16)
                consts += [self.key_matrix(b), scaled, mask.astype(BF16), np.ascontiguousarray(query.T)]
            kinds.append(4 * distinct.index(kind))
        return kinds, consts


def normalize(values):
    center = values - jnp.mean(values, axis=-1, keepdims=True)
    spread = jnp.mean(center * center, axis=-1, keepdims=True)
    return center * lax.rsqrt(spread + 1e-05)


def dot(a, b, dims=((1,), (0,))):
    return lax.dot_general(a, b, (dims, ((), ())), preferred_element_type=F32)


def flat_normed(ref):
    values = ref[...].astype(F32)
    return normalize(values.reshape(-1, values.shape[-1]))


def project(normed_ref, weight_ref, out_ref):
    step = 256
    for at in range(0, out_ref.shape[1], step):
        out_ref[:, at : at + step] = dot(normed_ref[...], weight_ref[:, at : at + step]).astype(BF16)


def padded_rows(values, total):
    if values.shape[0] == total:
        return values
    return jnp.concatenate([values, jnp.zeros((total - values.shape[0], values.shape[1]), values.dtype)], axis=0)


def rims_kernel(tokens_ref, east_ref, west_ref):
    columns = tokens_ref.shape[1]
    east_ref[...] = tokens_ref[:, columns - SIDE :]
    west_ref[...] = tokens_ref[:, :SIDE]


def rims(tokens):
    rows, _, width = tokens.shape
    vmem = pl.BlockSpec(memory_space=pltpu.VMEM)
    return pl.pallas_call(
        rims_kernel,
        in_specs=[vmem],
        out_specs=[vmem] * 2,
        out_shape=[jax.ShapeDtypeStruct((rows, SIDE, width), BF16)] * 2,
        compiler_params=params(16),
        name="rims",
    )(tokens)


def halves_kernel(weight_ref, upper_ref, lower_ref, sems):
    half = upper_ref.shape[0]
    copies = [
        pltpu.make_async_copy(weight_ref.at[k * half : (k + 1) * half], ref, sems.at[k])
        for k, ref in enumerate((upper_ref, lower_ref))
    ]
    for copy in copies:
        copy.start()
    for copy in copies:
        copy.wait()


def halves_of(weight):
    depth, block = weight.shape
    return pl.pallas_call(
        halves_kernel,
        in_specs=[pl.BlockSpec(memory_space=pl.ANY)],
        out_specs=[pl.BlockSpec(memory_space=pltpu.VMEM)] * 2,
        out_shape=[jax.ShapeDtypeStruct((depth // 2, block), BF16)] * 2,
        scratch_shapes=[pltpu.SemaphoreType.DMA((2,))],
        compiler_params=params(52),
        name="halves",
    )(weight)


def own_kernel(bands, tokens_ref, weight_ref, out_ref, kv_ref, normed_ref, q_ref, sems):
    width = q_ref.shape[1]
    chunk = weight_ref.shape[1] // sems.shape[0]
    places = []
    for n in range(sems.shape[0]):
        at = n * chunk
        places.append((q_ref, at) if at < width else (kv_ref, at - width))
    copies = [
        pltpu.make_async_copy(weight_ref.at[:, pl.ds(n * chunk, chunk)], ref.at[:, pl.ds(at, chunk)], sems.at[n])
        for n, (ref, at) in enumerate(places)
    ]
    for copy in copies:
        copy.start()
    normed = flat_normed(tokens_ref)
    for b in range(bands.count):
        at = bands.first[b] * bands.columns
        part = padded_rows(normed[at : at + bands.own[b]], bands.own_padded[b])
        normed_ref[bands.own_at[b] : bands.own_at[b] + bands.own_padded[b], :] = part.astype(BF16)
    step = 256
    for n, (ref, first) in enumerate(places):
        copies[n].wait()
        for at in range(0, chunk, step):
            part = ref[:, first + at : first + at + step]
            out_ref[:, n * chunk + at : n * chunk + at + step] = dot(normed_ref[...], part).astype(BF16)


def own_projection(bands, tokens, weight):
    width, out = weight.shape
    vmem = pl.BlockSpec(memory_space=pltpu.VMEM)
    return pl.pallas_call(
        functools.partial(own_kernel, bands),
        in_specs=[vmem, pl.BlockSpec(memory_space=pl.ANY)],
        out_specs=[vmem, vmem],
        out_shape=[
            jax.ShapeDtypeStruct((bands.own_total, out), BF16),
            jax.ShapeDtypeStruct((width, out - width), BF16),
        ],
        scratch_shapes=[
            pltpu.VMEM((bands.own_total, width), BF16),
            pltpu.VMEM((width, width), BF16),
            pltpu.SemaphoreType.DMA((3,)),
        ],
        compiler_params=params(42),
        cost_estimate=pl.CostEstimate(
            flops=2 * bands.own_total * width * out, bytes_accessed=2 * width * out, transcendentals=0
        ),
        name="own_projection",
    )(tokens, weight)


def attend(bands, some, kinds, consts, own_ref, outer, bias_ref, put, scratch):
    k_ref, v_ref, q_ref, p_ref, r_ref = scratch
    width = own_ref.shape[1] // 3
    block = width * GROUP // HEADS
    window = WLAT * WLON
    units = [(n, b, g) for n, b in enumerate(some) for g in range(HEADS // GROUP)]
    for u, (n, b, g) in enumerate(units):
        keys, query, mask, _ = consts[kinds[n] : kinds[n] + 4]
        own = slice(bands.own_at[b], bands.own_at[b] + bands.own_padded[b])
        for ref, skip in ((k_ref, 0), (v_ref, width)):
            parts = [own_ref[own, width + skip + g * block : width + skip + (g + 1) * block]]
            for out_ref, at, size in outer(b):
                parts.append(out_ref[at : at + size, skip + g * block : skip + (g + 1) * block])
            ref[u] = dot(keys[...], jnp.concatenate(parts, axis=0)).astype(BF16)
        total = query.shape[0]
        q_ref[u, :total] = dot(query[...], own_ref[own, g * block : (g + 1) * block]).astype(BF16) * mask[...]
    for u, (n, b, g) in enumerate(units):
        at = 0
        for c, count in enumerate(bands.counts_padded[b]):
            scores = dot(
                q_ref[u, at : at + count], k_ref[u, c * bands.window : c * bands.window + window], ((1,), (1,))
            )
            if b == 0:
                scores = scores + bias_ref[0:1, :window]
            if b == bands.count - 1:
                scores = scores + bias_ref[1:2, :window]
            raised = jnp.exp(scores - jnp.max(scores, axis=-1, keepdims=True))
            weights = raised * (1.0 / jnp.sum(raised, axis=-1, keepdims=True))
            p_ref[u, at : at + count, :window] = weights.astype(BF16)
            at += count
    for u, (n, b, g) in enumerate(units):
        mask = consts[kinds[n] + 2]
        at = 0
        for c, count in enumerate(bands.counts_padded[b]):
            mixed = dot(
                p_ref[u, at : at + count, :window], v_ref[u, c * bands.window : c * bands.window + window]
            )
            r_ref[u, at : at + count] = mixed.astype(BF16) * mask[at : at + count]
            at += count
    for u, (n, b, g) in enumerate(units):
        back = consts[kinds[n] + 3]
        put(b, g, dot(back[...], r_ref[u, : back.shape[1]]).astype(BF16))


def attend_scratch(bands, some, block):
    units = len(some) * HEADS // GROUP
    keys = len(bands.widths) * bands.window
    rows = max(sum(bands.counts_padded[b]) for b in some)
    return [
        pltpu.VMEM((units, keys, block), BF16),
        pltpu.VMEM((units, keys, block), BF16),
        pltpu.VMEM((units, rows, block), BF16),
        pltpu.VMEM((units, rows, 128), BF16),
        pltpu.VMEM((units, rows, block), BF16),
    ]


def merge_rows(patch_ref, cells, upper_ref, lower_ref, first):
    width = cells.shape[1]
    padded = patch_ref.shape[0] // 4
    parts = [dot(patch_ref[k * padded : (k + 1) * padded, :], cells) for k in range(4)]
    total = sum(jnp.sum(p, axis=-1, keepdims=True) for p in parts)
    mean = total * (1.0 / (4 * width))
    parts = [p - mean for p in parts]
    spread = sum(jnp.sum(p * p, axis=-1, keepdims=True) for p in parts)
    factor = lax.rsqrt(spread * (1.0 / (4 * width)) + 1e-05)
    for k in range(4):
        ref = (upper_ref, lower_ref)[k // 2]
        ref[first : first + padded, k % 2 * width : (k % 2 + 1) * width] = (parts[k] * factor).astype(BF16)


def middle_kernel(bands, some, kinds, tokens_ref, west_ref, east_ref, own_ref, weight_ref, out_w_ref, patch_ref, *rest):
    consts, rest = rest[:-11], rest[-11:]
    side_ref, middle_ref, upper_ref, lower_ref, normed_ref, attended_ref, *scratch = rest
    rows, columns, width = tokens_ref.shape
    west, east = flat_normed(west_ref), flat_normed(east_ref)
    for b in range(bands.count):
        at, size = bands.first[b] * SIDE, bands.height[b] * SIDE
        part = jnp.concatenate([west[at : at + size], east[at : at + size]], axis=0)
        normed_ref[bands.side_at[b] : bands.side_at[b] + bands.side[b], :] = part.astype(BF16)
    project(normed_ref, weight_ref, side_ref)

    def outer(b):
        return [(side_ref, bands.side_at[b], bands.side[b])]

    def put(b, g, value):
        at = bands.own_at[b] - bands.own_at[1]
        block = value.shape[1]
        attended_ref[at : at + bands.own_padded[b], g * block : (g + 1) * block] = value

    attend(bands, some, kinds, consts, own_ref, outer, None, put, scratch)
    mixed = dot(attended_ref[...], out_w_ref[...])
    middle = tokens_ref[RIM_LAT : rows - RIM_LAT].astype(F32) + mixed.reshape(-1, columns, width)
    middle_ref[...] = middle.astype(BF16)
    merge_rows(patch_ref, middle.reshape(-1, width).astype(BF16), upper_ref, lower_ref, 0)


def edge_kernel(bands, some, kinds, tokens_ref, north_ref, south_ref, bias_ref, own_ref, side_ref, inner_ref, inner_upper_ref, inner_lower_ref, weight_ref, out_w_ref, patch_ref, *rest):
    consts, rest = rest[:-11], rest[-11:]
    middle_ref, upper_ref, lower_ref, normed_ref, slab_ref, attended_ref, *scratch = rest
    rows, columns, width = tokens_ref.shape
    slab = bands.slab_padded
    for k, ref in enumerate((north_ref, south_ref)):
        normed_ref[k * slab : (k + 1) * slab, :] = padded_rows(flat_normed(ref), slab).astype(BF16)
    project(normed_ref, weight_ref, slab_ref)

    def outer(b):
        return [
            (side_ref, bands.side_at[b], bands.side[b]),
            (slab_ref, 0 if b == 0 else slab, slab),
        ]

    def put(b, g, value):
        block = value.shape[1]
        at = 0 if b == 0 else bands.own_padded[0]
        attended_ref[at : at + bands.own_padded[b], g * block : (g + 1) * block] = value

    attend(bands, some, kinds, consts, own_ref, outer, bias_ref, put, scratch)
    mixed = dot(attended_ref[...], out_w_ref[...])
    low = bands.own_padded[0]
    top = tokens_ref[:RIM_LAT].astype(F32) + mixed[: bands.own[0]].reshape(-1, columns, width)
    bottom = tokens_ref[rows - RIM_LAT :].astype(F32) + mixed[low : low + bands.own[-1]].reshape(-1, columns, width)
    middle_ref[:RIM_LAT] = top.astype(BF16)
    middle_ref[RIM_LAT : rows - RIM_LAT] = inner_ref[...]
    middle_ref[rows - RIM_LAT :] = bottom.astype(BF16)
    first, last = inner_ref[0].astype(F32), inner_ref[rows - 2 * RIM_LAT - 1].astype(F32)
    cells = jnp.concatenate([top.reshape(-1, width), first, last, bottom.reshape(-1, width)], axis=0)
    inner_count = inner_upper_ref.shape[0]
    upper_ref[:inner_count, :] = inner_upper_ref[...]
    lower_ref[:inner_count, :] = inner_lower_ref[...]
    merge_rows(patch_ref, cells.astype(BF16), upper_ref, lower_ref, inner_count)


def vmem_call(kernel, out, args, scratch, flops, name, mib=24, exps=0):
    vmem = pl.BlockSpec(memory_space=pltpu.VMEM)
    return pl.pallas_call(
        kernel,
        in_specs=[vmem] * len(args),
        out_specs=[vmem] * len(out),
        out_shape=[jax.ShapeDtypeStruct(shape, BF16) for shape in out],
        scratch_shapes=scratch,
        compiler_params=params(mib),
        cost_estimate=pl.CostEstimate(flops=flops, bytes_accessed=2**20, transcendentals=exps),
        name=name,
    )(*args)


def attention(bands, tokens, sides, qkv_weight, out_weight):
    rows, columns, width = tokens.shape
    block = width * GROUP // HEADS
    west = shift(sides[0], "lon", 1, True)
    east = shift(sides[1], "lon", -1, True)
    own, kv_weight = own_projection(bands, tokens, qkv_weight)

    def slab(part):
        return jnp.concatenate([west[part], tokens[part], east[part]], axis=1)

    north = shift(slab(slice(rows - RIM_LAT, rows)), "lat", 1, False)
    south = shift(slab(slice(0, RIM_LAT)), "lat", -1, False)
    inner = list(range(1, bands.count - 1))
    edges = [0, bands.count - 1]
    kinds, consts = bands.constants(inner, block)
    patch = bands.inner_patch_matrix()
    inner_count = patch.shape[0] // 4
    side, middle, upper, lower = vmem_call(
        functools.partial(middle_kernel, bands, inner, kinds),
        [
            (bands.side_total, 2 * width),
            (rows - 2 * RIM_LAT, columns, width),
            (inner_count, 2 * width),
            (inner_count, 2 * width),
        ],
        [tokens, west, east, own, kv_weight, out_weight, patch] + consts,
        [
            pltpu.VMEM((bands.side_total, width), BF16),
            pltpu.VMEM((bands.own_at[-1] - bands.own_at[1], width), BF16),
        ]
        + attend_scratch(bands, inner, block),
        5 * 10**9,
        "middle_attention",
        exps=500000,
    )
    kinds, consts = bands.constants(edges, block)
    patch = bands.edge_patch_matrix()
    count = inner_count + patch.shape[0] // 4
    return vmem_call(
        functools.partial(edge_kernel, bands, edges, kinds),
        [tokens.shape, (count, 2 * width), (count, 2 * width)],
        [tokens, north, south, key_bias(), own, side, middle, upper, lower, kv_weight, out_weight, patch] + consts,
        [
            pltpu.VMEM((2 * bands.slab_padded, width), BF16),
            pltpu.VMEM((2 * bands.slab_padded, 2 * width), BF16),
            pltpu.VMEM((bands.own_padded[0] + bands.own_padded[-1], width), BF16),
        ]
        + attend_scratch(bands, edges, block),
        6 * 10**9,
        "edge_attention",
        exps=300000,
    )


def shift(part, axis, step, wrap):
    size = lax.axis_size(axis)
    pairs = [(i, (i + step) % size) for i in range(size) if wrap or 0 <= i + step < size]
    return lax.ppermute(part, axis, pairs)


def key_bias():
    row = jnp.arange(8, dtype=jnp.int32)[:, None]
    key = jnp.arange(128, dtype=jnp.int32)[None, :] // WLON
    north = (row == 0) & (key < RIM_LAT) & (lax.axis_index("lat") == 0)
    south = (row == 1) & (key >= RIM_LAT) & (lax.axis_index("lat") == lax.axis_size("lat") - 1)
    return jnp.where(north | south, F32(-1e30), F32(0.0))


def place_index():
    me = lax.axis_index("lon")
    return jnp.stack([me // 2, me % 2]).astype(jnp.int32)


def merge_dots(place_ref, upper, lower, mine_ref, pair_ref, x_ref, x_pair_ref, y_ref, y_pair_ref, refs):
    half, block = x_ref.shape
    at = [pl.ds(pl.multiple_of((place_ref[1] + k) % 2 * block, block), block) for k in range(2)]
    own, x, y = refs
    for k, ref in enumerate((mine_ref, pair_ref)):
        own(at[k], dot(upper, ref[:half, :]), dot(lower, ref[half:, :]))
    for k, ref in enumerate((x_ref, x_pair_ref)):
        x(at[k], dot(upper, ref[...]))
    for k, ref in enumerate((y_ref, y_pair_ref)):
        y(at[k], dot(lower, ref[...]))


def merge_own_kernel(place_ref, upper_ref, lower_ref, *refs):
    weights, (own_ref, x_ref, y_ref), kept = refs[:6], refs[6:9], refs[9:]
    for ref, to in zip(weights, kept):
        to[...] = ref[...]

    def own(at, a, b):
        own_ref[:, at] = a + b

    def x(at, a):
        x_ref[:, at] = a

    def y(at, b):
        y_ref[:, at] = b

    merge_dots(place_ref, upper_ref[...], lower_ref[...], *weights, (own, x, y))


def merge_other_kernel(place_ref, upper_ref, lower_ref, *refs):
    weights, (to_y_ref, to_x_ref) = refs[:6], refs[6:]
    wide = to_x_ref.shape[1] // 2

    def own(at, a, b):
        to_y_ref[:, at] = a.astype(BF16)
        to_x_ref[:, at] = b.astype(BF16)

    def x(at, a):
        to_y_ref[:, pl.ds(pl.multiple_of(wide + at.start, at.size), at.size)] = a.astype(BF16)

    def y(at, b):
        to_x_ref[:, pl.ds(pl.multiple_of(wide + at.start, at.size), at.size)] = b.astype(BF16)

    merge_dots(place_ref, upper_ref[...], lower_ref[...], *weights, (own, x, y))


def combine_kernel(place_ref, own_ref, x_ref, y_ref, from_y_ref, from_x_ref, out_ref):
    wide = own_ref.shape[1]
    chip = place_ref[0]
    from_x, from_y = from_x_ref[...].astype(F32), from_y_ref[...].astype(F32)
    parts = [
        own_ref[...],
        x_ref[...] + from_x[:, :wide],
        y_ref[...] + from_y[:, :wide],
        from_x[:, wide:] + from_y[:, wide:],
    ]
    for m, part in enumerate(parts):
        out_ref[:, pl.ds(pl.multiple_of((chip ^ m) * wide, wide), wide)] = part.astype(BF16)


def local_call(kernel, out, place, args, flops, name, mib=12):
    vmem = pl.BlockSpec(memory_space=pltpu.VMEM)
    return pl.pallas_call(
        kernel,
        in_specs=[pl.BlockSpec(memory_space=pltpu.SMEM)] + [vmem] * len(args),
        out_specs=[vmem] * len(out),
        out_shape=out,
        compiler_params=params(mib),
        cost_estimate=pl.CostEstimate(flops=flops, bytes_accessed=2**20, transcendentals=0),
        name=name,
    )(place, *args)


def merge_by_squares(upper, lower, merge_weight, halves):
    half = merge_weight.shape[0] // 2
    block = merge_weight.shape[1]
    count = upper.shape[0]
    x = chip_swap(halves[0], 1)
    y = chip_swap(halves[1], 2)
    x_pair, y_pair, _ = lax.optimization_barrier((x, y, upper))
    weights = [merge_weight, core_swap(merge_weight), x, core_swap(x_pair), y, core_swap(y_pair)]
    place = place_index()
    from_y = chip_swap(upper, 2)
    from_x = chip_swap(lower, 1)
    flops = 16 * count * half * block
    wide = jax.ShapeDtypeStruct((count, 2 * block), F32)
    kept = [jax.ShapeDtypeStruct(w.shape, BF16) for w in weights]
    *own, a, b, c, d, e, f = local_call(
        merge_own_kernel, [wide] * 3 + kept, place, [upper, lower] + weights, flops, "merge_own", 20
    )
    weights = [a, b, c, d, e, f]
    pair = jax.ShapeDtypeStruct((count, 4 * block), BF16)
    to_y, to_x = local_call(merge_other_kernel, [pair] * 2, place, [from_y, from_x] + weights, flops, "merge_other")
    back_y, back_x = chip_swap(to_y, 2), chip_swap(to_x, 1)
    out = jax.ShapeDtypeStruct((count, 8 * block), BF16)
    return local_call(combine_kernel, [out], place, [*own, back_y, back_x], 0, "combine")[0]


def ffn_kernel(mine_ref, theirs_ref, up_ref, down_ref, out_mine_ref, low_ref, high_ref, normed_ref, hidden_ref):
    count = mine_ref.shape[0]
    for k, ref in enumerate((mine_ref, theirs_ref)):
        normed_ref[k * count : (k + 1) * count, :] = normalize(ref[...].astype(F32)).astype(BF16)
    hidden = hidden_ref.shape[1]
    step = 256
    for at in range(0, hidden, step):
        raw = dot(normed_ref[...], up_ref[:, at : at + step])
        active = 0.5 * raw * (1.0 + lax.erf(raw * np.float32(np.sqrt(0.5))))
        hidden_ref[:, at : at + step] = active.astype(BF16)
    half = low_ref.shape[1]
    for at in range(0, 2 * half, step):
        out = dot(hidden_ref[...], down_ref[:, at : at + step]).astype(BF16)
        out_mine_ref[:, at : at + step] = out[:count]
        ref = low_ref if at < half else high_ref
        ref[:, at % half : at % half + step] = out[count:]


def feed_forward(mine, theirs, up, down):
    count = mine.shape[0]
    width, hidden = up.shape
    vmem = pl.BlockSpec(memory_space=pltpu.VMEM)
    return pl.pallas_call(
        ffn_kernel,
        in_specs=[vmem] * 4,
        out_specs=[vmem] * 3,
        out_shape=[jax.ShapeDtypeStruct((count, width // n), BF16) for n in (1, 2, 2)],
        scratch_shapes=[pltpu.VMEM((2 * count, width), BF16), pltpu.VMEM((2 * count, hidden), BF16)],
        compiler_params=params(20),
        cost_estimate=pl.CostEstimate(
            flops=8 * count * width * hidden, bytes_accessed=4 * width * hidden, transcendentals=2 * count * hidden
        ),
        name="feed_forward",
    )(mine, theirs, up, down)


def added(mine, low, high):
    return (mine.astype(F32) + jnp.concatenate([low, high], axis=1).astype(F32)).astype(BF16)


def summed(mine, low, high):
    return added(mine, core_swap(low), core_swap(high))


def core_swap(value):
    size = lax.axis_size("lon")
    return lax.ppermute(value, "lon", [(i, i ^ 1) for i in range(size)])


def chip_swap(value, offset):
    size = lax.axis_size("lon")
    return lax.ppermute(value, "lon", [(i, i ^ (2 * offset)) for i in range(size)])


def cross(value, first, second):
    size = lax.axis_size("lon")
    return lax.ppermute(value, "lon", [(i, i ^ (2 * (second if i % 2 else first))) for i in range(size)])


def coarse_by_squares(upper, lower, merge_weight, halves, up, down):
    own = merge_by_squares(upper, lower, merge_weight, halves)
    near = cross(own, 1, 2)
    first = feed_forward(own, core_swap(own), up, down)
    near, *first = lax.optimization_barrier((near, *first))
    far = cross(near, 2, 1)
    near_mine, near_low, near_high = feed_forward(near, core_swap(near), up, down)
    later, near_mine = lax.optimization_barrier((own, near_mine))
    other = cross(later, 2, 1)
    near_low, far = lax.optimization_barrier((core_swap(near_low), far))
    mine, low, high = feed_forward(far, core_swap(far), up, down)
    low, other = lax.optimization_barrier((core_swap(low), other))
    far_sum = added(mine, low, core_swap(high))
    pair, far_sum = lax.optimization_barrier((core_swap(other), far_sum))
    relayed = cross(far_sum, 2, 1)
    mine, low, high = feed_forward(other, pair, up, down)
    relayed, low = lax.optimization_barrier((relayed, core_swap(low)))
    other_back = cross(added(mine, low, core_swap(high)), 2, 1)
    half = low.shape[1]
    near_back = []
    for part, at in ((near_low, 0), (core_swap(near_high), half)):
        columns = slice(at, at + half)
        total = near_mine[:, columns].astype(F32) + part.astype(F32) + relayed[:, columns].astype(F32)
        near_back.append(cross(total.astype(BF16), 1, 2))
    return [own, summed(*first), other_back], near_back


def coarse_by_chips(upper, lower, merge_weight, halves, up, down):
    weight = lax.all_gather(merge_weight, "lon", axis=1, tiled=True)
    patches = jnp.concatenate([upper, lower], axis=1)
    coarse = jnp.dot(patches, weight, preferred_element_type=F32).astype(BF16)
    chips = lax.axis_size("lon") // 2
    arrived = [coarse] + [chip_swap(coarse, m) for m in range(1, chips)]
    total = coarse.astype(F32)
    for m in range(chips):
        part = summed(*feed_forward(arrived[m], core_swap(arrived[m]), up, down))
        total = total + (chip_swap(part, m) if m else part).astype(F32)
    return [total.astype(BF16)], []


def finish_kernel(spans, *refs):
    *parts, low_ref, high_ref, out_ref = refs
    total = sum(ref[...].astype(F32) for ref in parts)
    if low_ref is not None:
        total = total + jnp.concatenate([low_ref[...], high_ref[...]], axis=1).astype(F32)
    for r, at in enumerate(spans):
        out_ref[r] = total[at : at + out_ref.shape[1]].astype(BF16)


def finish(bands, whole, halves):
    inner, edge = bands.inner_patches()
    half = bands.columns // 2
    start = up16(half * len(inner))
    place = {r: n * half for n, r in enumerate(inner)} | {r: start + n * half for n, r in enumerate(edge)}
    spans = [place[r] for r in range(bands.rows // 2)]
    vmem = pl.BlockSpec(memory_space=pltpu.VMEM)

    def kernel(*refs):
        finish_kernel(spans, *(refs if halves else (*refs[:-1], None, None, refs[-1])))

    return pl.pallas_call(
        kernel,
        in_specs=[vmem] * (len(whole) + len(halves)),
        out_specs=vmem,
        out_shape=jax.ShapeDtypeStruct((bands.rows // 2, half, whole[0].shape[1]), BF16),
        compiler_params=params(16),
        name="finish",
    )(*whole, *halves)


def per_device(tokens, qkv_weight, out_weight, merge_weight, up_weight, down_weight):
    rows, columns, width = tokens.shape
    bands = Bands(rows, columns)
    sides = rims(tokens)
    *sides, later = lax.optimization_barrier((*sides, merge_weight))
    halves = halves_of(later)
    middle_out, upper, lower = attention(bands, tokens, sides, qkv_weight, out_weight)
    coarse = coarse_by_squares if lax.axis_size("lon") == 8 else coarse_by_chips
    parts = coarse(upper, lower, merge_weight, halves, up_weight, down_weight)
    return (middle_out, finish(bands, *parts))


def solution(mesh):
    return jax.shard_map(
        per_device,
        mesh=mesh,
        in_specs=(P("lat", "lon", None), P(), P(), P(None, "lon"), P(None, "lon"), P("lon", None)),
        out_specs=(P("lat", "lon", None), P("lat", "lon", None)),
        check_vma=False,
    )
```

```python
import functools

import jax
import jax.numpy as jnp
import numpy as np
from jax import lax
from jax.experimental import pallas as pl
from jax.experimental.pallas import tpu as pltpu
from jax.sharding import PartitionSpec as P

HEADS = 16
WLAT = 6
WLON = 12
RIM_LAT = WLAT // 2
RIM_LON = WLON // 2
SIDE = 8
GROUP = 4
F32 = jnp.float32
BF16 = jnp.bfloat16


def up16(n):
    return -(-n // 16) * 16


def params(mib=48, **kw):
    return pltpu.CompilerParams(vmem_limit_bytes=mib * 2**20, **kw)


class Bands:
    def __init__(self, rows, columns):
        assert (rows - WLAT) % WLAT == 0 and (columns - WLON) % WLON == 0
        self.rows, self.columns = rows, columns
        inner = (rows - WLAT) // WLAT
        self.height = [RIM_LAT] + [WLAT] * inner + [RIM_LAT]
        self.count = len(self.height)
        self.first = [sum(self.height[:b]) for b in range(self.count)]
        self.widths = [RIM_LON] + [WLON] * ((columns - WLON) // WLON) + [RIM_LON]
        self.own = [h * columns for h in self.height]
        self.own_padded = [up16(n) for n in self.own]
        self.own_at = [sum(self.own_padded[:b]) for b in range(self.count)]
        self.own_total = sum(self.own_padded)
        self.side = [2 * h * SIDE for h in self.height]
        assert all(n % 16 == 0 for n in self.side)
        self.side_at = [sum(self.side[:b]) for b in range(self.count)]
        self.side_total = sum(self.side)
        self.slab = columns + 2 * SIDE
        self.slab_padded = up16(RIM_LAT * self.slab)
        self.window = up16(WLAT * WLON)
        self.counts = [[GROUP * h * w for w in self.widths] for h in self.height]
        self.counts_padded = [[up16(n) for n in row] for row in self.counts]

    def edge(self, b):
        return b in (0, self.count - 1)

    def sources(self, b):
        return self.own_padded[b] + self.side[b] + (self.slab_padded if self.edge(b) else 0)

    def source(self, b, i, j):
        columns, h, first = self.columns, self.height[b], self.first[b]
        at = self.own_padded[b]
        if not 0 <= i < self.rows:
            i = i + RIM_LAT if i < 0 else i - self.rows
            return at + self.side[b] + i * self.slab + j + SIDE
        if 0 <= j < columns:
            return (i - first) * columns + j
        at += (i - first) * SIDE
        return at + (j + SIDE if j < 0 else h * SIDE + j - columns)

    def key_matrix(self, b):
        g = np.zeros((len(self.widths) * self.window, self.sources(b)), np.float32)
        top = self.first[b] - (RIM_LAT if b == 0 else 0)
        for c in range(len(self.widths)):
            for i in range(WLAT):
                for j in range(WLON):
                    at = c * self.window + i * WLON + j
                    g[at, self.source(b, top + i, c * WLON - RIM_LON + j)] = 1
        return g.astype(BF16)

    def query_matrix(self, b):
        total = sum(self.counts_padded[b])
        g = np.zeros((total, self.own_padded[b]), np.float32)
        head = np.zeros((total,), np.int32)
        start = left = 0
        for width, padded in zip(self.widths, self.counts_padded[b]):
            at = start
            for k in range(GROUP):
                for i in range(self.height[b]):
                    for j in range(width):
                        g[at, i * self.columns + left + j] = 1
                        head[at] = k
                        at += 1
            left += width
            start += padded
        return g.astype(BF16), head

    def inner_patches(self):
        rows = range(self.rows // 2)
        inner = [r for r in rows if 2 * r >= RIM_LAT and 2 * r + 1 < self.rows - RIM_LAT]
        return inner, [r for r in rows if r not in inner]

    def patch_matrix(self, patch_rows, place, sources):
        half = self.columns // 2
        padded = up16(len(patch_rows) * half)
        g = np.zeros((4 * padded, sources), np.float32)
        for n, r in enumerate(patch_rows):
            for c in range(half):
                for k in range(4):
                    g[k * padded + n * half + c, place(2 * r + k // 2) + 2 * c + k % 2] = 1
        return g.astype(BF16)

    def inner_patch_matrix(self):
        return self.patch_matrix(
            self.inner_patches()[0],
            lambda i: (i - RIM_LAT) * self.columns,
            (self.rows - 2 * RIM_LAT) * self.columns,
        )

    def edge_patch_matrix(self):
        last = self.rows - RIM_LAT - 1
        return self.patch_matrix(
            self.inner_patches()[1],
            lambda i: (i if i <= RIM_LAT else RIM_LAT + 1 + i - last) * self.columns,
            2 * (RIM_LAT + 1) * self.columns,
        )

    def constants(self, some, block):
        distinct, kinds, consts = [], [], []
        for b in some:
            kind = (self.height[b], b == 0, b == self.count - 1)
            if kind not in distinct:
                distinct.append(kind)
                query, head = self.query_matrix(b)
                mask = head[:, None] == (np.arange(block) // (block // GROUP))[None, :]
                scale = np.float32((block // GROUP) ** -0.5)
                scaled = (query.astype(np.float32) * scale).astype(BF16)
                consts += [self.key_matrix(b), scaled, mask.astype(BF16), np.ascontiguousarray(query.T)]
            kinds.append(4 * distinct.index(kind))
        return kinds, consts


def normalize(values):
    center = values - jnp.mean(values, axis=-1, keepdims=True)
    spread = jnp.mean(center * center, axis=-1, keepdims=True)
    return center * lax.rsqrt(spread + 1e-05)


def dot(a, b, dims=((1,), (0,))):
    return lax.dot_general(a, b, (dims, ((), ())), preferred_element_type=F32)


def flat_normed(ref):
    values = ref[...].astype(F32)
    return normalize(values.reshape(-1, values.shape[-1]))


def project(normed_ref, weight_ref, out_ref):
    step = 256
    for at in range(0, out_ref.shape[1], step):
        out_ref[:, at : at + step] = dot(normed_ref[...], weight_ref[:, at : at + step]).astype(BF16)


def padded_rows(values, total):
    if values.shape[0] == total:
        return values
    return jnp.concatenate([values, jnp.zeros((total - values.shape[0], values.shape[1]), values.dtype)], axis=0)


def rims_kernel(tokens_ref, east_ref, west_ref):
    columns = tokens_ref.shape[1]
    east_ref[...] = tokens_ref[:, columns - SIDE :]
    west_ref[...] = tokens_ref[:, :SIDE]


def rims(tokens):
    rows, _, width = tokens.shape
    vmem = pl.BlockSpec(memory_space=pltpu.VMEM)
    return pl.pallas_call(
        rims_kernel,
        in_specs=[vmem],
        out_specs=[vmem] * 2,
        out_shape=[jax.ShapeDtypeStruct((rows, SIDE, width), BF16)] * 2,
        compiler_params=params(16),
        name="rims",
    )(tokens)


def halves_kernel(weight_ref, upper_ref, lower_ref, sems):
    half = upper_ref.shape[0]
    copies = [
        pltpu.make_async_copy(weight_ref.at[k * half : (k + 1) * half], ref, sems.at[k])
        for k, ref in enumerate((upper_ref, lower_ref))
    ]
    for copy in copies:
        copy.start()
    for copy in copies:
        copy.wait()


def halves_of(weight):
    depth, block = weight.shape
    return pl.pallas_call(
        halves_kernel,
        in_specs=[pl.BlockSpec(memory_space=pl.ANY)],
        out_specs=[pl.BlockSpec(memory_space=pltpu.VMEM)] * 2,
        out_shape=[jax.ShapeDtypeStruct((depth // 2, block), BF16)] * 2,
        scratch_shapes=[pltpu.SemaphoreType.DMA((2,))],
        compiler_params=params(52),
        name="halves",
    )(weight)


def own_kernel(bands, tokens_ref, weight_ref, out_ref, kv_ref, normed_ref, q_ref, sems):
    width = q_ref.shape[1]
    chunk = weight_ref.shape[1] // sems.shape[0]
    places = []
    for n in range(sems.shape[0]):
        at = n * chunk
        places.append((q_ref, at) if at < width else (kv_ref, at - width))
    copies = [
        pltpu.make_async_copy(weight_ref.at[:, pl.ds(n * chunk, chunk)], ref.at[:, pl.ds(at, chunk)], sems.at[n])
        for n, (ref, at) in enumerate(places)
    ]
    for copy in copies:
        copy.start()
    normed = flat_normed(tokens_ref)
    for b in range(bands.count):
        at = bands.first[b] * bands.columns
        part = padded_rows(normed[at : at + bands.own[b]], bands.own_padded[b])
        normed_ref[bands.own_at[b] : bands.own_at[b] + bands.own_padded[b], :] = part.astype(BF16)
    step = 256
    for n, (ref, first) in enumerate(places):
        copies[n].wait()
        for at in range(0, chunk, step):
            part = ref[:, first + at : first + at + step]
            out_ref[:, n * chunk + at : n * chunk + at + step] = dot(normed_ref[...], part).astype(BF16)


def own_projection(bands, tokens, weight):
    width, out = weight.shape
    vmem = pl.BlockSpec(memory_space=pltpu.VMEM)
    return pl.pallas_call(
        functools.partial(own_kernel, bands),
        in_specs=[vmem, pl.BlockSpec(memory_space=pl.ANY)],
        out_specs=[vmem, vmem],
        out_shape=[
            jax.ShapeDtypeStruct((bands.own_total, out), BF16),
            jax.ShapeDtypeStruct((width, out - width), BF16),
        ],
        scratch_shapes=[
            pltpu.VMEM((bands.own_total, width), BF16),
            pltpu.VMEM((width, width), BF16),
            pltpu.SemaphoreType.DMA((3,)),
        ],
        compiler_params=params(42),
        cost_estimate=pl.CostEstimate(
            flops=2 * bands.own_total * width * out, bytes_accessed=2 * width * out, transcendentals=0
        ),
        name="own_projection",
    )(tokens, weight)


def attend(bands, some, kinds, consts, own_ref, outer, bias_ref, put, scratch):
    k_ref, v_ref, q_ref, p_ref, r_ref = scratch
    width = own_ref.shape[1] // 3
    block = width * GROUP // HEADS
    window = WLAT * WLON
    units = [(n, b, g) for n, b in enumerate(some) for g in range(HEADS // GROUP)]
    for u, (n, b, g) in enumerate(units):
        keys, query, mask, _ = consts[kinds[n] : kinds[n] + 4]
        own = slice(bands.own_at[b], bands.own_at[b] + bands.own_padded[b])
        for ref, skip in ((k_ref, 0), (v_ref, width)):
            parts = [own_ref[own, width + skip + g * block : width + skip + (g + 1) * block]]
            for out_ref, at, size in outer(b):
                parts.append(out_ref[at : at + size, skip + g * block : skip + (g + 1) * block])
            ref[u] = dot(keys[...], jnp.concatenate(parts, axis=0)).astype(BF16)
        total = query.shape[0]
        q_ref[u, :total] = dot(query[...], own_ref[own, g * block : (g + 1) * block]).astype(BF16) * mask[...]
    for u, (n, b, g) in enumerate(units):
        at = 0
        for c, count in enumerate(bands.counts_padded[b]):
            scores = dot(
                q_ref[u, at : at + count], k_ref[u, c * bands.window : c * bands.window + window], ((1,), (1,))
            )
            if b == 0:
                scores = scores + bias_ref[0:1, :window]
            if b == bands.count - 1:
                scores = scores + bias_ref[1:2, :window]
            raised = jnp.exp(scores - jnp.max(scores, axis=-1, keepdims=True))
            weights = raised * (1.0 / jnp.sum(raised, axis=-1, keepdims=True))
            p_ref[u, at : at + count, :window] = weights.astype(BF16)
            at += count
    for u, (n, b, g) in enumerate(units):
        mask = consts[kinds[n] + 2]
        at = 0
        for c, count in enumerate(bands.counts_padded[b]):
            mixed = dot(
                p_ref[u, at : at + count, :window], v_ref[u, c * bands.window : c * bands.window + window]
            )
            r_ref[u, at : at + count] = mixed.astype(BF16) * mask[at : at + count]
            at += count
    for u, (n, b, g) in enumerate(units):
        back = consts[kinds[n] + 3]
        put(b, g, dot(back[...], r_ref[u, : back.shape[1]]).astype(BF16))


def attend_scratch(bands, some, block):
    units = len(some) * HEADS // GROUP
    keys = len(bands.widths) * bands.window
    rows = max(sum(bands.counts_padded[b]) for b in some)
    return [
        pltpu.VMEM((units, keys, block), BF16),
        pltpu.VMEM((units, keys, block), BF16),
        pltpu.VMEM((units, rows, block), BF16),
        pltpu.VMEM((units, rows, 128), BF16),
        pltpu.VMEM((units, rows, block), BF16),
    ]


def merge_rows(patch_ref, cells, upper_ref, lower_ref, first):
    width = cells.shape[1]
    padded = patch_ref.shape[0] // 4
    parts = [dot(patch_ref[k * padded : (k + 1) * padded, :], cells) for k in range(4)]
    total = sum(jnp.sum(p, axis=-1, keepdims=True) for p in parts)
    mean = total * (1.0 / (4 * width))
    parts = [p - mean for p in parts]
    spread = sum(jnp.sum(p * p, axis=-1, keepdims=True) for p in parts)
    factor = lax.rsqrt(spread * (1.0 / (4 * width)) + 1e-05)
    for k in range(4):
        ref = (upper_ref, lower_ref)[k // 2]
        ref[first : first + padded, k % 2 * width : (k % 2 + 1) * width] = (parts[k] * factor).astype(BF16)


def middle_kernel(bands, some, kinds, tokens_ref, west_ref, east_ref, own_ref, weight_ref, out_w_ref, patch_ref, *rest):
    consts, rest = rest[:-11], rest[-11:]
    side_ref, middle_ref, upper_ref, lower_ref, normed_ref, attended_ref, *scratch = rest
    rows, columns, width = tokens_ref.shape
    west, east = flat_normed(west_ref), flat_normed(east_ref)
    for b in range(bands.count):
        at, size = bands.first[b] * SIDE, bands.height[b] * SIDE
        part = jnp.concatenate([west[at : at + size], east[at : at + size]], axis=0)
        normed_ref[bands.side_at[b] : bands.side_at[b] + bands.side[b], :] = part.astype(BF16)
    project(normed_ref, weight_ref, side_ref)

    def outer(b):
        return [(side_ref, bands.side_at[b], bands.side[b])]

    def put(b, g, value):
        at = bands.own_at[b] - bands.own_at[1]
        block = value.shape[1]
        attended_ref[at : at + bands.own_padded[b], g * block : (g + 1) * block] = value

    attend(bands, some, kinds, consts, own_ref, outer, None, put, scratch)
    mixed = dot(attended_ref[...], out_w_ref[...])
    middle = tokens_ref[RIM_LAT : rows - RIM_LAT].astype(F32) + mixed.reshape(-1, columns, width)
    middle_ref[...] = middle.astype(BF16)
    merge_rows(patch_ref, middle.reshape(-1, width).astype(BF16), upper_ref, lower_ref, 0)


def edge_kernel(bands, some, kinds, tokens_ref, north_ref, south_ref, bias_ref, own_ref, side_ref, inner_ref, inner_upper_ref, inner_lower_ref, weight_ref, out_w_ref, patch_ref, *rest):
    consts, rest = rest[:-11], rest[-11:]
    middle_ref, upper_ref, lower_ref, normed_ref, slab_ref, attended_ref, *scratch = rest
    rows, columns, width = tokens_ref.shape
    slab = bands.slab_padded
    for k, ref in enumerate((north_ref, south_ref)):
        normed_ref[k * slab : (k + 1) * slab, :] = padded_rows(flat_normed(ref), slab).astype(BF16)
    project(normed_ref, weight_ref, slab_ref)

    def outer(b):
        return [
            (side_ref, bands.side_at[b], bands.side[b]),
            (slab_ref, 0 if b == 0 else slab, slab),
        ]

    def put(b, g, value):
        block = value.shape[1]
        at = 0 if b == 0 else bands.own_padded[0]
        attended_ref[at : at + bands.own_padded[b], g * block : (g + 1) * block] = value

    attend(bands, some, kinds, consts, own_ref, outer, bias_ref, put, scratch)
    mixed = dot(attended_ref[...], out_w_ref[...])
    low = bands.own_padded[0]
    top = tokens_ref[:RIM_LAT].astype(F32) + mixed[: bands.own[0]].reshape(-1, columns, width)
    bottom = tokens_ref[rows - RIM_LAT :].astype(F32) + mixed[low : low + bands.own[-1]].reshape(-1, columns, width)
    middle_ref[:RIM_LAT] = top.astype(BF16)
    middle_ref[RIM_LAT : rows - RIM_LAT] = inner_ref[...]
    middle_ref[rows - RIM_LAT :] = bottom.astype(BF16)
    first, last = inner_ref[0].astype(F32), inner_ref[rows - 2 * RIM_LAT - 1].astype(F32)
    cells = jnp.concatenate([top.reshape(-1, width), first, last, bottom.reshape(-1, width)], axis=0)
    inner_count = inner_upper_ref.shape[0]
    upper_ref[:inner_count, :] = inner_upper_ref[...]
    lower_ref[:inner_count, :] = inner_lower_ref[...]
    merge_rows(patch_ref, cells.astype(BF16), upper_ref, lower_ref, inner_count)


def vmem_call(kernel, out, args, scratch, flops, name, mib=24, exps=0):
    vmem = pl.BlockSpec(memory_space=pltpu.VMEM)
    return pl.pallas_call(
        kernel,
        in_specs=[vmem] * len(args),
        out_specs=[vmem] * len(out),
        out_shape=[jax.ShapeDtypeStruct(shape, BF16) for shape in out],
        scratch_shapes=scratch,
        compiler_params=params(mib),
        cost_estimate=pl.CostEstimate(flops=flops, bytes_accessed=2**20, transcendentals=exps),
        name=name,
    )(*args)


def attention(bands, tokens, sides, qkv_weight, out_weight):
    rows, columns, width = tokens.shape
    block = width * GROUP // HEADS
    west = shift(sides[0], "lon", 1, True)
    east = shift(sides[1], "lon", -1, True)
    own, kv_weight = own_projection(bands, tokens, qkv_weight)

    def slab(part):
        return jnp.concatenate([west[part], tokens[part], east[part]], axis=1)

    north = shift(slab(slice(rows - RIM_LAT, rows)), "lat", 1, False)
    south = shift(slab(slice(0, RIM_LAT)), "lat", -1, False)
    inner = list(range(1, bands.count - 1))
    edges = [0, bands.count - 1]
    kinds, consts = bands.constants(inner, block)
    patch = bands.inner_patch_matrix()
    inner_count = patch.shape[0] // 4
    side, middle, upper, lower = vmem_call(
        functools.partial(middle_kernel, bands, inner, kinds),
        [
            (bands.side_total, 2 * width),
            (rows - 2 * RIM_LAT, columns, width),
            (inner_count, 2 * width),
            (inner_count, 2 * width),
        ],
        [tokens, west, east, own, kv_weight, out_weight, patch] + consts,
        [
            pltpu.VMEM((bands.side_total, width), BF16),
            pltpu.VMEM((bands.own_at[-1] - bands.own_at[1], width), BF16),
        ]
        + attend_scratch(bands, inner, block),
        5 * 10**9,
        "middle_attention",
        exps=500000,
    )
    kinds, consts = bands.constants(edges, block)
    patch = bands.edge_patch_matrix()
    count = inner_count + patch.shape[0] // 4
    return vmem_call(
        functools.partial(edge_kernel, bands, edges, kinds),
        [tokens.shape, (count, 2 * width), (count, 2 * width)],
        [tokens, north, south, key_bias(), own, side, middle, upper, lower, kv_weight, out_weight, patch] + consts,
        [
            pltpu.VMEM((2 * bands.slab_padded, width), BF16),
            pltpu.VMEM((2 * bands.slab_padded, 2 * width), BF16),
            pltpu.VMEM((bands.own_padded[0] + bands.own_padded[-1], width), BF16),
        ]
        + attend_scratch(bands, edges, block),
        6 * 10**9,
        "edge_attention",
        exps=300000,
    )


def shift(part, axis, step, wrap):
    size = lax.axis_size(axis)
    pairs = [(i, (i + step) % size) for i in range(size) if wrap or 0 <= i + step < size]
    return lax.ppermute(part, axis, pairs)


def key_bias():
    row = jnp.arange(8, dtype=jnp.int32)[:, None]
    key = jnp.arange(128, dtype=jnp.int32)[None, :] // WLON
    north = (row == 0) & (key < RIM_LAT) & (lax.axis_index("lat") == 0)
    south = (row == 1) & (key >= RIM_LAT) & (lax.axis_index("lat") == lax.axis_size("lat") - 1)
    return jnp.where(north | south, F32(-1e30), F32(0.0))


def place_index():
    me = lax.axis_index("lon")
    return jnp.stack([me // 2, me % 2]).astype(jnp.int32)


def merge_dots(place_ref, upper, lower, mine_ref, pair_ref, x_ref, x_pair_ref, y_ref, y_pair_ref, refs):
    half, block = x_ref.shape
    at = [pl.ds(pl.multiple_of((place_ref[1] + k) % 2 * block, block), block) for k in range(2)]
    own, x, y = refs
    for k, ref in enumerate((mine_ref, pair_ref)):
        own(at[k], dot(upper, ref[:half, :]), dot(lower, ref[half:, :]))
    for k, ref in enumerate((x_ref, x_pair_ref)):
        x(at[k], dot(upper, ref[...]))
    for k, ref in enumerate((y_ref, y_pair_ref)):
        y(at[k], dot(lower, ref[...]))


def merge_own_kernel(place_ref, upper_ref, lower_ref, *refs):
    weights, (own_ref, x_ref, y_ref), kept = refs[:6], refs[6:9], refs[9:]
    for ref, to in zip(weights[1:], kept):
        to[...] = ref[...]

    def own(at, a, b):
        own_ref[:, at] = a + b

    def x(at, a):
        x_ref[:, at] = a

    def y(at, b):
        y_ref[:, at] = b

    merge_dots(place_ref, upper_ref[...], lower_ref[...], *weights, (own, x, y))


def merge_other_kernel(place_ref, upper_ref, lower_ref, *refs):
    weights, (to_y_ref, to_x_ref) = refs[:6], refs[6:]
    wide = to_x_ref.shape[1] // 2

    def own(at, a, b):
        to_y_ref[:, at] = a.astype(BF16)
        to_x_ref[:, at] = b.astype(BF16)

    def x(at, a):
        to_y_ref[:, pl.ds(pl.multiple_of(wide + at.start, at.size), at.size)] = a.astype(BF16)

    def y(at, b):
        to_x_ref[:, pl.ds(pl.multiple_of(wide + at.start, at.size), at.size)] = b.astype(BF16)

    merge_dots(place_ref, upper_ref[...], lower_ref[...], *weights, (own, x, y))


def combine_kernel(place_ref, own_ref, x_ref, y_ref, from_y_ref, from_x_ref, out_ref):
    wide = own_ref.shape[1]
    chip = place_ref[0]
    from_x, from_y = from_x_ref[...].astype(F32), from_y_ref[...].astype(F32)
    parts = [
        own_ref[...],
        x_ref[...] + from_x[:, :wide],
        y_ref[...] + from_y[:, :wide],
        from_x[:, wide:] + from_y[:, wide:],
    ]
    for m, part in enumerate(parts):
        out_ref[:, pl.ds(pl.multiple_of((chip ^ m) * wide, wide), wide)] = part.astype(BF16)


def local_call(kernel, out, place, args, flops, name, mib=12):
    vmem = pl.BlockSpec(memory_space=pltpu.VMEM)
    return pl.pallas_call(
        kernel,
        in_specs=[pl.BlockSpec(memory_space=pltpu.SMEM)] + [vmem] * len(args),
        out_specs=[vmem] * len(out),
        out_shape=out,
        compiler_params=params(mib),
        cost_estimate=pl.CostEstimate(flops=flops, bytes_accessed=2**20, transcendentals=0),
        name=name,
    )(place, *args)


def merge_by_squares(upper, lower, merge_weight, halves):
    half = merge_weight.shape[0] // 2
    block = merge_weight.shape[1]
    count = upper.shape[0]
    x = chip_swap(halves[0], 1)
    y = chip_swap(halves[1], 2)
    x_pair, y_pair, _ = lax.optimization_barrier((x, y, upper))
    weights = [merge_weight, core_swap(merge_weight), x, core_swap(x_pair), y, core_swap(y_pair)]
    place = place_index()
    from_y = chip_swap(upper, 2)
    from_x = chip_swap(lower, 1)
    flops = 16 * count * half * block
    wide = jax.ShapeDtypeStruct((count, 2 * block), F32)
    kept = [jax.ShapeDtypeStruct(w.shape, BF16) for w in weights[1:]]
    *own, b, c, d, e, f = local_call(
        merge_own_kernel, [wide] * 3 + kept, place, [upper, lower] + weights, flops, "merge_own", 20
    )
    weights = [merge_weight, b, c, d, e, f]
    pair = jax.ShapeDtypeStruct((count, 4 * block), BF16)
    to_y, to_x = local_call(merge_other_kernel, [pair] * 2, place, [from_y, from_x] + weights, flops, "merge_other")
    back_y, back_x = chip_swap(to_y, 2), chip_swap(to_x, 1)
    out = jax.ShapeDtypeStruct((count, 8 * block), BF16)
    return local_call(combine_kernel, [out], place, [*own, back_y, back_x], 0, "combine")[0]


def ffn_kernel(mine_ref, theirs_ref, up_ref, down_ref, out_mine_ref, low_ref, high_ref, normed_ref, hidden_ref):
    count = mine_ref.shape[0]
    for k, ref in enumerate((mine_ref, theirs_ref)):
        normed_ref[k * count : (k + 1) * count, :] = normalize(ref[...].astype(F32)).astype(BF16)
    hidden = hidden_ref.shape[1]
    step = 256
    for at in range(0, hidden, step):
        raw = dot(normed_ref[...], up_ref[:, at : at + step])
        active = 0.5 * raw * (1.0 + lax.erf(raw * np.float32(np.sqrt(0.5))))
        hidden_ref[:, at : at + step] = active.astype(BF16)
    half = low_ref.shape[1]
    for at in range(0, 2 * half, step):
        out = dot(hidden_ref[...], down_ref[:, at : at + step]).astype(BF16)
        out_mine_ref[:, at : at + step] = out[:count]
        ref = low_ref if at < half else high_ref
        ref[:, at % half : at % half + step] = out[count:]


def feed_forward(mine, theirs, up, down):
    count = mine.shape[0]
    width, hidden = up.shape
    vmem = pl.BlockSpec(memory_space=pltpu.VMEM)
    return pl.pallas_call(
        ffn_kernel,
        in_specs=[vmem] * 4,
        out_specs=[vmem] * 3,
        out_shape=[jax.ShapeDtypeStruct((count, width // n), BF16) for n in (1, 2, 2)],
        scratch_shapes=[pltpu.VMEM((2 * count, width), BF16), pltpu.VMEM((2 * count, hidden), BF16)],
        compiler_params=params(20),
        cost_estimate=pl.CostEstimate(
            flops=8 * count * width * hidden, bytes_accessed=4 * width * hidden, transcendentals=2 * count * hidden
        ),
        name="feed_forward",
    )(mine, theirs, up, down)


def added(mine, low, high):
    return (mine.astype(F32) + jnp.concatenate([low, high], axis=1).astype(F32)).astype(BF16)


def summed(mine, low, high):
    return added(mine, core_swap(low), core_swap(high))


def core_swap(value):
    size = lax.axis_size("lon")
    return lax.ppermute(value, "lon", [(i, i ^ 1) for i in range(size)])


def chip_swap(value, offset):
    size = lax.axis_size("lon")
    return lax.ppermute(value, "lon", [(i, i ^ (2 * offset)) for i in range(size)])


def cross(value, first, second):
    size = lax.axis_size("lon")
    return lax.ppermute(value, "lon", [(i, i ^ (2 * (second if i % 2 else first))) for i in range(size)])


def coarse_by_squares(upper, lower, merge_weight, halves, up, down):
    own = merge_by_squares(upper, lower, merge_weight, halves)
    near = cross(own, 1, 2)
    first = feed_forward(own, core_swap(own), up, down)
    near, *first = lax.optimization_barrier((near, *first))
    far = cross(near, 2, 1)
    near_mine, near_low, near_high = feed_forward(near, core_swap(near), up, down)
    later, near_mine = lax.optimization_barrier((own, near_mine))
    other = cross(later, 2, 1)
    near_low, far = lax.optimization_barrier((core_swap(near_low), far))
    mine, low, high = feed_forward(far, core_swap(far), up, down)
    low, other = lax.optimization_barrier((core_swap(low), other))
    far_sum = added(mine, low, core_swap(high))
    pair, far_sum = lax.optimization_barrier((core_swap(other), far_sum))
    relayed = cross(far_sum, 2, 1)
    mine, low, high = feed_forward(other, pair, up, down)
    relayed, low = lax.optimization_barrier((relayed, core_swap(low)))
    other_back = cross(added(mine, low, core_swap(high)), 2, 1)
    half = low.shape[1]
    near_back = []
    for part, at in ((near_low, 0), (core_swap(near_high), half)):
        columns = slice(at, at + half)
        total = near_mine[:, columns].astype(F32) + part.astype(F32) + relayed[:, columns].astype(F32)
        near_back.append(cross(total.astype(BF16), 1, 2))
    return [own, summed(*first), other_back], near_back


def coarse_by_chips(upper, lower, merge_weight, halves, up, down):
    weight = lax.all_gather(merge_weight, "lon", axis=1, tiled=True)
    patches = jnp.concatenate([upper, lower], axis=1)
    coarse = jnp.dot(patches, weight, preferred_element_type=F32).astype(BF16)
    chips = lax.axis_size("lon") // 2
    arrived = [coarse] + [chip_swap(coarse, m) for m in range(1, chips)]
    total = coarse.astype(F32)
    for m in range(chips):
        part = summed(*feed_forward(arrived[m], core_swap(arrived[m]), up, down))
        total = total + (chip_swap(part, m) if m else part).astype(F32)
    return [total.astype(BF16)], []


def finish_kernel(spans, *refs):
    *parts, low_ref, high_ref, out_ref = refs
    total = sum(ref[...].astype(F32) for ref in parts)
    if low_ref is not None:
        total = total + jnp.concatenate([low_ref[...], high_ref[...]], axis=1).astype(F32)
    for r, at in enumerate(spans):
        out_ref[r] = total[at : at + out_ref.shape[1]].astype(BF16)


def finish(bands, whole, halves):
    inner, edge = bands.inner_patches()
    half = bands.columns // 2
    start = up16(half * len(inner))
    place = {r: n * half for n, r in enumerate(inner)} | {r: start + n * half for n, r in enumerate(edge)}
    spans = [place[r] for r in range(bands.rows // 2)]
    vmem = pl.BlockSpec(memory_space=pltpu.VMEM)

    def kernel(*refs):
        finish_kernel(spans, *(refs if halves else (*refs[:-1], None, None, refs[-1])))

    return pl.pallas_call(
        kernel,
        in_specs=[vmem] * (len(whole) + len(halves)),
        out_specs=vmem,
        out_shape=jax.ShapeDtypeStruct((bands.rows // 2, half, whole[0].shape[1]), BF16),
        compiler_params=params(16),
        name="finish",
    )(*whole, *halves)


def per_device(tokens, qkv_weight, out_weight, merge_weight, up_weight, down_weight):
    rows, columns, width = tokens.shape
    bands = Bands(rows, columns)
    sides = rims(tokens)
    *sides, later = lax.optimization_barrier((*sides, merge_weight))
    halves = halves_of(later)
    middle_out, upper, lower = attention(bands, tokens, sides, qkv_weight, out_weight)
    coarse = coarse_by_squares if lax.axis_size("lon") == 8 else coarse_by_chips
    parts = coarse(upper, lower, merge_weight, halves, up_weight, down_weight)
    return (middle_out, finish(bands, *parts))


def solution(mesh):
    return jax.shard_map(
        per_device,
        mesh=mesh,
        in_specs=(P("lat", "lon", None), P(), P(), P(None, "lon"), P(None, "lon"), P("lon", None)),
        out_specs=(P("lat", "lon", None), P("lat", "lon", None)),
        check_vma=False,
    )
```
